512 devices in a mesh: gx: 16 (over z, core), gy: 32 (over x, y).
Axes of the slice: x: 4, y: 8, z: 8, core: 2. Of those that a mesh axis runs over, the one named last changes fastest.
Arguments:
- right_sides: float32 [64, 524288], P(None, ('gx', 'gy')), may hold values from -6 to 6
- points: float32 [3, 524288], P(None, ('gx', 'gy'))
- leaf_basis: bfloat16 [64, 524288], P(None, ('gx', 'gy')), may hold values from -0.75 to 0.75
- leaf_transfer: bfloat16 [64, 524288], P(None, ('gx', 'gy')), may hold values from -0.75 to 0.75
- upper_transfer: float32 [7, 2, 64, 64], replicated, may hold values from -0.5 to 0.5
- coupling: float32 [8, 3, 64, 64], replicated, may hold values from -0.109375 to 0.109375
- near_leaves: int32 [8192, 12], P(('gx', 'gy')), may hold values from 0 to 8191, as said below
- admissible: int32 [1020, 3], replicated, may hold values 0 or 1
Outputs:
- product: float32 [64, 524288], P(None, ('gx', 'gy'))
The draws below stay inside these ranges and needn't reach their ends.
Inputs may be any that keep to these rules, and one draw needn't show every extreme that they name: `near_leaves`: each row lists 12 different leaves, all owned by the four devices whose gx index and gy index equal those of the row's own device but for the lowest bit.
All inputs are finite; a program needn't handle non-finite values.
Results may differ from the reference program's by a relative error of at most 0.0037.
Values sent between devices are 32-bit elements; how exact they have to be, the bound alone decides.
No kernel may reach another device: no remote copies, remote signals or barrier semaphores. Data moves between devices by JAX's collectives and lax.ppermute only.
A program may use at most 128 MiB of HBM per device.

```python
import jax
import jax.numpy as jnp
import numpy as np
from jax import lax

LEAF = 64
RANK = 64
PROBES = 64
NEAR = 12
LEAVES_DEV = 16
LEVELS = 9
LEAVES = 8192
POINTS = 524288
NODES = 1020
N_GX = 16
N_GY = 32
DEVICES = 512


def bit_layout_drawn(count_x, count_y):
    bits_x = count_x.bit_length() - 1
    bits_y = count_y.bit_length() - 1
    layout = []
    used_x = 0
    used_y = 0
    while used_x < bits_x or used_y < bits_y:
        if used_x < bits_x:
            layout.append((0, used_x))
            used_x += 1
        if used_y < bits_y:
            layout.append((1, used_y))
            used_y += 1
    return layout


def device_codes_drawn(count_x, count_y):
    layout = bit_layout_drawn(count_x, count_y)
    codes = np.zeros(count_x * count_y, np.int32)
    for device in range(count_x * count_y):
        places = (device // count_y, device % count_y)
        value = 0
        for place, (axis, bit) in enumerate(layout):
            value += (places[axis] >> bit & 1) << place
        codes[device] = value
    return codes


def leaf_cells():
    codes = jnp.asarray(device_codes_drawn(N_GX, N_GY), jnp.int32)
    leaf = jnp.arange(LEAVES, dtype=jnp.int32)
    tree_code = codes[leaf // LEAVES_DEV] * LEAVES_DEV + leaf % LEAVES_DEV
    total_bits = max(1, (LEAVES - 1).bit_length())
    cells = []
    for axis in range(3):
        cell = jnp.zeros((LEAVES,), jnp.int32)
        level = 0
        while 3 * level + axis < total_bits:
            cell = cell + tree_code // 2 ** (3 * level + axis) % 2 * 2 ** level
            level += 1
        cells.append(cell)
    return jnp.stack(cells).astype(jnp.int32)


def draw_points(key, part):
    key = jax.random.fold_in(key, 11)
    corner = leaf_cells().astype(jnp.float32)
    jitter = jax.random.uniform(key, (3, LEAVES, LEAF), jnp.float32)
    return (corner[:, :, None] + jitter).reshape(3, POINTS)


def draw_near_leaves(key, part):
    key = jax.random.fold_in(key, 23)
    group = 4 * LEAVES_DEV
    keys = jax.random.split(key, LEAVES)

    def rank_row(row_key):
        return jax.random.permutation(row_key, group)
    tie_rank = jax.vmap(rank_row)(keys).astype(jnp.int32)
    leaf = jnp.arange(LEAVES, dtype=jnp.int32)
    device = leaf // LEAVES_DEV
    row_x = device // N_GY
    column_y = device % N_GY
    base_x = row_x - row_x % 2
    base_y = column_y - column_y % 2
    slots = jnp.arange(group, dtype=jnp.int32)
    member = slots // LEAVES_DEV
    within = slots % LEAVES_DEV
    holder = (base_x[:, None] + member[None, :] // 2) * N_GY + base_y[:, None] + member[None, :] % 2
    candidates = holder * LEAVES_DEV + within[None, :]
    cells = leaf_cells()
    offsets = jnp.take(cells, candidates, axis=1) - cells[:, :, None]
    distance = jnp.sum(offsets * offsets, axis=0)
    scores = distance * group + tie_rank
    ordering = jnp.argsort(scores, axis=1)[:, :NEAR]
    return jnp.take_along_axis(candidates, ordering, axis=1).astype(jnp.int32)


def set_ends(values, rng, least, top_value):
    spot = [jax.random.randint(jax.random.fold_in(rng, axis), (), 0, length) for axis, length in enumerate(values.shape)]
    widest = values.shape.index(max(values.shape))
    next_to = spot[:widest] + [(spot[widest] + 1) % values.shape[widest]] + spot[widest + 1:]
    return values.at[tuple(spot)].set(least).at[tuple(next_to)].set(top_value)


def levels(key, dims, cuts, smallest, high):
    level, own = 1.0, jax.random.fold_in(key, 6)
    for position, blocks in cuts:
        heights = jnp.exp(jax.random.uniform(jax.random.fold_in(own, position), (blocks,), jnp.float32, smallest / len(cuts), high / len(cuts)))
        level = level * jnp.repeat(heights, dims[position] // blocks).reshape([-1 if axis == position else 1 for axis in range(len(dims))])
    return level


def scatter_about(key, shape, deviation, reach, cuts=(), held_as=jnp.bfloat16):
    entries = jax.random.normal(key, shape, jnp.float32) * deviation
    if len(cuts) > 0:
        entries = levels(key, shape, cuts, -0.22, 0.18) * entries
    return jnp.clip(entries, min=-reach, max=reach).astype(held_as)


def setup_inputs(seed: int = 0) -> dict:
    key_list = jax.random.split(jax.random.key(seed), 9)
    right_sides = scatter_about(key_list[0], (PROBES, POINTS), 1.0, 6.0, ((1, 512),), jnp.float32)
    points = draw_points(jax.random.fold_in(key_list[8], 71), 0)
    leaf_basis = scatter_about(key_list[2], (RANK, POINTS), LEAF ** -0.5, 0.75, ((1, 512),))
    leaf_transfer = scatter_about(key_list[3], (RANK, LEAVES * RANK), RANK ** -0.5, 0.75, ((1, 512),))
    upper_transfer = scatter_about(key_list[4], (LEVELS - 2, 2, RANK, RANK), (2 * RANK) ** -0.5, 0.5, (), jnp.float32)
    coupling = scatter_about(key_list[5], (LEVELS - 1, 3, RANK, RANK), (3 * RANK * LEAVES_DEV) ** -0.5, 0.109375, (), jnp.float32)
    near_leaves = draw_near_leaves(jax.random.fold_in(key_list[8], 71), 0)
    admissible = set_ends((jax.random.randint(key_list[7], (NODES, 3), 0, 4) < 3).astype(jnp.int32), jax.random.fold_in(key_list[7], 1), 0, 1)
    return {"right_sides": right_sides, "points": points, "leaf_basis": leaf_basis, "leaf_transfer": leaf_transfer, "upper_transfer": upper_transfer, "coupling": coupling, "near_leaves": near_leaves, "admissible": admissible}


ROOT_THREE = 1.7320508075688772
LENGTH_SCALE = 0.6
AMPLITUDE = 0.25
NUGGET = 0.5
HIGHEST = lax.Precision.HIGHEST

def bit_layout(count_x, count_y):
    bits_x = count_x.bit_length() - 1
    bits_y = count_y.bit_length() - 1
    layout = []
    used_x = 0
    used_y = 0
    while used_x < bits_x or used_y < bits_y:
        if used_x < bits_x:
            layout.append((0, used_x))
            used_x += 1
        if used_y < bits_y:
            layout.append((1, used_y))
            used_y += 1
    return layout

def device_codes(count_x, count_y):
    layout = bit_layout(count_x, count_y)
    codes = np.zeros(count_x * count_y, np.int32)
    for device in range(count_x * count_y):
        places = (device // count_y, device % count_y)
        value = 0
        for place, (axis, bit) in enumerate(layout):
            value += (places[axis] >> bit & 1) << place
        codes[device] = value
    return codes

def matern(targets, sources):
    square = jnp.zeros((targets.shape[1], targets.shape[2], sources.shape[2]), jnp.float32)
    for axis in range(3):
        delta = targets[axis][:, :, None] - sources[axis][:, None, :]
        square = square + delta * delta
    scaled = ROOT_THREE / LENGTH_SCALE * jnp.sqrt(square)
    return AMPLITUDE * (1.0 + scaled) * jnp.exp(-scaled)

def climb_level(lower, upper, transfer):
    first = jnp.einsum('nrc,cp->nrp', lower, transfer[0], precision=HIGHEST)
    second = jnp.einsum('nrc,cp->nrp', upper, transfer[1], precision=HIGHEST)
    return first + second

def reference(right_sides, points, leaf_basis, leaf_transfer, upper_transfer, coupling, near_leaves, admissible):
    codes = device_codes(N_GX, N_GY)
    ordering = np.argsort(codes)
    values_leaf = right_sides.reshape(PROBES, LEAVES, LEAF)
    rounded_leaf = right_sides.astype(jnp.bfloat16).reshape(PROBES, LEAVES, LEAF)
    basis_leaf = leaf_basis.reshape(RANK, LEAVES, LEAF)
    points_leaf = points.reshape(3, LEAVES, LEAF)
    block_leaves = min(LEAVES_DEV, max(1, 512 // LEAF))

    def upward(device):
        first = (device * LEAVES_DEV).astype(jnp.int32)
        rounded = lax.dynamic_slice_in_dim(rounded_leaf, first, LEAVES_DEV, 1).astype(jnp.float32)
        basis = lax.dynamic_slice_in_dim(basis_leaf, first, LEAVES_DEV, 1).astype(jnp.float32)
        leaf_coeff = jnp.einsum('rlp,klp->rlk', rounded, basis).astype(jnp.bfloat16)
        transfer = lax.dynamic_slice_in_dim(leaf_transfer, (first * RANK).astype(jnp.int32), LEAVES_DEV * RANK, 1)
        return jnp.dot(leaf_coeff.reshape(PROBES, LEAVES_DEV * RANK), transfer.T, preferred_element_type=jnp.float32)
    device_coeff = lax.map(upward, jnp.arange(DEVICES, dtype=jnp.int32))
    climbs = [device_coeff[jnp.asarray(ordering, jnp.int32)]]
    for height in range(1, LEVELS - 1):
        paired = climbs[-1].reshape(-1, 2, PROBES, RANK)
        climbs.append(climb_level(paired[:, 0], paired[:, 1], upper_transfer[height - 1]))
    flags = admissible.astype(jnp.float32)
    far = []
    for height in range(LEVELS - 1):
        count = DEVICES // 2 ** height
        node = np.arange(count)
        start = 2 * DEVICES - 2 * DEVICES // 2 ** height
        total = None
        for flipped in (1, 2, 3):
            partner = node ^ flipped
            here = node % 4
            there = partner % 4
            offset = np.abs(there - here) - 1
            matrices = coupling[height][jnp.asarray(offset, jnp.int32)]
            matrices = jnp.where(jnp.asarray(there > here)[:, None, None], jnp.swapaxes(matrices, 1, 2), matrices)
            flag = flags[start:start + count, flipped - 1]
            product = jnp.einsum('nrc,nck->nrk', climbs[height][jnp.asarray(partner, jnp.int32)], matrices, precision=HIGHEST)
            term = flag[:, None, None] * product
            total = term if total is None else total + term
        far.append(total)
    down = far[LEVELS - 2]
    for height in range(LEVELS - 3, -1, -1):
        count = DEVICES // 2 ** height
        node = np.arange(count)
        transfer = upper_transfer[height][jnp.asarray(node % 2, jnp.int32)]
        parent = down[jnp.asarray(node // 2, jnp.int32)]
        down = far[height] + jnp.einsum('nrp,ncp->nrc', parent, transfer, precision=HIGHEST)
    device_down = down[jnp.asarray(codes, jnp.int32)]

    def downward(device):
        first = (device * LEAVES_DEV).astype(jnp.int32)
        own_down = lax.dynamic_index_in_dim(device_down, device, 0, keepdims=False).astype(jnp.bfloat16)
        transfer = lax.dynamic_slice_in_dim(leaf_transfer, (first * RANK).astype(jnp.int32), LEAVES_DEV * RANK, 1)
        leaf_down = jnp.dot(own_down, transfer, preferred_element_type=jnp.float32).astype(jnp.bfloat16)
        leaf_down = leaf_down.reshape(PROBES, LEAVES_DEV, RANK).astype(jnp.float32)
        basis = lax.dynamic_slice_in_dim(basis_leaf, first, LEAVES_DEV, 1).astype(jnp.float32)
        far_field = jnp.einsum('rlk,klp->rlp', leaf_down, basis)
        listed = lax.dynamic_slice_in_dim(near_leaves, first, LEAVES_DEV, 0)
        targets = lax.dynamic_slice_in_dim(points_leaf, first, LEAVES_DEV, 1)

        def near_block(begin):
            chosen = lax.dynamic_slice_in_dim(listed, begin, block_leaves, 0)
            source_values = jnp.take(values_leaf, chosen, axis=1).reshape(PROBES, block_leaves, NEAR * LEAF)
            source_points = jnp.take(points_leaf, chosen, axis=1).reshape(3, block_leaves, NEAR * LEAF)
            target_points = lax.dynamic_slice_in_dim(targets, begin, block_leaves, 1)
            weights = matern(target_points, source_points)
            return jnp.einsum('bts,rbs->rbt', weights, source_values, precision=HIGHEST)
        near_parts = lax.map(near_block, jnp.arange(0, LEAVES_DEV, block_leaves, dtype=jnp.int32))
        near_field = jnp.moveaxis(near_parts, 0, 1).reshape(PROBES, LEAVES_DEV, LEAF)
        values = lax.dynamic_slice_in_dim(values_leaf, first, LEAVES_DEV, 1)
        return near_field + far_field + NUGGET * values
    blocks = lax.map(downward, jnp.arange(DEVICES, dtype=jnp.int32))
    return jnp.moveaxis(blocks, 0, 1).reshape(PROBES, POINTS)
```

```python
import jax
import jax.numpy as jnp
from jax import lax
from jax.experimental import pallas as pl
from jax.experimental.pallas import tpu as pltpu
from jax.sharding import PartitionSpec as P

ROOT_THREE = 1.7320508075688772
LENGTH_SCALE = 0.6
AMPLITUDE = 0.25
NUGGET = 0.5
LOG2_E = 1.4426950408889634
BITS_X = 4
BITS_Y = 5
DEVICES = 512
LEVELS = 9
LEAVES = 16
LEAF = 64
RANK = 64
HALF = 64
LANES = 128
F32 = jnp.float32
BF16 = jnp.bfloat16
NT = (((1,), (1,)), ((), ()))
VMEM = pl.BlockSpec(memory_space=pltpu.VMEM)
SMEM = pl.BlockSpec(memory_space=pltpu.SMEM)
PARAMS = pltpu.CompilerParams(vmem_limit_bytes=40 * 1024 * 1024)


def places():
    listed = []
    for bit in range(max(BITS_X, BITS_Y)):
        if bit < BITS_X:
            listed.append(("x", bit))
        if bit < BITS_Y:
            listed.append(("y", bit))
    return listed


PLACES = places()
BELOW_X = [sum(axis == "x" for axis, _ in PLACES[:h]) for h in range(LEVELS)]
BELOW_Y = [sum(axis == "y" for axis, _ in PLACES[:h]) for h in range(LEVELS)]

CLIMB, DOWN, FAR = {}, {}, {}
for _h in range(LEVELS - 2):
    for _side in range(2 if PLACES[_h][0] == "y" else 1):
        CLIMB[_h, _side] = len(CLIMB)
for _h in range(LEVELS - 2):
    for _side in range(2 if PLACES[_h][0] == "x" else 1):
        DOWN[_h, _side] = len(CLIMB) + len(DOWN)
for _h in range(LEVELS - 1):
    for _term in range(3):
        FAR[_h, _term] = len(CLIMB) + len(DOWN) + len(FAR)
WEIGHTS = len(CLIMB) + len(DOWN) + len(FAR)


def low_lanes(rows):
    return lax.broadcasted_iota(jnp.int32, (rows, LANES), 1) < HALF


def split_lanes(value):
    high = value.astype(BF16).astype(F32)
    return jnp.where(low_lanes(value.shape[0]), high, value - high).astype(BF16)


def block_diagonal(basis):
    wide = basis.astype(F32)
    leaf = lax.broadcasted_iota(jnp.int32, wide.shape, 1) // LEAF
    return jnp.concatenate([jnp.where(leaf == l, wide, 0.0).astype(BF16) for l in range(4)], axis=0)


def up_kernel(right_ref, points_ref, basis_ref, transfer_ref, coeff_ref, send_ref):
    total = None
    for block in range(4):
        cols = slice(block * 256, block * 256 + 256)
        rounded = right_ref[:, cols].astype(BF16)
        leaf_coeff = lax.dot_general(
            rounded, block_diagonal(basis_ref[:, cols]), NT, preferred_element_type=F32
        ).astype(BF16)
        transfer = transfer_ref[:, cols]
        part = lax.dot_general(
            leaf_coeff,
            jnp.concatenate([transfer, transfer], axis=0),
            NT,
            preferred_element_type=F32,
        )
        total = part if total is None else total + part
    coeff_ref[...] = jnp.where(low_lanes(32), total[:32], total[32:])
    send_ref[:64, :] = right_ref[...]
    send_ref[64:72, :] = jnp.zeros((8, LEAVES * LEAF), F32)
    send_ref[64:67, :] = points_ref[...]


def weights_kernel(upper_ref, coupling_ref, admissible_ref, out_ref):
    index_x = lax.axis_index("gx")
    index_y = lax.axis_index("gy")
    side = [(index_x if axis == "x" else index_y) >> bit & 1 for axis, bit in PLACES]
    code = jnp.int32(0)
    for place in range(LEVELS):
        code = code + side[place] * 2**place

    def store(slot, wide):
        high = wide.astype(BF16)
        out_ref[slot, :64, :] = high
        out_ref[slot, 64:, :] = (wide - high.astype(F32)).astype(BF16)

    def plain(matrix):
        return jnp.concatenate([matrix, matrix], axis=1)

    def transposed(matrix):
        return jnp.concatenate([matrix, matrix], axis=0).T

    for h in range(LEVELS - 2):
        if PLACES[h][0] == "x":
            store(CLIMB[h, 0], plain(upper_ref[h, side[h]]))
            store(DOWN[h, 0], transposed(upper_ref[h, 0]))
            store(DOWN[h, 1], transposed(upper_ref[h, 1]))
        else:
            store(CLIMB[h, 0], plain(upper_ref[h, 0]))
            store(CLIMB[h, 1], plain(upper_ref[h, 1]))
            store(DOWN[h, 0], transposed(upper_ref[h, side[h]]))
    for h in range(LEVELS - 1):
        mine = code >> h
        row_start = 2 * DEVICES - 2 * DEVICES // 2**h
        if h == LEVELS - 2:
            terms = [(mine, 1), (mine, 2), (mine, 3)]
        else:
            step_x = 1 if PLACES[h][0] == "x" else 2
            step_y = 3 - step_x
            terms = [(mine, step_y), (mine ^ step_x, step_x), (mine ^ step_x, 3)]
        for term, (target, step) in enumerate(terms):
            here = target & 3
            there = here ^ step
            matrix = coupling_ref[h, jnp.abs(there - here) - 1]
            flag = admissible_ref[pl.ds(row_start + target, 1), step - 1 : step].astype(F32)
            upward = jnp.full((64, LANES), there - here, jnp.int32) > 0
            chosen = jnp.where(upward, transposed(matrix), plain(matrix))
            store(FAR[h, term], chosen * flag)


def tree_kernel(gathered_ref, weights_ref, out_ref, tie_ref, *scratch):
    coeff_refs = scratch[: LEVELS - 1]
    down_refs = scratch[LEVELS - 1 :]
    index_x = lax.axis_index("gx")
    index_y = lax.axis_index("gy")

    def weight(slot):
        high = weights_ref[slot, :64, :]
        low = weights_ref[slot, 64:, :]
        return jnp.concatenate([high, high, low, low], axis=0)

    def multiply(value, slot):
        twice = jnp.concatenate([value, value], axis=1)
        return jnp.dot(twice, weight(slot), preferred_element_type=F32)

    low = low_lanes(32)
    for source in range(2**BITS_Y):
        packed = gathered_ref[source]
        rolled = pltpu.roll(packed, HALF, 1)
        high = packed.astype(BF16).astype(F32)
        rest = packed - high
        high_rolled = pltpu.roll(high, HALF, 1)
        rest_rolled = rolled - high_rolled
        coeff_refs[0][source, :32, :] = jnp.where(low, high, rest_rolled).astype(BF16)
        coeff_refs[0][source, 32:, :] = jnp.where(low, high_rolled, rest).astype(BF16)
    for h in range(LEVELS - 2):
        count = coeff_refs[h].shape[0]
        if PLACES[h][0] == "x":
            value = coeff_refs[h][...].reshape(count * 64, LANES)
            result = multiply(value, CLIMB[h, 0])
        else:
            parts = []
            for bit in range(2):
                picked = [coeff_refs[h][node] for node in range(bit, count, 2)]
                parts.append(multiply(jnp.concatenate(picked, axis=0), CLIMB[h, bit]))
            result = parts[0] + parts[1]
        coeff_refs[h + 1][...] = split_lanes(result).reshape(coeff_refs[h + 1].shape)
    down = None
    for h in range(LEVELS - 2, -1, -1):
        own_y = index_y >> BELOW_Y[h]
        own_x = index_x >> BELOW_X[h]
        if h == LEVELS - 2:
            for step in range(1, 4):
                term = multiply(coeff_refs[h][own_y ^ step], FAR[h, step - 1])
                down = term if down is None else down + term
            continue
        value = split_lanes(down)
        count = down_refs[h].shape[0]
        if PLACES[h][0] == "x":
            for bit in range(2):
                part = multiply(value, DOWN[h, bit])
                for node in range(bit, count, 2):
                    down_refs[h][node] = part[node // 2 * 64 : node // 2 * 64 + 64]
        else:
            down_refs[h][...] = multiply(value, DOWN[h, 0]).reshape(count, 64, LANES)
        same = coeff_refs[h][own_y]
        other = coeff_refs[h][own_y ^ 1]
        down_refs[h][own_x] += multiply(other, FAR[h, 0])
        down_refs[h][own_x ^ 1] += multiply(same, FAR[h, 1]) + multiply(other, FAR[h, 2])
        if h > 0:
            down = down_refs[h][...].reshape(count * 64, LANES)
    for target in range(2**BITS_X):
        out_ref[target] = jnp.where(
            low, down_refs[0][target, :32, :], down_refs[0][target, 32:, :]
        )
    tie_ref[...] = jnp.zeros_like(tie_ref)


def near_kernel(listed_ref, own_ref, x_ref, y_ref, xy_ref, tie_ref, out_ref, values, rows, columns, sums):
    index_x = lax.axis_index("gx")
    index_y = lax.axis_index("gy")
    low = low_lanes(8)
    for block, ref in enumerate((own_ref, x_ref, y_ref, xy_ref)):
        for tile in range(LEAVES // 2):
            cols = slice(tile * LANES, tile * LANES + LANES)
            value = ref[:64, cols]
            flipped = jnp.concatenate([value, value], axis=0).T
            first = block * LEAVES + tile * 2
            values[first : first + 2] = split_lanes(flipped).reshape(2, LEAF, LANES)
            point = ref[64:72, cols]
            rolled = pltpu.roll(point, HALF, 1)
            rows[first] = jnp.where(low, point, rolled)
            rows[first + 1] = jnp.where(low, rolled, point)
            if block == 0:
                for axis in range(3):
                    spread = jnp.broadcast_to(point[axis : axis + 1], (LANES, LANES))
                    columns[axis, cols, :] = spread.T

    def local(leaf, place):
        listed = listed_ref[leaf, place]
        owner = listed >> 4
        flip_x = (owner >> BITS_Y ^ index_x) & 1
        flip_y = (owner ^ index_y) & 1
        return (flip_x + 2 * flip_y) * LEAVES + (listed & LEAVES - 1)

    def one_leaf(leaf, carry):
        here = pl.ds(pl.multiple_of(leaf * LEAF, LEAF), LEAF)
        total = None
        for quad in range(3):
            ids = [local(leaf, quad * 4 + place) for place in range(4)]
            highs = []
            rests = []
            for pair in range(2):
                source = jnp.where(low, rows[ids[pair * 2]], rows[ids[pair * 2 + 1]])
                square = None
                for axis in range(3):
                    delta = columns[axis, here, :] - source[axis : axis + 1]
                    square = delta * delta if square is None else square + delta * delta
                square = jnp.maximum(square, 1e-30)
                distance = square * lax.rsqrt(square)
                scale = ROOT_THREE / LENGTH_SCALE
                decay = jnp.exp2(distance * (-scale * LOG2_E))
                kernel = (distance * (AMPLITUDE * scale) + AMPLITUDE) * decay
                high = kernel.astype(BF16)
                highs.append(high)
                rests.append((kernel - high.astype(F32)).astype(BF16))
            weight = jnp.concatenate(
                [jnp.concatenate(highs, axis=1), jnp.concatenate(rests, axis=1)], axis=0
            )
            source_values = jnp.concatenate([values[n] for n in ids], axis=0)
            part = jnp.dot(weight, source_values, preferred_element_type=F32)
            total = part if total is None else total + part
        sums[here, :] = total[:64] + total[64:]
        return carry

    lax.fori_loop(0, LEAVES, one_leaf, 0)
    for tile in range(LEAVES // 2):
        cols = slice(tile * LANES, tile * LANES + LANES)
        flipped = sums[cols, :].T
        out_ref[:, cols] = flipped[:64] + flipped[64:] + NUGGET * own_ref[:64, cols]


def final_kernel(down_ref, near_ref, basis_ref, transfer_ref, out_ref):
    packed = down_ref[...]
    down = jnp.concatenate([packed[:, :HALF], packed[:, HALF:]], axis=0).astype(BF16)
    for block in range(4):
        cols = slice(block * 256, block * 256 + 256)
        leaf_down = jnp.dot(down, transfer_ref[:, cols], preferred_element_type=F32).astype(BF16)
        far = jnp.dot(leaf_down, block_diagonal(basis_ref[:, cols]), preferred_element_type=F32)
        out_ref[:, cols] = near_ref[:, cols] + far


def flip_pairs(count_x, count_y, flip_x, flip_y):
    return [
        (i * count_y + j, (i ^ flip_x) * count_y + (j ^ flip_y))
        for i in range(count_x)
        for j in range(count_y)
    ]


def body(
    right_sides,
    points,
    leaf_basis,
    leaf_transfer,
    upper_transfer,
    coupling,
    near_leaves,
    admissible,
):
    count_x = lax.axis_size("gx")
    count_y = lax.axis_size("gy")
    width = right_sides.shape[1]
    packed, send = pl.pallas_call(
        up_kernel,
        out_shape=(
            jax.ShapeDtypeStruct((32, LANES), F32),
            jax.ShapeDtypeStruct((72, width), F32),
        ),
        in_specs=[VMEM] * 4,
        out_specs=(VMEM, VMEM),
        compiler_params=PARAMS,
    )(right_sides, points, leaf_basis, leaf_transfer)
    gathered = lax.all_gather(packed, "gy", axis=0, tiled=False)
    from_x, from_y, from_xy = (
        lax.ppermute(send, ("gx", "gy"), flip_pairs(count_x, count_y, flip_x, flip_y))
        for flip_x, flip_y in ((1, 0), (0, 1), (1, 1))
    )
    weights = pl.pallas_call(
        weights_kernel,
        out_shape=jax.ShapeDtypeStruct((WEIGHTS, 128, LANES), BF16),
        in_specs=[VMEM] * 3,
        out_specs=VMEM,
        compiler_params=PARAMS,
    )(upper_transfer, coupling, admissible)
    scratch = [
        pltpu.VMEM((2 ** (BITS_Y - BELOW_Y[h]), 64, LANES), BF16) for h in range(LEVELS - 1)
    ] + [pltpu.VMEM((2 ** (BITS_X - BELOW_X[h]), 64, LANES), F32) for h in range(LEVELS - 2)]
    partial, tie = pl.pallas_call(
        tree_kernel,
        out_shape=(
            jax.ShapeDtypeStruct((2**BITS_X, 32, LANES), F32),
            jax.ShapeDtypeStruct((8, LANES), F32),
        ),
        in_specs=[VMEM] * 2,
        out_specs=(VMEM, VMEM),
        scratch_shapes=scratch,
        compiler_params=PARAMS,
    )(gathered, weights)
    down = lax.psum_scatter(partial, "gx", scatter_dimension=0, tiled=False)
    near = pl.pallas_call(
        near_kernel,
        out_shape=jax.ShapeDtypeStruct((64, width), F32),
        in_specs=[SMEM] + [VMEM] * 5,
        out_specs=VMEM,
        scratch_shapes=[
            pltpu.VMEM((4 * LEAVES, LEAF, LANES), BF16),
            pltpu.VMEM((4 * LEAVES, 8, LANES), F32),
            pltpu.VMEM((3, width, LANES), F32),
            pltpu.VMEM((width, LANES), F32),
        ],
        compiler_params=PARAMS,
    )(near_leaves, send, from_x, from_y, from_xy, tie)
    return pl.pallas_call(
        final_kernel,
        out_shape=jax.ShapeDtypeStruct((64, width), F32),
        in_specs=[VMEM] * 4,
        out_specs=VMEM,
        compiler_params=PARAMS,
    )(down, near, leaf_basis, leaf_transfer)


def solution(mesh):
    in_specs = (
        P(None, ("gx", "gy")),
        P(None, ("gx", "gy")),
        P(None, ("gx", "gy")),
        P(None, ("gx", "gy")),
        P(),
        P(),
        P(("gx", "gy"), None),
        P(),
    )
    out_specs = P(None, ("gx", "gy"))
    return jax.shard_map(body, mesh=mesh, in_specs=in_specs, out_specs=out_specs, check_vma=False)
```

```python
import jax
import jax.numpy as jnp
from jax import lax
from jax.experimental import pallas as pl
from jax.experimental.pallas import tpu as pltpu
from jax.sharding import PartitionSpec as P

ROOT_THREE = 1.7320508075688772
LENGTH_SCALE = 0.6
AMPLITUDE = 0.25
NUGGET = 0.5
LOG2_E = 1.4426950408889634
BITS_X = 4
BITS_Y = 5
DEVICES = 512
LEVELS = 9
LEAVES = 16
LEAF = 64
RANK = 64
HALF = 64
LANES = 128
F32 = jnp.float32
BF16 = jnp.bfloat16
NT = (((1,), (1,)), ((), ()))
VMEM = pl.BlockSpec(memory_space=pltpu.VMEM)
SMEM = pl.BlockSpec(memory_space=pltpu.SMEM)
PARAMS = pltpu.CompilerParams(vmem_limit_bytes=40 * 1024 * 1024)


def places():
    listed = []
    for bit in range(max(BITS_X, BITS_Y)):
        if bit < BITS_X:
            listed.append(("x", bit))
        if bit < BITS_Y:
            listed.append(("y", bit))
    return listed


PLACES = places()
BELOW_X = [sum(axis == "x" for axis, _ in PLACES[:h]) for h in range(LEVELS)]
BELOW_Y = [sum(axis == "y" for axis, _ in PLACES[:h]) for h in range(LEVELS)]

CLIMB, DOWN, FAR = {}, {}, {}
for _h in range(LEVELS - 2):
    for _side in range(2 if PLACES[_h][0] == "y" else 1):
        CLIMB[_h, _side] = len(CLIMB)
for _h in range(LEVELS - 2):
    for _side in range(2 if PLACES[_h][0] == "x" else 1):
        DOWN[_h, _side] = len(CLIMB) + len(DOWN)
for _h in range(LEVELS - 1):
    for _term in range(3):
        FAR[_h, _term] = len(CLIMB) + len(DOWN) + len(FAR)
WEIGHTS = len(CLIMB) + len(DOWN) + len(FAR)


def low_lanes(rows):
    return lax.broadcasted_iota(jnp.int32, (rows, LANES), 1) < HALF


def split_lanes(value):
    high = value.astype(BF16).astype(F32)
    return jnp.where(low_lanes(value.shape[0]), high, value - high).astype(BF16)


def block_diagonal(basis):
    wide = basis.astype(F32)
    leaf = lax.broadcasted_iota(jnp.int32, wide.shape, 1) // LEAF
    return jnp.concatenate([jnp.where(leaf == l, wide, 0.0).astype(BF16) for l in range(4)], axis=0)


def up_kernel(right_ref, points_ref, basis_ref, transfer_ref, coeff_ref, send_ref):
    total = None
    for block in range(4):
        cols = slice(block * 256, block * 256 + 256)
        rounded = right_ref[:, cols].astype(BF16)
        leaf_coeff = lax.dot_general(
            rounded, block_diagonal(basis_ref[:, cols]), NT, preferred_element_type=F32
        ).astype(BF16)
        transfer = transfer_ref[:, cols]
        part = lax.dot_general(
            leaf_coeff,
            jnp.concatenate([transfer, transfer], axis=0),
            NT,
            preferred_element_type=F32,
        )
        total = part if total is None else total + part
    packed = jnp.where(low_lanes(32), total[:32], total[32:])
    for target in range(2**BITS_Y):
        coeff_ref[target] = packed
    send_ref[:64, :] = right_ref[...]
    send_ref[64:72, :] = jnp.zeros((8, LEAVES * LEAF), F32)
    send_ref[64:67, :] = points_ref[...]


def weights_kernel(upper_ref, coupling_ref, admissible_ref, out_ref):
    index_x = lax.axis_index("gx")
    index_y = lax.axis_index("gy")
    side = [(index_x if axis == "x" else index_y) >> bit & 1 for axis, bit in PLACES]
    code = jnp.int32(0)
    for place in range(LEVELS):
        code = code + side[place] * 2**place

    def store(slot, wide):
        high = wide.astype(BF16)
        out_ref[slot, :64, :] = high
        out_ref[slot, 64:, :] = (wide - high.astype(F32)).astype(BF16)

    def plain(matrix):
        return jnp.concatenate([matrix, matrix], axis=1)

    def transposed(matrix):
        return jnp.concatenate([matrix, matrix], axis=0).T

    for h in range(LEVELS - 2):
        if PLACES[h][0] == "x":
            store(CLIMB[h, 0], plain(upper_ref[h, side[h]]))
            store(DOWN[h, 0], transposed(upper_ref[h, 0]))
            store(DOWN[h, 1], transposed(upper_ref[h, 1]))
        else:
            store(CLIMB[h, 0], plain(upper_ref[h, 0]))
            store(CLIMB[h, 1], plain(upper_ref[h, 1]))
            store(DOWN[h, 0], transposed(upper_ref[h, side[h]]))
    for h in range(LEVELS - 1):
        mine = code >> h
        row_start = 2 * DEVICES - 2 * DEVICES // 2**h
        if h == LEVELS - 2:
            terms = [(mine, 1), (mine, 2), (mine, 3)]
        else:
            step_x = 1 if PLACES[h][0] == "x" else 2
            step_y = 3 - step_x
            terms = [(mine, step_y), (mine ^ step_x, step_x), (mine ^ step_x, 3)]
        for term, (target, step) in enumerate(terms):
            here = target & 3
            there = here ^ step
            matrix = coupling_ref[h, jnp.abs(there - here) - 1]
            flag = admissible_ref[pl.ds(row_start + target, 1), step - 1 : step].astype(F32)
            upward = jnp.full((64, LANES), there - here, jnp.int32) > 0
            chosen = jnp.where(upward, transposed(matrix), plain(matrix))
            store(FAR[h, term], chosen * flag)


def tree_kernel(gathered_ref, weights_ref, out_ref, tie_ref, *scratch):
    coeff_refs = scratch[: LEVELS - 1]
    down_refs = scratch[LEVELS - 1 :]
    index_x = lax.axis_index("gx")
    index_y = lax.axis_index("gy")

    def weight(slot):
        high = weights_ref[slot, :64, :]
        low = weights_ref[slot, 64:, :]
        return jnp.concatenate([high, high, low, low], axis=0)

    def multiply(value, slot):
        twice = jnp.concatenate([value, value], axis=1)
        return jnp.dot(twice, weight(slot), preferred_element_type=F32)

    low = low_lanes(32)
    for source in range(2**BITS_Y):
        packed = gathered_ref[source]
        rolled = pltpu.roll(packed, HALF, 1)
        high = packed.astype(BF16).astype(F32)
        rest = packed - high
        high_rolled = pltpu.roll(high, HALF, 1)
        rest_rolled = rolled - high_rolled
        coeff_refs[0][source, :32, :] = jnp.where(low, high, rest_rolled).astype(BF16)
        coeff_refs[0][source, 32:, :] = jnp.where(low, high_rolled, rest).astype(BF16)
    for h in range(LEVELS - 2):
        count = coeff_refs[h].shape[0]
        if PLACES[h][0] == "x":
            value = coeff_refs[h][...].reshape(count * 64, LANES)
            result = multiply(value, CLIMB[h, 0])
        else:
            parts = []
            for bit in range(2):
                picked = [coeff_refs[h][node] for node in range(bit, count, 2)]
                parts.append(multiply(jnp.concatenate(picked, axis=0), CLIMB[h, bit]))
            result = parts[0] + parts[1]
        coeff_refs[h + 1][...] = split_lanes(result).reshape(coeff_refs[h + 1].shape)
    down = None
    for h in range(LEVELS - 2, -1, -1):
        own_y = index_y >> BELOW_Y[h]
        own_x = index_x >> BELOW_X[h]
        if h == LEVELS - 2:
            for step in range(1, 4):
                term = multiply(coeff_refs[h][own_y ^ step], FAR[h, step - 1])
                down = term if down is None else down + term
            continue
        value = split_lanes(down)
        count = down_refs[h].shape[0]
        if PLACES[h][0] == "x":
            for bit in range(2):
                part = multiply(value, DOWN[h, bit])
                for node in range(bit, count, 2):
                    down_refs[h][node] = part[node // 2 * 64 : node // 2 * 64 + 64]
        else:
            down_refs[h][...] = multiply(value, DOWN[h, 0]).reshape(count, 64, LANES)
        same = coeff_refs[h][own_y]
        other = coeff_refs[h][own_y ^ 1]
        down_refs[h][own_x] += multiply(other, FAR[h, 0])
        down_refs[h][own_x ^ 1] += multiply(same, FAR[h, 1]) + multiply(other, FAR[h, 2])
        if h > 0:
            down = down_refs[h][...].reshape(count * 64, LANES)
    for target in range(2**BITS_X):
        out_ref[target] = jnp.where(
            low, down_refs[0][target, :32, :], down_refs[0][target, 32:, :]
        )
    tie_ref[...] = jnp.zeros_like(tie_ref)


def near_kernel(listed_ref, own_ref, x_ref, y_ref, xy_ref, tie_ref, out_ref, values, rows, columns, sums):
    index_x = lax.axis_index("gx")
    index_y = lax.axis_index("gy")
    low = low_lanes(8)
    for block, ref in enumerate((own_ref, x_ref, y_ref, xy_ref)):
        for tile in range(LEAVES // 2):
            cols = slice(tile * LANES, tile * LANES + LANES)
            value = ref[:64, cols]
            flipped = jnp.concatenate([value, value], axis=0).T
            first = block * LEAVES + tile * 2
            values[first : first + 2] = split_lanes(flipped).reshape(2, LEAF, LANES)
            point = ref[64:72, cols]
            rolled = pltpu.roll(point, HALF, 1)
            rows[first] = jnp.where(low, point, rolled)
            rows[first + 1] = jnp.where(low, rolled, point)
            if block == 0:
                for axis in range(3):
                    spread = jnp.broadcast_to(point[axis : axis + 1], (LANES, LANES))
                    columns[axis, cols, :] = spread.T

    def local(leaf, place):
        listed = listed_ref[leaf, place]
        owner = listed >> 4
        flip_x = (owner >> BITS_Y ^ index_x) & 1
        flip_y = (owner ^ index_y) & 1
        return (flip_x + 2 * flip_y) * LEAVES + (listed & LEAVES - 1)

    def one_leaf(leaf, carry):
        here = pl.ds(pl.multiple_of(leaf * LEAF, LEAF), LEAF)
        total = None
        for quad in range(3):
            ids = [local(leaf, quad * 4 + place) for place in range(4)]
            highs = []
            rests = []
            for pair in range(2):
                source = jnp.where(low, rows[ids[pair * 2]], rows[ids[pair * 2 + 1]])
                square = None
                for axis in range(3):
                    delta = columns[axis, here, :] - source[axis : axis + 1]
                    square = delta * delta if square is None else square + delta * delta
                square = jnp.maximum(square, 1e-30)
                distance = square * lax.rsqrt(square)
                scale = ROOT_THREE / LENGTH_SCALE
                decay = jnp.exp2(distance * (-scale * LOG2_E))
                kernel = (distance * (AMPLITUDE * scale) + AMPLITUDE) * decay
                high = kernel.astype(BF16)
                highs.append(high)
                rests.append((kernel - high.astype(F32)).astype(BF16))
            weight = jnp.concatenate(
                [jnp.concatenate(highs, axis=1), jnp.concatenate(rests, axis=1)], axis=0
            )
            source_values = jnp.concatenate([values[n] for n in ids], axis=0)
            part = jnp.dot(weight, source_values, preferred_element_type=F32)
            total = part if total is None else total + part
        sums[here, :] = total[:64] + total[64:]
        return carry

    lax.fori_loop(0, LEAVES, one_leaf, 0)
    for tile in range(LEAVES // 2):
        cols = slice(tile * LANES, tile * LANES + LANES)
        flipped = sums[cols, :].T
        out_ref[:, cols] = flipped[:64] + flipped[64:] + NUGGET * own_ref[:64, cols]


def final_kernel(down_ref, near_ref, basis_ref, transfer_ref, out_ref):
    packed = down_ref[0]
    for source in range(1, 2**BITS_X):
        packed = packed + down_ref[source]
    down = jnp.concatenate([packed[:, :HALF], packed[:, HALF:]], axis=0).astype(BF16)
    for block in range(4):
        cols = slice(block * 256, block * 256 + 256)
        leaf_down = jnp.dot(down, transfer_ref[:, cols], preferred_element_type=F32).astype(BF16)
        far = jnp.dot(leaf_down, block_diagonal(basis_ref[:, cols]), preferred_element_type=F32)
        out_ref[:, cols] = near_ref[:, cols] + far


def body(
    right_sides,
    points,
    leaf_basis,
    leaf_transfer,
    upper_transfer,
    coupling,
    near_leaves,
    admissible,
):
    count_x = lax.axis_size("gx")
    count_y = lax.axis_size("gy")
    width = right_sides.shape[1]
    packed, send = pl.pallas_call(
        up_kernel,
        out_shape=(
            jax.ShapeDtypeStruct((2**BITS_Y, 32, LANES), F32),
            jax.ShapeDtypeStruct((72, width), F32),
        ),
        in_specs=[VMEM] * 4,
        out_specs=(VMEM, VMEM),
        compiler_params=PARAMS,
    )(right_sides, points, leaf_basis, leaf_transfer)
    gathered = lax.all_to_all(packed, "gy", split_axis=0, concat_axis=0, tiled=True)
    from_y = lax.ppermute(send, "gy", [(j, j ^ 1) for j in range(count_y)])
    swap_x = [(i, i ^ 1) for i in range(count_x)]
    from_x = lax.ppermute(send, "gx", swap_x)
    from_xy = lax.ppermute(from_y, "gx", swap_x)
    weights = pl.pallas_call(
        weights_kernel,
        out_shape=jax.ShapeDtypeStruct((WEIGHTS, 128, LANES), BF16),
        in_specs=[VMEM] * 3,
        out_specs=VMEM,
        compiler_params=PARAMS,
    )(upper_transfer, coupling, admissible)
    scratch = [
        pltpu.VMEM((2 ** (BITS_Y - BELOW_Y[h]), 64, LANES), BF16) for h in range(LEVELS - 1)
    ] + [pltpu.VMEM((2 ** (BITS_X - BELOW_X[h]), 64, LANES), F32) for h in range(LEVELS - 2)]
    partial, tie = pl.pallas_call(
        tree_kernel,
        out_shape=(
            jax.ShapeDtypeStruct((2**BITS_X, 32, LANES), F32),
            jax.ShapeDtypeStruct((8, LANES), F32),
        ),
        in_specs=[VMEM] * 2,
        out_specs=(VMEM, VMEM),
        scratch_shapes=scratch,
        compiler_params=PARAMS,
    )(gathered, weights)
    down = lax.all_to_all(partial, "gx", split_axis=0, concat_axis=0, tiled=True)
    near = pl.pallas_call(
        near_kernel,
        out_shape=jax.ShapeDtypeStruct((64, width), F32),
        in_specs=[SMEM] + [VMEM] * 5,
        out_specs=VMEM,
        scratch_shapes=[
            pltpu.VMEM((4 * LEAVES, LEAF, LANES), BF16),
            pltpu.VMEM((4 * LEAVES, 8, LANES), F32),
            pltpu.VMEM((3, width, LANES), F32),
            pltpu.VMEM((width, LANES), F32),
        ],
        compiler_params=PARAMS,
    )(near_leaves, send, from_x, from_y, from_xy, tie)
    return pl.pallas_call(
        final_kernel,
        out_shape=jax.ShapeDtypeStruct((64, width), F32),
        in_specs=[VMEM] * 4,
        out_specs=VMEM,
        compiler_params=PARAMS,
    )(down, near, leaf_basis, leaf_transfer)


def solution(mesh):
    in_specs = (
        P(None, ("gx", "gy")),
        P(None, ("gx", "gy")),
        P(None, ("gx", "gy")),
        P(None, ("gx", "gy")),
        P(),
        P(),
        P(("gx", "gy"), None),
        P(),
    )
    out_specs = P(None, ("gx", "gy"))
    return jax.shard_map(body, mesh=mesh, in_specs=in_specs, out_specs=out_specs, check_vma=False)
```

```python
import jax
import jax.numpy as jnp
from jax import lax
from jax.experimental import pallas as pl
from jax.experimental.pallas import tpu as pltpu
from jax.sharding import PartitionSpec as P

ROOT_THREE = 1.7320508075688772
LENGTH_SCALE = 0.6
AMPLITUDE = 0.25
NUGGET = 0.5
LOG2_E = 1.4426950408889634
BITS_Y = 5
DEVICES = 512
LEVELS = 9
LEAVES = 16
LEAF = 64
RANK = 64
HALF = 64
LANES = 128
F32 = jnp.float32
BF16 = jnp.bfloat16
NT = (((1,), (1,)), ((), ()))
VMEM = pl.BlockSpec(memory_space=pltpu.VMEM)
SMEM = pl.BlockSpec(memory_space=pltpu.SMEM)


PLACES = ("x0", "y0", "x1", "y1", "x2", "y2", "x3", "y3", "y4")
AXES = ("x3", "x2", "x1", "x0", "y4", "y3", "y2", "y1", "y0")
CLIMB = 0
DOWN = 14
FAR = 21
LOWER = 45
WEIGHTS = 46
SPLIT = 5


def low_lanes(rows):
    return lax.broadcasted_iota(jnp.int32, (rows, LANES), 1) < HALF


def split_lanes(value):
    high = value.astype(BF16).astype(F32)
    return jnp.where(low_lanes(value.shape[0]), high, value - high).astype(BF16)


def block_diagonal(basis):
    wide = basis.astype(F32)
    leaf = lax.broadcasted_iota(jnp.int32, wide.shape, 1) // LEAF
    return jnp.concatenate([jnp.where(leaf == l, wide, 0.0).astype(BF16) for l in range(4)], axis=0)


def tree_code():
    sides = [lax.axis_index(name) for name in PLACES]
    code = sides[0]
    for place in range(1, LEVELS):
        code = code + sides[place] * 2**place
    return sides, code


def pack(value):
    return jnp.where(low_lanes(32), value[:32], value[32:])


def unpack(packed):
    low = low_lanes(32)
    high = packed.astype(BF16).astype(F32)
    rest = packed - high
    high_rolled = pltpu.roll(high, HALF, 1)
    rest_rolled = pltpu.roll(rest, HALF, 1)
    return jnp.concatenate(
        [jnp.where(low, high, rest_rolled), jnp.where(low, high_rolled, rest)], axis=0
    ).astype(BF16)


def plain(matrix):
    return jnp.concatenate([matrix, matrix], axis=1)


def transposed(matrix):
    return jnp.concatenate([matrix, matrix], axis=0).T


def split_rows(wide):
    high = wide.astype(BF16)
    return jnp.concatenate([high, (wide - high.astype(F32)).astype(BF16)], axis=0)


def multiply(pairs):
    left = [piece for value, _ in pairs for piece in (value, value)]
    right = []
    for _, matrix in pairs:
        high, low = matrix[:64], matrix[64:]
        right += [high, high, low, low]
    return jnp.dot(
        jnp.concatenate(left, axis=1),
        jnp.concatenate(right, axis=0),
        preferred_element_type=F32,
    )


def climb(nodes, lower, upper):
    return multiply(
        [
            (jnp.concatenate(nodes[0::2], axis=0), lower),
            (jnp.concatenate(nodes[1::2], axis=0), upper),
        ]
    )


def as_nodes(value):
    return [value[row : row + 64] for row in range(0, value.shape[0], 64)]


def keep_partners(nodes, own, scratch, out_ref, first):
    for index, node in enumerate(nodes):
        scratch[index] = node
    for step in range(1, 4):
        out_ref[first + step - 1] = scratch[own ^ step]


def up_kernel(right_ref, points_ref, basis_ref, transfer_ref, coeff_ref, send_ref, points_in, basis_in, transfer_in, sems):
    copies = [
        pltpu.make_async_copy(right_ref, send_ref.at[0, pl.ds(0, 64)], sems.at[0]),
        pltpu.make_async_copy(basis_ref, basis_in, sems.at[1]),
        pltpu.make_async_copy(transfer_ref, transfer_in, sems.at[2]),
        pltpu.make_async_copy(points_ref, points_in, sems.at[3]),
    ]
    for copy in copies:
        copy.start()
    for copy in copies:
        copy.wait()
    total = None
    for block in range(4):
        cols = slice(block * 256, block * 256 + 256)
        rounded = send_ref[0, :64, cols].astype(BF16)
        leaf_coeff = lax.dot_general(
            rounded, block_diagonal(basis_in[:, cols]), NT, preferred_element_type=F32
        ).astype(BF16)
        transfer = transfer_in[:, cols]
        part = lax.dot_general(
            leaf_coeff,
            jnp.concatenate([transfer, transfer], axis=0),
            NT,
            preferred_element_type=F32,
        )
        total = part if total is None else total + part
    packed = pack(total)
    for target in range(8):
        coeff_ref[target] = packed
    send_ref[1, :64, :] = send_ref[0, :64, :]
    for copy in range(2):
        send_ref[copy, 64:72, :] = jnp.zeros((8, LEAVES * LEAF), F32)
        send_ref[copy, 64:67, :] = points_in[...]


def low_kernel(gathered_ref, upper_ref, send_ref, partners_ref, scratch):
    _, code = tree_code()
    nodes = [unpack(gathered_ref[source]) for source in range(8)]
    keep_partners(nodes, code & 7, scratch, partners_ref, 0)
    for h in range(2):
        result = climb(
            nodes, split_rows(plain(upper_ref[h, 0])), split_rows(plain(upper_ref[h, 1]))
        )
        if h == 0:
            nodes = as_nodes(split_lanes(result))
            keep_partners(nodes, code >> 1 & 3, scratch, partners_ref, 3)
    pair = [pack(node) for node in as_nodes(result)]
    for target in range(8):
        for side in range(2):
            send_ref[target, side] = pair[side]


def weights_kernel(upper_ref, coupling_ref, admissible_ref, partners_ref, out_ref, far_ref):
    sides, code = tree_code()
    for h in range(LEVELS - 2):
        out_ref[CLIMB + 2 * h] = split_rows(plain(upper_ref[h, 0]))
        out_ref[CLIMB + 2 * h + 1] = split_rows(plain(upper_ref[h, 1]))
        out_ref[DOWN + h] = split_rows(transposed(upper_ref[h, sides[h]]))
    for h in range(LEVELS - 1):
        mine = code >> h
        row = 2 * DEVICES - 2 * DEVICES // 2**h + mine
        flags = admissible_ref[pl.ds(row, 1), :].astype(F32)
        here = mine & 3
        for step in range(1, 4):
            there = here ^ step
            matrix = coupling_ref[h, jnp.abs(there - here) - 1]
            upward = jnp.full((64, LANES), there - here, jnp.int32) > 0
            chosen = jnp.where(upward, transposed(matrix), plain(matrix))
            out_ref[FAR + 3 * h + step - 1] = split_rows(chosen * flags[:, step - 1 : step])
    lower = transposed(upper_ref[SPLIT - 1, sides[SPLIT - 1]])
    for h in range(SPLIT - 2, -1, -1):
        lower = multiply([(split_lanes(lower), out_ref[DOWN + h])])
    out_ref[LOWER] = split_rows(lower)
    for h in range(2):
        far_ref[h] = multiply(
            [(partners_ref[3 * h + s], out_ref[FAR + 3 * h + s]) for s in range(3)]
        )


def middle_kernel(gathered_ref, weights_ref, send_ref, partners_ref, scratch):
    _, code = tree_code()
    nodes = [unpack(gathered_ref[node // 2, node % 2]) for node in range(16)]
    for h in range(2, 5):
        keep_partners(nodes, code >> h & len(nodes) - 1, scratch, partners_ref, 3 * (h - 2))
        result = climb(nodes, weights_ref[CLIMB + 2 * h], weights_ref[CLIMB + 2 * h + 1])
        nodes = as_nodes(split_lanes(result))
    pair = [pack(node) for node in as_nodes(result)]
    for target in range(8):
        for side in range(2):
            send_ref[target, side] = pair[side]


def lower_kernel(partners_ref, far_ref, weights_ref, out_ref):
    down = None
    for h in range(SPLIT - 1, -1, -1):
        if h >= 2:
            far = multiply(
                [(partners_ref[3 * (h - 2) + s], weights_ref[FAR + 3 * h + s]) for s in range(3)]
            )
        else:
            far = far_ref[h]
        if down is None:
            down = far
        else:
            down = far + multiply([(split_lanes(down), weights_ref[DOWN + h])])
    out_ref[...] = down


def near_kernel(listed_ref, own_ref, here_ref, there_ref, tie_ref, out_ref, values, rows, columns, sums):
    side_x = lax.axis_index("x0")
    low = low_lanes(8)
    for tile in range(LEAVES // 2):
        cols = slice(tile * LANES, tile * LANES + LANES)
        for axis in range(3):
            spread = jnp.broadcast_to(own_ref[0, 64 + axis : 65 + axis, cols], (LANES, LANES))
            columns[axis, cols, :] = spread.T
    for block in range(4):
        ref = (here_ref, there_ref)[block // 2]
        for tile in range(LEAVES // 2):
            cols = slice(tile * LANES, tile * LANES + LANES)
            value = ref[block % 2, :64, cols]
            first = block * LEAVES + tile * 2
            values[first : first + 2] = split_rows(value).T.reshape(2, LEAF, LANES)
            point = ref[block % 2, 64:72, cols]
            rolled = pltpu.roll(point, HALF, 1)
            rows[first] = jnp.where(low, point, rolled)
            rows[first + 1] = jnp.where(low, rolled, point)

    def local(leaf, place):
        listed = listed_ref[leaf, place]
        owner = listed >> 4
        flip_x = (owner >> BITS_Y ^ side_x) & 1
        return (2 * flip_x + (owner & 1)) * LEAVES + (listed & LEAVES - 1)

    def one_leaf(leaf, carry):
        here = pl.ds(pl.multiple_of(leaf * LEAF, LEAF), LEAF)
        total = None
        for quad in range(3):
            ids = [local(leaf, quad * 4 + place) for place in range(4)]
            highs = []
            rests = []
            for pair in range(2):
                source = jnp.where(low, rows[ids[pair * 2]], rows[ids[pair * 2 + 1]])
                square = None
                for axis in range(3):
                    delta = columns[axis, here, :] - source[axis : axis + 1]
                    square = delta * delta if square is None else square + delta * delta
                square = jnp.maximum(square, 1e-30)
                distance = square * lax.rsqrt(square)
                scale = ROOT_THREE / LENGTH_SCALE
                decay = jnp.exp2(distance * (-scale * LOG2_E))
                kernel = (distance * (AMPLITUDE * scale) + AMPLITUDE) * decay
                high = kernel.astype(BF16)
                highs.append(high)
                rests.append((kernel - high.astype(F32)).astype(BF16))
            weight = jnp.concatenate(
                [jnp.concatenate(highs, axis=1), jnp.concatenate(rests, axis=1)], axis=0
            )
            source_values = jnp.concatenate([values[n] for n in ids], axis=0)
            part = jnp.dot(weight, source_values, preferred_element_type=F32)
            total = part if total is None else total + part
        sums[here, :] = total[:64] + total[64:]
        return carry

    lax.fori_loop(0, LEAVES, one_leaf, 0, unroll=4)
    for tile in range(LEAVES // 2):
        cols = slice(tile * LANES, tile * LANES + LANES)
        flipped = sums[cols, :].T
        out_ref[:, cols] = flipped[:64] + flipped[64:] + NUGGET * own_ref[0, :64, cols]


def final_kernel(gathered_ref, weights_ref, lower_ref, near_ref, basis_ref, transfer_ref, out_ref, scratch):
    _, code = tree_code()
    nodes = [unpack(gathered_ref[node // 2, node % 2]) for node in range(16)]
    far = []
    for h in range(SPLIT, LEVELS - 1):
        own = code >> h & len(nodes) - 1
        for index, node in enumerate(nodes):
            scratch[h - SPLIT, index] = node
        far.append(
            multiply(
                [(scratch[h - SPLIT, own ^ s], weights_ref[FAR + 3 * h + s - 1]) for s in (1, 2, 3)]
            )
        )
        if h < LEVELS - 2:
            nodes = as_nodes(
                split_lanes(
                    climb(nodes, weights_ref[CLIMB + 2 * h], weights_ref[CLIMB + 2 * h + 1])
                )
            )
    down = far[-1]
    for h in range(LEVELS - 3, SPLIT - 1, -1):
        down = far[h - SPLIT] + multiply([(split_lanes(down), weights_ref[DOWN + h])])
    down = lower_ref[...] + multiply([(split_lanes(down), weights_ref[LOWER])])
    down = down[:, :HALF].astype(BF16)
    for block in range(4):
        cols = slice(block * 256, block * 256 + 256)
        leaf_down = jnp.dot(down, transfer_ref[:, cols], preferred_element_type=F32).astype(BF16)
        far_field = jnp.dot(
            leaf_down, block_diagonal(basis_ref[:, cols]), preferred_element_type=F32
        )
        out_ref[:, cols] = near_ref[:, cols] + far_field


def call(kernel, out_shape, in_specs, scratch_shapes, *operands, limit=40):
    shapes = tuple(jax.ShapeDtypeStruct(shape, dtype) for shape, dtype in out_shape)
    return pl.pallas_call(
        kernel,
        out_shape=shapes,
        in_specs=in_specs,
        out_specs=(VMEM,) * len(shapes),
        scratch_shapes=scratch_shapes,
        compiler_params=pltpu.CompilerParams(vmem_limit_bytes=limit * 1024 * 1024),
    )(*operands)


def exchange(value, names):
    return lax.all_to_all(value, names, split_axis=0, concat_axis=0, tiled=True)


def body(
    right_sides,
    points,
    leaf_basis,
    leaf_transfer,
    upper_transfer,
    coupling,
    near_leaves,
    admissible,
):
    width = right_sides.shape[1]
    coeff, send = call(
        up_kernel,
        [((8, 32, LANES), F32), ((2, 72, width), F32)],
        [pl.BlockSpec(memory_space=pltpu.HBM)] * 4,
        [
            pltpu.VMEM((3, width), F32),
            pltpu.VMEM((64, width), BF16),
            pltpu.VMEM((64, width), BF16),
            pltpu.SemaphoreType.DMA((4,)),
        ],
        right_sides,
        points,
        leaf_basis,
        leaf_transfer,
        limit=60,
    )
    gathered = exchange(coeff, ("x1", "y0", "x0"))
    here = exchange(send, "y0")
    pair, low_partners = call(
        low_kernel,
        [((8, 2, 32, LANES), F32), ((6, 64, LANES), BF16)],
        [VMEM] * 2,
        [pltpu.VMEM((8, 64, LANES), BF16)],
        gathered,
        upper_transfer,
    )
    gathered = exchange(pair, ("y2", "x2", "y1"))
    there = lax.ppermute(here, "x0", [(0, 1), (1, 0)])
    weights, low_far = call(
        weights_kernel,
        [((WEIGHTS, 128, LANES), BF16), ((2, 64, LANES), F32)],
        [VMEM] * 4,
        [],
        upper_transfer,
        coupling,
        admissible,
        low_partners,
    )
    pair, partners = call(
        middle_kernel,
        [((8, 2, 32, LANES), F32), ((9, 64, LANES), BF16)],
        [VMEM] * 2,
        [pltpu.VMEM((16, 64, LANES), BF16)],
        gathered,
        weights,
    )
    gathered = exchange(pair, ("y4", "y3", "x3"))
    (lower,) = call(
        lower_kernel, [((64, LANES), F32)], [VMEM] * 3, [], partners, low_far, weights
    )
    (near,) = call(
        near_kernel,
        [((64, width), F32)],
        [SMEM] + [VMEM] * 4,
        [
            pltpu.VMEM((4 * LEAVES, LEAF, LANES), BF16),
            pltpu.VMEM((4 * LEAVES, 8, LANES), F32),
            pltpu.VMEM((3, width, LANES), F32),
            pltpu.VMEM((width, LANES), F32),
        ],
        near_leaves,
        send,
        here,
        there,
        lower,
    )
    (product,) = call(
        final_kernel,
        [((64, width), F32)],
        [VMEM] * 6,
        [pltpu.VMEM((3, 16, 64, LANES), BF16)],
        gathered,
        weights,
        lower,
        near,
        leaf_basis,
        leaf_transfer,
    )
    return product


def solution(mesh):
    fine = jax.sharding.Mesh(mesh.devices.reshape((2,) * LEVELS), AXES)
    split = P(None, AXES)
    in_specs = (split, split, split, split, P(), P(), P(AXES, None), P())
    return jax.shard_map(body, mesh=fine, in_specs=in_specs, out_specs=split, check_vma=False)
```

```python
import jax
import jax.numpy as jnp
from jax import lax
from jax.experimental import pallas as pl
from jax.experimental.pallas import tpu as pltpu
from jax.sharding import PartitionSpec as P

ROOT_THREE = 1.7320508075688772
LENGTH_SCALE = 0.6
AMPLITUDE = 0.25
NUGGET = 0.5
LOG2_E = 1.4426950408889634
BITS_X = 4
BITS_Y = 5
DEVICES = 512
LEVELS = 9
LEAVES = 16
LEAF = 64
RANK = 64
HALF = 64
LANES = 128
F32 = jnp.float32
BF16 = jnp.bfloat16
NT = (((1,), (1,)), ((), ()))
VMEM = pl.BlockSpec(memory_space=pltpu.VMEM)
SMEM = pl.BlockSpec(memory_space=pltpu.SMEM)


def places():
    listed = []
    for bit in range(max(BITS_X, BITS_Y)):
        if bit < BITS_X:
            listed.append(("x", bit))
        if bit < BITS_Y:
            listed.append(("y", bit))
    return listed


PLACES = places()
BELOW_X = [sum(axis == "x" for axis, _ in PLACES[:h]) for h in range(LEVELS)]
BELOW_Y = [sum(axis == "y" for axis, _ in PLACES[:h]) for h in range(LEVELS)]

CLIMB, DOWN, FAR = {}, {}, {}
for _h in range(LEVELS - 2):
    for _side in range(2 if PLACES[_h][0] == "x" else 1):
        CLIMB[_h, _side] = len(CLIMB)
for _h in range(LEVELS - 2):
    for _side in range(2 if PLACES[_h][0] == "y" else 1):
        DOWN[_h, _side] = len(CLIMB) + len(DOWN)
for _h in range(LEVELS - 1):
    for _term in range(3):
        FAR[_h, _term] = len(CLIMB) + len(DOWN) + len(FAR)
WEIGHTS = len(CLIMB) + len(DOWN) + len(FAR)


def low_lanes(rows):
    return lax.broadcasted_iota(jnp.int32, (rows, LANES), 1) < HALF


def split_lanes(value):
    high = value.astype(BF16).astype(F32)
    return jnp.where(low_lanes(value.shape[0]), high, value - high).astype(BF16)


def split_rows(wide):
    high = wide.astype(BF16)
    return jnp.concatenate([high, (wide - high.astype(F32)).astype(BF16)], axis=0)


def block_diagonal(basis):
    wide = basis.astype(F32)
    leaf = lax.broadcasted_iota(jnp.int32, wide.shape, 1) // LEAF
    return jnp.concatenate([jnp.where(leaf == l, wide, 0.0).astype(BF16) for l in range(4)], axis=0)


def up_kernel(right_ref, points_ref, basis_ref, transfer_ref, coeff_ref, send_ref, points_in, basis_in, transfer_in, sems):
    copies = [
        pltpu.make_async_copy(right_ref, send_ref.at[pl.ds(0, 64)], sems.at[0]),
        pltpu.make_async_copy(basis_ref, basis_in, sems.at[1]),
        pltpu.make_async_copy(transfer_ref, transfer_in, sems.at[2]),
        pltpu.make_async_copy(points_ref, points_in, sems.at[3]),
    ]
    for copy in copies:
        copy.start()
    for copy in copies:
        copy.wait()
    total = None
    for block in range(4):
        cols = slice(block * 256, block * 256 + 256)
        rounded = send_ref[:64, cols].astype(BF16)
        leaf_coeff = lax.dot_general(
            rounded, block_diagonal(basis_in[:, cols]), NT, preferred_element_type=F32
        ).astype(BF16)
        transfer = transfer_in[:, cols]
        part = lax.dot_general(
            leaf_coeff,
            jnp.concatenate([transfer, transfer], axis=0),
            NT,
            preferred_element_type=F32,
        )
        total = part if total is None else total + part
    packed = jnp.where(low_lanes(32), total[:32], total[32:])
    for target in range(2**BITS_X):
        coeff_ref[target] = packed
    send_ref[64:72, :] = jnp.zeros((8, LEAVES * LEAF), F32)
    send_ref[64:67, :] = points_in[...]


def weights_kernel(upper_ref, coupling_ref, admissible_ref, out_ref):
    index_x = lax.axis_index("gx")
    index_y = lax.axis_index("gy")
    side = [(index_x if axis == "x" else index_y) >> bit & 1 for axis, bit in PLACES]
    code = jnp.int32(0)
    for place in range(LEVELS):
        code = code + side[place] * 2**place

    def store(slot, wide):
        high = wide.astype(BF16)
        out_ref[slot, :64, :] = high
        out_ref[slot, 64:, :] = (wide - high.astype(F32)).astype(BF16)

    def plain(matrix):
        return jnp.concatenate([matrix, matrix], axis=1)

    def transposed(matrix):
        return jnp.concatenate([matrix, matrix], axis=0).T

    for h in range(LEVELS - 2):
        if PLACES[h][0] == "y":
            store(CLIMB[h, 0], plain(upper_ref[h, side[h]]))
            store(DOWN[h, 0], transposed(upper_ref[h, 0]))
            store(DOWN[h, 1], transposed(upper_ref[h, 1]))
        else:
            store(CLIMB[h, 0], plain(upper_ref[h, 0]))
            store(CLIMB[h, 1], plain(upper_ref[h, 1]))
            store(DOWN[h, 0], transposed(upper_ref[h, side[h]]))
    for h in range(LEVELS - 1):
        mine = code >> h
        row_start = 2 * DEVICES - 2 * DEVICES // 2**h
        if h == LEVELS - 2:
            terms = [(mine ^ 1, 1), (mine ^ 2, 2), (mine ^ 3, 3)]
        else:
            step_x = 1 if PLACES[h][0] == "x" else 2
            step_y = 3 - step_x
            terms = [(mine, step_x), (mine ^ step_y, step_y), (mine ^ step_y, 3)]
        for term, (target, step) in enumerate(terms):
            here = target & 3
            there = here ^ step
            matrix = coupling_ref[h, jnp.abs(there - here) - 1]
            flag = admissible_ref[step - 1, row_start + target].astype(F32)
            upward = jnp.full((64, LANES), there - here, jnp.int32) > 0
            chosen = jnp.where(upward, transposed(matrix), plain(matrix))
            store(FAR[h, term], chosen * flag)


def tree_kernel(gathered_ref, weights_ref, out_ref, tie_ref, *scratch):
    coeff_refs = scratch[: LEVELS - 1]
    down_refs = scratch[LEVELS - 1 :]
    index_x = lax.axis_index("gx")
    index_y = lax.axis_index("gy")

    def weight(slot):
        high = weights_ref[slot, :64, :]
        low = weights_ref[slot, 64:, :]
        return [high, high, low, low]

    def multiply(pairs):
        left = [piece for value, _ in pairs for piece in (value, value)]
        right = [piece for _, slot in pairs for piece in weight(slot)]
        return jnp.dot(
            jnp.concatenate(left, axis=1),
            jnp.concatenate(right, axis=0),
            preferred_element_type=F32,
        )

    low = low_lanes(32)
    for source in range(2**BITS_X):
        packed = gathered_ref[source]
        rolled = pltpu.roll(packed, HALF, 1)
        high = packed.astype(BF16).astype(F32)
        rest = packed - high
        high_rolled = pltpu.roll(high, HALF, 1)
        rest_rolled = rolled - high_rolled
        coeff_refs[0][source, :32, :] = jnp.where(low, high, rest_rolled).astype(BF16)
        coeff_refs[0][source, 32:, :] = jnp.where(low, high_rolled, rest).astype(BF16)
    for h in range(LEVELS - 2):
        count = coeff_refs[h].shape[0]
        if PLACES[h][0] == "y":
            value = coeff_refs[h][...].reshape(count * 64, LANES)
            result = multiply([(value, CLIMB[h, 0])])
        else:
            sides = [
                jnp.concatenate([coeff_refs[h][n] for n in range(bit, count, 2)], axis=0)
                for bit in range(2)
            ]
            result = multiply([(sides[0], CLIMB[h, 0]), (sides[1], CLIMB[h, 1])])
        coeff_refs[h + 1][...] = split_lanes(result).reshape(coeff_refs[h + 1].shape)
    for h in range(LEVELS - 2, -1, -1):
        own_x = index_x >> BELOW_X[h]
        own_y = index_y >> BELOW_Y[h]
        count = down_refs[h].shape[0]
        if h == LEVELS - 2:
            down_refs[h][own_y] = jnp.zeros((64, LANES), F32)
            for step in range(1, 4):
                down_refs[h][own_y ^ step] = multiply([(coeff_refs[h][0], FAR[h, step - 1])])
            continue
        above = down_refs[h + 1].shape[0]
        value = split_lanes(down_refs[h + 1][...].reshape(above * 64, LANES))
        if PLACES[h][0] == "y":
            for bit in range(2):
                part = multiply([(value, DOWN[h, bit])])
                for node in range(above):
                    down_refs[h][node * 2 + bit] = part[node * 64 : node * 64 + 64]
        else:
            down_refs[h][...] = multiply([(value, DOWN[h, 0])]).reshape(count, 64, LANES)
        same = coeff_refs[h][own_x]
        other = coeff_refs[h][own_x ^ 1]
        down_refs[h][own_y] += multiply([(other, FAR[h, 0])])
        down_refs[h][own_y ^ 1] += multiply([(same, FAR[h, 1]), (other, FAR[h, 2])])
    for target in range(2**BITS_Y):
        out_ref[target] = jnp.where(
            low, down_refs[0][target, :32, :], down_refs[0][target, 32:, :]
        )
    tie_ref[...] = jnp.zeros_like(tie_ref)


def near_kernel(listed_ref, own_ref, x_ref, y_ref, xy_ref, tie_ref, out_ref, values, rows, columns, sums):
    index_x = lax.axis_index("gx")
    index_y = lax.axis_index("gy")
    low = low_lanes(8)
    for tile in range(LEAVES // 2):
        cols = slice(tile * LANES, tile * LANES + LANES)
        for axis in range(3):
            spread = jnp.broadcast_to(own_ref[64 + axis : 65 + axis, cols], (LANES, LANES))
            columns[axis, cols, :] = spread.T
    for block, ref in enumerate((own_ref, x_ref, y_ref, xy_ref)):
        for tile in range(LEAVES // 2):
            cols = slice(tile * LANES, tile * LANES + LANES)
            first = block * LEAVES + tile * 2
            values[first : first + 2] = split_rows(ref[:64, cols]).T.reshape(2, LEAF, LANES)
            point = ref[64:72, cols]
            rolled = pltpu.roll(point, HALF, 1)
            rows[first] = jnp.where(low, point, rolled)
            rows[first + 1] = jnp.where(low, rolled, point)

    def local(leaf, place):
        listed = listed_ref[leaf, place]
        owner = listed >> 4
        flip_x = (owner >> BITS_Y ^ index_x) & 1
        flip_y = (owner ^ index_y) & 1
        return (flip_x + 2 * flip_y) * LEAVES + (listed & LEAVES - 1)

    def one_leaf(leaf, carry):
        here = pl.ds(pl.multiple_of(leaf * LEAF, LEAF), LEAF)
        total = None
        for quad in range(3):
            ids = [local(leaf, quad * 4 + place) for place in range(4)]
            highs = []
            rests = []
            for pair in range(2):
                source = jnp.where(low, rows[ids[pair * 2]], rows[ids[pair * 2 + 1]])
                square = None
                for axis in range(3):
                    delta = columns[axis, here, :] - source[axis : axis + 1]
                    square = delta * delta if square is None else square + delta * delta
                square = jnp.maximum(square, 1e-30)
                distance = square * lax.rsqrt(square)
                scale = ROOT_THREE / LENGTH_SCALE
                decay = jnp.exp2(distance * (-scale * LOG2_E))
                kernel = (distance * (AMPLITUDE * scale) + AMPLITUDE) * decay
                high = kernel.astype(BF16)
                highs.append(high)
                rests.append((kernel - high.astype(F32)).astype(BF16))
            weight = jnp.concatenate(
                [jnp.concatenate(highs, axis=1), jnp.concatenate(rests, axis=1)], axis=0
            )
            source_values = jnp.concatenate([values[n] for n in ids], axis=0)
            part = jnp.dot(weight, source_values, preferred_element_type=F32)
            total = part if total is None else total + part
        sums[here, :] = total[:64] + total[64:]
        return carry

    lax.fori_loop(0, LEAVES, one_leaf, 0, unroll=4)
    for tile in range(LEAVES // 2):
        cols = slice(tile * LANES, tile * LANES + LANES)
        flipped = sums[cols, :].T
        out_ref[:, cols] = flipped[:64] + flipped[64:] + NUGGET * own_ref[:64, cols]


def final_kernel(down_ref, near_ref, basis_ref, transfer_ref, out_ref):
    packed = down_ref[0]
    for source in range(1, 2**BITS_Y):
        packed = packed + down_ref[source]
    down = jnp.concatenate([packed[:, :HALF], packed[:, HALF:]], axis=0).astype(BF16)
    for block in range(4):
        cols = slice(block * 256, block * 256 + 256)
        leaf_down = jnp.dot(down, transfer_ref[:, cols], preferred_element_type=F32).astype(BF16)
        far = jnp.dot(leaf_down, block_diagonal(basis_ref[:, cols]), preferred_element_type=F32)
        out_ref[:, cols] = near_ref[:, cols] + far


def call(kernel, out_shape, in_specs, scratch_shapes, *operands, limit=40):
    shapes = tuple(jax.ShapeDtypeStruct(shape, dtype) for shape, dtype in out_shape)
    return pl.pallas_call(
        kernel,
        out_shape=shapes,
        in_specs=in_specs,
        out_specs=(VMEM,) * len(shapes),
        scratch_shapes=scratch_shapes,
        compiler_params=pltpu.CompilerParams(vmem_limit_bytes=limit * 1024 * 1024),
    )(*operands)


def exchange(value, names):
    return lax.all_to_all(value, names, split_axis=0, concat_axis=0, tiled=True)


def body(
    right_sides,
    points,
    leaf_basis,
    leaf_transfer,
    upper_transfer,
    coupling,
    near_leaves,
    admissible,
):
    width = right_sides.shape[1]
    packed, send = call(
        up_kernel,
        [((2**BITS_X, 32, LANES), F32), ((72, width), F32)],
        [pl.BlockSpec(memory_space=pltpu.HBM)] * 4,
        [
            pltpu.VMEM((3, width), F32),
            pltpu.VMEM((64, width), BF16),
            pltpu.VMEM((64, width), BF16),
            pltpu.SemaphoreType.DMA((4,)),
        ],
        right_sides,
        points,
        leaf_basis,
        leaf_transfer,
        limit=60,
    )
    gathered = exchange(packed, "gx")
    from_y = lax.ppermute(send, "gy", [(j, j ^ 1) for j in range(2**BITS_Y)])
    swap_x = [(i, i ^ 1) for i in range(2**BITS_X)]
    from_x = lax.ppermute(send, "gx", swap_x)
    from_xy = lax.ppermute(from_y, "gx", swap_x)
    (weights,) = call(
        weights_kernel,
        [((WEIGHTS, 128, LANES), BF16)],
        [VMEM] * 2 + [SMEM],
        [],
        upper_transfer,
        coupling,
        admissible.T,
    )
    heights = range(LEVELS - 1)
    partial, tie = call(
        tree_kernel,
        [((2**BITS_Y, 32, LANES), F32), ((8, LANES), F32)],
        [VMEM] * 2,
        [pltpu.VMEM((2 ** (BITS_X - BELOW_X[h]), 64, LANES), BF16) for h in heights]
        + [pltpu.VMEM((2 ** (BITS_Y - BELOW_Y[h]), 64, LANES), F32) for h in heights],
        gathered,
        weights,
    )
    down = exchange(partial, "gy")
    (near,) = call(
        near_kernel,
        [((64, width), F32)],
        [SMEM] + [VMEM] * 5,
        [
            pltpu.VMEM((4 * LEAVES, LEAF, LANES), BF16),
            pltpu.VMEM((4 * LEAVES, 8, LANES), F32),
            pltpu.VMEM((3, width, LANES), F32),
            pltpu.VMEM((width, LANES), F32),
        ],
        near_leaves,
        send,
        from_x,
        from_y,
        from_xy,
        tie,
    )
    (product,) = call(
        final_kernel,
        [((64, width), F32)],
        [VMEM] * 4,
        [],
        down,
        near,
        leaf_basis,
        leaf_transfer,
    )
    return product


def solution(mesh):
    in_specs = (
        P(None, ("gx", "gy")),
        P(None, ("gx", "gy")),
        P(None, ("gx", "gy")),
        P(None, ("gx", "gy")),
        P(),
        P(),
        P(("gx", "gy"), None),
        P(),
    )
    out_specs = P(None, ("gx", "gy"))
    return jax.shard_map(body, mesh=mesh, in_specs=in_specs, out_specs=out_specs, check_vma=False)
```

```python
import jax
import jax.numpy as jnp
from jax import lax
from jax.experimental import pallas as pl
from jax.experimental.pallas import tpu as pltpu
from jax.sharding import PartitionSpec as P

ROOT_THREE = 1.7320508075688772
LENGTH_SCALE = 0.6
AMPLITUDE = 0.25
NUGGET = 0.5
LOG2_E = 1.4426950408889634
BITS_X = 4
BITS_Y = 5
DEVICES = 512
LEVELS = 9
LEAVES = 16
LEAF = 64
RANK = 64
HALF = 64
LANES = 128
F32 = jnp.float32
BF16 = jnp.bfloat16
NT = (((1,), (1,)), ((), ()))
VMEM = pl.BlockSpec(memory_space=pltpu.VMEM)
ANYWHERE = pl.BlockSpec(memory_space=pl.ANY)
SMEM = pl.BlockSpec(memory_space=pltpu.SMEM)


def places():
    listed = []
    for bit in range(max(BITS_X, BITS_Y)):
        if bit < BITS_X:
            listed.append(("x", bit))
        if bit < BITS_Y:
            listed.append(("y", bit))
    return listed


PLACES = places()
BELOW_X = [sum(axis == "x" for axis, _ in PLACES[:h]) for h in range(LEVELS)]
BELOW_Y = [sum(axis == "y" for axis, _ in PLACES[:h]) for h in range(LEVELS)]

CLIMB, DOWN, FAR = {}, {}, {}
for _h in range(LEVELS - 2):
    for _side in range(2 if PLACES[_h][0] == "x" else 1):
        CLIMB[_h, _side] = len(CLIMB)
for _h in range(LEVELS - 2):
    for _side in range(2 if PLACES[_h][0] == "y" else 1):
        DOWN[_h, _side] = len(CLIMB) + len(DOWN)
for _h in range(LEVELS - 1):
    for _term in range(3):
        FAR[_h, _term] = len(CLIMB) + len(DOWN) + len(FAR)
WEIGHTS = len(CLIMB) + len(DOWN) + len(FAR)


def low_lanes(rows):
    return lax.broadcasted_iota(jnp.int32, (rows, LANES), 1) < HALF


def split_lanes(value):
    high = value.astype(BF16).astype(F32)
    return jnp.where(low_lanes(value.shape[0]), high, value - high).astype(BF16)


def split_rows(wide):
    high = wide.astype(BF16)
    return jnp.concatenate([high, (wide - high.astype(F32)).astype(BF16)], axis=0)


def block_diagonal(basis):
    wide = basis.astype(F32)
    leaf = lax.broadcasted_iota(jnp.int32, wide.shape, 1) // LEAF
    return jnp.concatenate([jnp.where(leaf == l, wide, 0.0).astype(BF16) for l in range(4)], axis=0)


def up_kernel(right_ref, points_ref, basis_ref, transfer_ref, coeff_ref, send_ref, points_in, basis_in, transfer_in, sems):
    copies = [
        pltpu.make_async_copy(right_ref, send_ref.at[pl.ds(0, 64)], sems.at[0]),
        pltpu.make_async_copy(basis_ref, basis_in, sems.at[1]),
        pltpu.make_async_copy(transfer_ref, transfer_in, sems.at[2]),
        pltpu.make_async_copy(points_ref, points_in, sems.at[3]),
    ]
    for copy in copies:
        copy.start()
    for copy in copies:
        copy.wait()
    total = None
    for block in range(4):
        cols = slice(block * 256, block * 256 + 256)
        rounded = send_ref[:64, cols].astype(BF16)
        leaf_coeff = lax.dot_general(
            rounded, block_diagonal(basis_in[:, cols]), NT, preferred_element_type=F32
        ).astype(BF16)
        transfer = transfer_in[:, cols]
        part = lax.dot_general(
            leaf_coeff,
            jnp.concatenate([transfer, transfer], axis=0),
            NT,
            preferred_element_type=F32,
        )
        total = part if total is None else total + part
    packed = jnp.where(low_lanes(32), total[:32], total[32:])
    for target in range(2**BITS_X):
        coeff_ref[target] = packed
    send_ref[64:72, :] = jnp.zeros((8, LEAVES * LEAF), F32)
    send_ref[64:67, :] = points_in[...]


def weights_kernel(upper_ref, coupling_ref, admissible_ref, out_ref):
    index_x = lax.axis_index("gx")
    index_y = lax.axis_index("gy")
    side = [(index_x if axis == "x" else index_y) >> bit & 1 for axis, bit in PLACES]
    code = jnp.int32(0)
    for place in range(LEVELS):
        code = code + side[place] * 2**place

    def store(slot, wide):
        high = wide.astype(BF16)
        out_ref[slot, :64, :] = high
        out_ref[slot, 64:, :] = (wide - high.astype(F32)).astype(BF16)

    def plain(matrix):
        return jnp.concatenate([matrix, matrix], axis=1)

    def transposed(matrix):
        return jnp.concatenate([matrix, matrix], axis=0).T

    for h in range(LEVELS - 2):
        if PLACES[h][0] == "y":
            store(CLIMB[h, 0], plain(upper_ref[h, side[h]]))
            store(DOWN[h, 0], transposed(upper_ref[h, 0]))
            store(DOWN[h, 1], transposed(upper_ref[h, 1]))
        else:
            store(CLIMB[h, 0], plain(upper_ref[h, 0]))
            store(CLIMB[h, 1], plain(upper_ref[h, 1]))
            store(DOWN[h, 0], transposed(upper_ref[h, side[h]]))
    for h in range(LEVELS - 1):
        mine = code >> h
        row_start = 2 * DEVICES - 2 * DEVICES // 2**h
        if h == LEVELS - 2:
            terms = [(mine ^ 1, 1), (mine ^ 2, 2), (mine ^ 3, 3)]
        else:
            step_x = 1 if PLACES[h][0] == "x" else 2
            step_y = 3 - step_x
            terms = [(mine, step_x), (mine ^ step_y, step_y), (mine ^ step_y, 3)]
        for term, (target, step) in enumerate(terms):
            here = target & 3
            there = here ^ step
            matrix = coupling_ref[h, jnp.abs(there - here) - 1]
            flag = admissible_ref[step - 1, row_start + target].astype(F32)
            upward = jnp.full((64, LANES), there - here, jnp.int32) > 0
            chosen = jnp.where(upward, transposed(matrix), plain(matrix))
            store(FAR[h, term], chosen * flag)


def tree_kernel(gathered_ref, weights_ref, tie_in_ref, out_ref, tie_ref, *scratch):
    coeff_refs = scratch[: LEVELS - 1]
    down_refs = scratch[LEVELS - 1 :]
    index_x = lax.axis_index("gx")
    index_y = lax.axis_index("gy")

    def weight(slot):
        high = weights_ref[slot, :64, :]
        low = weights_ref[slot, 64:, :]
        return [high, high, low, low]

    def multiply(pairs):
        left = [piece for value, _ in pairs for piece in (value, value)]
        right = [piece for _, slot in pairs for piece in weight(slot)]
        return jnp.dot(
            jnp.concatenate(left, axis=1),
            jnp.concatenate(right, axis=0),
            preferred_element_type=F32,
        )

    low = low_lanes(32)
    for source in range(2**BITS_X):
        packed = gathered_ref[source]
        rolled = pltpu.roll(packed, HALF, 1)
        high = packed.astype(BF16).astype(F32)
        rest = packed - high
        high_rolled = pltpu.roll(high, HALF, 1)
        rest_rolled = rolled - high_rolled
        coeff_refs[0][source, :32, :] = jnp.where(low, high, rest_rolled).astype(BF16)
        coeff_refs[0][source, 32:, :] = jnp.where(low, high_rolled, rest).astype(BF16)
    for h in range(LEVELS - 2):
        count = coeff_refs[h].shape[0]
        if PLACES[h][0] == "y":
            value = coeff_refs[h][...].reshape(count * 64, LANES)
            result = multiply([(value, CLIMB[h, 0])])
        else:
            sides = [
                jnp.concatenate([coeff_refs[h][n] for n in range(bit, count, 2)], axis=0)
                for bit in range(2)
            ]
            result = multiply([(sides[0], CLIMB[h, 0]), (sides[1], CLIMB[h, 1])])
        coeff_refs[h + 1][...] = split_lanes(result).reshape(coeff_refs[h + 1].shape)
    for h in range(LEVELS - 2, -1, -1):
        own_x = index_x >> BELOW_X[h]
        own_y = index_y >> BELOW_Y[h]
        count = down_refs[h].shape[0]
        if h == LEVELS - 2:
            down_refs[h][own_y] = jnp.zeros((64, LANES), F32)
            for step in range(1, 4):
                down_refs[h][own_y ^ step] = multiply([(coeff_refs[h][0], FAR[h, step - 1])])
            continue
        above = down_refs[h + 1].shape[0]
        value = split_lanes(down_refs[h + 1][...].reshape(above * 64, LANES))
        if PLACES[h][0] == "y":
            for bit in range(2):
                part = multiply([(value, DOWN[h, bit])])
                for node in range(above):
                    down_refs[h][node * 2 + bit] = part[node * 64 : node * 64 + 64]
        else:
            down_refs[h][...] = multiply([(value, DOWN[h, 0])]).reshape(count, 64, LANES)
        same = coeff_refs[h][own_x]
        other = coeff_refs[h][own_x ^ 1]
        down_refs[h][own_y] += multiply([(other, FAR[h, 0])])
        down_refs[h][own_y ^ 1] += multiply([(same, FAR[h, 1]), (other, FAR[h, 2])])
    for target in range(2**BITS_Y):
        out_ref[target] = jnp.where(
            low, down_refs[0][target, :32, :], down_refs[0][target, 32:, :]
        )
    tie_ref[...] = jnp.zeros_like(tie_ref)


def near_kernel(listed_ref, own_ref, x_ref, y_ref, xy_ref, tie_ref, out_ref, values, rows, columns, sums):
    index_x = lax.axis_index("gx")
    index_y = lax.axis_index("gy")
    low = low_lanes(8)
    for tile in range(LEAVES // 2):
        cols = slice(tile * LANES, tile * LANES + LANES)
        for axis in range(3):
            spread = jnp.broadcast_to(own_ref[64 + axis : 65 + axis, cols], (LANES, LANES))
            columns[axis, cols, :] = spread.T
    for block, ref in enumerate((own_ref, x_ref, y_ref, xy_ref)):
        for tile in range(LEAVES // 2):
            cols = slice(tile * LANES, tile * LANES + LANES)
            first = block * LEAVES + tile * 2
            values[first : first + 2] = split_rows(ref[:64, cols]).T.reshape(2, LEAF, LANES)
            point = ref[64:72, cols]
            rolled = pltpu.roll(point, HALF, 1)
            rows[first] = jnp.where(low, point, rolled)
            rows[first + 1] = jnp.where(low, rolled, point)

    def local(leaf, place):
        listed = listed_ref[leaf, place]
        owner = listed >> 4
        flip_x = (owner >> BITS_Y ^ index_x) & 1
        flip_y = (owner ^ index_y) & 1
        return (flip_x + 2 * flip_y) * LEAVES + (listed & LEAVES - 1)

    def one_leaf(leaf, carry):
        here = pl.ds(pl.multiple_of(leaf * LEAF, LEAF), LEAF)
        total = None
        for quad in range(3):
            ids = [local(leaf, quad * 4 + place) for place in range(4)]
            highs = []
            rests = []
            for pair in range(2):
                source = jnp.where(low, rows[ids[pair * 2]], rows[ids[pair * 2 + 1]])
                square = None
                for axis in range(3):
                    delta = columns[axis, here, :] - source[axis : axis + 1]
                    square = delta * delta if square is None else square + delta * delta
                square = jnp.maximum(square, 1e-30)
                distance = square * lax.rsqrt(square)
                scale = ROOT_THREE / LENGTH_SCALE
                decay = jnp.exp2(distance * (-scale * LOG2_E))
                kernel = (distance * (AMPLITUDE * scale) + AMPLITUDE) * decay
                high = kernel.astype(BF16)
                highs.append(high)
                rests.append((kernel - high.astype(F32)).astype(BF16))
            weight = jnp.concatenate(
                [jnp.concatenate(highs, axis=1), jnp.concatenate(rests, axis=1)], axis=0
            )
            source_values = jnp.concatenate([values[n] for n in ids], axis=0)
            part = jnp.dot(weight, source_values, preferred_element_type=F32)
            total = part if total is None else total + part
        sums[here, :] = total[:64] + total[64:]
        return carry

    lax.fori_loop(0, LEAVES, one_leaf, 0, unroll=4)
    for tile in range(LEAVES // 2):
        cols = slice(tile * LANES, tile * LANES + LANES)
        flipped = sums[cols, :].T
        out_ref[:, cols] = flipped[:64] + flipped[64:] + NUGGET * own_ref[:64, cols]


def final_kernel(down_ref, near_ref, basis_ref, transfer_ref, out_ref):
    packed = down_ref[0]
    for source in range(1, 2**BITS_Y):
        packed = packed + down_ref[source]
    down = jnp.concatenate([packed[:, :HALF], packed[:, HALF:]], axis=0).astype(BF16)
    for block in range(4):
        cols = slice(block * 256, block * 256 + 256)
        leaf_down = jnp.dot(down, transfer_ref[:, cols], preferred_element_type=F32).astype(BF16)
        far = jnp.dot(leaf_down, block_diagonal(basis_ref[:, cols]), preferred_element_type=F32)
        out_ref[:, cols] = near_ref[:, cols] + far


def call(kernel, out_shape, in_specs, scratch_shapes, *operands, limit=40):
    shapes = tuple(jax.ShapeDtypeStruct(shape, dtype) for shape, dtype in out_shape)
    return pl.pallas_call(
        kernel,
        out_shape=shapes,
        in_specs=in_specs,
        out_specs=(VMEM,) * len(shapes),
        scratch_shapes=scratch_shapes,
        compiler_params=pltpu.CompilerParams(vmem_limit_bytes=limit * 1024 * 1024),
    )(*operands)


def exchange(value, names):
    return lax.all_to_all(value, names, split_axis=0, concat_axis=0, tiled=True)


def body(
    right_sides,
    points,
    leaf_basis,
    leaf_transfer,
    upper_transfer,
    coupling,
    near_leaves,
    admissible,
):
    width = right_sides.shape[1]
    packed, send = call(
        up_kernel,
        [((2**BITS_X, 32, LANES), F32), ((72, width), F32)],
        [pl.BlockSpec(memory_space=pltpu.HBM)] * 4,
        [
            pltpu.VMEM((3, width), F32),
            pltpu.VMEM((64, width), BF16),
            pltpu.VMEM((64, width), BF16),
            pltpu.SemaphoreType.DMA((4,)),
        ],
        right_sides,
        points,
        leaf_basis,
        leaf_transfer,
        limit=60,
    )
    gathered = exchange(packed, "gx")
    from_y = lax.ppermute(send, "gy", [(j, j ^ 1) for j in range(2**BITS_Y)])
    swap_x = [(i, i ^ 1) for i in range(2**BITS_X)]
    from_x = lax.ppermute(send, "gx", swap_x)
    from_xy = lax.ppermute(from_y, "gx", swap_x)
    (weights,) = call(
        weights_kernel,
        [((WEIGHTS, 128, LANES), BF16)],
        [VMEM] * 2 + [SMEM],
        [],
        upper_transfer,
        coupling,
        admissible.T,
    )
    heights = range(LEVELS - 1)
    partial, tie = call(
        tree_kernel,
        [((2**BITS_Y, 32, LANES), F32), ((8, LANES), F32)],
        [VMEM] * 2 + [ANYWHERE],
        [pltpu.VMEM((2 ** (BITS_X - BELOW_X[h]), 64, LANES), BF16) for h in heights]
        + [pltpu.VMEM((2 ** (BITS_Y - BELOW_Y[h]), 64, LANES), F32) for h in heights],
        gathered,
        weights,
        from_y,
    )
    down = exchange(partial, "gy")
    (near,) = call(
        near_kernel,
        [((64, width), F32)],
        [SMEM] + [VMEM] * 5,
        [
            pltpu.VMEM((4 * LEAVES, LEAF, LANES), BF16),
            pltpu.VMEM((4 * LEAVES, 8, LANES), F32),
            pltpu.VMEM((3, width, LANES), F32),
            pltpu.VMEM((width, LANES), F32),
        ],
        near_leaves,
        send,
        from_x,
        from_y,
        from_xy,
        tie,
    )
    (product,) = call(
        final_kernel,
        [((64, width), F32)],
        [VMEM] * 4,
        [],
        down,
        near,
        leaf_basis,
        leaf_transfer,
    )
    return product


def solution(mesh):
    in_specs = (
        P(None, ("gx", "gy")),
        P(None, ("gx", "gy")),
        P(None, ("gx", "gy")),
        P(None, ("gx", "gy")),
        P(),
        P(),
        P(("gx", "gy"), None),
        P(),
    )
    out_specs = P(None, ("gx", "gy"))
    return jax.shard_map(body, mesh=mesh, in_specs=in_specs, out_specs=out_specs, check_vma=False)
```

```python
import jax
import jax.numpy as jnp
from jax import lax
from jax.experimental import pallas as pl
from jax.experimental.pallas import tpu as pltpu
from jax.sharding import PartitionSpec as P

ROOT_THREE = 1.7320508075688772
LENGTH_SCALE = 0.6
AMPLITUDE = 0.25
NUGGET = 0.5
LOG2_E = 1.4426950408889634
BITS_X = 4
BITS_Y = 5
DEVICES = 512
LEVELS = 9
LEAVES = 16
LEAF = 64
RANK = 64
HALF = 64
LANES = 128
F32 = jnp.float32
BF16 = jnp.bfloat16
NT = (((1,), (1,)), ((), ()))
VMEM = pl.BlockSpec(memory_space=pltpu.VMEM)
ANYWHERE = pl.BlockSpec(memory_space=pl.ANY)
SMEM = pl.BlockSpec(memory_space=pltpu.SMEM)


def places():
    listed = []
    for bit in range(max(BITS_X, BITS_Y)):
        if bit < BITS_X:
            listed.append(("x", bit))
        if bit < BITS_Y:
            listed.append(("y", bit))
    return listed


PLACES = places()
BELOW_X = [sum(axis == "x" for axis, _ in PLACES[:h]) for h in range(LEVELS)]
BELOW_Y = [sum(axis == "y" for axis, _ in PLACES[:h]) for h in range(LEVELS)]

CLIMB, DOWN, FAR = {}, {}, {}
for _h in range(LEVELS - 2):
    for _side in range(2 if PLACES[_h][0] == "x" else 1):
        CLIMB[_h, _side] = len(CLIMB)
for _h in range(LEVELS - 2):
    for _side in range(2 if PLACES[_h][0] == "y" else 1):
        DOWN[_h, _side] = len(CLIMB) + len(DOWN)
for _h in range(LEVELS - 1):
    for _term in range(3):
        FAR[_h, _term] = len(CLIMB) + len(DOWN) + len(FAR)
WEIGHTS = len(CLIMB) + len(DOWN) + len(FAR)


def low_lanes(rows):
    return lax.broadcasted_iota(jnp.int32, (rows, LANES), 1) < HALF


def split_lanes(value):
    high = value.astype(BF16).astype(F32)
    return jnp.where(low_lanes(value.shape[0]), high, value - high).astype(BF16)


def split_rows(wide):
    high = wide.astype(BF16)
    return jnp.concatenate([high, (wide - high.astype(F32)).astype(BF16)], axis=0)


def block_diagonal(basis):
    wide = basis.astype(F32)
    leaf = lax.broadcasted_iota(jnp.int32, wide.shape, 1) // LEAF
    return jnp.concatenate([jnp.where(leaf == l, wide, 0.0).astype(BF16) for l in range(4)], axis=0)


def up_kernel(right_ref, points_ref, basis_ref, transfer_ref, coeff_ref, send_ref, points_in, basis_in, transfer_in, sems):
    copies = [
        pltpu.make_async_copy(right_ref, send_ref.at[pl.ds(0, 64)], sems.at[0]),
        pltpu.make_async_copy(basis_ref, basis_in, sems.at[1]),
        pltpu.make_async_copy(transfer_ref, transfer_in, sems.at[2]),
        pltpu.make_async_copy(points_ref, points_in, sems.at[3]),
    ]
    for copy in copies:
        copy.start()
    for copy in copies:
        copy.wait()
    total = None
    for block in range(4):
        cols = slice(block * 256, block * 256 + 256)
        rounded = send_ref[:64, cols].astype(BF16)
        leaf_coeff = lax.dot_general(
            rounded, block_diagonal(basis_in[:, cols]), NT, preferred_element_type=F32
        ).astype(BF16)
        transfer = transfer_in[:, cols]
        part = lax.dot_general(
            leaf_coeff,
            jnp.concatenate([transfer, transfer], axis=0),
            NT,
            preferred_element_type=F32,
        )
        total = part if total is None else total + part
    packed = jnp.where(low_lanes(32), total[:32], total[32:])
    coeff_ref[...] = packed
    send_ref[64:80, :] = jnp.zeros((16, LEAVES * LEAF), F32)
    send_ref[64:67, :] = points_in[...]
    for tile in range(8):
        send_ref[72:76, tile * LANES : tile * LANES + LANES] = packed[tile * 4 : tile * 4 + 4]


def device_index():
    core = lax.axis_index("core")
    return lax.axis_index("z") * 2 + core, lax.axis_index("gy"), core


def sent_coeff(ref):
    return jnp.concatenate(
        [ref[72:76, tile * LANES : tile * LANES + LANES] for tile in range(8)], axis=0
    )


def fold(value):
    rows = value.shape[0] // 2
    return jnp.where(low_lanes(rows), value[:rows], value[rows:])


def unfold(packed):
    low = low_lanes(packed.shape[0])
    rolled = pltpu.roll(packed, HALF, 1)
    return jnp.concatenate(
        [jnp.where(low, packed, rolled), jnp.where(low, rolled, packed)], axis=0
    )


def multiply(pairs):
    left = [piece for value, _ in pairs for piece in (value, value)]
    right = [piece for _, m in pairs for piece in (m[:64], m[:64], m[64:], m[64:])]
    return jnp.dot(
        jnp.concatenate(left, axis=1),
        jnp.concatenate(right, axis=0),
        preferred_element_type=F32,
    )


def pair_kernel(own_ref, other_ref, upper_ref, out_ref):
    core = lax.axis_index("core")
    mine = lax.broadcasted_iota(jnp.int32, (32, LANES), 1) // HALF == core
    pairs = []
    for packed, side in ((own_ref[...], core), (sent_coeff(other_ref), 1 - core)):
        half = jnp.where(mine, packed, pltpu.roll(packed, HALF, 1))
        matrix = upper_ref[0, side]
        pairs.append((split_lanes(half), split_rows(jnp.concatenate([matrix, matrix], axis=1))))
    result = fold(multiply(pairs))
    for target in range(out_ref.shape[0]):
        out_ref[target] = result


def weights_kernel(upper_ref, coupling_ref, admissible_ref, tie_ref, out_ref):
    index_x, index_y, _ = device_index()
    side = [(index_x if axis == "x" else index_y) >> bit & 1 for axis, bit in PLACES]
    code = jnp.int32(0)
    for place in range(LEVELS):
        code = code + side[place] * 2**place

    def store(slot, wide):
        high = wide.astype(BF16)
        out_ref[slot, :64, :] = high
        out_ref[slot, 64:, :] = (wide - high.astype(F32)).astype(BF16)

    def plain(matrix):
        return jnp.concatenate([matrix, matrix], axis=1)

    def transposed(matrix):
        return jnp.concatenate([matrix, matrix], axis=0).T

    for h in range(LEVELS - 2):
        if PLACES[h][0] == "y":
            store(CLIMB[h, 0], plain(upper_ref[h, side[h]]))
            store(DOWN[h, 0], transposed(upper_ref[h, 0]))
            store(DOWN[h, 1], transposed(upper_ref[h, 1]))
        else:
            store(CLIMB[h, 0], plain(upper_ref[h, 0]))
            store(CLIMB[h, 1], plain(upper_ref[h, 1]))
            store(DOWN[h, 0], transposed(upper_ref[h, side[h]]))
    for h in range(LEVELS - 1):
        mine = code >> h
        row_start = 2 * DEVICES - 2 * DEVICES // 2**h
        if h == 0:
            terms = [(mine, 1), (mine, 2), (mine, 3)]
        elif h == LEVELS - 2:
            terms = [(mine ^ 1, 1), (mine ^ 2, 2), (mine ^ 3, 3)]
        else:
            step_x = 1 if PLACES[h][0] == "x" else 2
            step_y = 3 - step_x
            terms = [(mine, step_x), (mine ^ step_y, step_y), (mine ^ step_y, 3)]
        for term, (target, step) in enumerate(terms):
            here = target & 3
            there = here ^ step
            matrix = coupling_ref[h, jnp.abs(there - here) - 1]
            flag = admissible_ref[step - 1, row_start + target].astype(F32)
            upward = jnp.full((64, LANES), there - here, jnp.int32) > 0
            chosen = jnp.where(upward, transposed(matrix), plain(matrix))
            store(FAR[h, term], chosen * flag)


def tree_kernel(gathered_ref, weights_ref, tie_in_ref, out_ref, tie_ref, *scratch):
    coeff_refs = dict(zip(range(1, LEVELS - 1), scratch[: LEVELS - 2]))
    down_refs = dict(zip(range(1, LEVELS - 1), scratch[LEVELS - 2 :]))
    index_x, index_y, _ = device_index()
    for source in range(gathered_ref.shape[0]):
        coeff_refs[1][source] = split_lanes(unfold(gathered_ref[source]))
    for h in range(1, LEVELS - 2):
        count = coeff_refs[h].shape[0]
        if PLACES[h][0] == "y":
            value = coeff_refs[h][...].reshape(count * 32, LANES)
            result = multiply([(value, weights_ref[CLIMB[h, 0]])])
        else:
            result = multiply(
                [
                    (
                        jnp.concatenate([coeff_refs[h][n] for n in range(bit, count, 2)], axis=0),
                        weights_ref[CLIMB[h, bit]],
                    )
                    for bit in range(2)
                ]
            )
        coeff_refs[h + 1][...] = split_lanes(result).reshape(coeff_refs[h + 1].shape)
    for h in range(LEVELS - 2, 0, -1):
        own_x = index_x >> BELOW_X[h]
        own_y = index_y >> BELOW_Y[h]
        count = down_refs[h].shape[0]
        if h == LEVELS - 2:
            down_refs[h][own_y] = jnp.zeros((32, LANES), F32)
            for step in range(1, 4):
                down_refs[h][own_y ^ step] = multiply(
                    [(coeff_refs[h][0], weights_ref[FAR[h, step - 1]])]
                )
            continue
        above = down_refs[h + 1].shape[0]
        value = split_lanes(down_refs[h + 1][...].reshape(above * 32, LANES))
        if PLACES[h][0] == "y":
            for bit in range(2):
                part = multiply([(value, weights_ref[DOWN[h, bit]])])
                for node in range(above):
                    down_refs[h][node * 2 + bit] = part[node * 32 : node * 32 + 32]
        else:
            down_refs[h][...] = multiply([(value, weights_ref[DOWN[h, 0]])]).reshape(
                count, 32, LANES
            )
        same = coeff_refs[h][own_x]
        other = coeff_refs[h][own_x ^ 1]
        down_refs[h][own_y] += multiply([(other, weights_ref[FAR[h, 0]])])
        down_refs[h][own_y ^ 1] += multiply(
            [(same, weights_ref[FAR[h, 1]]), (other, weights_ref[FAR[h, 2]])]
        )
    for target in range(2**BITS_Y):
        out_ref[target] = fold(down_refs[1][target])
    tie_ref[...] = jnp.zeros_like(tie_ref)


def sum_kernel(parts_ref, tie_ref, out_ref):
    total = parts_ref[0]
    for source in range(1, parts_ref.shape[0]):
        total = total + parts_ref[source]
    out_ref[...] = total


def near_kernel(
    listed_ref,
    own_ref,
    x_ref,
    y_ref,
    xy_ref,
    weights_ref,
    tie_ref,
    out_ref,
    far_ref,
    values,
    rows,
    columns,
    sums,
):
    _, index_y, core = device_index()
    far_ref[...] = multiply(
        [
            (split_lanes(unfold(sent_coeff(ref))), weights_ref[FAR[0, term]])
            for term, ref in enumerate((x_ref, y_ref, xy_ref))
        ]
    )
    low = low_lanes(8)
    for tile in range(LEAVES // 2):
        cols = slice(tile * LANES, tile * LANES + LANES)
        for axis in range(3):
            spread = jnp.broadcast_to(own_ref[64 + axis : 65 + axis, cols], (LANES, LANES))
            columns[axis, cols, :] = spread.T
    for block, ref in enumerate((own_ref, x_ref, y_ref, xy_ref)):
        for tile in range(LEAVES // 2):
            cols = slice(tile * LANES, tile * LANES + LANES)
            first = block * LEAVES + tile * 2
            values[first : first + 2] = split_rows(ref[:64, cols]).T.reshape(2, LEAF, LANES)
            point = ref[64:72, cols]
            rolled = pltpu.roll(point, HALF, 1)
            rows[first] = jnp.where(low, point, rolled)
            rows[first + 1] = jnp.where(low, rolled, point)

    def local(leaf, place):
        listed = listed_ref[leaf, place]
        owner = listed >> 4
        flip_x = (owner >> BITS_Y ^ core) & 1
        flip_y = (owner ^ index_y) & 1
        return (flip_x + 2 * flip_y) * LEAVES + (listed & LEAVES - 1)

    def one_leaf(leaf, carry):
        here = pl.ds(pl.multiple_of(leaf * LEAF, LEAF), LEAF)
        total = None
        for quad in range(3):
            ids = [local(leaf, quad * 4 + place) for place in range(4)]
            highs = []
            rests = []
            for pair in range(2):
                source = jnp.where(low, rows[ids[pair * 2]], rows[ids[pair * 2 + 1]])
                square = None
                for axis in range(3):
                    delta = columns[axis, here, :] - source[axis : axis + 1]
                    square = delta * delta if square is None else square + delta * delta
                square = jnp.maximum(square, 1e-30)
                distance = square * lax.rsqrt(square)
                scale = ROOT_THREE / LENGTH_SCALE
                decay = jnp.exp2(distance * (-scale * LOG2_E))
                kernel = (distance * (AMPLITUDE * scale) + AMPLITUDE) * decay
                high = kernel.astype(BF16)
                highs.append(high)
                rests.append((kernel - high.astype(F32)).astype(BF16))
            weight = jnp.concatenate(
                [jnp.concatenate(highs, axis=1), jnp.concatenate(rests, axis=1)], axis=0
            )
            source_values = jnp.concatenate([values[n] for n in ids], axis=0)
            part = jnp.dot(weight, source_values, preferred_element_type=F32)
            total = part if total is None else total + part
        sums[here, :] = total[:64] + total[64:]
        return carry

    lax.fori_loop(0, LEAVES, one_leaf, 0, unroll=4)
    for tile in range(LEAVES // 2):
        cols = slice(tile * LANES, tile * LANES + LANES)
        flipped = sums[cols, :].T
        out_ref[:, cols] = flipped[:64] + flipped[64:] + NUGGET * own_ref[:64, cols]


def final_kernel(own_ref, other_ref, far_ref, weights_ref, near_ref, basis_ref, transfer_ref, out_ref):
    first = jnp.full((32, LANES), lax.axis_index("core"), jnp.int32) == 0
    own = unfold(own_ref[...])
    other = unfold(other_ref[...])
    above = jnp.concatenate([jnp.where(first, own, other), jnp.where(first, other, own)], axis=0)
    down = far_ref[...] + multiply([(split_lanes(above), weights_ref[DOWN[0, 0]])])
    down = down[:, :HALF].astype(BF16)
    for block in range(4):
        cols = slice(block * 256, block * 256 + 256)
        leaf_down = jnp.dot(down, transfer_ref[:, cols], preferred_element_type=F32).astype(BF16)
        far = jnp.dot(leaf_down, block_diagonal(basis_ref[:, cols]), preferred_element_type=F32)
        out_ref[:, cols] = near_ref[:, cols] + far


def call(kernel, out_shape, in_specs, scratch_shapes, *operands, limit=40):
    shapes = tuple(jax.ShapeDtypeStruct(shape, dtype) for shape, dtype in out_shape)
    return pl.pallas_call(
        kernel,
        out_shape=shapes,
        in_specs=in_specs,
        out_specs=(VMEM,) * len(shapes),
        scratch_shapes=scratch_shapes,
        compiler_params=pltpu.CompilerParams(vmem_limit_bytes=limit * 1024 * 1024),
    )(*operands)


def exchange(value, names):
    return lax.all_to_all(value, names, split_axis=0, concat_axis=0, tiled=True)


def body(
    right_sides,
    points,
    leaf_basis,
    leaf_transfer,
    upper_transfer,
    coupling,
    near_leaves,
    admissible,
):
    width = right_sides.shape[1]
    count_z = lax.axis_size("z")
    count_y = lax.axis_size("gy")
    coeff, send = call(
        up_kernel,
        [((32, LANES), F32), ((80, width), F32)],
        [pl.BlockSpec(memory_space=pltpu.HBM)] * 4,
        [
            pltpu.VMEM((3, width), F32),
            pltpu.VMEM((64, width), BF16),
            pltpu.VMEM((64, width), BF16),
            pltpu.SemaphoreType.DMA((4,)),
        ],
        right_sides,
        points,
        leaf_basis,
        leaf_transfer,
        limit=60,
    )
    swap = [(0, 1), (1, 0)]
    from_x = lax.ppermute(send, "core", swap)
    from_y = lax.ppermute(send, "gy", [(j, j ^ 1) for j in range(count_y)])
    (pair,) = call(
        pair_kernel, [((count_z, 16, LANES), F32)], [VMEM] * 3, [], coeff, from_x, upper_transfer
    )
    gathered = exchange(pair, "z")
    (weights,) = call(
        weights_kernel,
        [((WEIGHTS, 128, LANES), BF16)],
        [VMEM] * 2 + [SMEM, ANYWHERE],
        [],
        upper_transfer,
        coupling,
        admissible.T,
        pair,
    )
    heights = range(1, LEVELS - 1)
    partial, tie = call(
        tree_kernel,
        [((count_y, 16, LANES), F32), ((8, LANES), F32)],
        [VMEM] * 2 + [ANYWHERE],
        [pltpu.VMEM((2 ** (BITS_X - BELOW_X[h]), 32, LANES), BF16) for h in heights]
        + [pltpu.VMEM((2 ** (BITS_Y - BELOW_Y[h]), 32, LANES), F32) for h in heights],
        gathered,
        weights,
        from_y,
    )
    parts = exchange(partial, "gy")
    from_xy = lax.ppermute(from_y, "core", swap)
    near, far = call(
        near_kernel,
        [((64, width), F32), ((64, LANES), F32)],
        [SMEM] + [VMEM] * 6,
        [
            pltpu.VMEM((4 * LEAVES, LEAF, LANES), BF16),
            pltpu.VMEM((4 * LEAVES, 8, LANES), F32),
            pltpu.VMEM((3, width, LANES), F32),
            pltpu.VMEM((width, LANES), F32),
        ],
        near_leaves,
        send,
        from_x,
        from_y,
        from_xy,
        weights,
        tie,
    )
    (own,) = call(sum_kernel, [((16, LANES), F32)], [VMEM, ANYWHERE], [], parts, far)
    other = lax.ppermute(own, "core", swap)
    (product,) = call(
        final_kernel,
        [((64, width), F32)],
        [VMEM] * 7,
        [],
        own,
        other,
        far,
        weights,
        near,
        leaf_basis,
        leaf_transfer,
    )
    return product


def solution(mesh):
    count_x, count_y = mesh.devices.shape
    chips = jax.sharding.Mesh(
        mesh.devices.reshape(count_x // 2, 2, count_y), ("z", "core", "gy")
    )
    every = ("z", "core", "gy")
    split = P(None, every)
    in_specs = (split, split, split, split, P(), P(), P(every, None), P())
    return jax.shard_map(body, mesh=chips, in_specs=in_specs, out_specs=split, check_vma=False)
```

```python
import jax
import jax.numpy as jnp
from jax import lax
from jax.experimental import pallas as pl
from jax.experimental.pallas import tpu as pltpu
from jax.sharding import PartitionSpec as P

ROOT_THREE = 1.7320508075688772
LENGTH_SCALE = 0.6
AMPLITUDE = 0.25
NUGGET = 0.5
LOG2_E = 1.4426950408889634
BITS_X = 4
BITS_Y = 5
DEVICES = 512
LEVELS = 9
LEAVES = 16
LEAF = 64
RANK = 64
HALF = 64
LANES = 128
F32 = jnp.float32
BF16 = jnp.bfloat16
NT = (((1,), (1,)), ((), ()))
VMEM = pl.BlockSpec(memory_space=pltpu.VMEM)
ANYWHERE = pl.BlockSpec(memory_space=pl.ANY)
SMEM = pl.BlockSpec(memory_space=pltpu.SMEM)


def places():
    listed = []
    for bit in range(max(BITS_X, BITS_Y)):
        if bit < BITS_X:
            listed.append(("x", bit))
        if bit < BITS_Y:
            listed.append(("y", bit))
    return listed


PLACES = places()
SOURCE = (2, 4, 6, 7)
TARGET = (1, 3, 5, 8)

CLIMB, DOWN, FAR = {}, {}, {}
for _h in range(1, LEVELS - 2):
    for _side in range(2 if _h in SOURCE else 1):
        CLIMB[_h, _side] = len(CLIMB)
for _h in range(LEVELS - 2):
    for _side in range(2 if _h in TARGET else 1):
        DOWN[_h, _side] = len(CLIMB) + len(DOWN)
for _h in range(LEVELS - 1):
    for _step in (1, 2, 3):
        FAR[_h, _step] = len(CLIMB) + len(DOWN) + len(FAR)
WEIGHTS = len(CLIMB) + len(DOWN) + len(FAR)


def above(chosen, h):
    return [place for place in chosen if place >= h]


def flipped(chosen, h, step):
    listed = above(chosen, h)
    return sum(1 << listed.index(h + p) for p in (0, 1) if step >> p & 1 and h + p in listed)


def low_lanes(rows):
    return lax.broadcasted_iota(jnp.int32, (rows, LANES), 1) < HALF


def split_lanes(value):
    high = value.astype(BF16).astype(F32)
    return jnp.where(low_lanes(value.shape[0]), high, value - high).astype(BF16)


def split_rows(wide):
    high = wide.astype(BF16)
    return jnp.concatenate([high, (wide - high.astype(F32)).astype(BF16)], axis=0)


def block_diagonal(basis):
    wide = basis.astype(F32)
    leaf = lax.broadcasted_iota(jnp.int32, wide.shape, 1) // LEAF
    return jnp.concatenate([jnp.where(leaf == l, wide, 0.0).astype(BF16) for l in range(4)], axis=0)


def up_kernel(
    right_ref,
    points_ref,
    basis_ref,
    transfer_ref,
    upper_ref,
    lifted_ref,
    send_ref,
    points_in,
    basis_in,
    transfer_in,
    upper_in,
    sems,
):
    copies = [
        pltpu.make_async_copy(right_ref, send_ref.at[pl.ds(0, 64)], sems.at[0]),
        pltpu.make_async_copy(basis_ref, basis_in, sems.at[1]),
        pltpu.make_async_copy(transfer_ref, transfer_in, sems.at[2]),
        pltpu.make_async_copy(points_ref, points_in, sems.at[3]),
        pltpu.make_async_copy(upper_ref.at[0, lax.axis_index("core")], upper_in, sems.at[4]),
    ]
    for copy in copies:
        copy.start()
    for copy in copies:
        copy.wait()
    total = None
    for block in range(4):
        cols = slice(block * 256, block * 256 + 256)
        rounded = send_ref[:64, cols].astype(BF16)
        leaf_coeff = lax.dot_general(
            rounded, block_diagonal(basis_in[:, cols]), NT, preferred_element_type=F32
        ).astype(BF16)
        transfer = transfer_in[:, cols]
        part = lax.dot_general(
            leaf_coeff,
            jnp.concatenate([transfer, transfer], axis=0),
            NT,
            preferred_element_type=F32,
        )
        total = part if total is None else total + part
    matrix = upper_in[...]
    wide = split_rows(jnp.concatenate([matrix, matrix], axis=1))
    lifted = fold(multiply([(split_lanes(total), wide)]))
    lifted_ref[...] = lifted
    send_ref[64:72, :] = jnp.zeros((8, LEAVES * LEAF), F32)
    send_ref[64:67, :] = points_in[...]
    for first, packed in ((72, fold(total)), (76, lifted)):
        for tile in range(8):
            cols = slice(tile * LANES, tile * LANES + LANES)
            send_ref[first : first + 4, cols] = packed[tile * 4 : tile * 4 + 4]


def device_index():
    core = lax.axis_index("core")
    index_y = lax.axis_index("xh") * 16 + lax.axis_index("xl") * 8 + lax.axis_index("y")
    return lax.axis_index("z") * 2 + core, index_y, core


def device_sides():
    index_x, index_y, _ = device_index()
    return [(index_x if axis == "x" else index_y) >> bit & 1 for axis, bit in PLACES]


def place_index(sides, listed):
    index = jnp.int32(0)
    for bit, place in enumerate(listed):
        index = index + sides[place] * 2**bit
    return index


def sent_coeff(ref, first):
    return jnp.concatenate(
        [ref[first : first + 4, tile * LANES : tile * LANES + LANES] for tile in range(8)], axis=0
    )


def fold(value):
    rows = value.shape[0] // 2
    return jnp.where(low_lanes(rows), value[:rows], value[rows:])


def unfold(packed):
    low = low_lanes(packed.shape[0])
    rolled = pltpu.roll(packed, HALF, 1)
    return jnp.concatenate(
        [jnp.where(low, packed, rolled), jnp.where(low, rolled, packed)], axis=0
    )


def multiply(pairs):
    left = [piece for value, _ in pairs for piece in (value, value)]
    right = [piece for _, m in pairs for piece in (m[:64], m[:64], m[64:], m[64:])]
    return jnp.dot(
        jnp.concatenate(left, axis=1),
        jnp.concatenate(right, axis=0),
        preferred_element_type=F32,
    )


def pair_kernel(own_ref, other_ref, out_ref):
    mine = lax.broadcasted_iota(jnp.int32, (32, LANES), 1) // HALF == lax.axis_index("core")
    both = own_ref[...] + sent_coeff(other_ref, 76)
    result = fold(jnp.where(mine, both, pltpu.roll(both, HALF, 1)))
    for target in range(out_ref.shape[0]):
        out_ref[target] = result


def weights_kernel(upper_ref, coupling_ref, admissible_ref, tie_ref, out_ref):
    sides = device_sides()
    code = place_index(sides, range(LEVELS))

    def plain(matrix):
        return jnp.concatenate([matrix, matrix], axis=1)

    def transposed(matrix):
        return jnp.concatenate([matrix, matrix], axis=0).T

    for h in range(LEVELS - 2):
        for side in range(2):
            own = sides[h] if (h, 1) not in CLIMB else side
            if (h, side) in CLIMB:
                out_ref[CLIMB[h, side]] = split_rows(plain(upper_ref[h, own]))
            own = sides[h] if (h, 1) not in DOWN else side
            if (h, side) in DOWN:
                out_ref[DOWN[h, side]] = split_rows(transposed(upper_ref[h, own]))
    for h in range(LEVELS - 1):
        first = 2 * DEVICES - 2 * DEVICES // 2**h
        for step in (1, 2, 3):
            turned = sum(1 << p for p in (0, 1) if step >> p & 1 and h + p in TARGET)
            target = (code >> h) ^ (turned if h else 0)
            here = target & 3
            there = here ^ step
            matrix = coupling_ref[h, jnp.abs(there - here) - 1]
            flag = admissible_ref[step - 1, first + target].astype(F32)
            upward = jnp.full((64, LANES), there - here, jnp.int32) > 0
            chosen = jnp.where(upward, transposed(matrix), plain(matrix))
            out_ref[FAR[h, step]] = split_rows(chosen * flag)


def tree_kernel(gathered_ref, weights_ref, tie_in_ref, out_ref, tie_ref, *scratch):
    coeff_refs = dict(zip(range(1, LEVELS - 1), scratch[: LEVELS - 2]))
    down_refs = dict(zip(range(1, LEVELS - 1), scratch[LEVELS - 2 :]))
    sides = device_sides()
    for source in range(gathered_ref.shape[0]):
        coeff_refs[1][source] = split_lanes(unfold(gathered_ref[source]))
    for h in range(1, LEVELS - 2):
        count = coeff_refs[h].shape[0]
        if h in SOURCE:
            result = multiply(
                [
                    (
                        jnp.concatenate([coeff_refs[h][n] for n in range(bit, count, 2)], axis=0),
                        weights_ref[CLIMB[h, bit]],
                    )
                    for bit in range(2)
                ]
            )
        else:
            value = coeff_refs[h][...].reshape(count * 32, LANES)
            result = multiply([(value, weights_ref[CLIMB[h, 0]])])
        coeff_refs[h + 1][...] = split_lanes(result).reshape(coeff_refs[h + 1].shape)
    for h in range(LEVELS - 2, 0, -1):
        source = place_index(sides, above(SOURCE, h))
        target = place_index(sides, above(TARGET, h))
        count = down_refs[h].shape[0]
        if h == LEVELS - 2:
            down_refs[h][...] = jnp.zeros((count, 32, LANES), F32)
        else:
            parents = down_refs[h + 1].shape[0]
            value = split_lanes(down_refs[h + 1][...].reshape(parents * 32, LANES))
            if h in TARGET:
                for bit in range(2):
                    part = multiply([(value, weights_ref[DOWN[h, bit]])])
                    for node in range(parents):
                        down_refs[h][node * 2 + bit] = part[node * 32 : node * 32 + 32]
            else:
                part = multiply([(value, weights_ref[DOWN[h, 0]])])
                down_refs[h][...] = part.reshape(count, 32, LANES)
        terms = {}
        for step in (1, 2, 3):
            pair = coeff_refs[h][source ^ flipped(SOURCE, h, step)], weights_ref[FAR[h, step]]
            terms.setdefault(flipped(TARGET, h, step), []).append(pair)
        for turned, pairs in terms.items():
            down_refs[h][target ^ turned] += multiply(pairs)
    for node in range(out_ref.shape[0]):
        out_ref[node] = fold(down_refs[1][node])
    tie_ref[...] = jnp.zeros_like(tie_ref)


def sum_kernel(parts_ref, tie_ref, out_ref):
    total = parts_ref[0]
    for source in range(1, parts_ref.shape[0]):
        total = total + parts_ref[source]
    out_ref[...] = total


def near_kernel(
    listed_ref,
    own_ref,
    x_ref,
    y_ref,
    xy_ref,
    weights_ref,
    tie_ref,
    out_ref,
    far_ref,
    values,
    rows,
    columns,
    sums,
):
    _, index_y, core = device_index()
    far_ref[...] = multiply(
        [
            (split_lanes(unfold(sent_coeff(ref, 72))), weights_ref[FAR[0, step]])
            for step, ref in enumerate((x_ref, y_ref, xy_ref), 1)
        ]
    )
    low = low_lanes(8)
    for tile in range(LEAVES // 2):
        cols = slice(tile * LANES, tile * LANES + LANES)
        for axis in range(3):
            spread = jnp.broadcast_to(own_ref[64 + axis : 65 + axis, cols], (LANES, LANES))
            columns[axis, cols, :] = spread.T
    for block, ref in enumerate((own_ref, x_ref, y_ref, xy_ref)):
        for tile in range(LEAVES // 2):
            cols = slice(tile * LANES, tile * LANES + LANES)
            first = block * LEAVES + tile * 2
            values[first : first + 2] = split_rows(ref[:64, cols]).T.reshape(2, LEAF, LANES)
            point = ref[64:72, cols]
            rolled = pltpu.roll(point, HALF, 1)
            rows[first] = jnp.where(low, point, rolled)
            rows[first + 1] = jnp.where(low, rolled, point)

    def local(leaf, place):
        listed = listed_ref[leaf, place]
        owner = listed >> 4
        flip_x = (owner >> BITS_Y ^ core) & 1
        flip_y = (owner ^ index_y) & 1
        return (flip_x + 2 * flip_y) * LEAVES + (listed & LEAVES - 1)

    def one_leaf(leaf, carry):
        here = pl.ds(pl.multiple_of(leaf * LEAF, LEAF), LEAF)
        total = None
        for quad in range(3):
            ids = [local(leaf, quad * 4 + place) for place in range(4)]
            highs = []
            rests = []
            for pair in range(2):
                source = jnp.where(low, rows[ids[pair * 2]], rows[ids[pair * 2 + 1]])
                square = None
                for axis in range(3):
                    delta = columns[axis, here, :] - source[axis : axis + 1]
                    square = delta * delta if square is None else square + delta * delta
                square = jnp.maximum(square, 1e-30)
                distance = square * lax.rsqrt(square)
                scale = ROOT_THREE / LENGTH_SCALE
                decay = jnp.exp2(distance * (-scale * LOG2_E))
                kernel = (distance * (AMPLITUDE * scale) + AMPLITUDE) * decay
                high = kernel.astype(BF16)
                highs.append(high)
                rests.append((kernel - high.astype(F32)).astype(BF16))
            weight = jnp.concatenate(
                [jnp.concatenate(highs, axis=1), jnp.concatenate(rests, axis=1)], axis=0
            )
            source_values = jnp.concatenate([values[n] for n in ids], axis=0)
            part = jnp.dot(weight, source_values, preferred_element_type=F32)
            total = part if total is None else total + part
        sums[here, :] = total[:64] + total[64:]
        return carry

    lax.fori_loop(0, LEAVES, one_leaf, 0, unroll=4)
    for tile in range(LEAVES // 2):
        cols = slice(tile * LANES, tile * LANES + LANES)
        flipped = sums[cols, :].T
        out_ref[:, cols] = flipped[:64] + flipped[64:] + NUGGET * own_ref[:64, cols]


def final_kernel(own_ref, other_ref, far_ref, weights_ref, near_ref, basis_ref, transfer_ref, out_ref):
    first = jnp.full((32, LANES), lax.axis_index("core"), jnp.int32) == 0
    own = unfold(own_ref[...])
    other = unfold(other_ref[...])
    above = jnp.concatenate([jnp.where(first, own, other), jnp.where(first, other, own)], axis=0)
    down = far_ref[...] + multiply([(split_lanes(above), weights_ref[DOWN[0, 0]])])
    down = down[:, :HALF].astype(BF16)
    for block in range(4):
        cols = slice(block * 256, block * 256 + 256)
        leaf_down = jnp.dot(down, transfer_ref[:, cols], preferred_element_type=F32).astype(BF16)
        far = jnp.dot(leaf_down, block_diagonal(basis_ref[:, cols]), preferred_element_type=F32)
        out_ref[:, cols] = near_ref[:, cols] + far


def call(kernel, out_shape, in_specs, scratch_shapes, *operands, limit=40):
    shapes = tuple(jax.ShapeDtypeStruct(shape, dtype) for shape, dtype in out_shape)
    return pl.pallas_call(
        kernel,
        out_shape=shapes,
        in_specs=in_specs,
        out_specs=(VMEM,) * len(shapes),
        scratch_shapes=scratch_shapes,
        compiler_params=pltpu.CompilerParams(vmem_limit_bytes=limit * 1024 * 1024),
    )(*operands)


def exchange(value, names):
    return lax.all_to_all(value, names, split_axis=0, concat_axis=0, tiled=True)


def body(
    right_sides,
    points,
    leaf_basis,
    leaf_transfer,
    upper_transfer,
    coupling,
    near_leaves,
    admissible,
):
    width = right_sides.shape[1]
    lifted, send = call(
        up_kernel,
        [((32, LANES), F32), ((80, width), F32)],
        [pl.BlockSpec(memory_space=pltpu.HBM)] * 5,
        [
            pltpu.VMEM((3, width), F32),
            pltpu.VMEM((64, width), BF16),
            pltpu.VMEM((64, width), BF16),
            pltpu.VMEM((64, 64), F32),
            pltpu.SemaphoreType.DMA((5,)),
        ],
        right_sides,
        points,
        leaf_basis,
        leaf_transfer,
        upper_transfer,
        limit=60,
    )
    swap = [(0, 1), (1, 0)]
    from_x = lax.ppermute(send, "core", swap)
    from_y = lax.ppermute(send, "y", [(j, j ^ 1) for j in range(lax.axis_size("y"))])
    (pair,) = call(
        pair_kernel, [((2 ** len(SOURCE), 16, LANES), F32)], [VMEM] * 2, [], lifted, from_x
    )
    gathered = exchange(pair, ("xl", "z"))
    (weights,) = call(
        weights_kernel,
        [((WEIGHTS, 128, LANES), BF16)],
        [VMEM] * 2 + [SMEM, ANYWHERE],
        [],
        upper_transfer,
        coupling,
        admissible.T,
        pair,
    )
    heights = range(1, LEVELS - 1)
    partial, tie = call(
        tree_kernel,
        [((2 ** len(TARGET), 16, LANES), F32), ((8, LANES), F32)],
        [VMEM] * 2 + [ANYWHERE],
        [pltpu.VMEM((2 ** len(above(SOURCE, h)), 32, LANES), BF16) for h in heights]
        + [pltpu.VMEM((2 ** len(above(TARGET, h)), 32, LANES), F32) for h in heights],
        gathered,
        weights,
        from_y,
    )
    parts = exchange(partial, ("xh", "y"))
    from_xy = lax.ppermute(from_y, "core", swap)
    near, far = call(
        near_kernel,
        [((64, width), F32), ((64, LANES), F32)],
        [SMEM] + [VMEM] * 6,
        [
            pltpu.VMEM((4 * LEAVES, LEAF, LANES), BF16),
            pltpu.VMEM((4 * LEAVES, 8, LANES), F32),
            pltpu.VMEM((3, width, LANES), F32),
            pltpu.VMEM((width, LANES), F32),
        ],
        near_leaves,
        send,
        from_x,
        from_y,
        from_xy,
        weights,
        tie,
    )
    (own,) = call(sum_kernel, [((16, LANES), F32)], [VMEM, ANYWHERE], [], parts, far)
    other = lax.ppermute(own, "core", swap)
    (product,) = call(
        final_kernel,
        [((64, width), F32)],
        [VMEM] * 7,
        [],
        own,
        other,
        far,
        weights,
        near,
        leaf_basis,
        leaf_transfer,
    )
    return product


def solution(mesh):
    every = ("z", "core", "xh", "xl", "y")
    fine = jax.sharding.Mesh(mesh.devices.reshape(8, 2, 2, 2, 8), every)
    split = P(None, every)
    in_specs = (split, split, split, split, P(), P(), P(every, None), P())
    return jax.shard_map(body, mesh=fine, in_specs=in_specs, out_specs=split, check_vma=False)
```

```python
import jax
import jax.numpy as jnp
from jax import lax
from jax.experimental import pallas as pl
from jax.experimental.pallas import tpu as pltpu
from jax.sharding import PartitionSpec as P

ROOT_THREE = 1.7320508075688772
LENGTH_SCALE = 0.6
AMPLITUDE = 0.25
NUGGET = 0.5
LOG2_E = 1.4426950408889634
BITS_X = 4
BITS_Y = 5
DEVICES = 512
LEVELS = 9
LEAVES = 16
LEAF = 64
RANK = 64
HALF = 64
LANES = 128
F32 = jnp.float32
BF16 = jnp.bfloat16
NT = (((1,), (1,)), ((), ()))
VMEM = pl.BlockSpec(memory_space=pltpu.VMEM)
ANYWHERE = pl.BlockSpec(memory_space=pl.ANY)
SMEM = pl.BlockSpec(memory_space=pltpu.SMEM)


def places():
    listed = []
    for bit in range(max(BITS_X, BITS_Y)):
        if bit < BITS_X:
            listed.append(("x", bit))
        if bit < BITS_Y:
            listed.append(("y", bit))
    return listed


PLACES = places()
SOURCE = (2, 4, 6, 7)
TARGET = (1, 3, 5, 8)

CLIMB, DOWN, FAR = {}, {}, {}
for _h in range(1, LEVELS - 2):
    for _side in range(2 if _h in SOURCE else 1):
        CLIMB[_h, _side] = len(CLIMB)
for _h in range(LEVELS - 2):
    for _side in range(2 if _h in TARGET else 1):
        DOWN[_h, _side] = len(CLIMB) + len(DOWN)
for _h in range(LEVELS - 1):
    for _step in (1, 2, 3):
        FAR[_h, _step] = len(CLIMB) + len(DOWN) + len(FAR)
WEIGHTS = len(CLIMB) + len(DOWN) + len(FAR)


def above(chosen, h):
    return [place for place in chosen if place >= h]


def flipped(chosen, h, step):
    listed = above(chosen, h)
    return sum(1 << listed.index(h + p) for p in (0, 1) if step >> p & 1 and h + p in listed)


def low_lanes(rows):
    return lax.broadcasted_iota(jnp.int32, (rows, LANES), 1) < HALF


def split_lanes(value):
    high = value.astype(BF16).astype(F32)
    return jnp.where(low_lanes(value.shape[0]), high, value - high).astype(BF16)


def split_rows(wide):
    high = wide.astype(BF16)
    return jnp.concatenate([high, (wide - high.astype(F32)).astype(BF16)], axis=0)


def block_diagonal(basis):
    wide = basis.astype(F32)
    leaf = lax.broadcasted_iota(jnp.int32, wide.shape, 1) // LEAF
    return jnp.concatenate([jnp.where(leaf == l, wide, 0.0).astype(BF16) for l in range(4)], axis=0)


def up_kernel(
    right_ref,
    points_ref,
    basis_ref,
    transfer_ref,
    upper_ref,
    lifted_ref,
    send_ref,
    points_in,
    basis_in,
    transfer_in,
    upper_in,
    sems,
):
    copies = [
        pltpu.make_async_copy(right_ref, send_ref.at[pl.ds(0, 64)], sems.at[0]),
        pltpu.make_async_copy(basis_ref, basis_in, sems.at[1]),
        pltpu.make_async_copy(transfer_ref, transfer_in, sems.at[2]),
        pltpu.make_async_copy(points_ref, points_in, sems.at[3]),
        pltpu.make_async_copy(upper_ref.at[0, lax.axis_index("core")], upper_in, sems.at[4]),
    ]
    for copy in copies:
        copy.start()
    for copy in copies:
        copy.wait()
    total = None
    for block in range(4):
        cols = slice(block * 256, block * 256 + 256)
        rounded = send_ref[:64, cols].astype(BF16)
        leaf_coeff = lax.dot_general(
            rounded, block_diagonal(basis_in[:, cols]), NT, preferred_element_type=F32
        ).astype(BF16)
        transfer = transfer_in[:, cols]
        part = lax.dot_general(
            leaf_coeff,
            jnp.concatenate([transfer, transfer], axis=0),
            NT,
            preferred_element_type=F32,
        )
        total = part if total is None else total + part
    matrix = upper_in[...]
    wide = split_rows(jnp.concatenate([matrix, matrix], axis=1))
    lifted = multiply([(split_lanes(total), wide)])
    halves = [fold(lifted[:32]), fold(lifted[32:])]
    for target in range(lifted_ref.shape[0]):
        lifted_ref[target] = halves[target % 2]
    send_ref[64:72, :] = jnp.zeros((8, LEAVES * LEAF), F32)
    send_ref[64:67, :] = points_in[...]
    packed = fold(total)
    for tile in range(8):
        cols = slice(tile * LANES, tile * LANES + LANES)
        send_ref[72:76, cols] = packed[tile * 4 : tile * 4 + 4]


def device_index():
    core = lax.axis_index("core")
    index_y = lax.axis_index("xh") * 16 + lax.axis_index("xl") * 8 + lax.axis_index("y")
    return lax.axis_index("z") * 2 + core, index_y, core


def device_sides():
    index_x, index_y, _ = device_index()
    return [(index_x if axis == "x" else index_y) >> bit & 1 for axis, bit in PLACES]


def place_index(sides, listed):
    index = jnp.int32(0)
    for bit, place in enumerate(listed):
        index = index + sides[place] * 2**bit
    return index


def sent_coeff(ref):
    return jnp.concatenate(
        [ref[72:76, tile * LANES : tile * LANES + LANES] for tile in range(8)], axis=0
    )


def fold(value):
    rows = value.shape[0] // 2
    return jnp.where(low_lanes(rows), value[:rows], value[rows:])


def unfold(packed):
    low = low_lanes(packed.shape[0])
    rolled = pltpu.roll(packed, HALF, 1)
    return jnp.concatenate(
        [jnp.where(low, packed, rolled), jnp.where(low, rolled, packed)], axis=0
    )


def multiply(pairs):
    left = [piece for value, _ in pairs for piece in (value, value)]
    right = [piece for _, m in pairs for piece in (m[:64], m[:64], m[64:], m[64:])]
    return jnp.dot(
        jnp.concatenate(left, axis=1),
        jnp.concatenate(right, axis=0),
        preferred_element_type=F32,
    )


def weights_kernel(upper_ref, coupling_ref, admissible_ref, out_ref):
    sides = device_sides()
    code = place_index(sides, range(LEVELS))

    def plain(matrix):
        return jnp.concatenate([matrix, matrix], axis=1)

    def transposed(matrix):
        return jnp.concatenate([matrix, matrix], axis=0).T

    for h in range(LEVELS - 2):
        for side in range(2):
            own = sides[h] if (h, 1) not in CLIMB else side
            if (h, side) in CLIMB:
                out_ref[CLIMB[h, side]] = split_rows(plain(upper_ref[h, own]))
            own = sides[h] if (h, 1) not in DOWN else side
            if (h, side) in DOWN:
                out_ref[DOWN[h, side]] = split_rows(transposed(upper_ref[h, own]))
    for h in range(LEVELS - 1):
        first = 2 * DEVICES - 2 * DEVICES // 2**h
        for step in (1, 2, 3):
            turned = sum(1 << p for p in (0, 1) if step >> p & 1 and h + p in TARGET)
            target = (code >> h) ^ (turned if h else 0)
            here = target & 3
            there = here ^ step
            matrix = coupling_ref[h, jnp.abs(there - here) - 1]
            flag = admissible_ref[step - 1, first + target].astype(F32)
            upward = jnp.full((64, LANES), there - here, jnp.int32) > 0
            chosen = jnp.where(upward, transposed(matrix), plain(matrix))
            out_ref[FAR[h, step]] = split_rows(chosen * flag)


def tree_kernel(gathered_ref, weights_ref, x_ref, y_ref, out_ref, tie_ref, *scratch):
    coeff_refs = dict(zip(range(1, LEVELS - 1), scratch[: LEVELS - 2]))
    down_refs = dict(zip(range(1, LEVELS - 1), scratch[LEVELS - 2 :]))
    sides = device_sides()
    for chip in range(gathered_ref.shape[0] // 2):
        both = gathered_ref[2 * chip] + gathered_ref[2 * chip + 1]
        coeff_refs[1][chip] = split_lanes(unfold(both))
    for h in range(1, LEVELS - 2):
        count = coeff_refs[h].shape[0]
        if h in SOURCE:
            result = multiply(
                [
                    (
                        jnp.concatenate([coeff_refs[h][n] for n in range(bit, count, 2)], axis=0),
                        weights_ref[CLIMB[h, bit]],
                    )
                    for bit in range(2)
                ]
            )
        else:
            value = coeff_refs[h][...].reshape(count * 32, LANES)
            result = multiply([(value, weights_ref[CLIMB[h, 0]])])
        coeff_refs[h + 1][...] = split_lanes(result).reshape(coeff_refs[h + 1].shape)
    for h in range(LEVELS - 2, 0, -1):
        source = place_index(sides, above(SOURCE, h))
        target = place_index(sides, above(TARGET, h))
        count = down_refs[h].shape[0]
        if h == LEVELS - 2:
            down_refs[h][...] = jnp.zeros((count, 32, LANES), F32)
        else:
            parents = down_refs[h + 1].shape[0]
            value = split_lanes(down_refs[h + 1][...].reshape(parents * 32, LANES))
            if h in TARGET:
                for bit in range(2):
                    part = multiply([(value, weights_ref[DOWN[h, bit]])])
                    for node in range(parents):
                        down_refs[h][node * 2 + bit] = part[node * 32 : node * 32 + 32]
            else:
                part = multiply([(value, weights_ref[DOWN[h, 0]])])
                down_refs[h][...] = part.reshape(count, 32, LANES)
        terms = {}
        for step in (1, 2, 3):
            pair = coeff_refs[h][source ^ flipped(SOURCE, h, step)], weights_ref[FAR[h, step]]
            terms.setdefault(flipped(TARGET, h, step), []).append(pair)
        for turned, pairs in terms.items():
            down_refs[h][target ^ turned] += multiply(pairs)
    for node in range(out_ref.shape[0]):
        out_ref[node] = fold(down_refs[1][node])
    tie_ref[...] = jnp.zeros_like(tie_ref)


def sum_kernel(parts_ref, tie_ref, out_ref):
    total = parts_ref[0]
    for source in range(1, parts_ref.shape[0]):
        total = total + parts_ref[source]
    out_ref[...] = total


def near_kernel(
    listed_ref,
    own_ref,
    x_ref,
    y_ref,
    xy_ref,
    weights_ref,
    tie_ref,
    out_ref,
    far_ref,
    values,
    rows,
    columns,
    sums,
):
    _, index_y, core = device_index()
    far_ref[...] = multiply(
        [
            (split_lanes(unfold(sent_coeff(ref))), weights_ref[FAR[0, step]])
            for step, ref in enumerate((x_ref, y_ref, xy_ref), 1)
        ]
    )
    low = low_lanes(8)
    for tile in range(LEAVES // 2):
        cols = slice(tile * LANES, tile * LANES + LANES)
        for axis in range(3):
            spread = jnp.broadcast_to(own_ref[64 + axis : 65 + axis, cols], (LANES, LANES))
            columns[axis, cols, :] = spread.T
    for block, ref in enumerate((own_ref, x_ref, y_ref, xy_ref)):
        for tile in range(LEAVES // 2):
            cols = slice(tile * LANES, tile * LANES + LANES)
            first = block * LEAVES + tile * 2
            values[first : first + 2] = split_rows(ref[:64, cols]).T.reshape(2, LEAF, LANES)
            point = ref[64:72, cols]
            rolled = pltpu.roll(point, HALF, 1)
            rows[first] = jnp.where(low, point, rolled)
            rows[first + 1] = jnp.where(low, rolled, point)

    def local(leaf, place):
        listed = listed_ref[leaf, place]
        owner = listed >> 4
        flip_x = (owner >> BITS_Y ^ core) & 1
        flip_y = (owner ^ index_y) & 1
        return (flip_x + 2 * flip_y) * LEAVES + (listed & LEAVES - 1)

    def one_leaf(leaf, carry):
        here = pl.ds(pl.multiple_of(leaf * LEAF, LEAF), LEAF)
        total = None
        for quad in range(3):
            ids = [local(leaf, quad * 4 + place) for place in range(4)]
            highs = []
            rests = []
            for pair in range(2):
                source = jnp.where(low, rows[ids[pair * 2]], rows[ids[pair * 2 + 1]])
                square = None
                for axis in range(3):
                    delta = columns[axis, here, :] - source[axis : axis + 1]
                    square = delta * delta if square is None else square + delta * delta
                square = jnp.maximum(square, 1e-30)
                distance = square * lax.rsqrt(square)
                scale = ROOT_THREE / LENGTH_SCALE
                decay = jnp.exp2(distance * (-scale * LOG2_E))
                kernel = (distance * (AMPLITUDE * scale) + AMPLITUDE) * decay
                high = kernel.astype(BF16)
                highs.append(high)
                rests.append((kernel - high.astype(F32)).astype(BF16))
            weight = jnp.concatenate(
                [jnp.concatenate(highs, axis=1), jnp.concatenate(rests, axis=1)], axis=0
            )
            source_values = jnp.concatenate([values[n] for n in ids], axis=0)
            part = jnp.dot(weight, source_values, preferred_element_type=F32)
            total = part if total is None else total + part
        sums[here, :] = total[:64] + total[64:]
        return carry

    lax.fori_loop(0, LEAVES, one_leaf, 0, unroll=4)
    for tile in range(LEAVES // 2):
        cols = slice(tile * LANES, tile * LANES + LANES)
        flipped = sums[cols, :].T
        out_ref[:, cols] = flipped[:64] + flipped[64:] + NUGGET * own_ref[:64, cols]


def final_kernel(own_ref, other_ref, far_ref, weights_ref, near_ref, basis_ref, transfer_ref, out_ref):
    first = jnp.full((32, LANES), lax.axis_index("core"), jnp.int32) == 0
    own = unfold(own_ref[...])
    other = unfold(other_ref[...])
    above = jnp.concatenate([jnp.where(first, own, other), jnp.where(first, other, own)], axis=0)
    down = far_ref[...] + multiply([(split_lanes(above), weights_ref[DOWN[0, 0]])])
    down = down[:, :HALF].astype(BF16)
    for block in range(4):
        cols = slice(block * 256, block * 256 + 256)
        leaf_down = jnp.dot(down, transfer_ref[:, cols], preferred_element_type=F32).astype(BF16)
        far = jnp.dot(leaf_down, block_diagonal(basis_ref[:, cols]), preferred_element_type=F32)
        out_ref[:, cols] = near_ref[:, cols] + far


def call(kernel, out_shape, in_specs, scratch_shapes, *operands, limit=40):
    shapes = tuple(jax.ShapeDtypeStruct(shape, dtype) for shape, dtype in out_shape)
    return pl.pallas_call(
        kernel,
        out_shape=shapes,
        in_specs=in_specs,
        out_specs=(VMEM,) * len(shapes),
        scratch_shapes=scratch_shapes,
        compiler_params=pltpu.CompilerParams(vmem_limit_bytes=limit * 1024 * 1024),
    )(*operands)


def exchange(value, names):
    return lax.all_to_all(value, names, split_axis=0, concat_axis=0, tiled=True)


def body(
    right_sides,
    points,
    leaf_basis,
    leaf_transfer,
    upper_transfer,
    coupling,
    near_leaves,
    admissible,
):
    width = right_sides.shape[1]
    lifted, send = call(
        up_kernel,
        [((2 ** len(SOURCE) * 2, 16, LANES), F32), ((80, width), F32)],
        [pl.BlockSpec(memory_space=pltpu.HBM)] * 5,
        [
            pltpu.VMEM((3, width), F32),
            pltpu.VMEM((64, width), BF16),
            pltpu.VMEM((64, width), BF16),
            pltpu.VMEM((64, 64), F32),
            pltpu.SemaphoreType.DMA((5,)),
        ],
        right_sides,
        points,
        leaf_basis,
        leaf_transfer,
        upper_transfer,
        limit=60,
    )
    swap = [(0, 1), (1, 0)]
    from_x = lax.ppermute(send, "core", swap)
    from_y = lax.ppermute(send, "y", [(j, j ^ 1) for j in range(lax.axis_size("y"))])
    gathered = exchange(lifted, ("xl", "z", "core"))
    (weights,) = call(
        weights_kernel,
        [((WEIGHTS, 128, LANES), BF16)],
        [VMEM] * 2 + [SMEM],
        [],
        upper_transfer,
        coupling,
        admissible.T,
    )
    heights = range(1, LEVELS - 1)
    partial, tie = call(
        tree_kernel,
        [((2 ** len(TARGET), 16, LANES), F32), ((8, LANES), F32)],
        [VMEM] * 2 + [ANYWHERE] * 2,
        [pltpu.VMEM((2 ** len(above(SOURCE, h)), 32, LANES), BF16) for h in heights]
        + [pltpu.VMEM((2 ** len(above(TARGET, h)), 32, LANES), F32) for h in heights],
        gathered,
        weights,
        from_x,
        from_y,
    )
    parts = exchange(partial, ("xh", "y"))
    from_xy = lax.ppermute(from_y, "core", swap)
    near, far = call(
        near_kernel,
        [((64, width), F32), ((64, LANES), F32)],
        [SMEM] + [VMEM] * 6,
        [
            pltpu.VMEM((4 * LEAVES, LEAF, LANES), BF16),
            pltpu.VMEM((4 * LEAVES, 8, LANES), F32),
            pltpu.VMEM((3, width, LANES), F32),
            pltpu.VMEM((width, LANES), F32),
        ],
        near_leaves,
        send,
        from_x,
        from_y,
        from_xy,
        weights,
        tie,
    )
    (own,) = call(sum_kernel, [((16, LANES), F32)], [VMEM, ANYWHERE], [], parts, far)
    other = lax.ppermute(own, "core", swap)
    (product,) = call(
        final_kernel,
        [((64, width), F32)],
        [VMEM] * 7,
        [],
        own,
        other,
        far,
        weights,
        near,
        leaf_basis,
        leaf_transfer,
    )
    return product


def solution(mesh):
    every = ("z", "core", "xh", "xl", "y")
    fine = jax.sharding.Mesh(mesh.devices.reshape(8, 2, 2, 2, 8), every)
    split = P(None, every)
    in_specs = (split, split, split, split, P(), P(), P(every, None), P())
    return jax.shard_map(body, mesh=fine, in_specs=in_specs, out_specs=split, check_vma=False)
```

```python
import jax
import jax.numpy as jnp
from jax import lax
from jax.experimental import pallas as pl
from jax.experimental.pallas import tpu as pltpu
from jax.sharding import PartitionSpec as P

ROOT_THREE = 1.7320508075688772
LENGTH_SCALE = 0.6
AMPLITUDE = 0.25
NUGGET = 0.5
LOG2_E = 1.4426950408889634
BITS_X = 4
BITS_Y = 5
DEVICES = 512
LEVELS = 9
LEAVES = 16
LEAF = 64
RANK = 64
HALF = 64
LANES = 128
F32 = jnp.float32
BF16 = jnp.bfloat16
NT = (((1,), (1,)), ((), ()))
VMEM = pl.BlockSpec(memory_space=pltpu.VMEM)
ANYWHERE = pl.BlockSpec(memory_space=pl.ANY)
SMEM = pl.BlockSpec(memory_space=pltpu.SMEM)


def places():
    listed = []
    for bit in range(max(BITS_X, BITS_Y)):
        if bit < BITS_X:
            listed.append(("x", bit))
        if bit < BITS_Y:
            listed.append(("y", bit))
    return listed


PLACES = places()
SOURCE = (2, 4, 6, 7)
TARGET = (1, 3, 5, 8)

CLIMB, DOWN, FAR = {}, {}, {}
for _h in range(1, LEVELS - 2):
    for _side in range(2 if _h in SOURCE else 1):
        CLIMB[_h, _side] = len(CLIMB)
for _h in range(LEVELS - 2):
    for _side in range(2 if _h in TARGET else 1):
        DOWN[_h, _side] = len(CLIMB) + len(DOWN)
for _h in range(LEVELS - 1):
    for _step in (1, 2, 3):
        FAR[_h, _step] = len(CLIMB) + len(DOWN) + len(FAR)
WEIGHTS = len(CLIMB) + len(DOWN) + len(FAR)


def above(chosen, h):
    return [place for place in chosen if place >= h]


def flipped(chosen, h, step):
    listed = above(chosen, h)
    return sum(1 << listed.index(h + p) for p in (0, 1) if step >> p & 1 and h + p in listed)


def low_lanes(rows):
    return lax.broadcasted_iota(jnp.int32, (rows, LANES), 1) < HALF


def split_lanes(value):
    high = value.astype(BF16).astype(F32)
    return jnp.where(low_lanes(value.shape[0]), high, value - high).astype(BF16)


def split_rows(wide):
    high = wide.astype(BF16)
    return jnp.concatenate([high, (wide - high.astype(F32)).astype(BF16)], axis=0)


def block_diagonal(basis):
    wide = basis.astype(F32)
    leaf = lax.broadcasted_iota(jnp.int32, wide.shape, 1) // LEAF
    return jnp.concatenate([jnp.where(leaf == l, wide, 0.0).astype(BF16) for l in range(4)], axis=0)


def up_kernel(
    right_ref,
    points_ref,
    basis_ref,
    transfer_ref,
    upper_ref,
    lifted_ref,
    send_ref,
    points_in,
    basis_in,
    transfer_in,
    upper_in,
    sems,
):
    copies = [
        pltpu.make_async_copy(right_ref, send_ref.at[pl.ds(0, 64)], sems.at[0]),
        pltpu.make_async_copy(basis_ref, basis_in, sems.at[1]),
        pltpu.make_async_copy(transfer_ref, transfer_in, sems.at[2]),
        pltpu.make_async_copy(points_ref, points_in, sems.at[3]),
        pltpu.make_async_copy(upper_ref.at[0, lax.axis_index("core")], upper_in, sems.at[4]),
    ]
    for copy in copies:
        copy.start()
    for copy in copies:
        copy.wait()
    total = None
    for block in range(4):
        cols = slice(block * 256, block * 256 + 256)
        rounded = send_ref[:64, cols].astype(BF16)
        leaf_coeff = lax.dot_general(
            rounded, block_diagonal(basis_in[:, cols]), NT, preferred_element_type=F32
        ).astype(BF16)
        transfer = transfer_in[:, cols]
        part = lax.dot_general(
            leaf_coeff,
            jnp.concatenate([transfer, transfer], axis=0),
            NT,
            preferred_element_type=F32,
        )
        total = part if total is None else total + part
    matrix = upper_in[...]
    wide = split_rows(jnp.concatenate([matrix, matrix], axis=1))
    lifted = multiply([(split_lanes(total), wide)])
    halves = [fold(lifted[:32]), fold(lifted[32:])]
    for target in range(lifted_ref.shape[0]):
        lifted_ref[target] = halves[target % 2]
    send_ref[64:67, :] = points_in[...]
    packed = fold(total)
    for tile in range(8):
        cols = slice(tile * LANES, tile * LANES + LANES)
        send_ref[67:71, cols] = packed[tile * 4 : tile * 4 + 4]
    send_ref[71:72, :] = jnp.zeros((1, LEAVES * LEAF), F32)


def device_index():
    core = lax.axis_index("core")
    index_y = lax.axis_index("xh") * 16 + lax.axis_index("xl") * 8 + lax.axis_index("y")
    return lax.axis_index("z") * 2 + core, index_y, core


def device_sides():
    index_x, index_y, _ = device_index()
    return [(index_x if axis == "x" else index_y) >> bit & 1 for axis, bit in PLACES]


def place_index(sides, listed):
    index = jnp.int32(0)
    for bit, place in enumerate(listed):
        index = index + sides[place] * 2**bit
    return index


def sent_coeff(ref):
    return jnp.concatenate(
        [ref[67:71, tile * LANES : tile * LANES + LANES] for tile in range(8)], axis=0
    )


def fold(value):
    rows = value.shape[0] // 2
    return jnp.where(low_lanes(rows), value[:rows], value[rows:])


def unfold(packed):
    low = low_lanes(packed.shape[0])
    rolled = pltpu.roll(packed, HALF, 1)
    return jnp.concatenate(
        [jnp.where(low, packed, rolled), jnp.where(low, rolled, packed)], axis=0
    )


def multiply(pairs):
    left = [piece for value, _ in pairs for piece in (value, value)]
    right = [piece for _, m in pairs for piece in (m[:64], m[:64], m[64:], m[64:])]
    return jnp.dot(
        jnp.concatenate(left, axis=1),
        jnp.concatenate(right, axis=0),
        preferred_element_type=F32,
    )


def weights_kernel(upper_ref, coupling_ref, admissible_ref, out_ref):
    sides = device_sides()
    code = place_index(sides, range(LEVELS))

    def plain(matrix):
        return jnp.concatenate([matrix, matrix], axis=1)

    def transposed(matrix):
        return jnp.concatenate([matrix, matrix], axis=0).T

    for h in range(LEVELS - 2):
        for side in range(2):
            own = sides[h] if (h, 1) not in CLIMB else side
            if (h, side) in CLIMB:
                out_ref[CLIMB[h, side]] = split_rows(plain(upper_ref[h, own]))
            own = sides[h] if (h, 1) not in DOWN else side
            if (h, side) in DOWN:
                out_ref[DOWN[h, side]] = split_rows(transposed(upper_ref[h, own]))
    for h in range(LEVELS - 1):
        first = 2 * DEVICES - 2 * DEVICES // 2**h
        for step in (1, 2, 3):
            turned = sum(1 << p for p in (0, 1) if step >> p & 1 and h + p in TARGET)
            target = (code >> h) ^ (turned if h else 0)
            here = target & 3
            there = here ^ step
            matrix = coupling_ref[h, jnp.abs(there - here) - 1]
            flag = admissible_ref[step - 1, first + target].astype(F32)
            upward = jnp.full((64, LANES), there - here, jnp.int32) > 0
            chosen = jnp.where(upward, transposed(matrix), plain(matrix))
            out_ref[FAR[h, step]] = split_rows(chosen * flag)


def tree_kernel(gathered_ref, weights_ref, x_ref, y_ref, out_ref, tie_ref, *scratch):
    coeff_refs = dict(zip(range(1, LEVELS - 1), scratch[: LEVELS - 2]))
    down_refs = dict(zip(range(1, LEVELS - 1), scratch[LEVELS - 2 :]))
    sides = device_sides()
    for chip in range(gathered_ref.shape[0] // 2):
        both = gathered_ref[2 * chip] + gathered_ref[2 * chip + 1]
        coeff_refs[1][chip] = split_lanes(unfold(both))
    for h in range(1, LEVELS - 2):
        count = coeff_refs[h].shape[0]
        if h in SOURCE:
            result = multiply(
                [
                    (
                        jnp.concatenate([coeff_refs[h][n] for n in range(bit, count, 2)], axis=0),
                        weights_ref[CLIMB[h, bit]],
                    )
                    for bit in range(2)
                ]
            )
        else:
            value = coeff_refs[h][...].reshape(count * 32, LANES)
            result = multiply([(value, weights_ref[CLIMB[h, 0]])])
        coeff_refs[h + 1][...] = split_lanes(result).reshape(coeff_refs[h + 1].shape)
    for h in range(LEVELS - 2, 0, -1):
        source = place_index(sides, above(SOURCE, h))
        target = place_index(sides, above(TARGET, h))
        count = down_refs[h].shape[0]
        if h == LEVELS - 2:
            down_refs[h][...] = jnp.zeros((count, 32, LANES), F32)
        else:
            parents = down_refs[h + 1].shape[0]
            value = split_lanes(down_refs[h + 1][...].reshape(parents * 32, LANES))
            if h in TARGET:
                for bit in range(2):
                    part = multiply([(value, weights_ref[DOWN[h, bit]])])
                    for node in range(parents):
                        down_refs[h][node * 2 + bit] = part[node * 32 : node * 32 + 32]
            else:
                part = multiply([(value, weights_ref[DOWN[h, 0]])])
                down_refs[h][...] = part.reshape(count, 32, LANES)
        terms = {}
        for step in (1, 2, 3):
            pair = coeff_refs[h][source ^ flipped(SOURCE, h, step)], weights_ref[FAR[h, step]]
            terms.setdefault(flipped(TARGET, h, step), []).append(pair)
        for turned, pairs in terms.items():
            down_refs[h][target ^ turned] += multiply(pairs)
    for node in range(out_ref.shape[0]):
        out_ref[node] = fold(down_refs[1][node])
    tie_ref[...] = jnp.zeros_like(tie_ref)


def sum_kernel(parts_ref, tie_ref, out_ref):
    total = parts_ref[0]
    for source in range(1, parts_ref.shape[0]):
        total = total + parts_ref[source]
    out_ref[...] = total


def near_kernel(
    listed_ref,
    own_ref,
    x_ref,
    y_ref,
    xy_ref,
    weights_ref,
    tie_ref,
    out_ref,
    far_ref,
    values,
    rows,
    columns,
    sums,
):
    _, index_y, core = device_index()
    far_ref[...] = multiply(
        [
            (split_lanes(unfold(sent_coeff(ref))), weights_ref[FAR[0, step]])
            for step, ref in enumerate((x_ref, y_ref, xy_ref), 1)
        ]
    )
    low = low_lanes(8)
    for tile in range(LEAVES // 2):
        cols = slice(tile * LANES, tile * LANES + LANES)
        for axis in range(3):
            spread = jnp.broadcast_to(own_ref[64 + axis : 65 + axis, cols], (LANES, LANES))
            columns[axis, cols, :] = spread.T
    for block, ref in enumerate((own_ref, x_ref, y_ref, xy_ref)):
        for tile in range(LEAVES // 2):
            cols = slice(tile * LANES, tile * LANES + LANES)
            first = block * LEAVES + tile * 2
            values[first : first + 2] = split_rows(ref[:64, cols]).T.reshape(2, LEAF, LANES)
            point = ref[64:72, cols]
            rolled = pltpu.roll(point, HALF, 1)
            rows[first] = jnp.where(low, point, rolled)
            rows[first + 1] = jnp.where(low, rolled, point)

    def local(leaf, place):
        listed = listed_ref[leaf, place]
        owner = listed >> 4
        flip_x = (owner >> BITS_Y ^ core) & 1
        flip_y = (owner ^ index_y) & 1
        return (flip_x + 2 * flip_y) * LEAVES + (listed & LEAVES - 1)

    def one_leaf(leaf, carry):
        here = pl.ds(pl.multiple_of(leaf * LEAF, LEAF), LEAF)
        total = None
        for quad in range(3):
            ids = [local(leaf, quad * 4 + place) for place in range(4)]
            highs = []
            rests = []
            for pair in range(2):
                source = jnp.where(low, rows[ids[pair * 2]], rows[ids[pair * 2 + 1]])
                square = None
                for axis in range(3):
                    delta = columns[axis, here, :] - source[axis : axis + 1]
                    square = delta * delta if square is None else square + delta * delta
                square = jnp.maximum(square, 1e-30)
                distance = square * lax.rsqrt(square)
                scale = ROOT_THREE / LENGTH_SCALE
                decay = jnp.exp2(distance * (-scale * LOG2_E))
                kernel = (distance * (AMPLITUDE * scale) + AMPLITUDE) * decay
                high = kernel.astype(BF16)
                highs.append(high)
                rests.append((kernel - high.astype(F32)).astype(BF16))
            weight = jnp.concatenate(
                [jnp.concatenate(highs, axis=1), jnp.concatenate(rests, axis=1)], axis=0
            )
            source_values = jnp.concatenate([values[n] for n in ids], axis=0)
            part = jnp.dot(weight, source_values, preferred_element_type=F32)
            total = part if total is None else total + part
        sums[here, :] = total[:64] + total[64:]
        return carry

    lax.fori_loop(0, LEAVES, one_leaf, 0, unroll=4)
    for tile in range(LEAVES // 2):
        cols = slice(tile * LANES, tile * LANES + LANES)
        flipped = sums[cols, :].T
        out_ref[:, cols] = flipped[:64] + flipped[64:] + NUGGET * own_ref[:64, cols]


def final_kernel(own_ref, other_ref, far_ref, weights_ref, near_ref, basis_ref, transfer_ref, out_ref):
    first = jnp.full((32, LANES), lax.axis_index("core"), jnp.int32) == 0
    own = unfold(own_ref[...])
    other = unfold(other_ref[...])
    above = jnp.concatenate([jnp.where(first, own, other), jnp.where(first, other, own)], axis=0)
    down = far_ref[...] + multiply([(split_lanes(above), weights_ref[DOWN[0, 0]])])
    down = down[:, :HALF].astype(BF16)
    for block in range(4):
        cols = slice(block * 256, block * 256 + 256)
        leaf_down = jnp.dot(down, transfer_ref[:, cols], preferred_element_type=F32).astype(BF16)
        far = jnp.dot(leaf_down, block_diagonal(basis_ref[:, cols]), preferred_element_type=F32)
        out_ref[:, cols] = near_ref[:, cols] + far


def call(kernel, out_shape, in_specs, scratch_shapes, *operands, limit=40):
    shapes = tuple(jax.ShapeDtypeStruct(shape, dtype) for shape, dtype in out_shape)
    return pl.pallas_call(
        kernel,
        out_shape=shapes,
        in_specs=in_specs,
        out_specs=(VMEM,) * len(shapes),
        scratch_shapes=scratch_shapes,
        compiler_params=pltpu.CompilerParams(vmem_limit_bytes=limit * 1024 * 1024),
    )(*operands)


def exchange(value, names):
    return lax.all_to_all(value, names, split_axis=0, concat_axis=0, tiled=True)


def body(
    right_sides,
    points,
    leaf_basis,
    leaf_transfer,
    upper_transfer,
    coupling,
    near_leaves,
    admissible,
):
    width = right_sides.shape[1]
    lifted, send = call(
        up_kernel,
        [((2 ** len(SOURCE) * 2, 16, LANES), F32), ((72, width), F32)],
        [pl.BlockSpec(memory_space=pltpu.HBM)] * 5,
        [
            pltpu.VMEM((3, width), F32),
            pltpu.VMEM((64, width), BF16),
            pltpu.VMEM((64, width), BF16),
            pltpu.VMEM((64, 64), F32),
            pltpu.SemaphoreType.DMA((5,)),
        ],
        right_sides,
        points,
        leaf_basis,
        leaf_transfer,
        upper_transfer,
        limit=60,
    )
    swap = [(0, 1), (1, 0)]
    from_x = lax.ppermute(send, "core", swap)
    from_y = lax.ppermute(send, "y", [(j, j ^ 1) for j in range(lax.axis_size("y"))])
    gathered = exchange(lifted, ("xl", "z", "core"))
    (weights,) = call(
        weights_kernel,
        [((WEIGHTS, 128, LANES), BF16)],
        [VMEM] * 2 + [SMEM],
        [],
        upper_transfer,
        coupling,
        admissible.T,
    )
    heights = range(1, LEVELS - 1)
    partial, tie = call(
        tree_kernel,
        [((2 ** len(TARGET), 16, LANES), F32), ((8, LANES), F32)],
        [VMEM] * 2 + [ANYWHERE] * 2,
        [pltpu.VMEM((2 ** len(above(SOURCE, h)), 32, LANES), BF16) for h in heights]
        + [pltpu.VMEM((2 ** len(above(TARGET, h)), 32, LANES), F32) for h in heights],
        gathered,
        weights,
        from_x,
        from_y,
    )
    parts = exchange(partial, ("xh", "y"))
    from_y, tie = lax.optimization_barrier((from_y, tie))
    from_xy = lax.ppermute(from_y, "core", swap)
    near, far = call(
        near_kernel,
        [((64, width), F32), ((64, LANES), F32)],
        [SMEM] + [VMEM] * 6,
        [
            pltpu.VMEM((4 * LEAVES, LEAF, LANES), BF16),
            pltpu.VMEM((4 * LEAVES, 8, LANES), F32),
            pltpu.VMEM((3, width, LANES), F32),
            pltpu.VMEM((width, LANES), F32),
        ],
        near_leaves,
        send,
        from_x,
        from_y,
        from_xy,
        weights,
        tie,
    )
    (own,) = call(sum_kernel, [((16, LANES), F32)], [VMEM, ANYWHERE], [], parts, far)
    other = lax.ppermute(own, "core", swap)
    (product,) = call(
        final_kernel,
        [((64, width), F32)],
        [VMEM] * 7,
        [],
        own,
        other,
        far,
        weights,
        near,
        leaf_basis,
        leaf_transfer,
    )
    return product


def solution(mesh):
    every = ("z", "core", "xh", "xl", "y")
    fine = jax.sharding.Mesh(mesh.devices.reshape(8, 2, 2, 2, 8), every)
    split = P(None, every)
    in_specs = (split, split, split, split, P(), P(), P(every, None), P())
    return jax.shard_map(body, mesh=fine, in_specs=in_specs, out_specs=split, check_vma=False)
```

```python
import jax
import jax.numpy as jnp
from jax import lax
from jax.experimental import pallas as pl
from jax.experimental.pallas import tpu as pltpu
from jax.sharding import PartitionSpec as P

ROOT_THREE = 1.7320508075688772
LENGTH_SCALE = 0.6
AMPLITUDE = 0.25
NUGGET = 0.5
LOG2_E = 1.4426950408889634
BITS_X = 4
BITS_Y = 5
DEVICES = 512
LEVELS = 9
LEAVES = 16
LEAF = 64
RANK = 64
HALF = 64
LANES = 128
F32 = jnp.float32
BF16 = jnp.bfloat16
NT = (((1,), (1,)), ((), ()))
VMEM = pl.BlockSpec(memory_space=pltpu.VMEM)
ANYWHERE = pl.BlockSpec(memory_space=pl.ANY)
SMEM = pl.BlockSpec(memory_space=pltpu.SMEM)


def places():
    listed = []
    for bit in range(max(BITS_X, BITS_Y)):
        if bit < BITS_X:
            listed.append(("x", bit))
        if bit < BITS_Y:
            listed.append(("y", bit))
    return listed


PLACES = places()
SOURCE = (2, 4, 6, 7)
TARGET = (1, 3, 5, 8)

CLIMB, DOWN, FAR = {}, {}, {}
for _h in range(1, LEVELS - 2):
    for _side in range(2 if _h in SOURCE else 1):
        CLIMB[_h, _side] = len(CLIMB)
for _h in range(LEVELS - 2):
    for _side in range(2 if _h in TARGET else 1):
        DOWN[_h, _side] = len(CLIMB) + len(DOWN)
for _h in range(LEVELS - 1):
    for _step in (1, 2, 3):
        FAR[_h, _step] = len(CLIMB) + len(DOWN) + len(FAR)
WEIGHTS = len(CLIMB) + len(DOWN) + len(FAR)


def above(chosen, h):
    return [place for place in chosen if place >= h]


def flipped(chosen, h, step):
    listed = above(chosen, h)
    return sum(1 << listed.index(h + p) for p in (0, 1) if step >> p & 1 and h + p in listed)


def low_lanes(rows):
    return lax.broadcasted_iota(jnp.int32, (rows, LANES), 1) < HALF


def split_lanes(value):
    high = value.astype(BF16).astype(F32)
    return jnp.where(low_lanes(value.shape[0]), high, value - high).astype(BF16)


def split_rows(wide):
    high = wide.astype(BF16)
    return jnp.concatenate([high, (wide - high.astype(F32)).astype(BF16)], axis=0)


def block_diagonal(basis):
    wide = basis.astype(F32)
    leaf = lax.broadcasted_iota(jnp.int32, wide.shape, 1) // LEAF
    return jnp.concatenate([jnp.where(leaf == l, wide, 0.0).astype(BF16) for l in range(4)], axis=0)


def up_kernel(
    right_ref,
    points_ref,
    basis_ref,
    transfer_ref,
    upper_ref,
    lifted_ref,
    send_ref,
    points_in,
    basis_in,
    transfer_in,
    upper_in,
    sems,
):
    copies = [
        pltpu.make_async_copy(right_ref, send_ref.at[pl.ds(0, 64)], sems.at[0]),
        pltpu.make_async_copy(basis_ref, basis_in, sems.at[1]),
        pltpu.make_async_copy(transfer_ref, transfer_in, sems.at[2]),
        pltpu.make_async_copy(points_ref, points_in, sems.at[3]),
        pltpu.make_async_copy(upper_ref.at[0, lax.axis_index("core")], upper_in, sems.at[4]),
    ]
    for copy in copies:
        copy.start()
    for copy in copies:
        copy.wait()
    total = None
    for block in range(4):
        cols = slice(block * 256, block * 256 + 256)
        rounded = send_ref[:64, cols].astype(BF16)
        leaf_coeff = lax.dot_general(
            rounded, block_diagonal(basis_in[:, cols]), NT, preferred_element_type=F32
        ).astype(BF16)
        transfer = transfer_in[:, cols]
        part = lax.dot_general(
            leaf_coeff,
            jnp.concatenate([transfer, transfer], axis=0),
            NT,
            preferred_element_type=F32,
        )
        total = part if total is None else total + part
    matrix = upper_in[...]
    wide = split_rows(jnp.concatenate([matrix, matrix], axis=1))
    lifted = multiply([(split_lanes(total), wide)])
    halves = [fold(lifted[:32]), fold(lifted[32:])]
    for target in range(lifted_ref.shape[0]):
        lifted_ref[target] = halves[target % 2]
    send_ref[64:67, :] = points_in[...]
    packed = fold(total)
    for tile in range(8):
        cols = slice(tile * LANES, tile * LANES + LANES)
        send_ref[67:71, cols] = packed[tile * 4 : tile * 4 + 4]
    send_ref[71:72, :] = jnp.zeros((1, LEAVES * LEAF), F32)


def device_index():
    core = lax.axis_index("core")
    index_y = lax.axis_index("xh") * 16 + lax.axis_index("xl") * 8 + lax.axis_index("y")
    return lax.axis_index("z") * 2 + core, index_y, core


def device_sides():
    index_x, index_y, _ = device_index()
    return [(index_x if axis == "x" else index_y) >> bit & 1 for axis, bit in PLACES]


def place_index(sides, listed):
    index = jnp.int32(0)
    for bit, place in enumerate(listed):
        index = index + sides[place] * 2**bit
    return index


def sent_coeff(ref):
    return jnp.concatenate(
        [ref[67:71, tile * LANES : tile * LANES + LANES] for tile in range(8)], axis=0
    )


def fold(value):
    rows = value.shape[0] // 2
    return jnp.where(low_lanes(rows), value[:rows], value[rows:])


def unfold(packed):
    low = low_lanes(packed.shape[0])
    rolled = pltpu.roll(packed, HALF, 1)
    return jnp.concatenate(
        [jnp.where(low, packed, rolled), jnp.where(low, rolled, packed)], axis=0
    )


def multiply(pairs):
    left = [piece for value, _ in pairs for piece in (value, value)]
    right = [piece for _, m in pairs for piece in (m[:64], m[:64], m[64:], m[64:])]
    return jnp.dot(
        jnp.concatenate(left, axis=1),
        jnp.concatenate(right, axis=0),
        preferred_element_type=F32,
    )


def weights_kernel(upper_ref, coupling_ref, admissible_ref, out_ref):
    sides = device_sides()
    code = place_index(sides, range(LEVELS))

    def plain(matrix):
        return jnp.concatenate([matrix, matrix], axis=1)

    def transposed(matrix):
        return jnp.concatenate([matrix, matrix], axis=0).T

    for h in range(LEVELS - 2):
        for side in range(2):
            own = sides[h] if (h, 1) not in CLIMB else side
            if (h, side) in CLIMB:
                out_ref[CLIMB[h, side]] = split_rows(plain(upper_ref[h, own]))
            own = sides[h] if (h, 1) not in DOWN else side
            if (h, side) in DOWN:
                out_ref[DOWN[h, side]] = split_rows(transposed(upper_ref[h, own]))
    for h in range(LEVELS - 1):
        first = 2 * DEVICES - 2 * DEVICES // 2**h
        for step in (1, 2, 3):
            turned = sum(1 << p for p in (0, 1) if step >> p & 1 and h + p in TARGET)
            target = (code >> h) ^ (turned if h else 0)
            here = target & 3
            there = here ^ step
            matrix = coupling_ref[h, jnp.abs(there - here) - 1]
            flag = admissible_ref[step - 1, first + target].astype(F32)
            upward = jnp.full((64, LANES), there - here, jnp.int32) > 0
            chosen = jnp.where(upward, transposed(matrix), plain(matrix))
            out_ref[FAR[h, step]] = split_rows(chosen * flag)


def tree_kernel(gathered_ref, weights_ref, x_ref, y_ref, out_ref, tie_ref, *scratch):
    coeff_refs = dict(zip(range(1, LEVELS - 1), scratch[: LEVELS - 2]))
    down_refs = dict(zip(range(1, LEVELS - 1), scratch[LEVELS - 2 :]))
    sides = device_sides()
    for chip in range(gathered_ref.shape[0] // 2):
        both = gathered_ref[2 * chip] + gathered_ref[2 * chip + 1]
        coeff_refs[1][chip] = split_lanes(unfold(both))
    for h in range(1, LEVELS - 2):
        count = coeff_refs[h].shape[0]
        if h in SOURCE:
            result = multiply(
                [
                    (
                        jnp.concatenate([coeff_refs[h][n] for n in range(bit, count, 2)], axis=0),
                        weights_ref[CLIMB[h, bit]],
                    )
                    for bit in range(2)
                ]
            )
        else:
            value = coeff_refs[h][...].reshape(count * 32, LANES)
            result = multiply([(value, weights_ref[CLIMB[h, 0]])])
        coeff_refs[h + 1][...] = split_lanes(result).reshape(coeff_refs[h + 1].shape)
    for h in range(LEVELS - 2, 0, -1):
        source = place_index(sides, above(SOURCE, h))
        target = place_index(sides, above(TARGET, h))
        count = down_refs[h].shape[0]
        if h == LEVELS - 2:
            down_refs[h][...] = jnp.zeros((count, 32, LANES), F32)
        else:
            parents = down_refs[h + 1].shape[0]
            value = split_lanes(down_refs[h + 1][...].reshape(parents * 32, LANES))
            if h in TARGET:
                for bit in range(2):
                    part = multiply([(value, weights_ref[DOWN[h, bit]])])
                    for node in range(parents):
                        down_refs[h][node * 2 + bit] = part[node * 32 : node * 32 + 32]
            else:
                part = multiply([(value, weights_ref[DOWN[h, 0]])])
                down_refs[h][...] = part.reshape(count, 32, LANES)
        terms = {}
        for step in (1, 2, 3):
            pair = coeff_refs[h][source ^ flipped(SOURCE, h, step)], weights_ref[FAR[h, step]]
            terms.setdefault(flipped(TARGET, h, step), []).append(pair)
        for turned, pairs in terms.items():
            down_refs[h][target ^ turned] += multiply(pairs)
    for node in range(out_ref.shape[0] // 2):
        part = fold(down_refs[1][node])
        out_ref[2 * node] = part
        out_ref[2 * node + 1] = part
    tie_ref[...] = jnp.zeros_like(tie_ref)


def near_kernel(
    listed_ref,
    own_ref,
    x_ref,
    y_ref,
    xy_ref,
    weights_ref,
    tie_ref,
    out_ref,
    far_ref,
    values,
    rows,
    columns,
    sums,
):
    _, index_y, core = device_index()
    far_ref[...] = multiply(
        [
            (split_lanes(unfold(sent_coeff(ref))), weights_ref[FAR[0, step]])
            for step, ref in enumerate((x_ref, y_ref, xy_ref), 1)
        ]
    )
    low = low_lanes(8)
    for tile in range(LEAVES // 2):
        cols = slice(tile * LANES, tile * LANES + LANES)
        for axis in range(3):
            spread = jnp.broadcast_to(own_ref[64 + axis : 65 + axis, cols], (LANES, LANES))
            columns[axis, cols, :] = spread.T
    for block, ref in enumerate((own_ref, x_ref, y_ref, xy_ref)):
        for tile in range(LEAVES // 2):
            cols = slice(tile * LANES, tile * LANES + LANES)
            first = block * LEAVES + tile * 2
            values[first : first + 2] = split_rows(ref[:64, cols]).T.reshape(2, LEAF, LANES)
            point = ref[64:72, cols]
            rolled = pltpu.roll(point, HALF, 1)
            rows[first] = jnp.where(low, point, rolled)
            rows[first + 1] = jnp.where(low, rolled, point)

    def local(leaf, place):
        listed = listed_ref[leaf, place]
        owner = listed >> 4
        flip_x = (owner >> BITS_Y ^ core) & 1
        flip_y = (owner ^ index_y) & 1
        return (flip_x + 2 * flip_y) * LEAVES + (listed & LEAVES - 1)

    def one_leaf(leaf, carry):
        here = pl.ds(pl.multiple_of(leaf * LEAF, LEAF), LEAF)
        total = None
        for quad in range(3):
            ids = [local(leaf, quad * 4 + place) for place in range(4)]
            highs = []
            rests = []
            for pair in range(2):
                source = jnp.where(low, rows[ids[pair * 2]], rows[ids[pair * 2 + 1]])
                square = None
                for axis in range(3):
                    delta = columns[axis, here, :] - source[axis : axis + 1]
                    square = delta * delta if square is None else square + delta * delta
                square = jnp.maximum(square, 1e-30)
                distance = square * lax.rsqrt(square)
                scale = ROOT_THREE / LENGTH_SCALE
                decay = jnp.exp2(distance * (-scale * LOG2_E))
                kernel = (distance * (AMPLITUDE * scale) + AMPLITUDE) * decay
                high = kernel.astype(BF16)
                highs.append(high)
                rests.append((kernel - high.astype(F32)).astype(BF16))
            weight = jnp.concatenate(
                [jnp.concatenate(highs, axis=1), jnp.concatenate(rests, axis=1)], axis=0
            )
            source_values = jnp.concatenate([values[n] for n in ids], axis=0)
            part = jnp.dot(weight, source_values, preferred_element_type=F32)
            total = part if total is None else total + part
        sums[here, :] = total[:64] + total[64:]
        return carry

    lax.fori_loop(0, LEAVES, one_leaf, 0, unroll=4)
    for tile in range(LEAVES // 2):
        cols = slice(tile * LANES, tile * LANES + LANES)
        flipped = sums[cols, :].T
        out_ref[:, cols] = flipped[:64] + flipped[64:] + NUGGET * own_ref[:64, cols]


def final_kernel(parts_ref, far_ref, weights_ref, near_ref, basis_ref, transfer_ref, out_ref):
    halves = [parts_ref[0], parts_ref[1]]
    for source in range(2, parts_ref.shape[0]):
        halves[source % 2] = halves[source % 2] + parts_ref[source]
    above = jnp.concatenate([unfold(half) for half in halves], axis=0)
    down = far_ref[...] + multiply([(split_lanes(above), weights_ref[DOWN[0, 0]])])
    down = down[:, :HALF].astype(BF16)
    for block in range(4):
        cols = slice(block * 256, block * 256 + 256)
        leaf_down = jnp.dot(down, transfer_ref[:, cols], preferred_element_type=F32).astype(BF16)
        far = jnp.dot(leaf_down, block_diagonal(basis_ref[:, cols]), preferred_element_type=F32)
        out_ref[:, cols] = near_ref[:, cols] + far


def call(kernel, out_shape, in_specs, scratch_shapes, *operands, limit=40):
    shapes = tuple(jax.ShapeDtypeStruct(shape, dtype) for shape, dtype in out_shape)
    return pl.pallas_call(
        kernel,
        out_shape=shapes,
        in_specs=in_specs,
        out_specs=(VMEM,) * len(shapes),
        scratch_shapes=scratch_shapes,
        compiler_params=pltpu.CompilerParams(vmem_limit_bytes=limit * 1024 * 1024),
    )(*operands)


def exchange(value, names):
    return lax.all_to_all(value, names, split_axis=0, concat_axis=0, tiled=True)


def body(
    right_sides,
    points,
    leaf_basis,
    leaf_transfer,
    upper_transfer,
    coupling,
    near_leaves,
    admissible,
):
    width = right_sides.shape[1]
    lifted, send = call(
        up_kernel,
        [((2 ** len(SOURCE) * 2, 16, LANES), F32), ((72, width), F32)],
        [pl.BlockSpec(memory_space=pltpu.HBM)] * 5,
        [
            pltpu.VMEM((3, width), F32),
            pltpu.VMEM((64, width), BF16),
            pltpu.VMEM((64, width), BF16),
            pltpu.VMEM((64, 64), F32),
            pltpu.SemaphoreType.DMA((5,)),
        ],
        right_sides,
        points,
        leaf_basis,
        leaf_transfer,
        upper_transfer,
        limit=60,
    )
    swap = [(0, 1), (1, 0)]
    from_x = lax.ppermute(send, "core", swap)
    from_y = lax.ppermute(send, "y", [(j, j ^ 1) for j in range(lax.axis_size("y"))])
    gathered = exchange(lifted, ("xl", "z", "core"))
    (weights,) = call(
        weights_kernel,
        [((WEIGHTS, 128, LANES), BF16)],
        [VMEM] * 2 + [SMEM],
        [],
        upper_transfer,
        coupling,
        admissible.T,
    )
    heights = range(1, LEVELS - 1)
    partial, tie = call(
        tree_kernel,
        [((2 ** len(TARGET) * 2, 16, LANES), F32), ((8, LANES), F32)],
        [VMEM] * 2 + [ANYWHERE] * 2,
        [pltpu.VMEM((2 ** len(above(SOURCE, h)), 32, LANES), BF16) for h in heights]
        + [pltpu.VMEM((2 ** len(above(TARGET, h)), 32, LANES), F32) for h in heights],
        gathered,
        weights,
        from_x,
        from_y,
    )
    parts = exchange(partial, ("xh", "y", "core"))
    from_xy = lax.ppermute(from_y, "core", swap)
    near, far = call(
        near_kernel,
        [((64, width), F32), ((64, LANES), F32)],
        [SMEM] + [VMEM] * 6,
        [
            pltpu.VMEM((4 * LEAVES, LEAF, LANES), BF16),
            pltpu.VMEM((4 * LEAVES, 8, LANES), F32),
            pltpu.VMEM((3, width, LANES), F32),
            pltpu.VMEM((width, LANES), F32),
        ],
        near_leaves,
        send,
        from_x,
        from_y,
        from_xy,
        weights,
        tie,
    )
    (product,) = call(
        final_kernel,
        [((64, width), F32)],
        [VMEM] * 6,
        [],
        parts,
        far,
        weights,
        near,
        leaf_basis,
        leaf_transfer,
    )
    return product


def solution(mesh):
    every = ("z", "core", "xh", "xl", "y")
    fine = jax.sharding.Mesh(mesh.devices.reshape(8, 2, 2, 2, 8), every)
    split = P(None, every)
    in_specs = (split, split, split, split, P(), P(), P(every, None), P())
    return jax.shard_map(body, mesh=fine, in_specs=in_specs, out_specs=split, check_vma=False)
```

```python
import jax
import jax.numpy as jnp
from jax import lax
from jax.experimental import pallas as pl
from jax.experimental.pallas import tpu as pltpu
from jax.sharding import PartitionSpec as P

ROOT_THREE = 1.7320508075688772
LENGTH_SCALE = 0.6
AMPLITUDE = 0.25
NUGGET = 0.5
LOG2_E = 1.4426950408889634
BITS_X = 4
BITS_Y = 5
DEVICES = 512
LEVELS = 9
LEAVES = 16
LEAF = 64
RANK = 64
HALF = 64
LANES = 128
F32 = jnp.float32
BF16 = jnp.bfloat16
NT = (((1,), (1,)), ((), ()))
VMEM = pl.BlockSpec(memory_space=pltpu.VMEM)
ANYWHERE = pl.BlockSpec(memory_space=pl.ANY)
SMEM = pl.BlockSpec(memory_space=pltpu.SMEM)


def places():
    listed = []
    for bit in range(max(BITS_X, BITS_Y)):
        if bit < BITS_X:
            listed.append(("x", bit))
        if bit < BITS_Y:
            listed.append(("y", bit))
    return listed


PLACES = places()
SOURCE = (2, 4, 6, 7, 8)
TARGET = (1, 3, 5)

CLIMB, DOWN, FAR = {}, {}, {}
for _h in range(1, LEVELS - 2):
    for _side in range(2 if _h in SOURCE else 1):
        CLIMB[_h, _side] = len(CLIMB)
for _h in range(LEVELS - 2):
    for _side in range(2 if _h in TARGET else 1):
        DOWN[_h, _side] = len(CLIMB) + len(DOWN)
for _h in range(LEVELS - 1):
    for _step in (1, 2, 3):
        FAR[_h, _step] = len(CLIMB) + len(DOWN) + len(FAR)
WEIGHTS = len(CLIMB) + len(DOWN) + len(FAR)


def above(chosen, h):
    return [place for place in chosen if place >= h]


def flipped(chosen, h, step):
    listed = above(chosen, h)
    return sum(1 << listed.index(h + p) for p in (0, 1) if step >> p & 1 and h + p in listed)


def low_lanes(rows):
    return lax.broadcasted_iota(jnp.int32, (rows, LANES), 1) < HALF


def split_lanes(value):
    high = value.astype(BF16).astype(F32)
    return jnp.where(low_lanes(value.shape[0]), high, value - high).astype(BF16)


def split_rows(wide):
    high = wide.astype(BF16)
    return jnp.concatenate([high, (wide - high.astype(F32)).astype(BF16)], axis=0)


def block_diagonal(basis):
    wide = basis.astype(F32)
    leaf = lax.broadcasted_iota(jnp.int32, wide.shape, 1) // LEAF
    return jnp.concatenate([jnp.where(leaf == l, wide, 0.0).astype(BF16) for l in range(4)], axis=0)


def up_kernel(
    right_ref,
    points_ref,
    basis_ref,
    transfer_ref,
    upper_ref,
    lifted_ref,
    send_ref,
    points_in,
    basis_in,
    transfer_in,
    upper_in,
    sems,
):
    copies = [
        pltpu.make_async_copy(right_ref, send_ref.at[pl.ds(0, 64)], sems.at[0]),
        pltpu.make_async_copy(basis_ref, basis_in, sems.at[1]),
        pltpu.make_async_copy(transfer_ref, transfer_in, sems.at[2]),
        pltpu.make_async_copy(points_ref, points_in, sems.at[3]),
        pltpu.make_async_copy(upper_ref.at[0, lax.axis_index("core")], upper_in, sems.at[4]),
    ]
    for copy in copies:
        copy.start()
    for copy in copies:
        copy.wait()
    total = None
    for block in range(4):
        cols = slice(block * 256, block * 256 + 256)
        rounded = send_ref[:64, cols].astype(BF16)
        leaf_coeff = lax.dot_general(
            rounded, block_diagonal(basis_in[:, cols]), NT, preferred_element_type=F32
        ).astype(BF16)
        transfer = transfer_in[:, cols]
        part = lax.dot_general(
            leaf_coeff,
            jnp.concatenate([transfer, transfer], axis=0),
            NT,
            preferred_element_type=F32,
        )
        total = part if total is None else total + part
    matrix = upper_in[...]
    wide = split_rows(jnp.concatenate([matrix, matrix], axis=1))
    lifted = fold(multiply([(split_lanes(total), wide)]))
    lifted_ref[...] = lifted
    send_ref[64:72, :] = jnp.zeros((8, LEAVES * LEAF), F32)
    send_ref[64:67, :] = points_in[...]
    for first, packed in ((72, fold(total)), (76, lifted)):
        for tile in range(8):
            cols = slice(tile * LANES, tile * LANES + LANES)
            send_ref[first : first + 4, cols] = packed[tile * 4 : tile * 4 + 4]


def device_index():
    core = lax.axis_index("core")
    index_y = lax.axis_index("xh") * 16 + lax.axis_index("xl") * 8 + lax.axis_index("y")
    return lax.axis_index("z") * 2 + core, index_y, core


def device_sides():
    index_x, index_y, _ = device_index()
    return [(index_x if axis == "x" else index_y) >> bit & 1 for axis, bit in PLACES]


def place_index(sides, listed):
    index = jnp.int32(0)
    for bit, place in enumerate(listed):
        index = index + sides[place] * 2**bit
    return index


def sent_coeff(ref, first):
    return jnp.concatenate(
        [ref[first : first + 4, tile * LANES : tile * LANES + LANES] for tile in range(8)], axis=0
    )


def fold(value):
    rows = value.shape[0] // 2
    return jnp.where(low_lanes(rows), value[:rows], value[rows:])


def unfold(packed):
    low = low_lanes(packed.shape[0])
    rolled = pltpu.roll(packed, HALF, 1)
    return jnp.concatenate(
        [jnp.where(low, packed, rolled), jnp.where(low, rolled, packed)], axis=0
    )


def multiply(pairs):
    left = [piece for value, _ in pairs for piece in (value, value)]
    right = [piece for _, m in pairs for piece in (m[:64], m[:64], m[64:], m[64:])]
    return jnp.dot(
        jnp.concatenate(left, axis=1),
        jnp.concatenate(right, axis=0),
        preferred_element_type=F32,
    )


def pair_kernel(own_ref, other_ref, out_ref):
    mine = lax.broadcasted_iota(jnp.int32, (32, LANES), 1) // HALF == lax.axis_index("core")
    both = own_ref[...] + sent_coeff(other_ref, 76)
    result = fold(jnp.where(mine, both, pltpu.roll(both, HALF, 1)))
    for target in range(out_ref.shape[0]):
        out_ref[target] = result


def weights_kernel(upper_ref, coupling_ref, admissible_ref, tie_ref, out_ref):
    sides = device_sides()
    code = place_index(sides, range(LEVELS))

    def plain(matrix):
        return jnp.concatenate([matrix, matrix], axis=1)

    def transposed(matrix):
        return jnp.concatenate([matrix, matrix], axis=0).T

    for h in range(LEVELS - 2):
        for side in range(2):
            own = sides[h] if (h, 1) not in CLIMB else side
            if (h, side) in CLIMB:
                out_ref[CLIMB[h, side]] = split_rows(plain(upper_ref[h, own]))
            own = sides[h] if (h, 1) not in DOWN else side
            if (h, side) in DOWN:
                out_ref[DOWN[h, side]] = split_rows(transposed(upper_ref[h, own]))
    for h in range(LEVELS - 1):
        first = 2 * DEVICES - 2 * DEVICES // 2**h
        for step in (1, 2, 3):
            turned = sum(1 << p for p in (0, 1) if step >> p & 1 and h + p in TARGET)
            target = (code >> h) ^ (turned if h else 0)
            here = target & 3
            there = here ^ step
            matrix = coupling_ref[h, jnp.abs(there - here) - 1]
            flag = admissible_ref[step - 1, first + target].astype(F32)
            upward = jnp.full((64, LANES), there - here, jnp.int32) > 0
            chosen = jnp.where(upward, transposed(matrix), plain(matrix))
            out_ref[FAR[h, step]] = split_rows(chosen * flag)


def tree_kernel(gathered_ref, weights_ref, tie_in_ref, out_ref, tie_ref, *scratch):
    coeff_refs = dict(zip(range(1, LEVELS - 1), scratch[: LEVELS - 2]))
    down_refs = dict(zip(range(1, LEVELS - 1), scratch[LEVELS - 2 :]))
    sides = device_sides()
    for source in range(gathered_ref.shape[0]):
        coeff_refs[1][source] = split_lanes(unfold(gathered_ref[source]))
    for h in range(1, LEVELS - 2):
        count = coeff_refs[h].shape[0]
        if h in SOURCE:
            result = multiply(
                [
                    (
                        jnp.concatenate([coeff_refs[h][n] for n in range(bit, count, 2)], axis=0),
                        weights_ref[CLIMB[h, bit]],
                    )
                    for bit in range(2)
                ]
            )
        else:
            value = coeff_refs[h][...].reshape(count * 32, LANES)
            result = multiply([(value, weights_ref[CLIMB[h, 0]])])
        coeff_refs[h + 1][...] = split_lanes(result).reshape(coeff_refs[h + 1].shape)
    for h in range(LEVELS - 2, 0, -1):
        source = place_index(sides, above(SOURCE, h))
        target = place_index(sides, above(TARGET, h))
        count = down_refs[h].shape[0]
        if h == LEVELS - 2:
            down_refs[h][...] = jnp.zeros((count, 32, LANES), F32)
        else:
            parents = down_refs[h + 1].shape[0]
            value = split_lanes(down_refs[h + 1][...].reshape(parents * 32, LANES))
            if h in TARGET:
                for bit in range(2):
                    part = multiply([(value, weights_ref[DOWN[h, bit]])])
                    for node in range(parents):
                        down_refs[h][node * 2 + bit] = part[node * 32 : node * 32 + 32]
            else:
                part = multiply([(value, weights_ref[DOWN[h, 0]])])
                down_refs[h][...] = part.reshape(count, 32, LANES)
        terms = {}
        for step in (1, 2, 3):
            pair = coeff_refs[h][source ^ flipped(SOURCE, h, step)], weights_ref[FAR[h, step]]
            terms.setdefault(flipped(TARGET, h, step), []).append(pair)
        for turned, pairs in terms.items():
            down_refs[h][target ^ turned] += multiply(pairs)
    for node in range(out_ref.shape[0]):
        out_ref[node] = fold(down_refs[1][node])
    tie_ref[...] = jnp.zeros_like(tie_ref)


def sum_kernel(parts_ref, tie_ref, out_ref):
    total = parts_ref[0]
    for source in range(1, parts_ref.shape[0]):
        total = total + parts_ref[source]
    out_ref[...] = total


def near_kernel(
    listed_ref,
    own_ref,
    x_ref,
    y_ref,
    xy_ref,
    weights_ref,
    tie_ref,
    out_ref,
    far_ref,
    values,
    rows,
    columns,
    sums,
):
    _, index_y, core = device_index()
    far_ref[...] = multiply(
        [
            (split_lanes(unfold(sent_coeff(ref, 72))), weights_ref[FAR[0, step]])
            for step, ref in enumerate((x_ref, y_ref, xy_ref), 1)
        ]
    )
    low = low_lanes(8)
    for tile in range(LEAVES // 2):
        cols = slice(tile * LANES, tile * LANES + LANES)
        for axis in range(3):
            spread = jnp.broadcast_to(own_ref[64 + axis : 65 + axis, cols], (LANES, LANES))
            columns[axis, cols, :] = spread.T
    for block, ref in enumerate((own_ref, x_ref, y_ref, xy_ref)):
        for tile in range(LEAVES // 2):
            cols = slice(tile * LANES, tile * LANES + LANES)
            first = block * LEAVES + tile * 2
            values[first : first + 2] = split_rows(ref[:64, cols]).T.reshape(2, LEAF, LANES)
            point = ref[64:72, cols]
            rolled = pltpu.roll(point, HALF, 1)
            rows[first] = jnp.where(low, point, rolled)
            rows[first + 1] = jnp.where(low, rolled, point)

    def local(leaf, place):
        listed = listed_ref[leaf, place]
        owner = listed >> 4
        flip_x = (owner >> BITS_Y ^ core) & 1
        flip_y = (owner ^ index_y) & 1
        return (flip_x + 2 * flip_y) * LEAVES + (listed & LEAVES - 1)

    def one_leaf(leaf, carry):
        here = pl.ds(pl.multiple_of(leaf * LEAF, LEAF), LEAF)
        total = None
        for quad in range(3):
            ids = [local(leaf, quad * 4 + place) for place in range(4)]
            highs = []
            rests = []
            for pair in range(2):
                source = jnp.where(low, rows[ids[pair * 2]], rows[ids[pair * 2 + 1]])
                square = None
                for axis in range(3):
                    delta = columns[axis, here, :] - source[axis : axis + 1]
                    square = delta * delta if square is None else square + delta * delta
                square = jnp.maximum(square, 1e-30)
                distance = square * lax.rsqrt(square)
                scale = ROOT_THREE / LENGTH_SCALE
                decay = jnp.exp2(distance * (-scale * LOG2_E))
                kernel = (distance * (AMPLITUDE * scale) + AMPLITUDE) * decay
                high = kernel.astype(BF16)
                highs.append(high)
                rests.append((kernel - high.astype(F32)).astype(BF16))
            weight = jnp.concatenate(
                [jnp.concatenate(highs, axis=1), jnp.concatenate(rests, axis=1)], axis=0
            )
            source_values = jnp.concatenate([values[n] for n in ids], axis=0)
            part = jnp.dot(weight, source_values, preferred_element_type=F32)
            total = part if total is None else total + part
        sums[here, :] = total[:64] + total[64:]
        return carry

    lax.fori_loop(0, LEAVES, one_leaf, 0, unroll=4)
    for tile in range(LEAVES // 2):
        cols = slice(tile * LANES, tile * LANES + LANES)
        flipped = sums[cols, :].T
        out_ref[:, cols] = flipped[:64] + flipped[64:] + NUGGET * own_ref[:64, cols]


def final_kernel(own_ref, other_ref, far_ref, weights_ref, near_ref, basis_ref, transfer_ref, out_ref):
    first = jnp.full((32, LANES), lax.axis_index("core"), jnp.int32) == 0
    own = unfold(own_ref[...])
    other = unfold(other_ref[...])
    above = jnp.concatenate([jnp.where(first, own, other), jnp.where(first, other, own)], axis=0)
    down = far_ref[...] + multiply([(split_lanes(above), weights_ref[DOWN[0, 0]])])
    down = down[:, :HALF].astype(BF16)
    for block in range(4):
        cols = slice(block * 256, block * 256 + 256)
        leaf_down = jnp.dot(down, transfer_ref[:, cols], preferred_element_type=F32).astype(BF16)
        far = jnp.dot(leaf_down, block_diagonal(basis_ref[:, cols]), preferred_element_type=F32)
        out_ref[:, cols] = near_ref[:, cols] + far


def call(kernel, out_shape, in_specs, scratch_shapes, *operands, limit=40):
    shapes = tuple(jax.ShapeDtypeStruct(shape, dtype) for shape, dtype in out_shape)
    return pl.pallas_call(
        kernel,
        out_shape=shapes,
        in_specs=in_specs,
        out_specs=(VMEM,) * len(shapes),
        scratch_shapes=scratch_shapes,
        compiler_params=pltpu.CompilerParams(vmem_limit_bytes=limit * 1024 * 1024),
    )(*operands)


def exchange(value, names):
    return lax.all_to_all(value, names, split_axis=0, concat_axis=0, tiled=True)


def body(
    right_sides,
    points,
    leaf_basis,
    leaf_transfer,
    upper_transfer,
    coupling,
    near_leaves,
    admissible,
):
    width = right_sides.shape[1]
    lifted, send = call(
        up_kernel,
        [((32, LANES), F32), ((80, width), F32)],
        [pl.BlockSpec(memory_space=pltpu.HBM)] * 5,
        [
            pltpu.VMEM((3, width), F32),
            pltpu.VMEM((64, width), BF16),
            pltpu.VMEM((64, width), BF16),
            pltpu.VMEM((64, 64), F32),
            pltpu.SemaphoreType.DMA((5,)),
        ],
        right_sides,
        points,
        leaf_basis,
        leaf_transfer,
        upper_transfer,
        limit=60,
    )
    swap = [(0, 1), (1, 0)]
    from_x = lax.ppermute(send, "core", swap)
    from_y = lax.ppermute(send, "y", [(j, j ^ 1) for j in range(lax.axis_size("y"))])
    (pair,) = call(
        pair_kernel, [((2 ** len(SOURCE), 16, LANES), F32)], [VMEM] * 2, [], lifted, from_x
    )
    gathered = exchange(pair, ("xh", "xl", "z"))
    (weights,) = call(
        weights_kernel,
        [((WEIGHTS, 128, LANES), BF16)],
        [VMEM] * 2 + [SMEM, ANYWHERE],
        [],
        upper_transfer,
        coupling,
        admissible.T,
        pair,
    )
    heights = range(1, LEVELS - 1)
    partial, tie = call(
        tree_kernel,
        [((2 ** len(TARGET), 16, LANES), F32), ((8, LANES), F32)],
        [VMEM] * 2 + [ANYWHERE],
        [pltpu.VMEM((2 ** len(above(SOURCE, h)), 32, LANES), BF16) for h in heights]
        + [pltpu.VMEM((2 ** len(above(TARGET, h)), 32, LANES), F32) for h in heights],
        gathered,
        weights,
        from_y,
    )
    parts = exchange(partial, "y")
    from_xy = lax.ppermute(from_y, "core", swap)
    near, far = call(
        near_kernel,
        [((64, width), F32), ((64, LANES), F32)],
        [SMEM] + [VMEM] * 6,
        [
            pltpu.VMEM((4 * LEAVES, LEAF, LANES), BF16),
            pltpu.VMEM((4 * LEAVES, 8, LANES), F32),
            pltpu.VMEM((3, width, LANES), F32),
            pltpu.VMEM((width, LANES), F32),
        ],
        near_leaves,
        send,
        from_x,
        from_y,
        from_xy,
        weights,
        tie,
    )
    (own,) = call(sum_kernel, [((16, LANES), F32)], [VMEM, ANYWHERE], [], parts, far)
    other = lax.ppermute(own, "core", swap)
    (product,) = call(
        final_kernel,
        [((64, width), F32)],
        [VMEM] * 7,
        [],
        own,
        other,
        far,
        weights,
        near,
        leaf_basis,
        leaf_transfer,
    )
    return product


def solution(mesh):
    every = ("z", "core", "xh", "xl", "y")
    fine = jax.sharding.Mesh(mesh.devices.reshape(8, 2, 2, 2, 8), every)
    split = P(None, every)
    in_specs = (split, split, split, split, P(), P(), P(every, None), P())
    return jax.shard_map(body, mesh=fine, in_specs=in_specs, out_specs=split, check_vma=False)
```

```python
import jax
import jax.numpy as jnp
from jax import lax
from jax.experimental import pallas as pl
from jax.experimental.pallas import tpu as pltpu
from jax.sharding import PartitionSpec as P

ROOT_THREE = 1.7320508075688772
LENGTH_SCALE = 0.6
AMPLITUDE = 0.25
NUGGET = 0.5
LOG2_E = 1.4426950408889634
BITS_X = 4
BITS_Y = 5
DEVICES = 512
LEVELS = 9
LEAVES = 16
LEAF = 64
RANK = 64
HALF = 64
LANES = 128
F32 = jnp.float32
BF16 = jnp.bfloat16
NT = (((1,), (1,)), ((), ()))
VMEM = pl.BlockSpec(memory_space=pltpu.VMEM)
ANYWHERE = pl.BlockSpec(memory_space=pl.ANY)
SMEM = pl.BlockSpec(memory_space=pltpu.SMEM)


def places():
    listed = []
    for bit in range(max(BITS_X, BITS_Y)):
        if bit < BITS_X:
            listed.append(("x", bit))
        if bit < BITS_Y:
            listed.append(("y", bit))
    return listed


PLACES = places()
SOURCE = (2, 4, 6)
TARGET = (1, 3, 5, 7, 8)

CLIMB, DOWN, FAR = {}, {}, {}
for _h in range(1, LEVELS - 2):
    for _side in range(2 if _h in SOURCE else 1):
        CLIMB[_h, _side] = len(CLIMB)
for _h in range(LEVELS - 2):
    for _side in range(2 if _h in TARGET else 1):
        DOWN[_h, _side] = len(CLIMB) + len(DOWN)
for _h in range(LEVELS - 1):
    for _step in (1, 2, 3):
        FAR[_h, _step] = len(CLIMB) + len(DOWN) + len(FAR)
WEIGHTS = len(CLIMB) + len(DOWN) + len(FAR)


def above(chosen, h):
    return [place for place in chosen if place >= h]


def flipped(chosen, h, step):
    listed = above(chosen, h)
    return sum(1 << listed.index(h + p) for p in (0, 1) if step >> p & 1 and h + p in listed)


def low_lanes(rows):
    return lax.broadcasted_iota(jnp.int32, (rows, LANES), 1) < HALF


def split_lanes(value):
    high = value.astype(BF16).astype(F32)
    return jnp.where(low_lanes(value.shape[0]), high, value - high).astype(BF16)


def split_rows(wide):
    high = wide.astype(BF16)
    return jnp.concatenate([high, (wide - high.astype(F32)).astype(BF16)], axis=0)


def block_diagonal(basis):
    wide = basis.astype(F32)
    leaf = lax.broadcasted_iota(jnp.int32, wide.shape, 1) // LEAF
    return jnp.concatenate([jnp.where(leaf == l, wide, 0.0).astype(BF16) for l in range(4)], axis=0)


def up_kernel(
    right_ref,
    points_ref,
    basis_ref,
    transfer_ref,
    upper_ref,
    lifted_ref,
    send_ref,
    points_in,
    basis_in,
    transfer_in,
    upper_in,
    sems,
):
    copies = [
        pltpu.make_async_copy(right_ref, send_ref.at[pl.ds(0, 64)], sems.at[0]),
        pltpu.make_async_copy(basis_ref, basis_in, sems.at[1]),
        pltpu.make_async_copy(transfer_ref, transfer_in, sems.at[2]),
        pltpu.make_async_copy(points_ref, points_in, sems.at[3]),
        pltpu.make_async_copy(upper_ref.at[0, lax.axis_index("core")], upper_in, sems.at[4]),
    ]
    for copy in copies:
        copy.start()
    for copy in copies:
        copy.wait()
    total = None
    for block in range(4):
        cols = slice(block * 256, block * 256 + 256)
        rounded = send_ref[:64, cols].astype(BF16)
        leaf_coeff = lax.dot_general(
            rounded, block_diagonal(basis_in[:, cols]), NT, preferred_element_type=F32
        ).astype(BF16)
        transfer = transfer_in[:, cols]
        part = lax.dot_general(
            leaf_coeff,
            jnp.concatenate([transfer, transfer], axis=0),
            NT,
            preferred_element_type=F32,
        )
        total = part if total is None else total + part
    matrix = upper_in[...]
    wide = split_rows(jnp.concatenate([matrix, matrix], axis=1))
    lifted = multiply([(split_lanes(total), wide)])
    halves = [fold(lifted[:32]), fold(lifted[32:])]
    for target in range(lifted_ref.shape[0]):
        lifted_ref[target] = halves[target % 2]
    send_ref[64:67, :] = points_in[...]
    packed = fold(total)
    for tile in range(8):
        cols = slice(tile * LANES, tile * LANES + LANES)
        send_ref[67:71, cols] = packed[tile * 4 : tile * 4 + 4]
    send_ref[71:72, :] = jnp.zeros((1, LEAVES * LEAF), F32)


def device_index():
    core = lax.axis_index("core")
    index_y = lax.axis_index("xh") * 16 + lax.axis_index("xl") * 8 + lax.axis_index("y")
    return lax.axis_index("z") * 2 + core, index_y, core


def device_sides():
    index_x, index_y, _ = device_index()
    return [(index_x if axis == "x" else index_y) >> bit & 1 for axis, bit in PLACES]


def place_index(sides, listed):
    index = jnp.int32(0)
    for bit, place in enumerate(listed):
        index = index + sides[place] * 2**bit
    return index


def sent_coeff(ref):
    return jnp.concatenate(
        [ref[67:71, tile * LANES : tile * LANES + LANES] for tile in range(8)], axis=0
    )


def fold(value):
    rows = value.shape[0] // 2
    return jnp.where(low_lanes(rows), value[:rows], value[rows:])


def unfold(packed):
    low = low_lanes(packed.shape[0])
    rolled = pltpu.roll(packed, HALF, 1)
    return jnp.concatenate(
        [jnp.where(low, packed, rolled), jnp.where(low, rolled, packed)], axis=0
    )


def multiply(pairs):
    left = [piece for value, _ in pairs for piece in (value, value)]
    right = [piece for _, m in pairs for piece in (m[:64], m[:64], m[64:], m[64:])]
    return jnp.dot(
        jnp.concatenate(left, axis=1),
        jnp.concatenate(right, axis=0),
        preferred_element_type=F32,
    )


def weights_kernel(upper_ref, coupling_ref, admissible_ref, out_ref):
    sides = device_sides()
    code = place_index(sides, range(LEVELS))

    def plain(matrix):
        return jnp.concatenate([matrix, matrix], axis=1)

    def transposed(matrix):
        return jnp.concatenate([matrix, matrix], axis=0).T

    for h in range(LEVELS - 2):
        for side in range(2):
            own = sides[h] if (h, 1) not in CLIMB else side
            if (h, side) in CLIMB:
                out_ref[CLIMB[h, side]] = split_rows(plain(upper_ref[h, own]))
            own = sides[h] if (h, 1) not in DOWN else side
            if (h, side) in DOWN:
                out_ref[DOWN[h, side]] = split_rows(transposed(upper_ref[h, own]))
    for h in range(LEVELS - 1):
        first = 2 * DEVICES - 2 * DEVICES // 2**h
        for step in (1, 2, 3):
            turned = sum(1 << p for p in (0, 1) if step >> p & 1 and h + p in TARGET)
            target = (code >> h) ^ (turned if h else 0)
            here = target & 3
            there = here ^ step
            matrix = coupling_ref[h, jnp.abs(there - here) - 1]
            flag = admissible_ref[step - 1, first + target].astype(F32)
            upward = jnp.full((64, LANES), there - here, jnp.int32) > 0
            chosen = jnp.where(upward, transposed(matrix), plain(matrix))
            out_ref[FAR[h, step]] = split_rows(chosen * flag)


def tree_kernel(gathered_ref, weights_ref, y_ref, out_ref, tie_ref, *scratch):
    coeff_refs = dict(zip(range(1, LEVELS - 1), scratch[: LEVELS - 2]))
    down_refs = dict(zip(range(1, LEVELS - 1), scratch[LEVELS - 2 :]))
    sides = device_sides()
    for chip in range(gathered_ref.shape[0] // 2):
        both = gathered_ref[2 * chip] + gathered_ref[2 * chip + 1]
        coeff_refs[1][chip] = split_lanes(unfold(both))
    for h in range(1, LEVELS - 2):
        count = coeff_refs[h].shape[0]
        if h in SOURCE:
            result = multiply(
                [
                    (
                        jnp.concatenate([coeff_refs[h][n] for n in range(bit, count, 2)], axis=0),
                        weights_ref[CLIMB[h, bit]],
                    )
                    for bit in range(2)
                ]
            )
        else:
            value = coeff_refs[h][...].reshape(count * 32, LANES)
            result = multiply([(value, weights_ref[CLIMB[h, 0]])])
        coeff_refs[h + 1][...] = split_lanes(result).reshape(coeff_refs[h + 1].shape)
    for h in range(LEVELS - 2, 0, -1):
        source = place_index(sides, above(SOURCE, h))
        target = place_index(sides, above(TARGET, h))
        count = down_refs[h].shape[0]
        if h == LEVELS - 2:
            down_refs[h][...] = jnp.zeros((count, 32, LANES), F32)
        else:
            parents = down_refs[h + 1].shape[0]
            value = split_lanes(down_refs[h + 1][...].reshape(parents * 32, LANES))
            if h in TARGET:
                for bit in range(2):
                    part = multiply([(value, weights_ref[DOWN[h, bit]])])
                    for node in range(parents):
                        down_refs[h][node * 2 + bit] = part[node * 32 : node * 32 + 32]
            else:
                part = multiply([(value, weights_ref[DOWN[h, 0]])])
                down_refs[h][...] = part.reshape(count, 32, LANES)
        terms = {}
        for step in (1, 2, 3):
            pair = coeff_refs[h][source ^ flipped(SOURCE, h, step)], weights_ref[FAR[h, step]]
            terms.setdefault(flipped(TARGET, h, step), []).append(pair)
        for turned, pairs in terms.items():
            down_refs[h][target ^ turned] += multiply(pairs)
    for node in range(out_ref.shape[0]):
        out_ref[node] = fold(down_refs[1][node])
    tie_ref[...] = jnp.zeros_like(tie_ref)


def sum_kernel(parts_ref, tie_ref, out_ref):
    total = parts_ref[0]
    for source in range(1, parts_ref.shape[0]):
        total = total + parts_ref[source]
    out_ref[...] = total


def near_kernel(
    listed_ref,
    own_ref,
    x_ref,
    y_ref,
    xy_ref,
    weights_ref,
    tie_ref,
    out_ref,
    far_ref,
    values,
    rows,
    columns,
    sums,
):
    _, index_y, core = device_index()
    far_ref[...] = multiply(
        [
            (split_lanes(unfold(sent_coeff(ref))), weights_ref[FAR[0, step]])
            for step, ref in enumerate((x_ref, y_ref, xy_ref), 1)
        ]
    )
    low = low_lanes(8)
    for tile in range(LEAVES // 2):
        cols = slice(tile * LANES, tile * LANES + LANES)
        for axis in range(3):
            spread = jnp.broadcast_to(own_ref[64 + axis : 65 + axis, cols], (LANES, LANES))
            columns[axis, cols, :] = spread.T
    for block, ref in enumerate((own_ref, x_ref, y_ref, xy_ref)):
        for tile in range(LEAVES // 2):
            cols = slice(tile * LANES, tile * LANES + LANES)
            first = block * LEAVES + tile * 2
            values[first : first + 2] = split_rows(ref[:64, cols]).T.reshape(2, LEAF, LANES)
            point = ref[64:72, cols]
            rolled = pltpu.roll(point, HALF, 1)
            rows[first] = jnp.where(low, point, rolled)
            rows[first + 1] = jnp.where(low, rolled, point)

    def local(leaf, place):
        listed = listed_ref[leaf, place]
        owner = listed >> 4
        flip_x = (owner >> BITS_Y ^ core) & 1
        flip_y = (owner ^ index_y) & 1
        return (flip_x + 2 * flip_y) * LEAVES + (listed & LEAVES - 1)

    def one_leaf(leaf, carry):
        here = pl.ds(pl.multiple_of(leaf * LEAF, LEAF), LEAF)
        total = None
        for quad in range(3):
            ids = [local(leaf, quad * 4 + place) for place in range(4)]
            highs = []
            rests = []
            for pair in range(2):
                source = jnp.where(low, rows[ids[pair * 2]], rows[ids[pair * 2 + 1]])
                square = None
                for axis in range(3):
                    delta = columns[axis, here, :] - source[axis : axis + 1]
                    square = delta * delta if square is None else square + delta * delta
                square = jnp.maximum(square, 1e-30)
                distance = square * lax.rsqrt(square)
                scale = ROOT_THREE / LENGTH_SCALE
                decay = jnp.exp2(distance * (-scale * LOG2_E))
                kernel = (distance * (AMPLITUDE * scale) + AMPLITUDE) * decay
                high = kernel.astype(BF16)
                highs.append(high)
                rests.append((kernel - high.astype(F32)).astype(BF16))
            weight = jnp.concatenate(
                [jnp.concatenate(highs, axis=1), jnp.concatenate(rests, axis=1)], axis=0
            )
            source_values = jnp.concatenate([values[n] for n in ids], axis=0)
            part = jnp.dot(weight, source_values, preferred_element_type=F32)
            total = part if total is None else total + part
        sums[here, :] = total[:64] + total[64:]
        return carry

    lax.fori_loop(0, LEAVES, one_leaf, 0, unroll=4)
    for tile in range(LEAVES // 2):
        cols = slice(tile * LANES, tile * LANES + LANES)
        flipped = sums[cols, :].T
        out_ref[:, cols] = flipped[:64] + flipped[64:] + NUGGET * own_ref[:64, cols]


def final_kernel(own_ref, other_ref, far_ref, weights_ref, near_ref, basis_ref, transfer_ref, out_ref):
    first = jnp.full((32, LANES), lax.axis_index("core"), jnp.int32) == 0
    own = unfold(own_ref[...])
    other = unfold(other_ref[...])
    above = jnp.concatenate([jnp.where(first, own, other), jnp.where(first, other, own)], axis=0)
    down = far_ref[...] + multiply([(split_lanes(above), weights_ref[DOWN[0, 0]])])
    down = down[:, :HALF].astype(BF16)
    for block in range(4):
        cols = slice(block * 256, block * 256 + 256)
        leaf_down = jnp.dot(down, transfer_ref[:, cols], preferred_element_type=F32).astype(BF16)
        far = jnp.dot(leaf_down, block_diagonal(basis_ref[:, cols]), preferred_element_type=F32)
        out_ref[:, cols] = near_ref[:, cols] + far


def call(kernel, out_shape, in_specs, scratch_shapes, *operands, limit=40):
    shapes = tuple(jax.ShapeDtypeStruct(shape, dtype) for shape, dtype in out_shape)
    return pl.pallas_call(
        kernel,
        out_shape=shapes,
        in_specs=in_specs,
        out_specs=(VMEM,) * len(shapes),
        scratch_shapes=scratch_shapes,
        compiler_params=pltpu.CompilerParams(vmem_limit_bytes=limit * 1024 * 1024),
    )(*operands)


def exchange(value, names):
    return lax.all_to_all(value, names, split_axis=0, concat_axis=0, tiled=True)


def body(
    right_sides,
    points,
    leaf_basis,
    leaf_transfer,
    upper_transfer,
    coupling,
    near_leaves,
    admissible,
):
    width = right_sides.shape[1]
    lifted, send = call(
        up_kernel,
        [((2 ** len(SOURCE) * 2, 16, LANES), F32), ((72, width), F32)],
        [pl.BlockSpec(memory_space=pltpu.HBM)] * 5,
        [
            pltpu.VMEM((3, width), F32),
            pltpu.VMEM((64, width), BF16),
            pltpu.VMEM((64, width), BF16),
            pltpu.VMEM((64, 64), F32),
            pltpu.SemaphoreType.DMA((5,)),
        ],
        right_sides,
        points,
        leaf_basis,
        leaf_transfer,
        upper_transfer,
        limit=60,
    )
    swap = [(0, 1), (1, 0)]
    from_x = lax.ppermute(send, "core", swap)
    from_y = lax.ppermute(send, "y", [(j, j ^ 1) for j in range(lax.axis_size("y"))])
    gathered = exchange(lifted, ("z", "core"))
    (weights,) = call(
        weights_kernel,
        [((WEIGHTS, 128, LANES), BF16)],
        [VMEM] * 2 + [SMEM],
        [],
        upper_transfer,
        coupling,
        admissible.T,
    )
    heights = range(1, LEVELS - 1)
    partial, tie = call(
        tree_kernel,
        [((2 ** len(TARGET), 16, LANES), F32), ((8, LANES), F32)],
        [VMEM] * 2 + [ANYWHERE],
        [pltpu.VMEM((2 ** len(above(SOURCE, h)), 32, LANES), BF16) for h in heights]
        + [pltpu.VMEM((2 ** len(above(TARGET, h)), 32, LANES), F32) for h in heights],
        gathered,
        weights,
        from_y,
    )
    parts = exchange(partial, ("xh", "xl", "y"))
    from_xy = lax.ppermute(from_y, "core", swap)
    near, far = call(
        near_kernel,
        [((64, width), F32), ((64, LANES), F32)],
        [SMEM] + [VMEM] * 6,
        [
            pltpu.VMEM((4 * LEAVES, LEAF, LANES), BF16),
            pltpu.VMEM((4 * LEAVES, 8, LANES), F32),
            pltpu.VMEM((3, width, LANES), F32),
            pltpu.VMEM((width, LANES), F32),
        ],
        near_leaves,
        send,
        from_x,
        from_y,
        from_xy,
        weights,
        tie,
    )
    (own,) = call(sum_kernel, [((16, LANES), F32)], [VMEM, ANYWHERE], [], parts, far)
    other = lax.ppermute(own, "core", swap)
    (product,) = call(
        final_kernel,
        [((64, width), F32)],
        [VMEM] * 7,
        [],
        own,
        other,
        far,
        weights,
        near,
        leaf_basis,
        leaf_transfer,
    )
    return product


def solution(mesh):
    every = ("z", "core", "xh", "xl", "y")
    fine = jax.sharding.Mesh(mesh.devices.reshape(8, 2, 2, 2, 8), every)
    split = P(None, every)
    in_specs = (split, split, split, split, P(), P(), P(every, None), P())
    return jax.shard_map(body, mesh=fine, in_specs=in_specs, out_specs=split, check_vma=False)
```

```python
import jax
import jax.numpy as jnp
from jax import lax
from jax.experimental import pallas as pl
from jax.experimental.pallas import tpu as pltpu
from jax.sharding import PartitionSpec as P

ROOT_THREE = 1.7320508075688772
LENGTH_SCALE = 0.6
AMPLITUDE = 0.25
NUGGET = 0.5
LOG2_E = 1.4426950408889634
BITS_X = 4
BITS_Y = 5
DEVICES = 512
LEVELS = 9
LEAVES = 16
LEAF = 64
RANK = 64
HALF = 64
LANES = 128
F32 = jnp.float32
BF16 = jnp.bfloat16
NT = (((1,), (1,)), ((), ()))
VMEM = pl.BlockSpec(memory_space=pltpu.VMEM)
ANYWHERE = pl.BlockSpec(memory_space=pl.ANY)
SMEM = pl.BlockSpec(memory_space=pltpu.SMEM)


def places():
    listed = []
    for bit in range(max(BITS_X, BITS_Y)):
        if bit < BITS_X:
            listed.append(("x", bit))
        if bit < BITS_Y:
            listed.append(("y", bit))
    return listed


PLACES = places()
SOURCE = (2, 4, 6)
TARGET = (1, 3, 5, 7, 8)
GROUP_X = [z * 2 + core for z in (7, 3, 6, 2, 5, 1, 4, 0) for core in (1, 0)]
GROUP_Y = [x * 8 + y for y in (3, 7, 1, 5, 2, 6, 0, 4) for x in (1, 3, 0, 2)]

CLIMB, DOWN, FAR = {}, {}, {}
for _h in range(1, LEVELS - 2):
    for _side in range(2 if _h in SOURCE else 1):
        CLIMB[_h, _side] = len(CLIMB)
for _h in range(LEVELS - 2):
    for _side in range(2 if _h in TARGET else 1):
        DOWN[_h, _side] = len(CLIMB) + len(DOWN)
for _h in range(LEVELS - 1):
    for _step in (1, 2, 3):
        FAR[_h, _step] = len(CLIMB) + len(DOWN) + len(FAR)
WEIGHTS = len(CLIMB) + len(DOWN) + len(FAR)


def above(chosen, h):
    return [place for place in chosen if place >= h]


def flipped(chosen, h, step):
    listed = above(chosen, h)
    return sum(1 << listed.index(h + p) for p in (0, 1) if step >> p & 1 and h + p in listed)


def low_lanes(rows):
    return lax.broadcasted_iota(jnp.int32, (rows, LANES), 1) < HALF


def split_lanes(value):
    high = value.astype(BF16).astype(F32)
    return jnp.where(low_lanes(value.shape[0]), high, value - high).astype(BF16)


def split_rows(wide):
    high = wide.astype(BF16)
    return jnp.concatenate([high, (wide - high.astype(F32)).astype(BF16)], axis=0)


def block_diagonal(basis):
    wide = basis.astype(F32)
    leaf = lax.broadcasted_iota(jnp.int32, wide.shape, 1) // LEAF
    return jnp.concatenate([jnp.where(leaf == l, wide, 0.0).astype(BF16) for l in range(4)], axis=0)


def up_kernel(
    right_ref,
    points_ref,
    basis_ref,
    transfer_ref,
    upper_ref,
    lifted_ref,
    send_ref,
    points_in,
    basis_in,
    transfer_in,
    upper_in,
    sems,
):
    copies = [
        pltpu.make_async_copy(right_ref, send_ref.at[pl.ds(0, 64)], sems.at[0]),
        pltpu.make_async_copy(basis_ref, basis_in, sems.at[1]),
        pltpu.make_async_copy(transfer_ref, transfer_in, sems.at[2]),
        pltpu.make_async_copy(points_ref, points_in, sems.at[3]),
        pltpu.make_async_copy(upper_ref.at[0, lax.axis_index("gx") & 1], upper_in, sems.at[4]),
    ]
    for copy in copies:
        copy.start()
    for copy in copies:
        copy.wait()
    total = None
    for block in range(4):
        cols = slice(block * 256, block * 256 + 256)
        rounded = send_ref[:64, cols].astype(BF16)
        leaf_coeff = lax.dot_general(
            rounded, block_diagonal(basis_in[:, cols]), NT, preferred_element_type=F32
        ).astype(BF16)
        transfer = transfer_in[:, cols]
        part = lax.dot_general(
            leaf_coeff,
            jnp.concatenate([transfer, transfer], axis=0),
            NT,
            preferred_element_type=F32,
        )
        total = part if total is None else total + part
    matrix = upper_in[...]
    wide = split_rows(jnp.concatenate([matrix, matrix], axis=1))
    lifted = multiply([(split_lanes(total), wide)])
    halves = [fold(lifted[:32]), fold(lifted[32:])]
    for target in range(lifted_ref.shape[0]):
        lifted_ref[target] = halves[GROUP_X[target] % 2]
    send_ref[64:67, :] = points_in[...]
    packed = fold(total)
    for tile in range(8):
        cols = slice(tile * LANES, tile * LANES + LANES)
        send_ref[67:71, cols] = packed[tile * 4 : tile * 4 + 4]
    send_ref[71:72, :] = jnp.zeros((1, LEAVES * LEAF), F32)


def device_index():
    index_x = lax.axis_index("gx")
    return index_x, lax.axis_index("gy"), index_x & 1


def device_sides():
    index_x, index_y, _ = device_index()
    return [(index_x if axis == "x" else index_y) >> bit & 1 for axis, bit in PLACES]


def place_index(sides, listed):
    index = jnp.int32(0)
    for bit, place in enumerate(listed):
        index = index + sides[place] * 2**bit
    return index


def sent_coeff(ref):
    return jnp.concatenate(
        [ref[67:71, tile * LANES : tile * LANES + LANES] for tile in range(8)], axis=0
    )


def fold(value):
    rows = value.shape[0] // 2
    return jnp.where(low_lanes(rows), value[:rows], value[rows:])


def unfold(packed):
    low = low_lanes(packed.shape[0])
    rolled = pltpu.roll(packed, HALF, 1)
    return jnp.concatenate(
        [jnp.where(low, packed, rolled), jnp.where(low, rolled, packed)], axis=0
    )


def multiply(pairs):
    left = [piece for value, _ in pairs for piece in (value, value)]
    right = [piece for _, m in pairs for piece in (m[:64], m[:64], m[64:], m[64:])]
    return jnp.dot(
        jnp.concatenate(left, axis=1),
        jnp.concatenate(right, axis=0),
        preferred_element_type=F32,
    )


def weights_kernel(upper_ref, coupling_ref, admissible_ref, out_ref):
    sides = device_sides()
    code = place_index(sides, range(LEVELS))

    def plain(matrix):
        return jnp.concatenate([matrix, matrix], axis=1)

    def transposed(matrix):
        return jnp.concatenate([matrix, matrix], axis=0).T

    for h in range(LEVELS - 2):
        for side in range(2):
            own = sides[h] if (h, 1) not in CLIMB else side
            if (h, side) in CLIMB:
                out_ref[CLIMB[h, side]] = split_rows(plain(upper_ref[h, own]))
            own = sides[h] if (h, 1) not in DOWN else side
            if (h, side) in DOWN:
                out_ref[DOWN[h, side]] = split_rows(transposed(upper_ref[h, own]))
    for h in range(LEVELS - 1):
        first = 2 * DEVICES - 2 * DEVICES // 2**h
        for step in (1, 2, 3):
            turned = sum(1 << p for p in (0, 1) if step >> p & 1 and h + p in TARGET)
            target = (code >> h) ^ (turned if h else 0)
            here = target & 3
            there = here ^ step
            matrix = coupling_ref[h, jnp.abs(there - here) - 1]
            flag = admissible_ref[step - 1, first + target].astype(F32)
            upward = jnp.full((64, LANES), there - here, jnp.int32) > 0
            chosen = jnp.where(upward, transposed(matrix), plain(matrix))
            out_ref[FAR[h, step]] = split_rows(chosen * flag)


def tree_kernel(gathered_ref, weights_ref, y_ref, out_ref, tie_ref, *scratch):
    coeff_refs = dict(zip(range(1, LEVELS - 1), scratch[: LEVELS - 2]))
    down_refs = dict(zip(range(1, LEVELS - 1), scratch[LEVELS - 2 :]))
    sides = device_sides()
    for chip in range(gathered_ref.shape[0] // 2):
        both = sum(gathered_ref[GROUP_X.index(2 * chip + core)] for core in range(2))
        coeff_refs[1][chip] = split_lanes(unfold(both))
    for h in range(1, LEVELS - 2):
        count = coeff_refs[h].shape[0]
        if h in SOURCE:
            result = multiply(
                [
                    (
                        jnp.concatenate([coeff_refs[h][n] for n in range(bit, count, 2)], axis=0),
                        weights_ref[CLIMB[h, bit]],
                    )
                    for bit in range(2)
                ]
            )
        else:
            value = coeff_refs[h][...].reshape(count * 32, LANES)
            result = multiply([(value, weights_ref[CLIMB[h, 0]])])
        coeff_refs[h + 1][...] = split_lanes(result).reshape(coeff_refs[h + 1].shape)
    for h in range(LEVELS - 2, 0, -1):
        source = place_index(sides, above(SOURCE, h))
        target = place_index(sides, above(TARGET, h))
        count = down_refs[h].shape[0]
        if h == LEVELS - 2:
            down_refs[h][...] = jnp.zeros((count, 32, LANES), F32)
        else:
            parents = down_refs[h + 1].shape[0]
            value = split_lanes(down_refs[h + 1][...].reshape(parents * 32, LANES))
            if h in TARGET:
                for bit in range(2):
                    part = multiply([(value, weights_ref[DOWN[h, bit]])])
                    for node in range(parents):
                        down_refs[h][node * 2 + bit] = part[node * 32 : node * 32 + 32]
            else:
                part = multiply([(value, weights_ref[DOWN[h, 0]])])
                down_refs[h][...] = part.reshape(count, 32, LANES)
        terms = {}
        for step in (1, 2, 3):
            pair = coeff_refs[h][source ^ flipped(SOURCE, h, step)], weights_ref[FAR[h, step]]
            terms.setdefault(flipped(TARGET, h, step), []).append(pair)
        for turned, pairs in terms.items():
            down_refs[h][target ^ turned] += multiply(pairs)
    for member, node in enumerate(GROUP_Y):
        out_ref[member] = fold(down_refs[1][node])
    tie_ref[...] = jnp.zeros_like(tie_ref)


def sum_kernel(parts_ref, tie_ref, out_ref):
    total = parts_ref[0]
    for source in range(1, parts_ref.shape[0]):
        total = total + parts_ref[source]
    out_ref[...] = total


def near_kernel(
    listed_ref,
    own_ref,
    x_ref,
    y_ref,
    xy_ref,
    weights_ref,
    tie_ref,
    out_ref,
    far_ref,
    values,
    rows,
    columns,
    sums,
):
    _, index_y, core = device_index()
    far_ref[...] = multiply(
        [
            (split_lanes(unfold(sent_coeff(ref))), weights_ref[FAR[0, step]])
            for step, ref in enumerate((x_ref, y_ref, xy_ref), 1)
        ]
    )
    low = low_lanes(8)
    for tile in range(LEAVES // 2):
        cols = slice(tile * LANES, tile * LANES + LANES)
        for axis in range(3):
            spread = jnp.broadcast_to(own_ref[64 + axis : 65 + axis, cols], (LANES, LANES))
            columns[axis, cols, :] = spread.T
    for block, ref in enumerate((own_ref, x_ref, y_ref, xy_ref)):
        for tile in range(LEAVES // 2):
            cols = slice(tile * LANES, tile * LANES + LANES)
            first = block * LEAVES + tile * 2
            values[first : first + 2] = split_rows(ref[:64, cols]).T.reshape(2, LEAF, LANES)
            point = ref[64:72, cols]
            rolled = pltpu.roll(point, HALF, 1)
            rows[first] = jnp.where(low, point, rolled)
            rows[first + 1] = jnp.where(low, rolled, point)

    def local(leaf, place):
        listed = listed_ref[leaf, place]
        owner = listed >> 4
        flip_x = (owner >> BITS_Y ^ core) & 1
        flip_y = (owner ^ index_y) & 1
        return (flip_x + 2 * flip_y) * LEAVES + (listed & LEAVES - 1)

    def one_leaf(leaf, carry):
        here = pl.ds(pl.multiple_of(leaf * LEAF, LEAF), LEAF)
        total = None
        for quad in range(3):
            ids = [local(leaf, quad * 4 + place) for place in range(4)]
            highs = []
            rests = []
            for pair in range(2):
                source = jnp.where(low, rows[ids[pair * 2]], rows[ids[pair * 2 + 1]])
                square = None
                for axis in range(3):
                    delta = columns[axis, here, :] - source[axis : axis + 1]
                    square = delta * delta if square is None else square + delta * delta
                square = jnp.maximum(square, 1e-30)
                distance = square * lax.rsqrt(square)
                scale = ROOT_THREE / LENGTH_SCALE
                decay = jnp.exp2(distance * (-scale * LOG2_E))
                kernel = (distance * (AMPLITUDE * scale) + AMPLITUDE) * decay
                high = kernel.astype(BF16)
                highs.append(high)
                rests.append((kernel - high.astype(F32)).astype(BF16))
            weight = jnp.concatenate(
                [jnp.concatenate(highs, axis=1), jnp.concatenate(rests, axis=1)], axis=0
            )
            source_values = jnp.concatenate([values[n] for n in ids], axis=0)
            part = jnp.dot(weight, source_values, preferred_element_type=F32)
            total = part if total is None else total + part
        sums[here, :] = total[:64] + total[64:]
        return carry

    lax.fori_loop(0, LEAVES, one_leaf, 0, unroll=4)
    for tile in range(LEAVES // 2):
        cols = slice(tile * LANES, tile * LANES + LANES)
        flipped = sums[cols, :].T
        out_ref[:, cols] = flipped[:64] + flipped[64:] + NUGGET * own_ref[:64, cols]


def final_kernel(own_ref, other_ref, far_ref, weights_ref, near_ref, basis_ref, transfer_ref, out_ref):
    first = jnp.full((32, LANES), lax.axis_index("gx") & 1, jnp.int32) == 0
    own = unfold(own_ref[...])
    other = unfold(other_ref[...])
    above = jnp.concatenate([jnp.where(first, own, other), jnp.where(first, other, own)], axis=0)
    down = far_ref[...] + multiply([(split_lanes(above), weights_ref[DOWN[0, 0]])])
    down = down[:, :HALF].astype(BF16)
    for block in range(4):
        cols = slice(block * 256, block * 256 + 256)
        leaf_down = jnp.dot(down, transfer_ref[:, cols], preferred_element_type=F32).astype(BF16)
        far = jnp.dot(leaf_down, block_diagonal(basis_ref[:, cols]), preferred_element_type=F32)
        out_ref[:, cols] = near_ref[:, cols] + far


def call(kernel, out_shape, in_specs, scratch_shapes, *operands, limit=40):
    shapes = tuple(jax.ShapeDtypeStruct(shape, dtype) for shape, dtype in out_shape)
    return pl.pallas_call(
        kernel,
        out_shape=shapes,
        in_specs=in_specs,
        out_specs=(VMEM,) * len(shapes),
        scratch_shapes=scratch_shapes,
        compiler_params=pltpu.CompilerParams(vmem_limit_bytes=limit * 1024 * 1024),
    )(*operands)


def exchange(value, name, group):
    return lax.all_to_all(
        value, name, split_axis=0, concat_axis=0, axis_index_groups=[group], tiled=True
    )


def body(
    right_sides,
    points,
    leaf_basis,
    leaf_transfer,
    upper_transfer,
    coupling,
    near_leaves,
    admissible,
):
    width = right_sides.shape[1]
    lifted, send = call(
        up_kernel,
        [((2 ** len(SOURCE) * 2, 16, LANES), F32), ((72, width), F32)],
        [pl.BlockSpec(memory_space=pltpu.HBM)] * 5,
        [
            pltpu.VMEM((3, width), F32),
            pltpu.VMEM((64, width), BF16),
            pltpu.VMEM((64, width), BF16),
            pltpu.VMEM((64, 64), F32),
            pltpu.SemaphoreType.DMA((5,)),
        ],
        right_sides,
        points,
        leaf_basis,
        leaf_transfer,
        upper_transfer,
        limit=60,
    )
    swap = [(i, i ^ 1) for i in range(2**BITS_X)]
    from_x = lax.ppermute(send, "gx", swap)
    from_y = lax.ppermute(send, "gy", [(j, j ^ 1) for j in range(2**BITS_Y)])
    gathered = exchange(lifted, "gx", GROUP_X)
    (weights,) = call(
        weights_kernel,
        [((WEIGHTS, 128, LANES), BF16)],
        [VMEM] * 2 + [SMEM],
        [],
        upper_transfer,
        coupling,
        admissible.T,
    )
    heights = range(1, LEVELS - 1)
    partial, tie = call(
        tree_kernel,
        [((2 ** len(TARGET), 16, LANES), F32), ((8, LANES), F32)],
        [VMEM] * 2 + [ANYWHERE],
        [pltpu.VMEM((2 ** len(above(SOURCE, h)), 32, LANES), BF16) for h in heights]
        + [pltpu.VMEM((2 ** len(above(TARGET, h)), 32, LANES), F32) for h in heights],
        gathered,
        weights,
        from_y,
    )
    parts = exchange(partial, "gy", GROUP_Y)
    from_xy = lax.ppermute(from_y, "gx", swap)
    near, far = call(
        near_kernel,
        [((64, width), F32), ((64, LANES), F32)],
        [SMEM] + [VMEM] * 6,
        [
            pltpu.VMEM((4 * LEAVES, LEAF, LANES), BF16),
            pltpu.VMEM((4 * LEAVES, 8, LANES), F32),
            pltpu.VMEM((3, width, LANES), F32),
            pltpu.VMEM((width, LANES), F32),
        ],
        near_leaves,
        send,
        from_x,
        from_y,
        from_xy,
        weights,
        tie,
    )
    (own,) = call(sum_kernel, [((16, LANES), F32)], [VMEM, ANYWHERE], [], parts, far)
    other = lax.ppermute(own, "gx", swap)
    (product,) = call(
        final_kernel,
        [((64, width), F32)],
        [VMEM] * 7,
        [],
        own,
        other,
        far,
        weights,
        near,
        leaf_basis,
        leaf_transfer,
    )
    return product


def solution(mesh):
    split = P(None, ("gx", "gy"))
    in_specs = (split, split, split, split, P(), P(), P(("gx", "gy"), None), P())
    return jax.shard_map(body, mesh=mesh, in_specs=in_specs, out_specs=split, check_vma=False)
```

```python
import jax
import jax.numpy as jnp
from jax import lax
from jax.experimental import pallas as pl
from jax.experimental.pallas import tpu as pltpu
from jax.sharding import PartitionSpec as P

ROOT_THREE = 1.7320508075688772
LENGTH_SCALE = 0.6
AMPLITUDE = 0.25
NUGGET = 0.5
LOG2_E = 1.4426950408889634
BITS_X = 4
BITS_Y = 5
DEVICES = 512
LEVELS = 9
LEAVES = 16
LEAF = 64
RANK = 64
HALF = 64
LANES = 128
F32 = jnp.float32
BF16 = jnp.bfloat16
NT = (((1,), (1,)), ((), ()))
VMEM = pl.BlockSpec(memory_space=pltpu.VMEM)
ANYWHERE = pl.BlockSpec(memory_space=pl.ANY)
SMEM = pl.BlockSpec(memory_space=pltpu.SMEM)


def places():
    listed = []
    for bit in range(max(BITS_X, BITS_Y)):
        if bit < BITS_X:
            listed.append(("x", bit))
        if bit < BITS_Y:
            listed.append(("y", bit))
    return listed


PLACES = places()
SOURCE = (2, 4, 6)
TARGET = (1, 3, 5, 7, 8)
GROUP_X = [z * 2 + core for z in (7, 3, 6, 2, 5, 1, 4, 0) for core in (1, 0)]
GROUP_Y = [x * 8 + y for y in (3, 7, 1, 5, 2, 6, 0, 4) for x in (1, 3, 0, 2)]

CLIMB, DOWN, FAR = {}, {}, {}
for _h in range(1, LEVELS - 2):
    for _side in range(2 if _h in SOURCE else 1):
        CLIMB[_h, _side] = len(CLIMB)
for _h in range(LEVELS - 2):
    for _side in range(2 if _h in TARGET else 1):
        DOWN[_h, _side] = len(CLIMB) + len(DOWN)
for _h in range(LEVELS - 1):
    for _step in (1, 2, 3):
        FAR[_h, _step] = len(CLIMB) + len(DOWN) + len(FAR)
WEIGHTS = len(CLIMB) + len(DOWN) + len(FAR)


def above(chosen, h):
    return [place for place in chosen if place >= h]


def flipped(chosen, h, step):
    listed = above(chosen, h)
    return sum(1 << listed.index(h + p) for p in (0, 1) if step >> p & 1 and h + p in listed)


def low_lanes(rows):
    return lax.broadcasted_iota(jnp.int32, (rows, LANES), 1) < HALF


def split_lanes(value):
    high = value.astype(BF16).astype(F32)
    return jnp.where(low_lanes(value.shape[0]), high, value - high).astype(BF16)


def split_rows(wide):
    high = wide.astype(BF16)
    return jnp.concatenate([high, (wide - high.astype(F32)).astype(BF16)], axis=0)


def block_diagonal(basis):
    wide = basis.astype(F32)
    leaf = lax.broadcasted_iota(jnp.int32, wide.shape, 1) // LEAF
    return jnp.concatenate([jnp.where(leaf == l, wide, 0.0).astype(BF16) for l in range(4)], axis=0)


def up_kernel(
    right_ref,
    points_ref,
    basis_ref,
    transfer_ref,
    upper_ref,
    lifted_ref,
    send_ref,
    points_in,
    basis_in,
    transfer_in,
    upper_in,
    sems,
):
    copies = [
        pltpu.make_async_copy(right_ref, send_ref.at[pl.ds(0, 64)], sems.at[0]),
        pltpu.make_async_copy(basis_ref, basis_in, sems.at[1]),
        pltpu.make_async_copy(transfer_ref, transfer_in, sems.at[2]),
        pltpu.make_async_copy(points_ref, points_in, sems.at[3]),
        pltpu.make_async_copy(upper_ref.at[0, lax.axis_index("gx") & 1], upper_in, sems.at[4]),
    ]
    for copy in copies:
        copy.start()
    for copy in copies:
        copy.wait()
    total = None
    for block in range(4):
        cols = slice(block * 256, block * 256 + 256)
        rounded = send_ref[:64, cols].astype(BF16)
        leaf_coeff = lax.dot_general(
            rounded, block_diagonal(basis_in[:, cols]), NT, preferred_element_type=F32
        ).astype(BF16)
        transfer = transfer_in[:, cols]
        part = lax.dot_general(
            leaf_coeff,
            jnp.concatenate([transfer, transfer], axis=0),
            NT,
            preferred_element_type=F32,
        )
        total = part if total is None else total + part
    matrix = upper_in[...]
    wide = split_rows(jnp.concatenate([matrix, matrix], axis=1))
    lifted = multiply([(split_lanes(total), wide)])
    halves = [fold(lifted[:32]), fold(lifted[32:])]
    for target in range(lifted_ref.shape[0]):
        lifted_ref[target] = halves[GROUP_X[target] % 2]
    send_ref[64:67, :] = points_in[...]
    packed = fold(total)
    for tile in range(8):
        cols = slice(tile * LANES, tile * LANES + LANES)
        send_ref[67:71, cols] = packed[tile * 4 : tile * 4 + 4]
    send_ref[71:72, :] = jnp.zeros((1, LEAVES * LEAF), F32)


def as_nodes(value):
    return [value[row : row + 32] for row in range(0, value.shape[0], 32)]


def device_index():
    index_x = lax.axis_index("gx")
    return index_x, lax.axis_index("gy"), index_x & 1


def device_sides():
    index_x, index_y, _ = device_index()
    return [(index_x if axis == "x" else index_y) >> bit & 1 for axis, bit in PLACES]


def place_index(sides, listed):
    index = jnp.int32(0)
    for bit, place in enumerate(listed):
        index = index + sides[place] * 2**bit
    return index


def sent_coeff(ref):
    return jnp.concatenate(
        [ref[67:71, tile * LANES : tile * LANES + LANES] for tile in range(8)], axis=0
    )


def fold(value):
    rows = value.shape[0] // 2
    return jnp.where(low_lanes(rows), value[:rows], value[rows:])


def unfold(packed):
    low = low_lanes(packed.shape[0])
    rolled = pltpu.roll(packed, HALF, 1)
    return jnp.concatenate(
        [jnp.where(low, packed, rolled), jnp.where(low, rolled, packed)], axis=0
    )


def multiply(pairs):
    left = [piece for value, _ in pairs for piece in (value, value)]
    right = [piece for _, m in pairs for piece in (m[:64], m[:64], m[64:], m[64:])]
    return jnp.dot(
        jnp.concatenate(left, axis=1),
        jnp.concatenate(right, axis=0),
        preferred_element_type=F32,
    )


def weights_kernel(upper_ref, coupling_ref, admissible_ref, out_ref):
    sides = device_sides()
    code = place_index(sides, range(LEVELS))

    def plain(matrix):
        return jnp.concatenate([matrix, matrix], axis=1)

    def transposed(matrix):
        return jnp.concatenate([matrix, matrix], axis=0).T

    for h in range(LEVELS - 2):
        for side in range(2):
            matrix = upper_ref[h, sides[h] ^ side]
            if (h, side) in CLIMB:
                out_ref[CLIMB[h, side]] = split_rows(plain(matrix))
            if (h, side) in DOWN:
                out_ref[DOWN[h, side]] = split_rows(transposed(matrix))
    for h in range(LEVELS - 1):
        first = 2 * DEVICES - 2 * DEVICES // 2**h
        for step in (1, 2, 3):
            turned = sum(1 << p for p in (0, 1) if step >> p & 1 and h + p in TARGET)
            target = (code >> h) ^ (turned if h else 0)
            here = target & 3
            there = here ^ step
            matrix = coupling_ref[h, jnp.abs(there - here) - 1]
            flag = admissible_ref[step - 1, first + target].astype(F32)
            upward = jnp.full((64, LANES), there - here, jnp.int32) > 0
            chosen = jnp.where(upward, transposed(matrix), plain(matrix))
            out_ref[FAR[h, step]] = split_rows(chosen * flag)


def tree_kernel(gathered_ref, weights_ref, y_ref, out_ref, tie_ref, downs):
    sides = device_sides()
    own_source = place_index(sides, SOURCE)
    own_target = place_index(sides, TARGET)
    nodes = []
    for relative in range(2 ** len(SOURCE)):
        far_z = own_source ^ relative ^ 7
        first = (far_z & 3) * 4 + (far_z >> 2) * 2
        nodes.append(split_lanes(unfold(gathered_ref[first] + gathered_ref[first + 1])))
    levels = {1: nodes}
    for h in range(1, LEVELS - 2):
        if h in SOURCE:
            pairs = [
                (jnp.concatenate(nodes[bit::2], axis=0), weights_ref[CLIMB[h, bit]])
                for bit in range(2)
            ]
        else:
            pairs = [(jnp.concatenate(nodes, axis=0), weights_ref[CLIMB[h, 0]])]
        nodes = as_nodes(split_lanes(multiply(pairs)))
        levels[h + 1] = nodes
    down = None
    for h in range(LEVELS - 2, 0, -1):
        if down is None:
            down = [jnp.zeros((32, LANES), F32)] * 2 ** len(above(TARGET, h))
        else:
            value = split_lanes(jnp.concatenate(down, axis=0))
            parts = [
                as_nodes(multiply([(value, weights_ref[DOWN[h, bit]])]))
                for bit in range(2 if h in TARGET else 1)
            ]
            down = [part for group in zip(*parts) for part in group]
        terms = {}
        for step in (1, 2, 3):
            pair = levels[h][flipped(SOURCE, h, step)], weights_ref[FAR[h, step]]
            terms.setdefault(flipped(TARGET, h, step), []).append(pair)
        for turned, pairs in terms.items():
            down[turned] = down[turned] + multiply(pairs)
    for relative, part in enumerate(down):
        downs[relative] = fold(part)
    for member, node in enumerate(GROUP_Y):
        out_ref[member] = downs[own_target ^ node]
    tie_ref[...] = jnp.zeros_like(tie_ref)


def sum_kernel(parts_ref, tie_ref, out_ref):
    total = parts_ref[0]
    for source in range(1, parts_ref.shape[0]):
        total = total + parts_ref[source]
    out_ref[...] = total


def near_kernel(
    listed_ref,
    own_ref,
    x_ref,
    y_ref,
    xy_ref,
    weights_ref,
    tie_ref,
    out_ref,
    far_ref,
    values,
    rows,
    columns,
    sums,
):
    _, index_y, core = device_index()
    far_ref[...] = multiply(
        [
            (split_lanes(unfold(sent_coeff(ref))), weights_ref[FAR[0, step]])
            for step, ref in enumerate((x_ref, y_ref, xy_ref), 1)
        ]
    )
    low = low_lanes(8)
    for tile in range(LEAVES // 2):
        cols = slice(tile * LANES, tile * LANES + LANES)
        for axis in range(3):
            spread = jnp.broadcast_to(own_ref[64 + axis : 65 + axis, cols], (LANES, LANES))
            columns[axis, cols, :] = spread.T
    for block, ref in enumerate((own_ref, x_ref, y_ref, xy_ref)):
        for tile in range(LEAVES // 2):
            cols = slice(tile * LANES, tile * LANES + LANES)
            first = block * LEAVES + tile * 2
            values[first : first + 2] = split_rows(ref[:64, cols]).T.reshape(2, LEAF, LANES)
            point = ref[64:72, cols]
            rolled = pltpu.roll(point, HALF, 1)
            rows[first] = jnp.where(low, point, rolled)
            rows[first + 1] = jnp.where(low, rolled, point)

    def local(leaf, place):
        listed = listed_ref[leaf, place]
        owner = listed >> 4
        flip_x = (owner >> BITS_Y ^ core) & 1
        flip_y = (owner ^ index_y) & 1
        return (flip_x + 2 * flip_y) * LEAVES + (listed & LEAVES - 1)

    def one_leaf(leaf, carry):
        here = pl.ds(pl.multiple_of(leaf * LEAF, LEAF), LEAF)
        total = None
        for quad in range(3):
            ids = [local(leaf, quad * 4 + place) for place in range(4)]
            highs = []
            rests = []
            for pair in range(2):
                source = jnp.where(low, rows[ids[pair * 2]], rows[ids[pair * 2 + 1]])
                square = None
                for axis in range(3):
                    delta = columns[axis, here, :] - source[axis : axis + 1]
                    square = delta * delta if square is None else square + delta * delta
                square = jnp.maximum(square, 1e-30)
                distance = square * lax.rsqrt(square)
                scale = ROOT_THREE / LENGTH_SCALE
                decay = jnp.exp2(distance * (-scale * LOG2_E))
                kernel = (distance * (AMPLITUDE * scale) + AMPLITUDE) * decay
                high = kernel.astype(BF16)
                highs.append(high)
                rests.append((kernel - high.astype(F32)).astype(BF16))
            weight = jnp.concatenate(
                [jnp.concatenate(highs, axis=1), jnp.concatenate(rests, axis=1)], axis=0
            )
            source_values = jnp.concatenate([values[n] for n in ids], axis=0)
            part = jnp.dot(weight, source_values, preferred_element_type=F32)
            total = part if total is None else total + part
        sums[here, :] = total[:64] + total[64:]
        return carry

    lax.fori_loop(0, LEAVES, one_leaf, 0, unroll=4)
    for tile in range(LEAVES // 2):
        cols = slice(tile * LANES, tile * LANES + LANES)
        flipped = sums[cols, :].T
        out_ref[:, cols] = flipped[:64] + flipped[64:] + NUGGET * own_ref[:64, cols]


def final_kernel(own_ref, other_ref, far_ref, weights_ref, near_ref, basis_ref, transfer_ref, out_ref):
    first = jnp.full((32, LANES), lax.axis_index("gx") & 1, jnp.int32) == 0
    own = unfold(own_ref[...])
    other = unfold(other_ref[...])
    above = jnp.concatenate([jnp.where(first, own, other), jnp.where(first, other, own)], axis=0)
    down = far_ref[...] + multiply([(split_lanes(above), weights_ref[DOWN[0, 0]])])
    down = down[:, :HALF].astype(BF16)
    for block in range(4):
        cols = slice(block * 256, block * 256 + 256)
        leaf_down = jnp.dot(down, transfer_ref[:, cols], preferred_element_type=F32).astype(BF16)
        far = jnp.dot(leaf_down, block_diagonal(basis_ref[:, cols]), preferred_element_type=F32)
        out_ref[:, cols] = near_ref[:, cols] + far


def call(kernel, out_shape, in_specs, scratch_shapes, *operands, limit=40):
    shapes = tuple(jax.ShapeDtypeStruct(shape, dtype) for shape, dtype in out_shape)
    return pl.pallas_call(
        kernel,
        out_shape=shapes,
        in_specs=in_specs,
        out_specs=(VMEM,) * len(shapes),
        scratch_shapes=scratch_shapes,
        compiler_params=pltpu.CompilerParams(vmem_limit_bytes=limit * 1024 * 1024),
    )(*operands)


def exchange(value, name, group):
    return lax.all_to_all(
        value, name, split_axis=0, concat_axis=0, axis_index_groups=[group], tiled=True
    )


def body(
    right_sides,
    points,
    leaf_basis,
    leaf_transfer,
    upper_transfer,
    coupling,
    near_leaves,
    admissible,
):
    width = right_sides.shape[1]
    lifted, send = call(
        up_kernel,
        [((2 ** len(SOURCE) * 2, 16, LANES), F32), ((72, width), F32)],
        [pl.BlockSpec(memory_space=pltpu.HBM)] * 5,
        [
            pltpu.VMEM((3, width), F32),
            pltpu.VMEM((64, width), BF16),
            pltpu.VMEM((64, width), BF16),
            pltpu.VMEM((64, 64), F32),
            pltpu.SemaphoreType.DMA((5,)),
        ],
        right_sides,
        points,
        leaf_basis,
        leaf_transfer,
        upper_transfer,
        limit=60,
    )
    swap = [(i, i ^ 1) for i in range(2**BITS_X)]
    from_x = lax.ppermute(send, "gx", swap)
    from_y = lax.ppermute(send, "gy", [(j, j ^ 1) for j in range(2**BITS_Y)])
    gathered = exchange(lifted, "gx", GROUP_X)
    (weights,) = call(
        weights_kernel,
        [((WEIGHTS, 128, LANES), BF16)],
        [VMEM] * 2 + [SMEM],
        [],
        upper_transfer,
        coupling,
        admissible.T,
    )
    partial, tie = call(
        tree_kernel,
        [((2 ** len(TARGET), 16, LANES), F32), ((8, LANES), F32)],
        [VMEM] * 2 + [ANYWHERE],
        [pltpu.VMEM((2 ** len(TARGET), 16, LANES), F32)],
        gathered,
        weights,
        from_y,
    )
    parts = exchange(partial, "gy", GROUP_Y)
    from_xy = lax.ppermute(from_y, "gx", swap)
    near, far = call(
        near_kernel,
        [((64, width), F32), ((64, LANES), F32)],
        [SMEM] + [VMEM] * 6,
        [
            pltpu.VMEM((4 * LEAVES, LEAF, LANES), BF16),
            pltpu.VMEM((4 * LEAVES, 8, LANES), F32),
            pltpu.VMEM((3, width, LANES), F32),
            pltpu.VMEM((width, LANES), F32),
        ],
        near_leaves,
        send,
        from_x,
        from_y,
        from_xy,
        weights,
        tie,
    )
    (own,) = call(sum_kernel, [((16, LANES), F32)], [VMEM, ANYWHERE], [], parts, far)
    other = lax.ppermute(own, "gx", swap)
    (product,) = call(
        final_kernel,
        [((64, width), F32)],
        [VMEM] * 7,
        [],
        own,
        other,
        far,
        weights,
        near,
        leaf_basis,
        leaf_transfer,
    )
    return product


def solution(mesh):
    split = P(None, ("gx", "gy"))
    in_specs = (split, split, split, split, P(), P(), P(("gx", "gy"), None), P())
    return jax.shard_map(body, mesh=mesh, in_specs=in_specs, out_specs=split, check_vma=False)
```

```python
import jax
import jax.numpy as jnp
from jax import lax
from jax.experimental import pallas as pl
from jax.experimental.pallas import tpu as pltpu
from jax.sharding import PartitionSpec as P

ROOT_THREE = 1.7320508075688772
LENGTH_SCALE = 0.6
AMPLITUDE = 0.25
NUGGET = 0.5
LOG2_E = 1.4426950408889634
BITS_X = 4
BITS_Y = 5
DEVICES = 512
LEVELS = 9
LEAVES = 16
LEAF = 64
RANK = 64
HALF = 64
LANES = 128
F32 = jnp.float32
BF16 = jnp.bfloat16
NT = (((1,), (1,)), ((), ()))
VMEM = pl.BlockSpec(memory_space=pltpu.VMEM)
ANYWHERE = pl.BlockSpec(memory_space=pl.ANY)
SMEM = pl.BlockSpec(memory_space=pltpu.SMEM)


def places():
    listed = []
    for bit in range(max(BITS_X, BITS_Y)):
        if bit < BITS_X:
            listed.append(("x", bit))
        if bit < BITS_Y:
            listed.append(("y", bit))
    return listed


PLACES = places()
SOURCE = (2, 4, 6)
TARGET = (1, 3, 5, 7, 8)
GROUP_X = [z * 2 + core for z in (7, 3, 6, 2, 5, 1, 4, 0) for core in (1, 0)]
GROUP_Y = [x * 8 + y for y in (3, 7, 1, 5, 2, 6, 4, 0) for x in (1, 3, 2, 0)]

CLIMB, DOWN, FAR = {}, {}, {}
for _h in range(1, LEVELS - 2):
    for _side in range(2 if _h in SOURCE else 1):
        CLIMB[_h, _side] = len(CLIMB)
for _h in range(LEVELS - 2):
    for _side in range(2 if _h in TARGET else 1):
        DOWN[_h, _side] = len(CLIMB) + len(DOWN)
for _h in range(LEVELS - 1):
    for _step in (1, 2, 3):
        FAR[_h, _step] = len(CLIMB) + len(DOWN) + len(FAR)
WEIGHTS = len(CLIMB) + len(DOWN) + len(FAR)


def above(chosen, h):
    return [place for place in chosen if place >= h]


def flipped(chosen, h, step):
    listed = above(chosen, h)
    return sum(1 << listed.index(h + p) for p in (0, 1) if step >> p & 1 and h + p in listed)


def low_lanes(rows):
    return lax.broadcasted_iota(jnp.int32, (rows, LANES), 1) < HALF


def split_lanes(value):
    high = value.astype(BF16).astype(F32)
    return jnp.where(low_lanes(value.shape[0]), high, value - high).astype(BF16)


def split_rows(wide):
    high = wide.astype(BF16)
    return jnp.concatenate([high, (wide - high.astype(F32)).astype(BF16)], axis=0)


def block_diagonal(basis):
    wide = basis.astype(F32)
    leaf = lax.broadcasted_iota(jnp.int32, wide.shape, 1) // LEAF
    return jnp.concatenate([jnp.where(leaf == l, wide, 0.0).astype(BF16) for l in range(4)], axis=0)


def up_kernel(
    right_ref,
    points_ref,
    basis_ref,
    transfer_ref,
    upper_ref,
    lifted_ref,
    send_ref,
    points_in,
    basis_in,
    transfer_in,
    upper_in,
    sems,
):
    copies = [
        pltpu.make_async_copy(right_ref, send_ref.at[pl.ds(0, 64)], sems.at[0]),
        pltpu.make_async_copy(basis_ref, basis_in, sems.at[1]),
        pltpu.make_async_copy(transfer_ref, transfer_in, sems.at[2]),
        pltpu.make_async_copy(points_ref, points_in, sems.at[3]),
        pltpu.make_async_copy(upper_ref.at[0, lax.axis_index("gx") & 1], upper_in, sems.at[4]),
    ]
    for copy in copies:
        copy.start()
    for copy in copies:
        copy.wait()
    total = None
    for block in range(4):
        cols = slice(block * 256, block * 256 + 256)
        rounded = send_ref[:64, cols].astype(BF16)
        leaf_coeff = lax.dot_general(
            rounded, block_diagonal(basis_in[:, cols]), NT, preferred_element_type=F32
        ).astype(BF16)
        transfer = transfer_in[:, cols]
        part = lax.dot_general(
            leaf_coeff,
            jnp.concatenate([transfer, transfer], axis=0),
            NT,
            preferred_element_type=F32,
        )
        total = part if total is None else total + part
    matrix = upper_in[...]
    wide = split_rows(jnp.concatenate([matrix, matrix], axis=1))
    lifted = multiply([(split_lanes(total), wide)])
    halves = [fold(lifted[:32]), fold(lifted[32:])]
    for target in range(lifted_ref.shape[0]):
        lifted_ref[target] = halves[GROUP_X[target] % 2]
    send_ref[64:67, :] = points_in[...]
    packed = fold(total)
    for tile in range(8):
        cols = slice(tile * LANES, tile * LANES + LANES)
        send_ref[67:71, cols] = packed[tile * 4 : tile * 4 + 4]
    send_ref[71:72, :] = jnp.zeros((1, LEAVES * LEAF), F32)


def as_nodes(value):
    return [value[row : row + 32] for row in range(0, value.shape[0], 32)]


def device_index():
    index_x = lax.axis_index("gx")
    return index_x, lax.axis_index("gy"), index_x & 1


def device_sides():
    index_x, index_y, _ = device_index()
    return [(index_x if axis == "x" else index_y) >> bit & 1 for axis, bit in PLACES]


def place_index(sides, listed):
    index = jnp.int32(0)
    for bit, place in enumerate(listed):
        index = index + sides[place] * 2**bit
    return index


def sent_coeff(ref):
    return jnp.concatenate(
        [ref[67:71, tile * LANES : tile * LANES + LANES] for tile in range(8)], axis=0
    )


def fold(value):
    rows = value.shape[0] // 2
    return jnp.where(low_lanes(rows), value[:rows], value[rows:])


def unfold(packed):
    low = low_lanes(packed.shape[0])
    rolled = pltpu.roll(packed, HALF, 1)
    return jnp.concatenate(
        [jnp.where(low, packed, rolled), jnp.where(low, rolled, packed)], axis=0
    )


def multiply(pairs):
    left = [piece for value, _ in pairs for piece in (value, value)]
    right = [piece for _, m in pairs for piece in (m[:64], m[:64], m[64:], m[64:])]
    return jnp.dot(
        jnp.concatenate(left, axis=1),
        jnp.concatenate(right, axis=0),
        preferred_element_type=F32,
    )


def weights_kernel(upper_ref, coupling_ref, admissible_ref, out_ref):
    sides = device_sides()
    code = place_index(sides, range(LEVELS))

    def plain(matrix):
        return jnp.concatenate([matrix, matrix], axis=1)

    def transposed(matrix):
        return jnp.concatenate([matrix, matrix], axis=0).T

    for h in range(LEVELS - 2):
        for side in range(2):
            matrix = upper_ref[h, sides[h] ^ side]
            if (h, side) in CLIMB:
                out_ref[CLIMB[h, side]] = split_rows(plain(matrix))
            if (h, side) in DOWN:
                out_ref[DOWN[h, side]] = split_rows(transposed(matrix))
    for h in range(LEVELS - 1):
        first = 2 * DEVICES - 2 * DEVICES // 2**h
        for step in (1, 2, 3):
            turned = sum(1 << p for p in (0, 1) if step >> p & 1 and h + p in TARGET)
            target = (code >> h) ^ (turned if h else 0)
            here = target & 3
            there = here ^ step
            matrix = coupling_ref[h, jnp.abs(there - here) - 1]
            flag = admissible_ref[step - 1, first + target].astype(F32)
            upward = jnp.full((64, LANES), there - here, jnp.int32) > 0
            chosen = jnp.where(upward, transposed(matrix), plain(matrix))
            out_ref[FAR[h, step]] = split_rows(chosen * flag)


def tree_kernel(gathered_ref, weights_ref, y_ref, out_ref, tie_ref, downs):
    sides = device_sides()
    own_source = place_index(sides, SOURCE)
    own_target = place_index(sides, TARGET)
    nodes = []
    for relative in range(2 ** len(SOURCE)):
        far_z = own_source ^ relative ^ 7
        first = (far_z & 3) * 4 + (far_z >> 2) * 2
        nodes.append(split_lanes(unfold(gathered_ref[first] + gathered_ref[first + 1])))
    levels = {1: nodes}
    for h in range(1, LEVELS - 2):
        if h in SOURCE:
            pairs = [
                (jnp.concatenate(nodes[bit::2], axis=0), weights_ref[CLIMB[h, bit]])
                for bit in range(2)
            ]
        else:
            pairs = [(jnp.concatenate(nodes, axis=0), weights_ref[CLIMB[h, 0]])]
        nodes = as_nodes(split_lanes(multiply(pairs)))
        levels[h + 1] = nodes
    down = None
    for h in range(LEVELS - 2, 0, -1):
        if down is None:
            down = [jnp.zeros((32, LANES), F32)] * 2 ** len(above(TARGET, h))
        else:
            value = split_lanes(jnp.concatenate(down, axis=0))
            parts = [
                as_nodes(multiply([(value, weights_ref[DOWN[h, bit]])]))
                for bit in range(2 if h in TARGET else 1)
            ]
            down = [part for group in zip(*parts) for part in group]
        terms = {}
        for step in (1, 2, 3):
            pair = levels[h][flipped(SOURCE, h, step)], weights_ref[FAR[h, step]]
            terms.setdefault(flipped(TARGET, h, step), []).append(pair)
        for turned, pairs in terms.items():
            down[turned] = down[turned] + multiply(pairs)
    for relative, part in enumerate(down):
        downs[relative] = fold(part)
    for member, node in enumerate(GROUP_Y):
        out_ref[member] = downs[own_target ^ node]
    tie_ref[...] = jnp.zeros_like(tie_ref)


def sum_kernel(parts_ref, tie_ref, out_ref):
    total = parts_ref[0]
    for source in range(1, parts_ref.shape[0]):
        total = total + parts_ref[source]
    out_ref[...] = total


def near_kernel(
    listed_ref,
    own_ref,
    x_ref,
    y_ref,
    xy_ref,
    weights_ref,
    tie_ref,
    out_ref,
    far_ref,
    values,
    rows,
    columns,
    sums,
):
    _, index_y, core = device_index()
    far_ref[...] = multiply(
        [
            (split_lanes(unfold(sent_coeff(ref))), weights_ref[FAR[0, step]])
            for step, ref in enumerate((x_ref, y_ref, xy_ref), 1)
        ]
    )
    low = low_lanes(8)
    for tile in range(LEAVES // 2):
        cols = slice(tile * LANES, tile * LANES + LANES)
        for axis in range(3):
            spread = jnp.broadcast_to(own_ref[64 + axis : 65 + axis, cols], (LANES, LANES))
            columns[axis, cols, :] = spread.T
    for block, ref in enumerate((own_ref, x_ref, y_ref, xy_ref)):
        for tile in range(LEAVES // 2):
            cols = slice(tile * LANES, tile * LANES + LANES)
            first = block * LEAVES + tile * 2
            values[first : first + 2] = split_rows(ref[:64, cols]).T.reshape(2, LEAF, LANES)
            point = ref[64:72, cols]
            rolled = pltpu.roll(point, HALF, 1)
            rows[first] = jnp.where(low, point, rolled)
            rows[first + 1] = jnp.where(low, rolled, point)

    def local(leaf, place):
        listed = listed_ref[leaf, place]
        owner = listed >> 4
        flip_x = (owner >> BITS_Y ^ core) & 1
        flip_y = (owner ^ index_y) & 1
        return (flip_x + 2 * flip_y) * LEAVES + (listed & LEAVES - 1)

    def one_leaf(leaf, carry):
        here = pl.ds(pl.multiple_of(leaf * LEAF, LEAF), LEAF)
        total = None
        for quad in range(3):
            ids = [local(leaf, quad * 4 + place) for place in range(4)]
            kernels = []
            for pair in range(2):
                source = jnp.where(low, rows[ids[pair * 2]], rows[ids[pair * 2 + 1]])
                square = None
                for axis in range(3):
                    delta = columns[axis, here, :] - source[axis : axis + 1]
                    square = delta * delta if square is None else square + delta * delta
                square = jnp.maximum(square, 1e-30)
                distance = square * lax.rsqrt(square)
                scale = ROOT_THREE / LENGTH_SCALE
                decay = jnp.exp2(distance * (-scale * LOG2_E))
                kernel = (distance * (AMPLITUDE * scale) + AMPLITUDE) * decay
                kernels.append(kernel.astype(BF16))
            weight = jnp.concatenate(kernels, axis=1)
            source_values = jnp.concatenate([values[n] for n in ids], axis=0)
            part = jnp.dot(weight, source_values, preferred_element_type=F32)
            total = part if total is None else total + part
        sums[here, :] = total
        return carry

    lax.fori_loop(0, LEAVES, one_leaf, 0, unroll=4)
    for tile in range(LEAVES // 2):
        cols = slice(tile * LANES, tile * LANES + LANES)
        flipped = sums[cols, :].T
        out_ref[:, cols] = flipped[:64] + flipped[64:] + NUGGET * own_ref[:64, cols]


def final_kernel(own_ref, other_ref, far_ref, weights_ref, near_ref, basis_ref, transfer_ref, out_ref):
    first = jnp.full((32, LANES), lax.axis_index("gx") & 1, jnp.int32) == 0
    own = unfold(own_ref[...])
    other = unfold(other_ref[...])
    above = jnp.concatenate([jnp.where(first, own, other), jnp.where(first, other, own)], axis=0)
    down = far_ref[...] + multiply([(split_lanes(above), weights_ref[DOWN[0, 0]])])
    down = down[:, :HALF].astype(BF16)
    for block in range(4):
        cols = slice(block * 256, block * 256 + 256)
        leaf_down = jnp.dot(down, transfer_ref[:, cols], preferred_element_type=F32).astype(BF16)
        far = jnp.dot(leaf_down, block_diagonal(basis_ref[:, cols]), preferred_element_type=F32)
        out_ref[:, cols] = near_ref[:, cols] + far


def call(kernel, out_shape, in_specs, scratch_shapes, *operands, limit=40):
    shapes = tuple(jax.ShapeDtypeStruct(shape, dtype) for shape, dtype in out_shape)
    return pl.pallas_call(
        kernel,
        out_shape=shapes,
        in_specs=in_specs,
        out_specs=(VMEM,) * len(shapes),
        scratch_shapes=scratch_shapes,
        compiler_params=pltpu.CompilerParams(vmem_limit_bytes=limit * 1024 * 1024),
    )(*operands)


def exchange(value, name, group):
    return lax.all_to_all(
        value, name, split_axis=0, concat_axis=0, axis_index_groups=[group], tiled=True
    )


def body(
    right_sides,
    points,
    leaf_basis,
    leaf_transfer,
    upper_transfer,
    coupling,
    near_leaves,
    admissible,
):
    width = right_sides.shape[1]
    lifted, send = call(
        up_kernel,
        [((2 ** len(SOURCE) * 2, 16, LANES), F32), ((72, width), F32)],
        [pl.BlockSpec(memory_space=pltpu.HBM)] * 5,
        [
            pltpu.VMEM((3, width), F32),
            pltpu.VMEM((64, width), BF16),
            pltpu.VMEM((64, width), BF16),
            pltpu.VMEM((64, 64), F32),
            pltpu.SemaphoreType.DMA((5,)),
        ],
        right_sides,
        points,
        leaf_basis,
        leaf_transfer,
        upper_transfer,
        limit=60,
    )
    swap = [(i, i ^ 1) for i in range(2**BITS_X)]
    from_x = lax.ppermute(send, "gx", swap)
    from_y = lax.ppermute(send, "gy", [(j, j ^ 1) for j in range(2**BITS_Y)])
    gathered = exchange(lifted, "gx", GROUP_X)
    (weights,) = call(
        weights_kernel,
        [((WEIGHTS, 128, LANES), BF16)],
        [VMEM] * 2 + [SMEM],
        [],
        upper_transfer,
        coupling,
        admissible.T,
    )
    partial, tie = call(
        tree_kernel,
        [((2 ** len(TARGET), 16, LANES), F32), ((8, LANES), F32)],
        [VMEM] * 2 + [ANYWHERE],
        [pltpu.VMEM((2 ** len(TARGET), 16, LANES), F32)],
        gathered,
        weights,
        from_y,
    )
    parts = exchange(partial, "gy", GROUP_Y)
    from_xy = lax.ppermute(from_y, "gx", swap)
    near, far = call(
        near_kernel,
        [((64, width), F32), ((64, LANES), F32)],
        [SMEM] + [VMEM] * 6,
        [
            pltpu.VMEM((4 * LEAVES, LEAF, LANES), BF16),
            pltpu.VMEM((4 * LEAVES, 8, LANES), F32),
            pltpu.VMEM((3, width, LANES), F32),
            pltpu.VMEM((width, LANES), F32),
        ],
        near_leaves,
        send,
        from_x,
        from_y,
        from_xy,
        weights,
        tie,
    )
    (own,) = call(sum_kernel, [((16, LANES), F32)], [VMEM, ANYWHERE], [], parts, far)
    other = lax.ppermute(own, "gx", swap)
    (product,) = call(
        final_kernel,
        [((64, width), F32)],
        [VMEM] * 7,
        [],
        own,
        other,
        far,
        weights,
        near,
        leaf_basis,
        leaf_transfer,
    )
    return product


def solution(mesh):
    split = P(None, ("gx", "gy"))
    in_specs = (split, split, split, split, P(), P(), P(("gx", "gy"), None), P())
    return jax.shard_map(body, mesh=mesh, in_specs=in_specs, out_specs=split, check_vma=False)
```

```python
import jax
import jax.numpy as jnp
from jax import lax
from jax.experimental import pallas as pl
from jax.experimental.pallas import tpu as pltpu
from jax.sharding import PartitionSpec as P

ROOT_THREE = 1.7320508075688772
LENGTH_SCALE = 0.6
AMPLITUDE = 0.25
NUGGET = 0.5
LOG2_E = 1.4426950408889634
BITS_X = 4
BITS_Y = 5
DEVICES = 512
LEVELS = 9
LEAVES = 16
LEAF = 64
RANK = 64
HALF = 64
LANES = 128
F32 = jnp.float32
BF16 = jnp.bfloat16
NT = (((1,), (1,)), ((), ()))
VMEM = pl.BlockSpec(memory_space=pltpu.VMEM)
ANYWHERE = pl.BlockSpec(memory_space=pl.ANY)
SMEM = pl.BlockSpec(memory_space=pltpu.SMEM)


def places():
    listed = []
    for bit in range(max(BITS_X, BITS_Y)):
        if bit < BITS_X:
            listed.append(("x", bit))
        if bit < BITS_Y:
            listed.append(("y", bit))
    return listed


PLACES = places()
SOURCE = (2, 4, 6)
TARGET = (1, 3, 5, 7, 8)
GROUP_X = [z * 2 + core for z in (7, 3, 6, 2, 5, 1, 4, 0) for core in (1, 0)]
GROUP_Y = [x * 8 + y for y in (3, 7, 1, 5, 2, 6, 4, 0) for x in (1, 3, 2, 0)]

CLIMB, DOWN, FAR = {}, {}, {}
for _h in range(1, LEVELS - 2):
    for _side in range(2 if _h in SOURCE else 1):
        CLIMB[_h, _side] = len(CLIMB)
for _h in range(LEVELS - 2):
    for _side in range(2 if _h in TARGET else 1):
        DOWN[_h, _side] = len(CLIMB) + len(DOWN)
for _h in range(LEVELS - 1):
    for _step in (1, 2, 3):
        FAR[_h, _step] = len(CLIMB) + len(DOWN) + len(FAR)
WEIGHTS = len(CLIMB) + len(DOWN) + len(FAR)


def above(chosen, h):
    return [place for place in chosen if place >= h]


def flipped(chosen, h, step):
    listed = above(chosen, h)
    return sum(1 << listed.index(h + p) for p in (0, 1) if step >> p & 1 and h + p in listed)


def low_lanes(rows):
    return lax.broadcasted_iota(jnp.int32, (rows, LANES), 1) < HALF


def split_lanes(value):
    high = value.astype(BF16).astype(F32)
    return jnp.where(low_lanes(value.shape[0]), high, value - high).astype(BF16)


def split_rows(wide):
    high = wide.astype(BF16)
    return jnp.concatenate([high, (wide - high.astype(F32)).astype(BF16)], axis=0)


def block_diagonal(basis):
    wide = basis.astype(F32)
    leaf = lax.broadcasted_iota(jnp.int32, wide.shape, 1) // LEAF
    return jnp.concatenate([jnp.where(leaf == l, wide, 0.0).astype(BF16) for l in range(4)], axis=0)


def up_kernel(
    right_ref,
    points_ref,
    basis_ref,
    transfer_ref,
    upper_ref,
    lifted_ref,
    send_ref,
    points_in,
    basis_in,
    transfer_in,
    upper_in,
    sems,
):
    copies = [
        pltpu.make_async_copy(right_ref, send_ref.at[pl.ds(0, 64)], sems.at[0]),
        pltpu.make_async_copy(basis_ref, basis_in, sems.at[1]),
        pltpu.make_async_copy(transfer_ref, transfer_in, sems.at[2]),
        pltpu.make_async_copy(points_ref, points_in, sems.at[3]),
        pltpu.make_async_copy(upper_ref.at[0, lax.axis_index("gx") & 1], upper_in, sems.at[4]),
    ]
    for copy in copies:
        copy.start()
    for copy in copies:
        copy.wait()
    total = None
    for block in range(4):
        cols = slice(block * 256, block * 256 + 256)
        rounded = send_ref[:64, cols].astype(BF16)
        leaf_coeff = lax.dot_general(
            rounded, block_diagonal(basis_in[:, cols]), NT, preferred_element_type=F32
        ).astype(BF16)
        transfer = transfer_in[:, cols]
        part = lax.dot_general(
            leaf_coeff,
            jnp.concatenate([transfer, transfer], axis=0),
            NT,
            preferred_element_type=F32,
        )
        total = part if total is None else total + part
    matrix = upper_in[...]
    wide = split_rows(jnp.concatenate([matrix, matrix], axis=1))
    lifted = multiply([(split_lanes(total), wide)])
    halves = [fold(lifted[:32]), fold(lifted[32:])]
    for target in range(lifted_ref.shape[0]):
        lifted_ref[target] = halves[GROUP_X[target] % 2]
    send_ref[64:67, :] = points_in[...]
    packed = fold(total)
    for tile in range(8):
        cols = slice(tile * LANES, tile * LANES + LANES)
        send_ref[67:71, cols] = packed[tile * 4 : tile * 4 + 4]
    send_ref[71:72, :] = jnp.zeros((1, LEAVES * LEAF), F32)


def as_nodes(value):
    return [value[row : row + 32] for row in range(0, value.shape[0], 32)]


def device_index():
    index_x = lax.axis_index("gx")
    return index_x, lax.axis_index("gy"), index_x & 1


def device_sides():
    index_x, index_y, _ = device_index()
    return [(index_x if axis == "x" else index_y) >> bit & 1 for axis, bit in PLACES]


def place_index(sides, listed):
    index = jnp.int32(0)
    for bit, place in enumerate(listed):
        index = index + sides[place] * 2**bit
    return index


def sent_coeff(ref):
    return jnp.concatenate(
        [ref[67:71, tile * LANES : tile * LANES + LANES] for tile in range(8)], axis=0
    )


def fold(value):
    rows = value.shape[0] // 2
    return jnp.where(low_lanes(rows), value[:rows], value[rows:])


def unfold(packed):
    low = low_lanes(packed.shape[0])
    rolled = pltpu.roll(packed, HALF, 1)
    return jnp.concatenate(
        [jnp.where(low, packed, rolled), jnp.where(low, rolled, packed)], axis=0
    )


def multiply(pairs):
    left = [piece for value, _ in pairs for piece in (value, value)]
    right = [piece for _, m in pairs for piece in (m[:64], m[:64], m[64:], m[64:])]
    return jnp.dot(
        jnp.concatenate(left, axis=1),
        jnp.concatenate(right, axis=0),
        preferred_element_type=F32,
    )


def weights_kernel(upper_ref, coupling_ref, admissible_ref, out_ref):
    sides = device_sides()
    code = place_index(sides, range(LEVELS))

    def plain(matrix):
        return jnp.concatenate([matrix, matrix], axis=1)

    def transposed(matrix):
        return jnp.concatenate([matrix, matrix], axis=0).T

    for h in range(LEVELS - 2):
        for side in range(2):
            matrix = upper_ref[h, sides[h] ^ side]
            if (h, side) in CLIMB:
                out_ref[CLIMB[h, side]] = split_rows(plain(matrix))
            if (h, side) in DOWN:
                out_ref[DOWN[h, side]] = split_rows(transposed(matrix))
    for h in range(LEVELS - 1):
        first = 2 * DEVICES - 2 * DEVICES // 2**h
        for step in (1, 2, 3):
            turned = sum(1 << p for p in (0, 1) if step >> p & 1 and h + p in TARGET)
            target = (code >> h) ^ (turned if h else 0)
            here = target & 3
            there = here ^ step
            matrix = coupling_ref[h, jnp.abs(there - here) - 1]
            flag = admissible_ref[step - 1, first + target].astype(F32)
            upward = jnp.full((64, LANES), there - here, jnp.int32) > 0
            chosen = jnp.where(upward, transposed(matrix), plain(matrix))
            out_ref[FAR[h, step]] = split_rows(chosen * flag)


def tree_kernel(gathered_ref, weights_ref, out_ref, tie_ref, downs):
    sides = device_sides()
    own_source = place_index(sides, SOURCE)
    own_target = place_index(sides, TARGET)
    nodes = []
    for relative in range(2 ** len(SOURCE)):
        far_z = own_source ^ relative ^ 7
        first = (far_z & 3) * 4 + (far_z >> 2) * 2
        nodes.append(split_lanes(unfold(gathered_ref[first] + gathered_ref[first + 1])))
    levels = {1: nodes}
    for h in range(1, LEVELS - 2):
        if h in SOURCE:
            pairs = [
                (jnp.concatenate(nodes[bit::2], axis=0), weights_ref[CLIMB[h, bit]])
                for bit in range(2)
            ]
        else:
            pairs = [(jnp.concatenate(nodes, axis=0), weights_ref[CLIMB[h, 0]])]
        nodes = as_nodes(split_lanes(multiply(pairs)))
        levels[h + 1] = nodes
    down = None
    for h in range(LEVELS - 2, 0, -1):
        if down is None:
            down = [jnp.zeros((32, LANES), F32)] * 2 ** len(above(TARGET, h))
        else:
            value = split_lanes(jnp.concatenate(down, axis=0))
            parts = [
                as_nodes(multiply([(value, weights_ref[DOWN[h, bit]])]))
                for bit in range(2 if h in TARGET else 1)
            ]
            down = [part for group in zip(*parts) for part in group]
        terms = {}
        for step in (1, 2, 3):
            pair = levels[h][flipped(SOURCE, h, step)], weights_ref[FAR[h, step]]
            terms.setdefault(flipped(TARGET, h, step), []).append(pair)
        for turned, pairs in terms.items():
            down[turned] = down[turned] + multiply(pairs)
    for relative, part in enumerate(down):
        downs[relative] = fold(part)
    for member, node in enumerate(GROUP_Y):
        out_ref[member] = downs[own_target ^ node]
    tie_ref[...] = jnp.zeros_like(tie_ref)


def sum_kernel(parts_ref, tie_ref, out_ref):
    total = parts_ref[0]
    for source in range(1, parts_ref.shape[0]):
        total = total + parts_ref[source]
    out_ref[...] = total


def near_kernel(
    listed_ref,
    own_ref,
    x_ref,
    y_ref,
    xy_ref,
    weights_ref,
    tie_ref,
    out_ref,
    far_ref,
    values,
    rows,
    columns,
    sums,
):
    _, index_y, core = device_index()
    far_ref[...] = multiply(
        [
            (split_lanes(unfold(sent_coeff(ref))), weights_ref[FAR[0, step]])
            for step, ref in enumerate((x_ref, y_ref, xy_ref), 1)
        ]
    )
    low = low_lanes(8)
    for tile in range(LEAVES // 2):
        cols = slice(tile * LANES, tile * LANES + LANES)
        for axis in range(3):
            spread = jnp.broadcast_to(own_ref[64 + axis : 65 + axis, cols], (LANES, LANES))
            columns[axis, cols, :] = spread.T
    for block, ref in enumerate((own_ref, x_ref, y_ref, xy_ref)):
        for tile in range(LEAVES // 2):
            cols = slice(tile * LANES, tile * LANES + LANES)
            first = block * LEAVES + tile * 2
            values[first : first + 2] = split_rows(ref[:64, cols]).T.reshape(2, LEAF, LANES)
            point = ref[64:72, cols]
            rolled = pltpu.roll(point, HALF, 1)
            rows[first] = jnp.where(low, point, rolled)
            rows[first + 1] = jnp.where(low, rolled, point)

    def local(leaf, place):
        listed = listed_ref[leaf, place]
        owner = listed >> 4
        flip_x = (owner >> BITS_Y ^ core) & 1
        flip_y = (owner ^ index_y) & 1
        return (flip_x + 2 * flip_y) * LEAVES + (listed & LEAVES - 1)

    def one_leaf(leaf, carry):
        here = pl.ds(pl.multiple_of(leaf * LEAF, LEAF), LEAF)
        total = None
        for quad in range(3):
            ids = [local(leaf, quad * 4 + place) for place in range(4)]
            kernels = []
            for pair in range(2):
                source = jnp.where(low, rows[ids[pair * 2]], rows[ids[pair * 2 + 1]])
                square = None
                for axis in range(3):
                    delta = columns[axis, here, :] - source[axis : axis + 1]
                    square = delta * delta if square is None else square + delta * delta
                square = jnp.maximum(square, 1e-30)
                distance = square * lax.rsqrt(square)
                scale = ROOT_THREE / LENGTH_SCALE
                decay = jnp.exp2(distance * (-scale * LOG2_E))
                kernel = (distance * (AMPLITUDE * scale) + AMPLITUDE) * decay
                kernels.append(kernel.astype(BF16))
            weight = jnp.concatenate(kernels, axis=1)
            source_values = jnp.concatenate([values[n] for n in ids], axis=0)
            part = jnp.dot(weight, source_values, preferred_element_type=F32)
            total = part if total is None else total + part
        sums[here, :] = total
        return carry

    lax.fori_loop(0, LEAVES, one_leaf, 0, unroll=4)
    for tile in range(LEAVES // 2):
        cols = slice(tile * LANES, tile * LANES + LANES)
        flipped = sums[cols, :].T
        out_ref[:, cols] = flipped[:64] + flipped[64:] + NUGGET * own_ref[:64, cols]


def final_kernel(own_ref, other_ref, far_ref, weights_ref, near_ref, basis_ref, transfer_ref, out_ref):
    first = jnp.full((32, LANES), lax.axis_index("gx") & 1, jnp.int32) == 0
    own = unfold(own_ref[...])
    other = unfold(other_ref[...])
    above = jnp.concatenate([jnp.where(first, own, other), jnp.where(first, other, own)], axis=0)
    down = far_ref[...] + multiply([(split_lanes(above), weights_ref[DOWN[0, 0]])])
    down = down[:, :HALF].astype(BF16)
    for block in range(4):
        cols = slice(block * 256, block * 256 + 256)
        leaf_down = jnp.dot(down, transfer_ref[:, cols], preferred_element_type=F32).astype(BF16)
        far = jnp.dot(leaf_down, block_diagonal(basis_ref[:, cols]), preferred_element_type=F32)
        out_ref[:, cols] = near_ref[:, cols] + far


def call(kernel, out_shape, in_specs, scratch_shapes, *operands, limit=40):
    shapes = tuple(jax.ShapeDtypeStruct(shape, dtype) for shape, dtype in out_shape)
    return pl.pallas_call(
        kernel,
        out_shape=shapes,
        in_specs=in_specs,
        out_specs=(VMEM,) * len(shapes),
        scratch_shapes=scratch_shapes,
        compiler_params=pltpu.CompilerParams(vmem_limit_bytes=limit * 1024 * 1024),
    )(*operands)


def exchange(value, name, group):
    return lax.all_to_all(
        value, name, split_axis=0, concat_axis=0, axis_index_groups=[group], tiled=True
    )


def body(
    right_sides,
    points,
    leaf_basis,
    leaf_transfer,
    upper_transfer,
    coupling,
    near_leaves,
    admissible,
):
    width = right_sides.shape[1]
    lifted, send = call(
        up_kernel,
        [((2 ** len(SOURCE) * 2, 16, LANES), F32), ((72, width), F32)],
        [pl.BlockSpec(memory_space=pltpu.HBM)] * 5,
        [
            pltpu.VMEM((3, width), F32),
            pltpu.VMEM((64, width), BF16),
            pltpu.VMEM((64, width), BF16),
            pltpu.VMEM((64, 64), F32),
            pltpu.SemaphoreType.DMA((5,)),
        ],
        right_sides,
        points,
        leaf_basis,
        leaf_transfer,
        upper_transfer,
        limit=60,
    )
    swap = [(i, i ^ 1) for i in range(2**BITS_X)]
    from_x = lax.ppermute(send, "gx", swap)
    from_y = lax.ppermute(send, "gy", [(j, j ^ 1) for j in range(2**BITS_Y)])
    gathered = exchange(lifted, "gx", GROUP_X)
    (weights,) = call(
        weights_kernel,
        [((WEIGHTS, 128, LANES), BF16)],
        [VMEM] * 2 + [SMEM],
        [],
        upper_transfer,
        coupling,
        admissible.T,
    )
    partial, tie = call(
        tree_kernel,
        [((2 ** len(TARGET), 16, LANES), F32), ((8, LANES), F32)],
        [VMEM] * 2,
        [pltpu.VMEM((2 ** len(TARGET), 16, LANES), F32)],
        gathered,
        weights,
    )
    partial, from_y = lax.optimization_barrier((partial, from_y))
    parts = exchange(partial, "gy", GROUP_Y)
    from_xy = lax.ppermute(from_y, "gx", swap)
    near, far = call(
        near_kernel,
        [((64, width), F32), ((64, LANES), F32)],
        [SMEM] + [VMEM] * 6,
        [
            pltpu.VMEM((4 * LEAVES, LEAF, LANES), BF16),
            pltpu.VMEM((4 * LEAVES, 8, LANES), F32),
            pltpu.VMEM((3, width, LANES), F32),
            pltpu.VMEM((width, LANES), F32),
        ],
        near_leaves,
        send,
        from_x,
        from_y,
        from_xy,
        weights,
        tie,
    )
    (own,) = call(sum_kernel, [((16, LANES), F32)], [VMEM, ANYWHERE], [], parts, far)
    other = lax.ppermute(own, "gx", swap)
    (product,) = call(
        final_kernel,
        [((64, width), F32)],
        [VMEM] * 7,
        [],
        own,
        other,
        far,
        weights,
        near,
        leaf_basis,
        leaf_transfer,
    )
    return product


def solution(mesh):
    split = P(None, ("gx", "gy"))
    in_specs = (split, split, split, split, P(), P(), P(("gx", "gy"), None), P())
    return jax.shard_map(body, mesh=mesh, in_specs=in_specs, out_specs=split, check_vma=False)
```

```python
import jax
import jax.numpy as jnp
from jax import lax
from jax.experimental import pallas as pl
from jax.experimental.pallas import tpu as pltpu
from jax.sharding import PartitionSpec as P

ROOT_THREE = 1.7320508075688772
LENGTH_SCALE = 0.6
AMPLITUDE = 0.25
NUGGET = 0.5
LOG2_E = 1.4426950408889634
BITS_X = 4
BITS_Y = 5
DEVICES = 512
LEVELS = 9
LEAVES = 16
LEAF = 64
RANK = 64
HALF = 64
LANES = 128
F32 = jnp.float32
BF16 = jnp.bfloat16
NT = (((1,), (1,)), ((), ()))
VMEM = pl.BlockSpec(memory_space=pltpu.VMEM)
ANYWHERE = pl.BlockSpec(memory_space=pl.ANY)
SMEM = pl.BlockSpec(memory_space=pltpu.SMEM)


def places():
    listed = []
    for bit in range(max(BITS_X, BITS_Y)):
        if bit < BITS_X:
            listed.append(("x", bit))
        if bit < BITS_Y:
            listed.append(("y", bit))
    return listed


PLACES = places()
SOURCE = (2, 4, 6)
TARGET = (1, 3, 5, 7, 8)
GROUP_X = [z * 2 + core for z in (7, 3, 6, 2, 5, 1, 4, 0) for core in (1, 0)]
GROUP_Y = [x * 8 + y for y in (3, 7, 1, 5, 2, 6, 4, 0) for x in (1, 3, 2, 0)]

CLIMB, DOWN, FAR = {}, {}, {}
for _h in range(1, LEVELS - 2):
    for _side in range(2 if _h in SOURCE else 1):
        CLIMB[_h, _side] = len(CLIMB)
for _h in range(LEVELS - 2):
    for _side in range(2 if _h in TARGET else 1):
        DOWN[_h, _side] = len(CLIMB) + len(DOWN)
for _h in range(LEVELS - 1):
    for _step in (1, 2, 3):
        FAR[_h, _step] = len(CLIMB) + len(DOWN) + len(FAR)
WEIGHTS = len(CLIMB) + len(DOWN) + len(FAR)


def above(chosen, h):
    return [place for place in chosen if place >= h]


def flipped(chosen, h, step):
    listed = above(chosen, h)
    return sum(1 << listed.index(h + p) for p in (0, 1) if step >> p & 1 and h + p in listed)


def low_lanes(rows):
    return lax.broadcasted_iota(jnp.int32, (rows, LANES), 1) < HALF


def split_lanes(value):
    high = value.astype(BF16).astype(F32)
    return jnp.where(low_lanes(value.shape[0]), high, value - high).astype(BF16)


def split_rows(wide):
    high = wide.astype(BF16)
    return jnp.concatenate([high, (wide - high.astype(F32)).astype(BF16)], axis=0)


def block_diagonal(basis):
    wide = basis.astype(F32)
    leaf = lax.broadcasted_iota(jnp.int32, wide.shape, 1) // LEAF
    return jnp.concatenate([jnp.where(leaf == l, wide, 0.0).astype(BF16) for l in range(4)], axis=0)


def up_kernel(
    right_ref,
    points_ref,
    basis_ref,
    transfer_ref,
    upper_ref,
    lifted_ref,
    send_ref,
    points_in,
    basis_in,
    transfer_in,
    upper_in,
    sems,
):
    copies = [
        pltpu.make_async_copy(right_ref, send_ref.at[pl.ds(0, 64)], sems.at[0]),
        pltpu.make_async_copy(basis_ref, basis_in, sems.at[1]),
        pltpu.make_async_copy(transfer_ref, transfer_in, sems.at[2]),
        pltpu.make_async_copy(points_ref, points_in, sems.at[3]),
        pltpu.make_async_copy(upper_ref.at[0, lax.axis_index("gx") & 1], upper_in, sems.at[4]),
    ]
    for copy in copies:
        copy.start()
    for copy in copies:
        copy.wait()
    total = None
    for block in range(4):
        cols = slice(block * 256, block * 256 + 256)
        rounded = send_ref[:64, cols].astype(BF16)
        leaf_coeff = lax.dot_general(
            rounded, block_diagonal(basis_in[:, cols]), NT, preferred_element_type=F32
        ).astype(BF16)
        transfer = transfer_in[:, cols]
        part = lax.dot_general(
            leaf_coeff,
            jnp.concatenate([transfer, transfer], axis=0),
            NT,
            preferred_element_type=F32,
        )
        total = part if total is None else total + part
    matrix = upper_in[...]
    wide = split_rows(jnp.concatenate([matrix, matrix], axis=1))
    lifted = multiply([(split_lanes(total), wide)])
    halves = [fold(lifted[:32]), fold(lifted[32:])]
    for target in range(lifted_ref.shape[0]):
        lifted_ref[target] = halves[GROUP_X[target] % 2]
    send_ref[64:67, :] = points_in[...]
    packed = fold(total)
    for tile in range(8):
        cols = slice(tile * LANES, tile * LANES + LANES)
        send_ref[67:71, cols] = packed[tile * 4 : tile * 4 + 4]
    send_ref[71:72, :] = jnp.zeros((1, LEAVES * LEAF), F32)


def as_nodes(value):
    return [value[row : row + 32] for row in range(0, value.shape[0], 32)]


def device_index():
    index_x = lax.axis_index("gx")
    return index_x, lax.axis_index("gy"), index_x & 1


def device_sides():
    index_x, index_y, _ = device_index()
    return [(index_x if axis == "x" else index_y) >> bit & 1 for axis, bit in PLACES]


def place_index(sides, listed):
    index = jnp.int32(0)
    for bit, place in enumerate(listed):
        index = index + sides[place] * 2**bit
    return index


def sent_coeff(ref):
    return jnp.concatenate(
        [ref[67:71, tile * LANES : tile * LANES + LANES] for tile in range(8)], axis=0
    )


def fold(value):
    rows = value.shape[0] // 2
    return jnp.where(low_lanes(rows), value[:rows], value[rows:])


def unfold(packed):
    low = low_lanes(packed.shape[0])
    rolled = pltpu.roll(packed, HALF, 1)
    return jnp.concatenate(
        [jnp.where(low, packed, rolled), jnp.where(low, rolled, packed)], axis=0
    )


def multiply(pairs):
    left = [piece for value, _ in pairs for piece in (value, value)]
    right = [piece for _, m in pairs for piece in (m[:64], m[:64], m[64:], m[64:])]
    return jnp.dot(
        jnp.concatenate(left, axis=1),
        jnp.concatenate(right, axis=0),
        preferred_element_type=F32,
    )


def weights_kernel(upper_ref, coupling_ref, admissible_ref, out_ref):
    sides = device_sides()
    code = place_index(sides, range(LEVELS))

    def plain(matrix):
        return jnp.concatenate([matrix, matrix], axis=1)

    def transposed(matrix):
        return jnp.concatenate([matrix, matrix], axis=0).T

    for h in range(LEVELS - 2):
        for side in range(2):
            matrix = upper_ref[h, sides[h] ^ side]
            if (h, side) in CLIMB:
                out_ref[CLIMB[h, side]] = split_rows(plain(matrix))
            if (h, side) in DOWN:
                out_ref[DOWN[h, side]] = split_rows(transposed(matrix))
    for h in range(LEVELS - 1):
        first = 2 * DEVICES - 2 * DEVICES // 2**h
        for step in (1, 2, 3):
            turned = sum(1 << p for p in (0, 1) if step >> p & 1 and h + p in TARGET)
            target = (code >> h) ^ (turned if h else 0)
            here = target & 3
            there = here ^ step
            matrix = coupling_ref[h, jnp.abs(there - here) - 1]
            flag = admissible_ref[step - 1, first + target].astype(F32)
            upward = jnp.full((64, LANES), there - here, jnp.int32) > 0
            chosen = jnp.where(upward, transposed(matrix), plain(matrix))
            out_ref[FAR[h, step]] = split_rows(chosen * flag)


def tree_kernel(gathered_ref, weights_ref, out_ref, tie_ref, downs):
    sides = device_sides()
    own_source = place_index(sides, SOURCE)
    own_target = place_index(sides, TARGET)
    nodes = []
    for relative in range(2 ** len(SOURCE)):
        far_z = own_source ^ relative ^ 7
        first = (far_z & 3) * 4 + (far_z >> 2) * 2
        nodes.append(split_lanes(unfold(gathered_ref[first] + gathered_ref[first + 1])))
    levels = {1: nodes}
    for h in range(1, LEVELS - 2):
        if h in SOURCE:
            pairs = [
                (jnp.concatenate(nodes[bit::2], axis=0), weights_ref[CLIMB[h, bit]])
                for bit in range(2)
            ]
        else:
            pairs = [(jnp.concatenate(nodes, axis=0), weights_ref[CLIMB[h, 0]])]
        nodes = as_nodes(split_lanes(multiply(pairs)))
        levels[h + 1] = nodes
    down = None
    for h in range(LEVELS - 2, 0, -1):
        if down is None:
            down = [jnp.zeros((32, LANES), F32)] * 2 ** len(above(TARGET, h))
        else:
            value = split_lanes(jnp.concatenate(down, axis=0))
            parts = [
                as_nodes(multiply([(value, weights_ref[DOWN[h, bit]])]))
                for bit in range(2 if h in TARGET else 1)
            ]
            down = [part for group in zip(*parts) for part in group]
        terms = {}
        for step in (1, 2, 3):
            pair = levels[h][flipped(SOURCE, h, step)], weights_ref[FAR[h, step]]
            terms.setdefault(flipped(TARGET, h, step), []).append(pair)
        for turned, pairs in terms.items():
            down[turned] = down[turned] + multiply(pairs)
    for relative, part in enumerate(down):
        downs[relative] = fold(part)
    for member, node in enumerate(GROUP_Y):
        out_ref[member] = downs[own_target ^ node]
    tie_ref[...] = jnp.zeros_like(tie_ref)


def sum_kernel(parts_ref, tie_ref, out_ref):
    total = parts_ref[0]
    for source in range(1, parts_ref.shape[0]):
        total = total + parts_ref[source]
    out_ref[...] = total


def near_kernel(
    listed_ref,
    own_ref,
    x_ref,
    y_ref,
    xy_ref,
    weights_ref,
    tie_ref,
    out_ref,
    far_ref,
    values,
    rows,
    columns,
    sums,
):
    _, index_y, core = device_index()
    far_ref[...] = multiply(
        [
            (split_lanes(unfold(sent_coeff(ref))), weights_ref[FAR[0, step]])
            for step, ref in enumerate((x_ref, y_ref, xy_ref), 1)
        ]
    )
    low = low_lanes(8)
    for tile in range(LEAVES // 2):
        cols = slice(tile * LANES, tile * LANES + LANES)
        for axis in range(3):
            spread = jnp.broadcast_to(own_ref[64 + axis : 65 + axis, cols], (LANES, LANES))
            columns[axis, cols, :] = spread.T
    for block, ref in enumerate((own_ref, x_ref, y_ref, xy_ref)):
        for tile in range(LEAVES // 2):
            cols = slice(tile * LANES, tile * LANES + LANES)
            first = block * LEAVES + tile * 2
            values[first : first + 2] = split_rows(ref[:64, cols]).T.reshape(2, LEAF, LANES)
            point = ref[64:72, cols]
            rolled = pltpu.roll(point, HALF, 1)
            rows[first] = jnp.where(low, point, rolled)
            rows[first + 1] = jnp.where(low, rolled, point)

    def local(leaf, place):
        listed = listed_ref[leaf, place]
        owner = listed >> 4
        flip_x = (owner >> BITS_Y ^ core) & 1
        flip_y = (owner ^ index_y) & 1
        return (flip_x + 2 * flip_y) * LEAVES + (listed & LEAVES - 1)

    def one_leaf(leaf, carry):
        here = pl.ds(pl.multiple_of(leaf * LEAF, LEAF), LEAF)
        total = None
        for quad in range(3):
            ids = [local(leaf, quad * 4 + place) for place in range(4)]
            kernels = []
            for pair in range(2):
                source = jnp.where(low, rows[ids[pair * 2]], rows[ids[pair * 2 + 1]])
                square = None
                for axis in range(3):
                    delta = columns[axis, here, :] - source[axis : axis + 1]
                    square = delta * delta if square is None else square + delta * delta
                square = jnp.maximum(square, 1e-30)
                distance = square * lax.rsqrt(square)
                scale = ROOT_THREE / LENGTH_SCALE
                decay = jnp.exp2(distance * (-scale * LOG2_E))
                kernel = (distance * (AMPLITUDE * scale) + AMPLITUDE) * decay
                kernels.append(kernel.astype(BF16))
            weight = jnp.concatenate(kernels, axis=1)
            source_values = jnp.concatenate([values[n] for n in ids], axis=0)
            part = jnp.dot(weight, source_values, preferred_element_type=F32)
            total = part if total is None else total + part
        sums[here, :] = total
        return carry

    lax.fori_loop(0, LEAVES, one_leaf, 0, unroll=4)
    for tile in range(LEAVES // 2):
        cols = slice(tile * LANES, tile * LANES + LANES)
        flipped = sums[cols, :].T
        out_ref[:, cols] = flipped[:64] + flipped[64:] + NUGGET * own_ref[:64, cols]


def final_kernel(own_ref, other_ref, far_ref, weights_ref, near_ref, basis_ref, transfer_ref, out_ref):
    first = jnp.full((32, LANES), lax.axis_index("gx") & 1, jnp.int32) == 0
    own = unfold(own_ref[...])
    other = unfold(other_ref[...])
    above = jnp.concatenate([jnp.where(first, own, other), jnp.where(first, other, own)], axis=0)
    down = far_ref[...] + multiply([(split_lanes(above), weights_ref[DOWN[0, 0]])])
    down = down[:, :HALF].astype(BF16)
    for block in range(4):
        cols = slice(block * 256, block * 256 + 256)
        leaf_down = jnp.dot(down, transfer_ref[:, cols], preferred_element_type=F32).astype(BF16)
        far = jnp.dot(leaf_down, block_diagonal(basis_ref[:, cols]), preferred_element_type=F32)
        out_ref[:, cols] = near_ref[:, cols] + far


def call(kernel, out_shape, in_specs, scratch_shapes, *operands, limit=40, cost=None):
    shapes = tuple(jax.ShapeDtypeStruct(shape, dtype) for shape, dtype in out_shape)
    return pl.pallas_call(
        kernel,
        out_shape=shapes,
        in_specs=in_specs,
        out_specs=(VMEM,) * len(shapes),
        scratch_shapes=scratch_shapes,
        cost_estimate=cost,
        compiler_params=pltpu.CompilerParams(vmem_limit_bytes=limit * 1024 * 1024),
    )(*operands)


def exchange(value, name, group):
    return lax.all_to_all(
        value, name, split_axis=0, concat_axis=0, axis_index_groups=[group], tiled=True
    )


def body(
    right_sides,
    points,
    leaf_basis,
    leaf_transfer,
    upper_transfer,
    coupling,
    near_leaves,
    admissible,
):
    width = right_sides.shape[1]
    lifted, send = call(
        up_kernel,
        [((2 ** len(SOURCE) * 2, 16, LANES), F32), ((72, width), F32)],
        [pl.BlockSpec(memory_space=pltpu.HBM)] * 5,
        [
            pltpu.VMEM((3, width), F32),
            pltpu.VMEM((64, width), BF16),
            pltpu.VMEM((64, width), BF16),
            pltpu.VMEM((64, 64), F32),
            pltpu.SemaphoreType.DMA((5,)),
        ],
        right_sides,
        points,
        leaf_basis,
        leaf_transfer,
        upper_transfer,
        limit=60,
    )
    swap = [(i, i ^ 1) for i in range(2**BITS_X)]
    from_x = lax.ppermute(send, "gx", swap)
    from_y = lax.ppermute(send, "gy", [(j, j ^ 1) for j in range(2**BITS_Y)])
    gathered = exchange(lifted, "gx", GROUP_X)
    (weights,) = call(
        weights_kernel,
        [((WEIGHTS, 128, LANES), BF16)],
        [VMEM] * 2 + [SMEM],
        [],
        upper_transfer,
        coupling,
        admissible.T,
    )
    partial, tie = call(
        tree_kernel,
        [((2 ** len(TARGET), 16, LANES), F32), ((8, LANES), F32)],
        [VMEM] * 2,
        [pltpu.VMEM((2 ** len(TARGET), 16, LANES), F32)],
        gathered,
        weights,
        cost=pl.CostEstimate(flops=4 * 10**9, bytes_accessed=12 * 10**6, transcendentals=0),
    )
    partial, from_y = lax.optimization_barrier((partial, from_y))
    parts = exchange(partial, "gy", GROUP_Y)
    from_xy = lax.ppermute(from_y, "gx", swap)
    near, far = call(
        near_kernel,
        [((64, width), F32), ((64, LANES), F32)],
        [SMEM] + [VMEM] * 6,
        [
            pltpu.VMEM((4 * LEAVES, LEAF, LANES), BF16),
            pltpu.VMEM((4 * LEAVES, 8, LANES), F32),
            pltpu.VMEM((3, width, LANES), F32),
            pltpu.VMEM((width, LANES), F32),
        ],
        near_leaves,
        send,
        from_x,
        from_y,
        from_xy,
        weights,
        tie,
    )
    (own,) = call(sum_kernel, [((16, LANES), F32)], [VMEM, ANYWHERE], [], parts, far)
    other = lax.ppermute(own, "gx", swap)
    (product,) = call(
        final_kernel,
        [((64, width), F32)],
        [VMEM] * 7,
        [],
        own,
        other,
        far,
        weights,
        near,
        leaf_basis,
        leaf_transfer,
    )
    return product


def solution(mesh):
    split = P(None, ("gx", "gy"))
    in_specs = (split, split, split, split, P(), P(), P(("gx", "gy"), None), P())
    return jax.shard_map(body, mesh=mesh, in_specs=in_specs, out_specs=split, check_vma=False)
```

```python
import jax
import jax.numpy as jnp
from jax import lax
from jax.experimental import pallas as pl
from jax.experimental.pallas import tpu as pltpu
from jax.sharding import PartitionSpec as P

ROOT_THREE = 1.7320508075688772
LENGTH_SCALE = 0.6
AMPLITUDE = 0.25
NUGGET = 0.5
LOG2_E = 1.4426950408889634
BITS_X = 4
BITS_Y = 5
DEVICES = 512
LEVELS = 9
LEAVES = 16
LEAF = 64
RANK = 64
HALF = 64
LANES = 128
F32 = jnp.float32
BF16 = jnp.bfloat16
NT = (((1,), (1,)), ((), ()))
VMEM = pl.BlockSpec(memory_space=pltpu.VMEM)
ANYWHERE = pl.BlockSpec(memory_space=pl.ANY)
SMEM = pl.BlockSpec(memory_space=pltpu.SMEM)


def places():
    listed = []
    for bit in range(max(BITS_X, BITS_Y)):
        if bit < BITS_X:
            listed.append(("x", bit))
        if bit < BITS_Y:
            listed.append(("y", bit))
    return listed


PLACES = places()
SOURCE = (2, 4, 6)
TARGET = (1, 3, 5, 7, 8)
GROUP_X = [z * 2 + core for z in (7, 3, 6, 2, 5, 1, 4, 0) for core in (1, 0)]
GROUP_Y = [x * 8 + y for y in (3, 7, 1, 5, 2, 6, 4, 0) for x in (1, 3, 2, 0)]

CLIMB, DOWN, FAR = {}, {}, {}
for _h in range(1, LEVELS - 2):
    for _side in range(2 if _h in SOURCE else 1):
        CLIMB[_h, _side] = len(CLIMB)
for _h in range(LEVELS - 2):
    for _side in range(2 if _h in TARGET else 1):
        DOWN[_h, _side] = len(CLIMB) + len(DOWN)
for _h in range(LEVELS - 1):
    for _step in (1, 2, 3):
        FAR[_h, _step] = len(CLIMB) + len(DOWN) + len(FAR)
WEIGHTS = len(CLIMB) + len(DOWN) + len(FAR)


def above(chosen, h):
    return [place for place in chosen if place >= h]


def flipped(chosen, h, step):
    listed = above(chosen, h)
    return sum(1 << listed.index(h + p) for p in (0, 1) if step >> p & 1 and h + p in listed)


def low_lanes(rows):
    return lax.broadcasted_iota(jnp.int32, (rows, LANES), 1) < HALF


def split_lanes(value):
    high = value.astype(BF16).astype(F32)
    return jnp.where(low_lanes(value.shape[0]), high, value - high).astype(BF16)


def split_rows(wide):
    high = wide.astype(BF16)
    return jnp.concatenate([high, (wide - high.astype(F32)).astype(BF16)], axis=0)


def block_diagonal(basis):
    wide = basis.astype(F32)
    leaf = lax.broadcasted_iota(jnp.int32, wide.shape, 1) // LEAF
    return jnp.concatenate([jnp.where(leaf == l, wide, 0.0).astype(BF16) for l in range(4)], axis=0)


def up_kernel(
    right_ref,
    points_ref,
    basis_ref,
    transfer_ref,
    upper_ref,
    lifted_ref,
    send_ref,
    points_in,
    basis_in,
    transfer_in,
    upper_in,
    sems,
):
    copies = [
        pltpu.make_async_copy(right_ref, send_ref.at[pl.ds(0, 64)], sems.at[0]),
        pltpu.make_async_copy(basis_ref, basis_in, sems.at[1]),
        pltpu.make_async_copy(transfer_ref, transfer_in, sems.at[2]),
        pltpu.make_async_copy(points_ref, points_in, sems.at[3]),
        pltpu.make_async_copy(upper_ref.at[0, lax.axis_index("gx") & 1], upper_in, sems.at[4]),
    ]
    for copy in copies:
        copy.start()
    for copy in copies:
        copy.wait()
    total = None
    for block in range(4):
        cols = slice(block * 256, block * 256 + 256)
        rounded = send_ref[:64, cols].astype(BF16)
        leaf_coeff = lax.dot_general(
            rounded, block_diagonal(basis_in[:, cols]), NT, preferred_element_type=F32
        ).astype(BF16)
        transfer = transfer_in[:, cols]
        part = lax.dot_general(
            leaf_coeff,
            jnp.concatenate([transfer, transfer], axis=0),
            NT,
            preferred_element_type=F32,
        )
        total = part if total is None else total + part
    matrix = upper_in[...]
    wide = split_rows(jnp.concatenate([matrix, matrix], axis=1))
    lifted = multiply([(split_lanes(total), wide)])
    halves = [fold(lifted[:32]), fold(lifted[32:])]
    for target in range(lifted_ref.shape[0]):
        lifted_ref[target] = halves[GROUP_X[target] % 2]
    send_ref[64:67, :] = points_in[...]
    packed = fold(total)
    for tile in range(8):
        cols = slice(tile * LANES, tile * LANES + LANES)
        send_ref[67:71, cols] = packed[tile * 4 : tile * 4 + 4]
    send_ref[71:72, :] = jnp.zeros((1, LEAVES * LEAF), F32)


def as_nodes(value):
    return [value[row : row + 32] for row in range(0, value.shape[0], 32)]


def device_index():
    index_x = lax.axis_index("gx")
    return index_x, lax.axis_index("gy"), index_x & 1


def device_sides():
    index_x, index_y, _ = device_index()
    return [(index_x if axis == "x" else index_y) >> bit & 1 for axis, bit in PLACES]


def place_index(sides, listed):
    index = jnp.int32(0)
    for bit, place in enumerate(listed):
        index = index + sides[place] * 2**bit
    return index


def sent_coeff(ref):
    return jnp.concatenate(
        [ref[67:71, tile * LANES : tile * LANES + LANES] for tile in range(8)], axis=0
    )


def fold(value):
    rows = value.shape[0] // 2
    return jnp.where(low_lanes(rows), value[:rows], value[rows:])


def unfold(packed):
    low = low_lanes(packed.shape[0])
    rolled = pltpu.roll(packed, HALF, 1)
    return jnp.concatenate(
        [jnp.where(low, packed, rolled), jnp.where(low, rolled, packed)], axis=0
    )


def multiply(pairs):
    left = [piece for value, _ in pairs for piece in (value, value)]
    right = [piece for _, m in pairs for piece in (m[:64], m[:64], m[64:], m[64:])]
    return jnp.dot(
        jnp.concatenate(left, axis=1),
        jnp.concatenate(right, axis=0),
        preferred_element_type=F32,
    )


def weights_kernel(upper_ref, coupling_ref, admissible_ref, out_ref):
    sides = device_sides()
    code = place_index(sides, range(LEVELS))

    def plain(matrix):
        return jnp.concatenate([matrix, matrix], axis=1)

    def transposed(matrix):
        return jnp.concatenate([matrix, matrix], axis=0).T

    for h in range(LEVELS - 2):
        for side in range(2):
            matrix = upper_ref[h, sides[h] ^ side]
            if (h, side) in CLIMB:
                out_ref[CLIMB[h, side]] = split_rows(plain(matrix))
            if (h, side) in DOWN:
                out_ref[DOWN[h, side]] = split_rows(transposed(matrix))
    for h in range(LEVELS - 1):
        first = 2 * DEVICES - 2 * DEVICES // 2**h
        for step in (1, 2, 3):
            turned = sum(1 << p for p in (0, 1) if step >> p & 1 and h + p in TARGET)
            target = (code >> h) ^ (turned if h else 0)
            here = target & 3
            there = here ^ step
            matrix = coupling_ref[h, jnp.abs(there - here) - 1]
            flag = admissible_ref[step - 1, first + target].astype(F32)
            upward = jnp.full((64, LANES), there - here, jnp.int32) > 0
            chosen = jnp.where(upward, transposed(matrix), plain(matrix))
            out_ref[FAR[h, step]] = split_rows(chosen * flag)


def tree_kernel(gathered_ref, weights_ref, out_ref, tie_ref, downs):
    sides = device_sides()
    own_source = place_index(sides, SOURCE)
    own_target = place_index(sides, TARGET)
    nodes = []
    for relative in range(2 ** len(SOURCE)):
        far_z = own_source ^ relative ^ 7
        first = (far_z & 3) * 4 + (far_z >> 2) * 2
        nodes.append(split_lanes(unfold(gathered_ref[first] + gathered_ref[first + 1])))
    levels = {1: nodes}
    for h in range(1, LEVELS - 2):
        if h in SOURCE:
            pairs = [
                (jnp.concatenate(nodes[bit::2], axis=0), weights_ref[CLIMB[h, bit]])
                for bit in range(2)
            ]
        else:
            pairs = [(jnp.concatenate(nodes, axis=0), weights_ref[CLIMB[h, 0]])]
        nodes = as_nodes(split_lanes(multiply(pairs)))
        levels[h + 1] = nodes
    down = None
    for h in range(LEVELS - 2, 0, -1):
        if down is None:
            down = [jnp.zeros((32, LANES), F32)] * 2 ** len(above(TARGET, h))
        else:
            value = split_lanes(jnp.concatenate(down, axis=0))
            parts = [
                as_nodes(multiply([(value, weights_ref[DOWN[h, bit]])]))
                for bit in range(2 if h in TARGET else 1)
            ]
            down = [part for group in zip(*parts) for part in group]
        terms = {}
        for step in (1, 2, 3):
            pair = levels[h][flipped(SOURCE, h, step)], weights_ref[FAR[h, step]]
            terms.setdefault(flipped(TARGET, h, step), []).append(pair)
        for turned, pairs in terms.items():
            down[turned] = down[turned] + multiply(pairs)
    for relative, part in enumerate(down):
        downs[relative] = fold(part)
    for member, node in enumerate(GROUP_Y):
        out_ref[member] = downs[own_target ^ node]
    tie_ref[...] = jnp.zeros_like(tie_ref)


def sum_kernel(parts_ref, tie_ref, out_ref):
    total = parts_ref[0]
    for source in range(1, parts_ref.shape[0]):
        total = total + parts_ref[source]
    out_ref[...] = total


def near_kernel(
    listed_ref,
    own_ref,
    x_ref,
    y_ref,
    xy_ref,
    weights_ref,
    tie_ref,
    out_ref,
    far_ref,
    values,
    rows,
    columns,
    sums,
):
    _, index_y, core = device_index()
    far_ref[...] = multiply(
        [
            (split_lanes(unfold(sent_coeff(ref))), weights_ref[FAR[0, step]])
            for step, ref in enumerate((x_ref, y_ref, xy_ref), 1)
        ]
    )
    low = low_lanes(8)
    for tile in range(LEAVES // 2):
        cols = slice(tile * LANES, tile * LANES + LANES)
        for axis in range(3):
            spread = jnp.broadcast_to(own_ref[64 + axis : 65 + axis, cols], (LANES, LANES))
            columns[axis, cols, :] = spread.T
    for block, ref in enumerate((own_ref, x_ref, y_ref, xy_ref)):
        for tile in range(LEAVES // 2):
            cols = slice(tile * LANES, tile * LANES + LANES)
            first = block * LEAVES + tile * 2
            values[first : first + 2] = split_rows(ref[:64, cols]).T.reshape(2, LEAF, LANES)
            point = ref[64:72, cols]
            rolled = pltpu.roll(point, HALF, 1)
            rows[first] = jnp.where(low, point, rolled)
            rows[first + 1] = jnp.where(low, rolled, point)

    def local(leaf, place):
        listed = listed_ref[leaf, place]
        owner = listed >> 4
        flip_x = (owner >> BITS_Y ^ core) & 1
        flip_y = (owner ^ index_y) & 1
        return (flip_x + 2 * flip_y) * LEAVES + (listed & LEAVES - 1)

    def one_leaf(leaf, carry):
        here = pl.ds(pl.multiple_of(leaf * LEAF, LEAF), LEAF)
        total = None
        for quad in range(3):
            ids = [local(leaf, quad * 4 + place) for place in range(4)]
            kernels = []
            for pair in range(2):
                source = jnp.where(low, rows[ids[pair * 2]], rows[ids[pair * 2 + 1]])
                square = None
                for axis in range(3):
                    delta = columns[axis, here, :] - source[axis : axis + 1]
                    square = delta * delta if square is None else square + delta * delta
                square = jnp.maximum(square, 1e-30)
                distance = square * lax.rsqrt(square)
                scale = ROOT_THREE / LENGTH_SCALE
                decay = jnp.exp2(distance * (-scale * LOG2_E))
                kernel = (distance * (AMPLITUDE * scale) + AMPLITUDE) * decay
                kernels.append(kernel.astype(BF16))
            weight = jnp.concatenate(kernels, axis=1)
            source_values = jnp.concatenate([values[n] for n in ids], axis=0)
            part = jnp.dot(weight, source_values, preferred_element_type=F32)
            total = part if total is None else total + part
        sums[here, :] = total
        return carry

    lax.fori_loop(0, LEAVES, one_leaf, 0, unroll=4)
    for tile in range(LEAVES // 2):
        cols = slice(tile * LANES, tile * LANES + LANES)
        flipped = sums[cols, :].T
        out_ref[:, cols] = flipped[:64] + flipped[64:] + NUGGET * own_ref[:64, cols]


def final_kernel(own_ref, other_ref, far_ref, weights_ref, near_ref, basis_ref, transfer_ref, out_ref):
    first = jnp.full((32, LANES), lax.axis_index("gx") & 1, jnp.int32) == 0
    own = unfold(own_ref[...])
    other = unfold(other_ref[...])
    above = jnp.concatenate([jnp.where(first, own, other), jnp.where(first, other, own)], axis=0)
    down = far_ref[...] + multiply([(split_lanes(above), weights_ref[DOWN[0, 0]])])
    down = down[:, :HALF].astype(BF16)
    for block in range(4):
        cols = slice(block * 256, block * 256 + 256)
        leaf_down = jnp.dot(down, transfer_ref[:, cols], preferred_element_type=F32).astype(BF16)
        far = jnp.dot(leaf_down, block_diagonal(basis_ref[:, cols]), preferred_element_type=F32)
        out_ref[:, cols] = near_ref[:, cols] + far


def call(kernel, out_shape, in_specs, scratch_shapes, *operands, limit=40, cost=None):
    shapes = tuple(jax.ShapeDtypeStruct(shape, dtype) for shape, dtype in out_shape)
    return pl.pallas_call(
        kernel,
        out_shape=shapes,
        in_specs=in_specs,
        out_specs=(VMEM,) * len(shapes),
        scratch_shapes=scratch_shapes,
        cost_estimate=cost,
        compiler_params=pltpu.CompilerParams(vmem_limit_bytes=limit * 1024 * 1024),
    )(*operands)


def exchange(value, name, group):
    return lax.all_to_all(
        value, name, split_axis=0, concat_axis=0, axis_index_groups=[group], tiled=True
    )


def body(
    right_sides,
    points,
    leaf_basis,
    leaf_transfer,
    upper_transfer,
    coupling,
    near_leaves,
    admissible,
):
    width = right_sides.shape[1]
    lifted, send = call(
        up_kernel,
        [((2 ** len(SOURCE) * 2, 16, LANES), F32), ((72, width), F32)],
        [pl.BlockSpec(memory_space=pltpu.HBM)] * 5,
        [
            pltpu.VMEM((3, width), F32),
            pltpu.VMEM((64, width), BF16),
            pltpu.VMEM((64, width), BF16),
            pltpu.VMEM((64, 64), F32),
            pltpu.SemaphoreType.DMA((5,)),
        ],
        right_sides,
        points,
        leaf_basis,
        leaf_transfer,
        upper_transfer,
        limit=60,
    )
    swap = [(i, i ^ 1) for i in range(2**BITS_X)]
    from_x = lax.ppermute(send, "gx", swap)
    from_y = lax.ppermute(send, "gy", [(j, j ^ 1) for j in range(2**BITS_Y)])
    gathered = exchange(lifted, "gx", GROUP_X)
    (weights,) = call(
        weights_kernel,
        [((WEIGHTS, 128, LANES), BF16)],
        [VMEM] * 2 + [SMEM],
        [],
        upper_transfer,
        coupling,
        admissible.T,
    )
    partial, tie = call(
        tree_kernel,
        [((2 ** len(TARGET), 16, LANES), F32), ((8, LANES), F32)],
        [VMEM] * 2,
        [pltpu.VMEM((2 ** len(TARGET), 16, LANES), F32)],
        gathered,
        weights,
        cost=pl.CostEstimate(flops=4 * 10**9, bytes_accessed=12 * 10**6, transcendentals=0),
    )
    parts = exchange(partial, "gy", GROUP_Y)
    from_xy = lax.ppermute(from_y, "gx", swap)
    near, far = call(
        near_kernel,
        [((64, width), F32), ((64, LANES), F32)],
        [SMEM] + [VMEM] * 6,
        [
            pltpu.VMEM((4 * LEAVES, LEAF, LANES), BF16),
            pltpu.VMEM((4 * LEAVES, 8, LANES), F32),
            pltpu.VMEM((3, width, LANES), F32),
            pltpu.VMEM((width, LANES), F32),
        ],
        near_leaves,
        send,
        from_x,
        from_y,
        from_xy,
        weights,
        tie,
    )
    (own,) = call(sum_kernel, [((16, LANES), F32)], [VMEM, ANYWHERE], [], parts, far)
    other = lax.ppermute(own, "gx", swap)
    (product,) = call(
        final_kernel,
        [((64, width), F32)],
        [VMEM] * 7,
        [],
        own,
        other,
        far,
        weights,
        near,
        leaf_basis,
        leaf_transfer,
    )
    return product


def solution(mesh):
    split = P(None, ("gx", "gy"))
    in_specs = (split, split, split, split, P(), P(), P(("gx", "gy"), None), P())
    return jax.shard_map(body, mesh=mesh, in_specs=in_specs, out_specs=split, check_vma=False)
```

```python
import itertools

import jax
import jax.numpy as jnp
from jax import lax
from jax.experimental import pallas as pl
from jax.experimental.pallas import tpu as pltpu
from jax.sharding import PartitionSpec as P

ROOT_THREE = 1.7320508075688772
LENGTH_SCALE = 0.6
AMPLITUDE = 0.25
NUGGET = 0.5
LOG2_E = 1.4426950408889634
BITS_X = 4
BITS_Y = 5
DEVICES = 512
LEVELS = 9
LEAVES = 16
LEAF = 64
RANK = 64
HALF = 64
LANES = 128
F32 = jnp.float32
BF16 = jnp.bfloat16
NT = (((1,), (1,)), ((), ()))
VMEM = pl.BlockSpec(memory_space=pltpu.VMEM)
ANYWHERE = pl.BlockSpec(memory_space=pl.ANY)
SMEM = pl.BlockSpec(memory_space=pltpu.SMEM)


def places():
    listed = []
    for bit in range(max(BITS_X, BITS_Y)):
        if bit < BITS_X:
            listed.append(("x", bit))
        if bit < BITS_Y:
            listed.append(("y", bit))
    return listed


PLACES = places()
SOURCE = (2, 4, 6)
TARGET = (1, 3, 5, 7, 8)
GROUP_X = [z * 2 + core for z in (7, 3, 6, 2, 5, 1, 4, 0) for core in (1, 0)]
GROUP_Y = [x * 8 + y for y in (3, 7, 1, 5, 2, 6, 4, 0) for x in (1, 3, 2, 0)]

CLIMB, DOWN, CLIMB2, DOWN2, FAR = {}, {}, {}, {}, {}
ODD = (1, 3, 5)
_slots = itertools.count()
for _h in ODD:
    CLIMB[_h, 0] = next(_slots)
    for _side in range(2):
        DOWN[_h, _side] = next(_slots)
        CLIMB2[_h, _side] = next(_slots)
        DOWN2[_h, _side] = next(_slots)
DOWN[0, 0] = next(_slots)
for _h in range(LEVELS - 1):
    for _step in (1, 2, 3):
        FAR[_h, _step] = next(_slots)
WEIGHTS = next(_slots)


def above(chosen, h):
    return [place for place in chosen if place >= h]


def flipped(chosen, h, step):
    listed = above(chosen, h)
    return sum(1 << listed.index(h + p) for p in (0, 1) if step >> p & 1 and h + p in listed)


def low_lanes(rows):
    return lax.broadcasted_iota(jnp.int32, (rows, LANES), 1) < HALF


def split_lanes(value):
    high = value.astype(BF16).astype(F32)
    return jnp.where(low_lanes(value.shape[0]), high, value - high).astype(BF16)


def split_rows(wide):
    high = wide.astype(BF16)
    return jnp.concatenate([high, (wide - high.astype(F32)).astype(BF16)], axis=0)


def block_diagonal(basis):
    wide = basis.astype(F32)
    leaf = lax.broadcasted_iota(jnp.int32, wide.shape, 1) // LEAF
    return jnp.concatenate([jnp.where(leaf == l, wide, 0.0).astype(BF16) for l in range(4)], axis=0)


def up_kernel(
    right_ref,
    points_ref,
    basis_ref,
    transfer_ref,
    upper_ref,
    lifted_ref,
    send_ref,
    points_in,
    basis_in,
    transfer_in,
    upper_in,
    sems,
):
    copies = [
        pltpu.make_async_copy(right_ref, send_ref.at[pl.ds(0, 64)], sems.at[0]),
        pltpu.make_async_copy(basis_ref, basis_in, sems.at[1]),
        pltpu.make_async_copy(transfer_ref, transfer_in, sems.at[2]),
        pltpu.make_async_copy(points_ref, points_in, sems.at[3]),
        pltpu.make_async_copy(upper_ref.at[0, lax.axis_index("gx") & 1], upper_in, sems.at[4]),
    ]
    for copy in copies:
        copy.start()
    for copy in copies:
        copy.wait()
    total = None
    for block in range(4):
        cols = slice(block * 256, block * 256 + 256)
        rounded = send_ref[:64, cols].astype(BF16)
        leaf_coeff = lax.dot_general(
            rounded, block_diagonal(basis_in[:, cols]), NT, preferred_element_type=F32
        ).astype(BF16)
        transfer = transfer_in[:, cols]
        part = lax.dot_general(
            leaf_coeff,
            jnp.concatenate([transfer, transfer], axis=0),
            NT,
            preferred_element_type=F32,
        )
        total = part if total is None else total + part
    matrix = upper_in[...]
    wide = split_rows(jnp.concatenate([matrix, matrix], axis=1))
    lifted = multiply([(split_lanes(total), wide)])
    halves = [fold(lifted[:32]), fold(lifted[32:])]
    for target in range(lifted_ref.shape[0]):
        lifted_ref[target] = halves[GROUP_X[target] % 2]
    send_ref[64:67, :] = points_in[...]
    packed = fold(total)
    for tile in range(8):
        cols = slice(tile * LANES, tile * LANES + LANES)
        send_ref[67:71, cols] = packed[tile * 4 : tile * 4 + 4]
    send_ref[71:72, :] = jnp.zeros((1, LEAVES * LEAF), F32)


def as_nodes(value):
    return [value[row : row + 32] for row in range(0, value.shape[0], 32)]


def device_index():
    index_x = lax.axis_index("gx")
    return index_x, lax.axis_index("gy"), index_x & 1


def device_sides():
    index_x, index_y, _ = device_index()
    return [(index_x if axis == "x" else index_y) >> bit & 1 for axis, bit in PLACES]


def place_index(sides, listed):
    index = jnp.int32(0)
    for bit, place in enumerate(listed):
        index = index + sides[place] * 2**bit
    return index


def sent_coeff(ref):
    return jnp.concatenate(
        [ref[67:71, tile * LANES : tile * LANES + LANES] for tile in range(8)], axis=0
    )


def fold(value):
    rows = value.shape[0] // 2
    return jnp.where(low_lanes(rows), value[:rows], value[rows:])


def unfold(packed):
    low = low_lanes(packed.shape[0])
    rolled = pltpu.roll(packed, HALF, 1)
    return jnp.concatenate(
        [jnp.where(low, packed, rolled), jnp.where(low, rolled, packed)], axis=0
    )


def multiply(pairs):
    left = [piece for value, _ in pairs for piece in (value, value)]
    right = [piece for _, m in pairs for piece in (m[:64], m[:64], m[64:], m[64:])]
    return jnp.dot(
        jnp.concatenate(left, axis=1),
        jnp.concatenate(right, axis=0),
        preferred_element_type=F32,
    )


def weights_kernel(upper_ref, coupling_ref, admissible_ref, out_ref):
    sides = device_sides()
    code = place_index(sides, range(LEVELS))

    def plain(matrix):
        return jnp.concatenate([matrix, matrix], axis=1)

    def transposed(matrix):
        return jnp.concatenate([matrix, matrix], axis=0).T

    out_ref[DOWN[0, 0]] = split_rows(transposed(upper_ref[0, sides[0]]))
    for h in ODD:
        low = [upper_ref[h, sides[h] ^ side] for side in range(2)]
        high = [split_rows(plain(upper_ref[h + 1, sides[h + 1] ^ side])) for side in range(2)]
        own = split_lanes(plain(low[0]))
        both = [multiply([(own, matrix)]) for matrix in high]
        turned = multiply([(split_lanes(plain(low[1])), high[0])])
        out_ref[CLIMB[h, 0]] = split_rows(plain(low[0]))
        for side in range(2):
            out_ref[DOWN[h, side]] = split_rows(transposed(low[side]))
            out_ref[CLIMB2[h, side]] = split_rows(both[side])
        out_ref[DOWN2[h, 0]] = split_rows(transposed(both[0][:, :HALF]))
        out_ref[DOWN2[h, 1]] = split_rows(transposed(turned[:, :HALF]))
    for h in range(LEVELS - 1):
        first = 2 * DEVICES - 2 * DEVICES // 2**h
        for step in (1, 2, 3):
            turned = sum(1 << p for p in (0, 1) if step >> p & 1 and h + p in TARGET)
            target = (code >> h) ^ (turned if h else 0)
            here = target & 3
            there = here ^ step
            matrix = coupling_ref[h, jnp.abs(there - here) - 1]
            flag = admissible_ref[step - 1, first + target].astype(F32)
            upward = jnp.full((64, LANES), there - here, jnp.int32) > 0
            chosen = jnp.where(upward, transposed(matrix), plain(matrix))
            out_ref[FAR[h, step]] = split_rows(chosen * flag)


def tree_kernel(gathered_ref, weights_ref, out_ref, tie_ref, downs):
    sides = device_sides()
    own_source = place_index(sides, SOURCE)
    own_target = place_index(sides, TARGET)
    nodes = []
    for relative in range(2 ** len(SOURCE)):
        far_z = own_source ^ relative ^ 7
        first = (far_z & 3) * 4 + (far_z >> 2) * 2
        nodes.append(split_lanes(unfold(gathered_ref[first] + gathered_ref[first + 1])))
    levels = {1: nodes}
    for h in ODD:
        pairs = [
            (jnp.concatenate(nodes[bit::2], axis=0), weights_ref[CLIMB2[h, bit]])
            for bit in range(2)
        ]
        single = multiply([(jnp.concatenate(nodes, axis=0), weights_ref[CLIMB[h, 0]])])
        levels[h + 1] = as_nodes(split_lanes(single))
        nodes = as_nodes(split_lanes(multiply(pairs)))
        levels[h + 2] = nodes

    def coupled(h):
        terms = {}
        for step in (1, 2, 3):
            pair = levels[h][flipped(SOURCE, h, step)], weights_ref[FAR[h, step]]
            terms.setdefault(flipped(TARGET, h, step), []).append(pair)
        return {turned: multiply(pairs) for turned, pairs in terms.items()}

    far = coupled(LEVELS - 2)
    zero = jnp.zeros((32, LANES), F32)
    down = [far.get(n, zero) for n in range(2 ** len(above(TARGET, LEVELS - 2)))]
    for h in reversed(ODD):
        value = split_lanes(jnp.concatenate(down, axis=0))
        between = coupled(h + 1)
        extra = split_lanes(jnp.concatenate([between[0], between[1]], axis=0))
        parts = [as_nodes(multiply([(value, weights_ref[DOWN2[h, bit]])])) for bit in range(2)]
        down = [part for group in zip(*parts) for part in group]
        for bit in range(2):
            for parent, part in enumerate(as_nodes(multiply([(extra, weights_ref[DOWN[h, bit]])]))):
                down[2 * parent + bit] = down[2 * parent + bit] + part
        for turned, part in coupled(h).items():
            down[turned] = down[turned] + part
    for relative, part in enumerate(down):
        downs[relative] = fold(part)
    for member, node in enumerate(GROUP_Y):
        out_ref[member] = downs[own_target ^ node]
    tie_ref[...] = jnp.zeros_like(tie_ref)


def sum_kernel(parts_ref, tie_ref, out_ref):
    total = parts_ref[0]
    for source in range(1, parts_ref.shape[0]):
        total = total + parts_ref[source]
    out_ref[...] = total


def near_kernel(
    listed_ref,
    own_ref,
    x_ref,
    y_ref,
    xy_ref,
    weights_ref,
    tie_ref,
    out_ref,
    far_ref,
    values,
    rows,
    columns,
    sums,
):
    _, index_y, core = device_index()
    far_ref[...] = multiply(
        [
            (split_lanes(unfold(sent_coeff(ref))), weights_ref[FAR[0, step]])
            for step, ref in enumerate((x_ref, y_ref, xy_ref), 1)
        ]
    )
    low = low_lanes(8)
    for tile in range(LEAVES // 2):
        cols = slice(tile * LANES, tile * LANES + LANES)
        for axis in range(3):
            spread = jnp.broadcast_to(own_ref[64 + axis : 65 + axis, cols], (LANES, LANES))
            columns[axis, cols, :] = spread.T
    for block, ref in enumerate((own_ref, x_ref, y_ref, xy_ref)):
        for tile in range(LEAVES // 2):
            cols = slice(tile * LANES, tile * LANES + LANES)
            first = block * LEAVES + tile * 2
            values[first : first + 2] = split_rows(ref[:64, cols]).T.reshape(2, LEAF, LANES)
            point = ref[64:72, cols]
            rolled = pltpu.roll(point, HALF, 1)
            rows[first] = jnp.where(low, point, rolled)
            rows[first + 1] = jnp.where(low, rolled, point)

    def local(leaf, place):
        listed = listed_ref[leaf, place]
        owner = listed >> 4
        flip_x = (owner >> BITS_Y ^ core) & 1
        flip_y = (owner ^ index_y) & 1
        return (flip_x + 2 * flip_y) * LEAVES + (listed & LEAVES - 1)

    def one_leaf(leaf, carry):
        here = pl.ds(pl.multiple_of(leaf * LEAF, LEAF), LEAF)
        total = None
        for quad in range(3):
            ids = [local(leaf, quad * 4 + place) for place in range(4)]
            kernels = []
            for pair in range(2):
                source = jnp.where(low, rows[ids[pair * 2]], rows[ids[pair * 2 + 1]])
                square = None
                for axis in range(3):
                    delta = columns[axis, here, :] - source[axis : axis + 1]
                    square = delta * delta if square is None else square + delta * delta
                square = jnp.maximum(square, 1e-30)
                distance = square * lax.rsqrt(square)
                scale = ROOT_THREE / LENGTH_SCALE
                decay = jnp.exp2(distance * (-scale * LOG2_E))
                kernel = (distance * (AMPLITUDE * scale) + AMPLITUDE) * decay
                kernels.append(kernel.astype(BF16))
            weight = jnp.concatenate(kernels, axis=1)
            source_values = jnp.concatenate([values[n] for n in ids], axis=0)
            part = jnp.dot(weight, source_values, preferred_element_type=F32)
            total = part if total is None else total + part
        sums[here, :] = total
        return carry

    lax.fori_loop(0, LEAVES, one_leaf, 0, unroll=4)
    for tile in range(LEAVES // 2):
        cols = slice(tile * LANES, tile * LANES + LANES)
        flipped = sums[cols, :].T
        out_ref[:, cols] = flipped[:64] + flipped[64:] + NUGGET * own_ref[:64, cols]


def final_kernel(own_ref, other_ref, far_ref, weights_ref, near_ref, basis_ref, transfer_ref, out_ref):
    first = jnp.full((32, LANES), lax.axis_index("gx") & 1, jnp.int32) == 0
    own = unfold(own_ref[...])
    other = unfold(other_ref[...])
    above = jnp.concatenate([jnp.where(first, own, other), jnp.where(first, other, own)], axis=0)
    down = far_ref[...] + multiply([(split_lanes(above), weights_ref[DOWN[0, 0]])])
    down = down[:, :HALF].astype(BF16)
    for block in range(4):
        cols = slice(block * 256, block * 256 + 256)
        leaf_down = jnp.dot(down, transfer_ref[:, cols], preferred_element_type=F32).astype(BF16)
        far = jnp.dot(leaf_down, block_diagonal(basis_ref[:, cols]), preferred_element_type=F32)
        out_ref[:, cols] = near_ref[:, cols] + far


def call(kernel, out_shape, in_specs, scratch_shapes, *operands, limit=40, cost=None):
    shapes = tuple(jax.ShapeDtypeStruct(shape, dtype) for shape, dtype in out_shape)
    return pl.pallas_call(
        kernel,
        out_shape=shapes,
        in_specs=in_specs,
        out_specs=(VMEM,) * len(shapes),
        scratch_shapes=scratch_shapes,
        cost_estimate=cost,
        compiler_params=pltpu.CompilerParams(vmem_limit_bytes=limit * 1024 * 1024),
    )(*operands)


def exchange(value, name, group):
    return lax.all_to_all(
        value, name, split_axis=0, concat_axis=0, axis_index_groups=[group], tiled=True
    )


def body(
    right_sides,
    points,
    leaf_basis,
    leaf_transfer,
    upper_transfer,
    coupling,
    near_leaves,
    admissible,
):
    width = right_sides.shape[1]
    lifted, send = call(
        up_kernel,
        [((2 ** len(SOURCE) * 2, 16, LANES), F32), ((72, width), F32)],
        [pl.BlockSpec(memory_space=pltpu.HBM)] * 5,
        [
            pltpu.VMEM((3, width), F32),
            pltpu.VMEM((64, width), BF16),
            pltpu.VMEM((64, width), BF16),
            pltpu.VMEM((64, 64), F32),
            pltpu.SemaphoreType.DMA((5,)),
        ],
        right_sides,
        points,
        leaf_basis,
        leaf_transfer,
        upper_transfer,
        limit=60,
    )
    swap = [(i, i ^ 1) for i in range(2**BITS_X)]
    from_x = lax.ppermute(send, "gx", swap)
    from_y = lax.ppermute(send, "gy", [(j, j ^ 1) for j in range(2**BITS_Y)])
    gathered = exchange(lifted, "gx", GROUP_X)
    (weights,) = call(
        weights_kernel,
        [((WEIGHTS, 128, LANES), BF16)],
        [VMEM] * 2 + [SMEM],
        [],
        upper_transfer,
        coupling,
        admissible.T,
    )
    partial, tie = call(
        tree_kernel,
        [((2 ** len(TARGET), 16, LANES), F32), ((8, LANES), F32)],
        [VMEM] * 2,
        [pltpu.VMEM((2 ** len(TARGET), 16, LANES), F32)],
        gathered,
        weights,
        cost=pl.CostEstimate(flops=4 * 10**9, bytes_accessed=12 * 10**6, transcendentals=0),
    )
    parts = exchange(partial, "gy", GROUP_Y)
    from_xy = lax.ppermute(from_y, "gx", swap)
    near, far = call(
        near_kernel,
        [((64, width), F32), ((64, LANES), F32)],
        [SMEM] + [VMEM] * 6,
        [
            pltpu.VMEM((4 * LEAVES, LEAF, LANES), BF16),
            pltpu.VMEM((4 * LEAVES, 8, LANES), F32),
            pltpu.VMEM((3, width, LANES), F32),
            pltpu.VMEM((width, LANES), F32),
        ],
        near_leaves,
        send,
        from_x,
        from_y,
        from_xy,
        weights,
        tie,
    )
    (own,) = call(sum_kernel, [((16, LANES), F32)], [VMEM, ANYWHERE], [], parts, far)
    other = lax.ppermute(own, "gx", swap)
    (product,) = call(
        final_kernel,
        [((64, width), F32)],
        [VMEM] * 7,
        [],
        own,
        other,
        far,
        weights,
        near,
        leaf_basis,
        leaf_transfer,
    )
    return product


def solution(mesh):
    split = P(None, ("gx", "gy"))
    in_specs = (split, split, split, split, P(), P(), P(("gx", "gy"), None), P())
    return jax.shard_map(body, mesh=mesh, in_specs=in_specs, out_specs=split, check_vma=False)
```

```python
import itertools

import jax
import jax.numpy as jnp
from jax import lax
from jax.experimental import pallas as pl
from jax.experimental.pallas import tpu as pltpu
from jax.sharding import PartitionSpec as P

ROOT_THREE = 1.7320508075688772
LENGTH_SCALE = 0.6
AMPLITUDE = 0.25
NUGGET = 0.5
LOG2_E = 1.4426950408889634
BITS_X = 4
BITS_Y = 5
DEVICES = 512
LEVELS = 9
LEAVES = 16
LEAF = 64
RANK = 64
HALF = 64
LANES = 128
F32 = jnp.float32
BF16 = jnp.bfloat16
NT = (((1,), (1,)), ((), ()))
VMEM = pl.BlockSpec(memory_space=pltpu.VMEM)
ANYWHERE = pl.BlockSpec(memory_space=pl.ANY)
SMEM = pl.BlockSpec(memory_space=pltpu.SMEM)


def places():
    listed = []
    for bit in range(max(BITS_X, BITS_Y)):
        if bit < BITS_X:
            listed.append(("x", bit))
        if bit < BITS_Y:
            listed.append(("y", bit))
    return listed


PLACES = places()
SOURCE = (2, 4, 6)
TARGET = (1, 3, 5, 7, 8)
GROUP_X = [z * 2 + core for z in (7, 3, 6, 2, 5, 1, 4, 0) for core in (1, 0)]
GROUP_Y = [x * 8 + y for y in (3, 7, 1, 5, 2, 6, 4, 0) for x in (1, 3, 2, 0)]

CLIMB, DOWN, CLIMB2, DOWN2, FAR = {}, {}, {}, {}, {}
ODD = (1, 3, 5)
_slots = itertools.count()
for _h in ODD:
    CLIMB[_h, 0] = next(_slots)
    for _side in range(2):
        DOWN[_h, _side] = next(_slots)
        CLIMB2[_h, _side] = next(_slots)
        DOWN2[_h, _side] = next(_slots)
DOWN[0, 0] = next(_slots)
for _h in range(LEVELS - 1):
    for _step in (1, 2, 3):
        FAR[_h, _step] = next(_slots)
WEIGHTS = next(_slots)


def above(chosen, h):
    return [place for place in chosen if place >= h]


def flipped(chosen, h, step):
    listed = above(chosen, h)
    return sum(1 << listed.index(h + p) for p in (0, 1) if step >> p & 1 and h + p in listed)


def low_lanes(rows):
    return lax.broadcasted_iota(jnp.int32, (rows, LANES), 1) < HALF


def split_lanes(value):
    high = value.astype(BF16).astype(F32)
    return jnp.where(low_lanes(value.shape[0]), high, value - high).astype(BF16)


def split_rows(wide):
    high = wide.astype(BF16)
    return jnp.concatenate([high, (wide - high.astype(F32)).astype(BF16)], axis=0)


def block_diagonal(basis):
    wide = basis.astype(F32)
    leaf = lax.broadcasted_iota(jnp.int32, wide.shape, 1) // LEAF
    return jnp.concatenate([jnp.where(leaf == l, wide, 0.0).astype(BF16) for l in range(4)], axis=0)


def up_kernel(
    right_ref,
    points_ref,
    basis_ref,
    transfer_ref,
    upper_ref,
    lifted_ref,
    send_ref,
    points_in,
    basis_in,
    transfer_in,
    upper_in,
    sems,
):
    copies = [
        pltpu.make_async_copy(right_ref, send_ref.at[pl.ds(0, 64)], sems.at[0]),
        pltpu.make_async_copy(basis_ref, basis_in, sems.at[1]),
        pltpu.make_async_copy(transfer_ref, transfer_in, sems.at[2]),
        pltpu.make_async_copy(points_ref, points_in, sems.at[3]),
        pltpu.make_async_copy(upper_ref.at[0, lax.axis_index("gx") & 1], upper_in, sems.at[4]),
    ]
    for copy in copies:
        copy.start()
    copies[1].wait()
    diagonals = [block_diagonal(basis_in[:, b * 256 : b * 256 + 256]) for b in range(4)]
    copies[0].wait()
    leaf_coeffs = [
        lax.dot_general(
            send_ref[:64, b * 256 : b * 256 + 256].astype(BF16),
            diagonals[b],
            NT,
            preferred_element_type=F32,
        ).astype(BF16)
        for b in range(4)
    ]
    for copy in copies[2:]:
        copy.wait()
    total = None
    for block in range(4):
        transfer = transfer_in[:, block * 256 : block * 256 + 256]
        part = lax.dot_general(
            leaf_coeffs[block],
            jnp.concatenate([transfer, transfer], axis=0),
            NT,
            preferred_element_type=F32,
        )
        total = part if total is None else total + part
    matrix = upper_in[...]
    wide = split_rows(jnp.concatenate([matrix, matrix], axis=1))
    lifted = multiply([(split_lanes(total), wide)])
    halves = [fold(lifted[:32]), fold(lifted[32:])]
    for target in range(lifted_ref.shape[0]):
        lifted_ref[target] = halves[GROUP_X[target] % 2]
    send_ref[64:67, :] = points_in[...]
    packed = fold(total)
    for tile in range(8):
        cols = slice(tile * LANES, tile * LANES + LANES)
        send_ref[67:71, cols] = packed[tile * 4 : tile * 4 + 4]
    send_ref[71:72, :] = jnp.zeros((1, LEAVES * LEAF), F32)


def as_nodes(value):
    return [value[row : row + 32] for row in range(0, value.shape[0], 32)]


def device_index():
    index_x = lax.axis_index("gx")
    return index_x, lax.axis_index("gy"), index_x & 1


def device_sides():
    index_x, index_y, _ = device_index()
    return [(index_x if axis == "x" else index_y) >> bit & 1 for axis, bit in PLACES]


def place_index(sides, listed):
    index = jnp.int32(0)
    for bit, place in enumerate(listed):
        index = index + sides[place] * 2**bit
    return index


def sent_coeff(ref):
    return jnp.concatenate(
        [ref[67:71, tile * LANES : tile * LANES + LANES] for tile in range(8)], axis=0
    )


def fold(value):
    rows = value.shape[0] // 2
    return jnp.where(low_lanes(rows), value[:rows], value[rows:])


def unfold(packed):
    low = low_lanes(packed.shape[0])
    rolled = pltpu.roll(packed, HALF, 1)
    return jnp.concatenate(
        [jnp.where(low, packed, rolled), jnp.where(low, rolled, packed)], axis=0
    )


def multiply(pairs):
    left = [piece for value, _ in pairs for piece in (value, value)]
    right = [piece for _, m in pairs for piece in (m[:64], m[:64], m[64:], m[64:])]
    return jnp.dot(
        jnp.concatenate(left, axis=1),
        jnp.concatenate(right, axis=0),
        preferred_element_type=F32,
    )


def weights_kernel(upper_ref, coupling_ref, admissible_ref, out_ref):
    sides = device_sides()
    code = place_index(sides, range(LEVELS))

    def plain(matrix):
        return jnp.concatenate([matrix, matrix], axis=1)

    def transposed(matrix):
        return jnp.concatenate([matrix, matrix], axis=0).T

    out_ref[DOWN[0, 0]] = split_rows(transposed(upper_ref[0, sides[0]]))
    for h in ODD:
        low = [upper_ref[h, sides[h] ^ side] for side in range(2)]
        high = [split_rows(plain(upper_ref[h + 1, sides[h + 1] ^ side])) for side in range(2)]
        own = split_lanes(plain(low[0]))
        both = [multiply([(own, matrix)]) for matrix in high]
        turned = multiply([(split_lanes(plain(low[1])), high[0])])
        out_ref[CLIMB[h, 0]] = split_rows(plain(low[0]))
        for side in range(2):
            out_ref[DOWN[h, side]] = split_rows(transposed(low[side]))
            out_ref[CLIMB2[h, side]] = split_rows(both[side])
        out_ref[DOWN2[h, 0]] = split_rows(transposed(both[0][:, :HALF]))
        out_ref[DOWN2[h, 1]] = split_rows(transposed(turned[:, :HALF]))
    for h in range(LEVELS - 1):
        first = 2 * DEVICES - 2 * DEVICES // 2**h
        for step in (1, 2, 3):
            turned = sum(1 << p for p in (0, 1) if step >> p & 1 and h + p in TARGET)
            target = (code >> h) ^ (turned if h else 0)
            here = target & 3
            there = here ^ step
            matrix = coupling_ref[h, jnp.abs(there - here) - 1]
            flag = admissible_ref[step - 1, first + target].astype(F32)
            upward = jnp.full((64, LANES), there - here, jnp.int32) > 0
            chosen = jnp.where(upward, transposed(matrix), plain(matrix))
            out_ref[FAR[h, step]] = split_rows(chosen * flag)


def tree_kernel(gathered_ref, weights_ref, out_ref, tie_ref, downs):
    sides = device_sides()
    own_source = place_index(sides, SOURCE)
    own_target = place_index(sides, TARGET)
    nodes = []
    for relative in range(2 ** len(SOURCE)):
        far_z = own_source ^ relative ^ 7
        first = (far_z & 3) * 4 + (far_z >> 2) * 2
        nodes.append(split_lanes(unfold(gathered_ref[first] + gathered_ref[first + 1])))
    levels = {1: nodes}
    for h in ODD:
        pairs = [
            (jnp.concatenate(nodes[bit::2], axis=0), weights_ref[CLIMB2[h, bit]])
            for bit in range(2)
        ]
        single = multiply([(jnp.concatenate(nodes, axis=0), weights_ref[CLIMB[h, 0]])])
        levels[h + 1] = as_nodes(split_lanes(single))
        nodes = as_nodes(split_lanes(multiply(pairs)))
        levels[h + 2] = nodes

    def coupled(h):
        terms = {}
        for step in (1, 2, 3):
            pair = levels[h][flipped(SOURCE, h, step)], weights_ref[FAR[h, step]]
            terms.setdefault(flipped(TARGET, h, step), []).append(pair)
        return {turned: multiply(pairs) for turned, pairs in terms.items()}

    far = coupled(LEVELS - 2)
    zero = jnp.zeros((32, LANES), F32)
    down = [far.get(n, zero) for n in range(2 ** len(above(TARGET, LEVELS - 2)))]
    for h in reversed(ODD):
        value = split_lanes(jnp.concatenate(down, axis=0))
        between = coupled(h + 1)
        extra = split_lanes(jnp.concatenate([between[0], between[1]], axis=0))
        parts = [as_nodes(multiply([(value, weights_ref[DOWN2[h, bit]])])) for bit in range(2)]
        down = [part for group in zip(*parts) for part in group]
        for bit in range(2):
            for parent, part in enumerate(as_nodes(multiply([(extra, weights_ref[DOWN[h, bit]])]))):
                down[2 * parent + bit] = down[2 * parent + bit] + part
        for turned, part in coupled(h).items():
            down[turned] = down[turned] + part
    for relative, part in enumerate(down):
        downs[relative] = fold(part)
    for member, node in enumerate(GROUP_Y):
        out_ref[member] = downs[own_target ^ node]
    tie_ref[...] = jnp.zeros_like(tie_ref)


def sum_kernel(parts_ref, tie_ref, out_ref):
    total = parts_ref[0]
    for source in range(1, parts_ref.shape[0]):
        total = total + parts_ref[source]
    out_ref[...] = total


def near_kernel(
    listed_ref,
    own_ref,
    x_ref,
    y_ref,
    xy_ref,
    weights_ref,
    tie_ref,
    out_ref,
    far_ref,
    values,
    rows,
    columns,
    sums,
):
    _, index_y, core = device_index()
    far_ref[...] = multiply(
        [
            (split_lanes(unfold(sent_coeff(ref))), weights_ref[FAR[0, step]])
            for step, ref in enumerate((x_ref, y_ref, xy_ref), 1)
        ]
    )
    low = low_lanes(8)
    for tile in range(LEAVES // 2):
        cols = slice(tile * LANES, tile * LANES + LANES)
        for axis in range(3):
            spread = jnp.broadcast_to(own_ref[64 + axis : 65 + axis, cols], (LANES, LANES))
            columns[axis, cols, :] = spread.T
    for block, ref in enumerate((own_ref, x_ref, y_ref, xy_ref)):
        for tile in range(LEAVES // 2):
            cols = slice(tile * LANES, tile * LANES + LANES)
            first = block * LEAVES + tile * 2
            values[first : first + 2] = split_rows(ref[:64, cols]).T.reshape(2, LEAF, LANES)
            point = ref[64:72, cols]
            rolled = pltpu.roll(point, HALF, 1)
            rows[first] = jnp.where(low, point, rolled)
            rows[first + 1] = jnp.where(low, rolled, point)

    def local(leaf, place):
        listed = listed_ref[leaf, place]
        owner = listed >> 4
        flip_x = (owner >> BITS_Y ^ core) & 1
        flip_y = (owner ^ index_y) & 1
        return (flip_x + 2 * flip_y) * LEAVES + (listed & LEAVES - 1)

    def one_leaf(leaf, carry):
        here = pl.ds(pl.multiple_of(leaf * LEAF, LEAF), LEAF)
        total = None
        for quad in range(3):
            ids = [local(leaf, quad * 4 + place) for place in range(4)]
            kernels = []
            for pair in range(2):
                source = jnp.where(low, rows[ids[pair * 2]], rows[ids[pair * 2 + 1]])
                square = None
                for axis in range(3):
                    delta = columns[axis, here, :] - source[axis : axis + 1]
                    square = delta * delta if square is None else square + delta * delta
                square = jnp.maximum(square, 1e-30)
                distance = square * lax.rsqrt(square)
                scale = ROOT_THREE / LENGTH_SCALE
                decay = jnp.exp2(distance * (-scale * LOG2_E))
                kernel = (distance * (AMPLITUDE * scale) + AMPLITUDE) * decay
                kernels.append(kernel.astype(BF16))
            weight = jnp.concatenate(kernels, axis=1)
            source_values = jnp.concatenate([values[n] for n in ids], axis=0)
            part = jnp.dot(weight, source_values, preferred_element_type=F32)
            total = part if total is None else total + part
        sums[here, :] = total
        return carry

    lax.fori_loop(0, LEAVES, one_leaf, 0, unroll=8)
    for tile in range(LEAVES // 2):
        cols = slice(tile * LANES, tile * LANES + LANES)
        flipped = sums[cols, :].T
        out_ref[:, cols] = flipped[:64] + flipped[64:] + NUGGET * own_ref[:64, cols]


def final_kernel(own_ref, other_ref, far_ref, weights_ref, near_ref, basis_ref, transfer_ref, out_ref):
    first = jnp.full((32, LANES), lax.axis_index("gx") & 1, jnp.int32) == 0
    own = unfold(own_ref[...])
    other = unfold(other_ref[...])
    above = jnp.concatenate([jnp.where(first, own, other), jnp.where(first, other, own)], axis=0)
    down = far_ref[...] + multiply([(split_lanes(above), weights_ref[DOWN[0, 0]])])
    down = down[:, :HALF].astype(BF16)
    for block in range(4):
        cols = slice(block * 256, block * 256 + 256)
        leaf_down = jnp.dot(down, transfer_ref[:, cols], preferred_element_type=F32).astype(BF16)
        far = jnp.dot(leaf_down, block_diagonal(basis_ref[:, cols]), preferred_element_type=F32)
        out_ref[:, cols] = near_ref[:, cols] + far


def call(kernel, out_shape, in_specs, scratch_shapes, *operands, limit=40, cost=None):
    shapes = tuple(jax.ShapeDtypeStruct(shape, dtype) for shape, dtype in out_shape)
    return pl.pallas_call(
        kernel,
        out_shape=shapes,
        in_specs=in_specs,
        out_specs=(VMEM,) * len(shapes),
        scratch_shapes=scratch_shapes,
        cost_estimate=cost,
        compiler_params=pltpu.CompilerParams(vmem_limit_bytes=limit * 1024 * 1024),
    )(*operands)


def exchange(value, name, group):
    return lax.all_to_all(
        value, name, split_axis=0, concat_axis=0, axis_index_groups=[group], tiled=True
    )


def body(
    right_sides,
    points,
    leaf_basis,
    leaf_transfer,
    upper_transfer,
    coupling,
    near_leaves,
    admissible,
):
    width = right_sides.shape[1]
    lifted, send = call(
        up_kernel,
        [((2 ** len(SOURCE) * 2, 16, LANES), F32), ((72, width), F32)],
        [pl.BlockSpec(memory_space=pltpu.HBM)] * 5,
        [
            pltpu.VMEM((3, width), F32),
            pltpu.VMEM((64, width), BF16),
            pltpu.VMEM((64, width), BF16),
            pltpu.VMEM((64, 64), F32),
            pltpu.SemaphoreType.DMA((5,)),
        ],
        right_sides,
        points,
        leaf_basis,
        leaf_transfer,
        upper_transfer,
        limit=60,
    )
    swap = [(i, i ^ 1) for i in range(2**BITS_X)]
    from_x = lax.ppermute(send, "gx", swap)
    from_y = lax.ppermute(send, "gy", [(j, j ^ 1) for j in range(2**BITS_Y)])
    gathered = exchange(lifted, "gx", GROUP_X)
    (weights,) = call(
        weights_kernel,
        [((WEIGHTS, 128, LANES), BF16)],
        [VMEM] * 2 + [SMEM],
        [],
        upper_transfer,
        coupling,
        admissible.T,
    )
    partial, tie = call(
        tree_kernel,
        [((2 ** len(TARGET), 16, LANES), F32), ((8, LANES), F32)],
        [VMEM] * 2,
        [pltpu.VMEM((2 ** len(TARGET), 16, LANES), F32)],
        gathered,
        weights,
        cost=pl.CostEstimate(flops=4 * 10**9, bytes_accessed=12 * 10**6, transcendentals=0),
    )
    parts = exchange(partial, "gy", GROUP_Y)
    from_xy = lax.ppermute(from_y, "gx", swap)
    near, far = call(
        near_kernel,
        [((64, width), F32), ((64, LANES), F32)],
        [SMEM] + [VMEM] * 6,
        [
            pltpu.VMEM((4 * LEAVES, LEAF, LANES), BF16),
            pltpu.VMEM((4 * LEAVES, 8, LANES), F32),
            pltpu.VMEM((3, width, LANES), F32),
            pltpu.VMEM((width, LANES), F32),
        ],
        near_leaves,
        send,
        from_x,
        from_y,
        from_xy,
        weights,
        tie,
    )
    (own,) = call(sum_kernel, [((16, LANES), F32)], [VMEM, ANYWHERE], [], parts, far)
    other = lax.ppermute(own, "gx", swap)
    (product,) = call(
        final_kernel,
        [((64, width), F32)],
        [VMEM] * 7,
        [],
        own,
        other,
        far,
        weights,
        near,
        leaf_basis,
        leaf_transfer,
    )
    return product


def solution(mesh):
    split = P(None, ("gx", "gy"))
    in_specs = (split, split, split, split, P(), P(), P(("gx", "gy"), None), P())
    return jax.shard_map(body, mesh=mesh, in_specs=in_specs, out_specs=split, check_vma=False)
```

```python
import itertools

import jax
import jax.numpy as jnp
from jax import lax
from jax.experimental import pallas as pl
from jax.experimental.pallas import tpu as pltpu
from jax.sharding import PartitionSpec as P

ROOT_THREE = 1.7320508075688772
LENGTH_SCALE = 0.6
AMPLITUDE = 0.25
NUGGET = 0.5
LOG2_E = 1.4426950408889634
BITS_X = 4
BITS_Y = 5
DEVICES = 512
LEVELS = 9
LEAVES = 16
LEAF = 64
RANK = 64
HALF = 64
LANES = 128
F32 = jnp.float32
BF16 = jnp.bfloat16
NT = (((1,), (1,)), ((), ()))
VMEM = pl.BlockSpec(memory_space=pltpu.VMEM)
ANYWHERE = pl.BlockSpec(memory_space=pl.ANY)
SMEM = pl.BlockSpec(memory_space=pltpu.SMEM)


def places():
    listed = []
    for bit in range(max(BITS_X, BITS_Y)):
        if bit < BITS_X:
            listed.append(("x", bit))
        if bit < BITS_Y:
            listed.append(("y", bit))
    return listed


PLACES = places()
SOURCE = (2, 4, 6)
TARGET = (1, 3, 5, 7, 8)
GROUP_X = [z * 2 + core for z in (7, 3, 6, 2, 5, 1, 4, 0) for core in (1, 0)]
GROUP_Y = [x * 8 + y for y in (3, 7, 1, 5, 2, 6, 4, 0) for x in (1, 3, 2, 0)]

CLIMB, DOWN, CLIMB2, DOWN2, FAR = {}, {}, {}, {}, {}
ODD = (1, 3, 5)
_slots = itertools.count()
for _h in ODD:
    CLIMB[_h, 0] = next(_slots)
    for _side in range(2):
        DOWN[_h, _side] = next(_slots)
        CLIMB2[_h, _side] = next(_slots)
        DOWN2[_h, _side] = next(_slots)
DOWN[0, 0] = next(_slots)
for _h in range(LEVELS - 1):
    for _step in (1, 2, 3):
        FAR[_h, _step] = next(_slots)
WEIGHTS = next(_slots)


def above(chosen, h):
    return [place for place in chosen if place >= h]


def flipped(chosen, h, step):
    listed = above(chosen, h)
    return sum(1 << listed.index(h + p) for p in (0, 1) if step >> p & 1 and h + p in listed)


def low_lanes(rows):
    return lax.broadcasted_iota(jnp.int32, (rows, LANES), 1) < HALF


def split_lanes(value):
    high = value.astype(BF16).astype(F32)
    return jnp.where(low_lanes(value.shape[0]), high, value - high).astype(BF16)


def split_rows(wide):
    high = wide.astype(BF16)
    return jnp.concatenate([high, (wide - high.astype(F32)).astype(BF16)], axis=0)


def block_diagonal(basis):
    wide = basis.astype(F32)
    leaf = lax.broadcasted_iota(jnp.int32, wide.shape, 1) // LEAF
    return jnp.concatenate([jnp.where(leaf == l, wide, 0.0).astype(BF16) for l in range(4)], axis=0)


def up_kernel(
    right_ref,
    points_ref,
    basis_ref,
    transfer_ref,
    upper_ref,
    lifted_ref,
    send_ref,
    right_in,
    tail,
    lifted_out,
    points_in,
    basis_in,
    transfer_in,
    upper_in,
    sems,
):
    copies = [
        pltpu.make_async_copy(right_ref, right_in, sems.at[0]),
        pltpu.make_async_copy(basis_ref, basis_in, sems.at[1]),
        pltpu.make_async_copy(transfer_ref, transfer_in, sems.at[2]),
        pltpu.make_async_copy(points_ref, points_in, sems.at[3]),
        pltpu.make_async_copy(upper_ref.at[0, lax.axis_index("gx") & 1], upper_in, sems.at[4]),
    ]
    for copy in copies:
        copy.start()
    straight = pltpu.make_async_copy(right_ref, send_ref.at[pl.ds(0, 64)], sems.at[5])
    straight.start()
    copies[1].wait()
    diagonals = [block_diagonal(basis_in[:, b * 256 : b * 256 + 256]) for b in range(4)]
    copies[0].wait()
    leaf_coeffs = [
        lax.dot_general(
            right_in[:, b * 256 : b * 256 + 256].astype(BF16),
            diagonals[b],
            NT,
            preferred_element_type=F32,
        ).astype(BF16)
        for b in range(4)
    ]
    for copy in copies[2:]:
        copy.wait()
    total = None
    for block in range(4):
        transfer = transfer_in[:, block * 256 : block * 256 + 256]
        part = lax.dot_general(
            leaf_coeffs[block],
            jnp.concatenate([transfer, transfer], axis=0),
            NT,
            preferred_element_type=F32,
        )
        total = part if total is None else total + part
    matrix = upper_in[...]
    wide = split_rows(jnp.concatenate([matrix, matrix], axis=1))
    lifted = multiply([(split_lanes(total), wide)])
    halves = [fold(lifted[:32]), fold(lifted[32:])]
    for target in range(lifted_out.shape[0]):
        lifted_out[target] = halves[GROUP_X[target] % 2]
    lifted_copy = pltpu.make_async_copy(lifted_out, lifted_ref, sems.at[6])
    lifted_copy.start()
    tail[0:3, :] = points_in[...]
    packed = fold(total)
    for tile in range(8):
        cols = slice(tile * LANES, tile * LANES + LANES)
        tail[3:7, cols] = packed[tile * 4 : tile * 4 + 4]
    tail[7:8, :] = jnp.zeros((1, LEAVES * LEAF), F32)
    tail_copy = pltpu.make_async_copy(tail, send_ref.at[pl.ds(64, 8)], sems.at[7])
    tail_copy.start()
    for copy in (straight, lifted_copy, tail_copy):
        copy.wait()


def as_nodes(value):
    return [value[row : row + 32] for row in range(0, value.shape[0], 32)]


def device_index():
    index_x = lax.axis_index("gx")
    return index_x, lax.axis_index("gy"), index_x & 1


def device_sides():
    index_x, index_y, _ = device_index()
    return [(index_x if axis == "x" else index_y) >> bit & 1 for axis, bit in PLACES]


def place_index(sides, listed):
    index = jnp.int32(0)
    for bit, place in enumerate(listed):
        index = index + sides[place] * 2**bit
    return index


def sent_coeff(ref):
    return jnp.concatenate(
        [ref[67:71, tile * LANES : tile * LANES + LANES] for tile in range(8)], axis=0
    )


def fold(value):
    rows = value.shape[0] // 2
    return jnp.where(low_lanes(rows), value[:rows], value[rows:])


def unfold(packed):
    low = low_lanes(packed.shape[0])
    rolled = pltpu.roll(packed, HALF, 1)
    return jnp.concatenate(
        [jnp.where(low, packed, rolled), jnp.where(low, rolled, packed)], axis=0
    )


def multiply(pairs):
    left = [piece for value, _ in pairs for piece in (value, value)]
    right = [piece for _, m in pairs for piece in (m[:64], m[:64], m[64:], m[64:])]
    return jnp.dot(
        jnp.concatenate(left, axis=1),
        jnp.concatenate(right, axis=0),
        preferred_element_type=F32,
    )


def weights_kernel(upper_ref, coupling_ref, admissible_ref, out_ref):
    sides = device_sides()
    code = place_index(sides, range(LEVELS))

    def plain(matrix):
        return jnp.concatenate([matrix, matrix], axis=1)

    def transposed(matrix):
        return jnp.concatenate([matrix, matrix], axis=0).T

    out_ref[DOWN[0, 0]] = split_rows(transposed(upper_ref[0, sides[0]]))
    for h in ODD:
        low = [upper_ref[h, sides[h] ^ side] for side in range(2)]
        high = [split_rows(plain(upper_ref[h + 1, sides[h + 1] ^ side])) for side in range(2)]
        own = split_lanes(plain(low[0]))
        both = [multiply([(own, matrix)]) for matrix in high]
        turned = multiply([(split_lanes(plain(low[1])), high[0])])
        out_ref[CLIMB[h, 0]] = split_rows(plain(low[0]))
        for side in range(2):
            out_ref[DOWN[h, side]] = split_rows(transposed(low[side]))
            out_ref[CLIMB2[h, side]] = split_rows(both[side])
        out_ref[DOWN2[h, 0]] = split_rows(transposed(both[0][:, :HALF]))
        out_ref[DOWN2[h, 1]] = split_rows(transposed(turned[:, :HALF]))
    for h in range(LEVELS - 1):
        first = 2 * DEVICES - 2 * DEVICES // 2**h
        for step in (1, 2, 3):
            turned = sum(1 << p for p in (0, 1) if step >> p & 1 and h + p in TARGET)
            target = (code >> h) ^ (turned if h else 0)
            here = target & 3
            there = here ^ step
            matrix = coupling_ref[h, jnp.abs(there - here) - 1]
            flag = admissible_ref[step - 1, first + target].astype(F32)
            upward = jnp.full((64, LANES), there - here, jnp.int32) > 0
            chosen = jnp.where(upward, transposed(matrix), plain(matrix))
            out_ref[FAR[h, step]] = split_rows(chosen * flag)


def tree_kernel(gathered_ref, weights_ref, out_ref, tie_ref, downs):
    sides = device_sides()
    own_source = place_index(sides, SOURCE)
    own_target = place_index(sides, TARGET)
    nodes = []
    for relative in range(2 ** len(SOURCE)):
        far_z = own_source ^ relative ^ 7
        first = (far_z & 3) * 4 + (far_z >> 2) * 2
        nodes.append(split_lanes(unfold(gathered_ref[first] + gathered_ref[first + 1])))
    levels = {1: nodes}
    for h in ODD:
        pairs = [
            (jnp.concatenate(nodes[bit::2], axis=0), weights_ref[CLIMB2[h, bit]])
            for bit in range(2)
        ]
        single = multiply([(jnp.concatenate(nodes, axis=0), weights_ref[CLIMB[h, 0]])])
        levels[h + 1] = as_nodes(split_lanes(single))
        nodes = as_nodes(split_lanes(multiply(pairs)))
        levels[h + 2] = nodes

    def coupled(h):
        terms = {}
        for step in (1, 2, 3):
            pair = levels[h][flipped(SOURCE, h, step)], weights_ref[FAR[h, step]]
            terms.setdefault(flipped(TARGET, h, step), []).append(pair)
        return {turned: multiply(pairs) for turned, pairs in terms.items()}

    far = coupled(LEVELS - 2)
    zero = jnp.zeros((32, LANES), F32)
    down = [far.get(n, zero) for n in range(2 ** len(above(TARGET, LEVELS - 2)))]
    for h in reversed(ODD):
        value = split_lanes(jnp.concatenate(down, axis=0))
        between = coupled(h + 1)
        extra = split_lanes(jnp.concatenate([between[0], between[1]], axis=0))
        parts = [as_nodes(multiply([(value, weights_ref[DOWN2[h, bit]])])) for bit in range(2)]
        down = [part for group in zip(*parts) for part in group]
        for bit in range(2):
            for parent, part in enumerate(as_nodes(multiply([(extra, weights_ref[DOWN[h, bit]])]))):
                down[2 * parent + bit] = down[2 * parent + bit] + part
        for turned, part in coupled(h).items():
            down[turned] = down[turned] + part
    for relative, part in enumerate(down):
        downs[relative] = fold(part)
    for member, node in enumerate(GROUP_Y):
        out_ref[member] = downs[own_target ^ node]
    tie_ref[...] = jnp.zeros_like(tie_ref)


def sum_kernel(parts_ref, tie_ref, out_ref):
    total = parts_ref[0]
    for source in range(1, parts_ref.shape[0]):
        total = total + parts_ref[source]
    out_ref[...] = total


def near_kernel(
    listed_ref,
    own_ref,
    x_ref,
    y_ref,
    xy_ref,
    weights_ref,
    tie_ref,
    out_ref,
    far_ref,
    values,
    rows,
    columns,
    sums,
):
    _, index_y, core = device_index()
    far_ref[...] = multiply(
        [
            (split_lanes(unfold(sent_coeff(ref))), weights_ref[FAR[0, step]])
            for step, ref in enumerate((x_ref, y_ref, xy_ref), 1)
        ]
    )
    low = low_lanes(8)
    for tile in range(LEAVES // 2):
        cols = slice(tile * LANES, tile * LANES + LANES)
        for axis in range(3):
            spread = jnp.broadcast_to(own_ref[64 + axis : 65 + axis, cols], (LANES, LANES))
            columns[axis, cols, :] = spread.T
    for block, ref in enumerate((own_ref, x_ref, y_ref, xy_ref)):
        for tile in range(LEAVES // 2):
            cols = slice(tile * LANES, tile * LANES + LANES)
            first = block * LEAVES + tile * 2
            values[first : first + 2] = split_rows(ref[:64, cols]).T.reshape(2, LEAF, LANES)
            point = ref[64:72, cols]
            rolled = pltpu.roll(point, HALF, 1)
            rows[first] = jnp.where(low, point, rolled)
            rows[first + 1] = jnp.where(low, rolled, point)

    def local(leaf, place):
        listed = listed_ref[leaf, place]
        owner = listed >> 4
        flip_x = (owner >> BITS_Y ^ core) & 1
        flip_y = (owner ^ index_y) & 1
        return (flip_x + 2 * flip_y) * LEAVES + (listed & LEAVES - 1)

    def one_leaf(leaf, carry):
        here = pl.ds(pl.multiple_of(leaf * LEAF, LEAF), LEAF)
        total = None
        for quad in range(3):
            ids = [local(leaf, quad * 4 + place) for place in range(4)]
            kernels = []
            for pair in range(2):
                source = jnp.where(low, rows[ids[pair * 2]], rows[ids[pair * 2 + 1]])
                square = None
                for axis in range(3):
                    delta = columns[axis, here, :] - source[axis : axis + 1]
                    square = delta * delta if square is None else square + delta * delta
                square = jnp.maximum(square, 1e-30)
                distance = square * lax.rsqrt(square)
                scale = ROOT_THREE / LENGTH_SCALE
                decay = jnp.exp2(distance * (-scale * LOG2_E))
                kernel = (distance * (AMPLITUDE * scale) + AMPLITUDE) * decay
                kernels.append(kernel.astype(BF16))
            weight = jnp.concatenate(kernels, axis=1)
            source_values = jnp.concatenate([values[n] for n in ids], axis=0)
            part = jnp.dot(weight, source_values, preferred_element_type=F32)
            total = part if total is None else total + part
        sums[here, :] = total
        return carry

    lax.fori_loop(0, LEAVES, one_leaf, 0, unroll=8)
    for tile in range(LEAVES // 2):
        cols = slice(tile * LANES, tile * LANES + LANES)
        flipped = sums[cols, :].T
        out_ref[:, cols] = flipped[:64] + flipped[64:] + NUGGET * own_ref[:64, cols]


def final_kernel(own_ref, other_ref, far_ref, weights_ref, near_ref, basis_ref, transfer_ref, out_ref):
    first = jnp.full((32, LANES), lax.axis_index("gx") & 1, jnp.int32) == 0
    own = unfold(own_ref[...])
    other = unfold(other_ref[...])
    above = jnp.concatenate([jnp.where(first, own, other), jnp.where(first, other, own)], axis=0)
    down = far_ref[...] + multiply([(split_lanes(above), weights_ref[DOWN[0, 0]])])
    down = down[:, :HALF].astype(BF16)
    for block in range(4):
        cols = slice(block * 256, block * 256 + 256)
        leaf_down = jnp.dot(down, transfer_ref[:, cols], preferred_element_type=F32).astype(BF16)
        far = jnp.dot(leaf_down, block_diagonal(basis_ref[:, cols]), preferred_element_type=F32)
        out_ref[:, cols] = near_ref[:, cols] + far


def call(kernel, out_shape, in_specs, scratch_shapes, *operands, limit=40, cost=None, out=VMEM):
    shapes = tuple(jax.ShapeDtypeStruct(shape, dtype) for shape, dtype in out_shape)
    return pl.pallas_call(
        kernel,
        out_shape=shapes,
        in_specs=in_specs,
        out_specs=(out,) * len(shapes),
        scratch_shapes=scratch_shapes,
        cost_estimate=cost,
        compiler_params=pltpu.CompilerParams(vmem_limit_bytes=limit * 1024 * 1024),
    )(*operands)


def exchange(value, name, group):
    return lax.all_to_all(
        value, name, split_axis=0, concat_axis=0, axis_index_groups=[group], tiled=True
    )


def body(
    right_sides,
    points,
    leaf_basis,
    leaf_transfer,
    upper_transfer,
    coupling,
    near_leaves,
    admissible,
):
    width = right_sides.shape[1]
    lifted, send = call(
        up_kernel,
        [((2 ** len(SOURCE) * 2, 16, LANES), F32), ((72, width), F32)],
        [pl.BlockSpec(memory_space=pltpu.HBM)] * 5,
        [
            pltpu.VMEM((64, width), F32),
            pltpu.VMEM((8, width), F32),
            pltpu.VMEM((2 ** len(SOURCE) * 2, 16, LANES), F32),
            pltpu.VMEM((3, width), F32),
            pltpu.VMEM((64, width), BF16),
            pltpu.VMEM((64, width), BF16),
            pltpu.VMEM((64, 64), F32),
            pltpu.SemaphoreType.DMA((8,)),
        ],
        right_sides,
        points,
        leaf_basis,
        leaf_transfer,
        upper_transfer,
        limit=60,
        out=pl.BlockSpec(memory_space=pltpu.HBM),
    )
    swap = [(i, i ^ 1) for i in range(2**BITS_X)]
    from_x = lax.ppermute(send, "gx", swap)
    from_y = lax.ppermute(send, "gy", [(j, j ^ 1) for j in range(2**BITS_Y)])
    gathered = exchange(lifted, "gx", GROUP_X)
    (weights,) = call(
        weights_kernel,
        [((WEIGHTS, 128, LANES), BF16)],
        [VMEM] * 2 + [SMEM],
        [],
        upper_transfer,
        coupling,
        admissible.T,
    )
    partial, tie = call(
        tree_kernel,
        [((2 ** len(TARGET), 16, LANES), F32), ((8, LANES), F32)],
        [VMEM] * 2,
        [pltpu.VMEM((2 ** len(TARGET), 16, LANES), F32)],
        gathered,
        weights,
        cost=pl.CostEstimate(flops=4 * 10**9, bytes_accessed=12 * 10**6, transcendentals=0),
    )
    parts = exchange(partial, "gy", GROUP_Y)
    from_xy = lax.ppermute(from_y, "gx", swap)
    near, far = call(
        near_kernel,
        [((64, width), F32), ((64, LANES), F32)],
        [SMEM] + [VMEM] * 6,
        [
            pltpu.VMEM((4 * LEAVES, LEAF, LANES), BF16),
            pltpu.VMEM((4 * LEAVES, 8, LANES), F32),
            pltpu.VMEM((3, width, LANES), F32),
            pltpu.VMEM((width, LANES), F32),
        ],
        near_leaves,
        send,
        from_x,
        from_y,
        from_xy,
        weights,
        tie,
    )
    (own,) = call(sum_kernel, [((16, LANES), F32)], [VMEM, ANYWHERE], [], parts, far)
    other = lax.ppermute(own, "gx", swap)
    (product,) = call(
        final_kernel,
        [((64, width), F32)],
        [VMEM] * 7,
        [],
        own,
        other,
        far,
        weights,
        near,
        leaf_basis,
        leaf_transfer,
    )
    return product


def solution(mesh):
    split = P(None, ("gx", "gy"))
    in_specs = (split, split, split, split, P(), P(), P(("gx", "gy"), None), P())
    return jax.shard_map(body, mesh=mesh, in_specs=in_specs, out_specs=split, check_vma=False)
```

```python
import itertools

import jax
import jax.numpy as jnp
from jax import lax
from jax.experimental import pallas as pl
from jax.experimental.pallas import tpu as pltpu
from jax.sharding import PartitionSpec as P

ROOT_THREE = 1.7320508075688772
LENGTH_SCALE = 0.6
AMPLITUDE = 0.25
NUGGET = 0.5
LOG2_E = 1.4426950408889634
BITS_X = 4
BITS_Y = 5
DEVICES = 512
LEVELS = 9
LEAVES = 16
LEAF = 64
RANK = 64
HALF = 64
LANES = 128
F32 = jnp.float32
BF16 = jnp.bfloat16
NT = (((1,), (1,)), ((), ()))
VMEM = pl.BlockSpec(memory_space=pltpu.VMEM)
ANYWHERE = pl.BlockSpec(memory_space=pl.ANY)
SMEM = pl.BlockSpec(memory_space=pltpu.SMEM)


def places():
    listed = []
    for bit in range(max(BITS_X, BITS_Y)):
        if bit < BITS_X:
            listed.append(("x", bit))
        if bit < BITS_Y:
            listed.append(("y", bit))
    return listed


PLACES = places()
SOURCE = (2, 4, 6)
TARGET = (1, 3, 5, 7, 8)
GROUP_X = [z * 2 + core for z in (7, 3, 6, 2, 5, 1, 4, 0) for core in (1, 0)]
GROUP_Y = [x * 8 + y for y in (3, 7, 1, 5, 2, 6, 4, 0) for x in (1, 3, 2, 0)]

CLIMB, DOWN, CLIMB2, DOWN2, FAR = {}, {}, {}, {}, {}
ODD = (1, 3, 5)
_slots = itertools.count()
for _h in ODD:
    CLIMB[_h, 0] = next(_slots)
    for _side in range(2):
        DOWN[_h, _side] = next(_slots)
        CLIMB2[_h, _side] = next(_slots)
        DOWN2[_h, _side] = next(_slots)
DOWN[0, 0] = next(_slots)
for _h in range(LEVELS - 1):
    for _step in (1, 2, 3):
        FAR[_h, _step] = next(_slots)
WEIGHTS = next(_slots)


def above(chosen, h):
    return [place for place in chosen if place >= h]


def flipped(chosen, h, step):
    listed = above(chosen, h)
    return sum(1 << listed.index(h + p) for p in (0, 1) if step >> p & 1 and h + p in listed)


def low_lanes(rows):
    return lax.broadcasted_iota(jnp.int32, (rows, LANES), 1) < HALF


def split_lanes(value):
    high = value.astype(BF16).astype(F32)
    return jnp.where(low_lanes(value.shape[0]), high, value - high).astype(BF16)


def split_rows(wide):
    high = wide.astype(BF16)
    return jnp.concatenate([high, (wide - high.astype(F32)).astype(BF16)], axis=0)


def block_diagonal(basis):
    wide = basis.astype(F32)
    leaf = lax.broadcasted_iota(jnp.int32, wide.shape, 1) // LEAF
    return jnp.concatenate([jnp.where(leaf == l, wide, 0.0).astype(BF16) for l in range(4)], axis=0)


def up_kernel(
    right_ref,
    points_ref,
    basis_ref,
    transfer_ref,
    upper_ref,
    lifted_ref,
    send_ref,
    right_in,
    tail,
    lifted_out,
    points_in,
    basis_in,
    transfer_in,
    upper_in,
    sems,
):
    copies = [
        pltpu.make_async_copy(right_ref, right_in, sems.at[0]),
        pltpu.make_async_copy(basis_ref, basis_in, sems.at[1]),
        pltpu.make_async_copy(transfer_ref, transfer_in, sems.at[2]),
        pltpu.make_async_copy(points_ref, points_in, sems.at[3]),
        pltpu.make_async_copy(upper_ref.at[0, lax.axis_index("gx") & 1], upper_in, sems.at[4]),
    ]
    for copy in copies:
        copy.start()
    copies[1].wait()
    diagonals = [block_diagonal(basis_in[:, b * 256 : b * 256 + 256]) for b in range(4)]
    copies[0].wait()
    straight = pltpu.make_async_copy(right_in, send_ref.at[pl.ds(0, 64)], sems.at[5])
    straight.start()
    leaf_coeffs = [
        lax.dot_general(
            right_in[:, b * 256 : b * 256 + 256].astype(BF16),
            diagonals[b],
            NT,
            preferred_element_type=F32,
        ).astype(BF16)
        for b in range(4)
    ]
    for copy in copies[2:]:
        copy.wait()
    total = None
    for block in range(4):
        transfer = transfer_in[:, block * 256 : block * 256 + 256]
        part = lax.dot_general(
            leaf_coeffs[block],
            jnp.concatenate([transfer, transfer], axis=0),
            NT,
            preferred_element_type=F32,
        )
        total = part if total is None else total + part
    matrix = upper_in[...]
    wide = split_rows(jnp.concatenate([matrix, matrix], axis=1))
    lifted = multiply([(split_lanes(total), wide)])
    halves = [fold(lifted[:32]), fold(lifted[32:])]
    for target in range(lifted_out.shape[0]):
        lifted_out[target] = halves[GROUP_X[target] % 2]
    lifted_copy = pltpu.make_async_copy(lifted_out, lifted_ref, sems.at[6])
    lifted_copy.start()
    tail[0:3, :] = points_in[...]
    packed = fold(total)
    for tile in range(8):
        cols = slice(tile * LANES, tile * LANES + LANES)
        tail[3:7, cols] = packed[tile * 4 : tile * 4 + 4]
    tail[7:8, :] = jnp.zeros((1, LEAVES * LEAF), F32)
    tail_copy = pltpu.make_async_copy(tail, send_ref.at[pl.ds(64, 8)], sems.at[7])
    tail_copy.start()
    for copy in (straight, lifted_copy, tail_copy):
        copy.wait()


def as_nodes(value):
    return [value[row : row + 32] for row in range(0, value.shape[0], 32)]


def device_index():
    index_x = lax.axis_index("gx")
    return index_x, lax.axis_index("gy"), index_x & 1


def device_sides():
    index_x, index_y, _ = device_index()
    return [(index_x if axis == "x" else index_y) >> bit & 1 for axis, bit in PLACES]


def place_index(sides, listed):
    index = jnp.int32(0)
    for bit, place in enumerate(listed):
        index = index + sides[place] * 2**bit
    return index


def sent_coeff(ref):
    return jnp.concatenate(
        [ref[67:71, tile * LANES : tile * LANES + LANES] for tile in range(8)], axis=0
    )


def fold(value):
    rows = value.shape[0] // 2
    return jnp.where(low_lanes(rows), value[:rows], value[rows:])


def unfold(packed):
    low = low_lanes(packed.shape[0])
    rolled = pltpu.roll(packed, HALF, 1)
    return jnp.concatenate(
        [jnp.where(low, packed, rolled), jnp.where(low, rolled, packed)], axis=0
    )


def multiply(pairs):
    left = [piece for value, _ in pairs for piece in (value, value)]
    right = [piece for _, m in pairs for piece in (m[:64], m[:64], m[64:], m[64:])]
    return jnp.dot(
        jnp.concatenate(left, axis=1),
        jnp.concatenate(right, axis=0),
        preferred_element_type=F32,
    )


def weights_kernel(upper_ref, coupling_ref, admissible_ref, out_ref):
    sides = device_sides()
    code = place_index(sides, range(LEVELS))

    def plain(matrix):
        return jnp.concatenate([matrix, matrix], axis=1)

    def transposed(matrix):
        return jnp.concatenate([matrix, matrix], axis=0).T

    out_ref[DOWN[0, 0]] = split_rows(transposed(upper_ref[0, sides[0]]))
    for h in ODD:
        low = [upper_ref[h, sides[h] ^ side] for side in range(2)]
        high = [split_rows(plain(upper_ref[h + 1, sides[h + 1] ^ side])) for side in range(2)]
        own = split_lanes(plain(low[0]))
        both = [multiply([(own, matrix)]) for matrix in high]
        turned = multiply([(split_lanes(plain(low[1])), high[0])])
        out_ref[CLIMB[h, 0]] = split_rows(plain(low[0]))
        for side in range(2):
            out_ref[DOWN[h, side]] = split_rows(transposed(low[side]))
            out_ref[CLIMB2[h, side]] = split_rows(both[side])
        out_ref[DOWN2[h, 0]] = split_rows(transposed(both[0][:, :HALF]))
        out_ref[DOWN2[h, 1]] = split_rows(transposed(turned[:, :HALF]))
    for h in range(LEVELS - 1):
        first = 2 * DEVICES - 2 * DEVICES // 2**h
        for step in (1, 2, 3):
            turned = sum(1 << p for p in (0, 1) if step >> p & 1 and h + p in TARGET)
            target = (code >> h) ^ (turned if h else 0)
            here = target & 3
            there = here ^ step
            matrix = coupling_ref[h, jnp.abs(there - here) - 1]
            flag = admissible_ref[step - 1, first + target].astype(F32)
            upward = jnp.full((64, LANES), there - here, jnp.int32) > 0
            chosen = jnp.where(upward, transposed(matrix), plain(matrix))
            out_ref[FAR[h, step]] = split_rows(chosen * flag)


def tree_kernel(gathered_ref, weights_ref, out_ref, tie_ref, downs):
    sides = device_sides()
    own_source = place_index(sides, SOURCE)
    own_target = place_index(sides, TARGET)
    nodes = []
    for relative in range(2 ** len(SOURCE)):
        far_z = own_source ^ relative ^ 7
        first = (far_z & 3) * 4 + (far_z >> 2) * 2
        nodes.append(split_lanes(unfold(gathered_ref[first] + gathered_ref[first + 1])))
    levels = {1: nodes}
    for h in ODD:
        pairs = [
            (jnp.concatenate(nodes[bit::2], axis=0), weights_ref[CLIMB2[h, bit]])
            for bit in range(2)
        ]
        single = multiply([(jnp.concatenate(nodes, axis=0), weights_ref[CLIMB[h, 0]])])
        levels[h + 1] = as_nodes(split_lanes(single))
        nodes = as_nodes(split_lanes(multiply(pairs)))
        levels[h + 2] = nodes

    def coupled(h):
        terms = {}
        for step in (1, 2, 3):
            pair = levels[h][flipped(SOURCE, h, step)], weights_ref[FAR[h, step]]
            terms.setdefault(flipped(TARGET, h, step), []).append(pair)
        return {turned: multiply(pairs) for turned, pairs in terms.items()}

    far = coupled(LEVELS - 2)
    zero = jnp.zeros((32, LANES), F32)
    down = [far.get(n, zero) for n in range(2 ** len(above(TARGET, LEVELS - 2)))]
    for h in reversed(ODD):
        value = split_lanes(jnp.concatenate(down, axis=0))
        between = coupled(h + 1)
        extra = split_lanes(jnp.concatenate([between[0], between[1]], axis=0))
        parts = [as_nodes(multiply([(value, weights_ref[DOWN2[h, bit]])])) for bit in range(2)]
        down = [part for group in zip(*parts) for part in group]
        for bit in range(2):
            for parent, part in enumerate(as_nodes(multiply([(extra, weights_ref[DOWN[h, bit]])]))):
                down[2 * parent + bit] = down[2 * parent + bit] + part
        for turned, part in coupled(h).items():
            down[turned] = down[turned] + part
    for relative, part in enumerate(down):
        downs[relative] = fold(part)
    for member, node in enumerate(GROUP_Y):
        out_ref[member] = downs[own_target ^ node]
    tie_ref[...] = jnp.zeros_like(tie_ref)


def sum_kernel(parts_ref, tie_ref, out_ref):
    total = parts_ref[0]
    for source in range(1, parts_ref.shape[0]):
        total = total + parts_ref[source]
    out_ref[...] = total


def near_kernel(
    listed_ref,
    own_ref,
    x_ref,
    y_ref,
    xy_ref,
    weights_ref,
    tie_ref,
    out_ref,
    far_ref,
    values,
    rows,
    columns,
    sums,
):
    _, index_y, core = device_index()
    far_ref[...] = multiply(
        [
            (split_lanes(unfold(sent_coeff(ref))), weights_ref[FAR[0, step]])
            for step, ref in enumerate((x_ref, y_ref, xy_ref), 1)
        ]
    )
    low = low_lanes(8)
    for tile in range(LEAVES // 2):
        cols = slice(tile * LANES, tile * LANES + LANES)
        for axis in range(3):
            spread = jnp.broadcast_to(own_ref[64 + axis : 65 + axis, cols], (LANES, LANES))
            columns[axis, cols, :] = spread.T
    for block, ref in enumerate((own_ref, x_ref, y_ref, xy_ref)):
        for tile in range(LEAVES // 2):
            cols = slice(tile * LANES, tile * LANES + LANES)
            first = block * LEAVES + tile * 2
            values[first : first + 2] = split_rows(ref[:64, cols]).T.reshape(2, LEAF, LANES)
            point = ref[64:72, cols]
            rolled = pltpu.roll(point, HALF, 1)
            rows[first] = jnp.where(low, point, rolled)
            rows[first + 1] = jnp.where(low, rolled, point)

    def local(leaf, place):
        listed = listed_ref[leaf, place]
        owner = listed >> 4
        flip_x = (owner >> BITS_Y ^ core) & 1
        flip_y = (owner ^ index_y) & 1
        return (flip_x + 2 * flip_y) * LEAVES + (listed & LEAVES - 1)

    def one_leaf(leaf, carry):
        here = pl.ds(pl.multiple_of(leaf * LEAF, LEAF), LEAF)
        total = None
        for quad in range(3):
            ids = [local(leaf, quad * 4 + place) for place in range(4)]
            kernels = []
            for pair in range(2):
                source = jnp.where(low, rows[ids[pair * 2]], rows[ids[pair * 2 + 1]])
                square = None
                for axis in range(3):
                    delta = columns[axis, here, :] - source[axis : axis + 1]
                    square = delta * delta if square is None else square + delta * delta
                square = jnp.maximum(square, 1e-30)
                distance = square * lax.rsqrt(square)
                scale = ROOT_THREE / LENGTH_SCALE
                decay = jnp.exp2(distance * (-scale * LOG2_E))
                kernel = (distance * (AMPLITUDE * scale) + AMPLITUDE) * decay
                kernels.append(kernel.astype(BF16))
            weight = jnp.concatenate(kernels, axis=1)
            source_values = jnp.concatenate([values[n] for n in ids], axis=0)
            part = jnp.dot(weight, source_values, preferred_element_type=F32)
            total = part if total is None else total + part
        sums[here, :] = total
        return carry

    lax.fori_loop(0, LEAVES, one_leaf, 0, unroll=8)
    for tile in range(LEAVES // 2):
        cols = slice(tile * LANES, tile * LANES + LANES)
        flipped = sums[cols, :].T
        out_ref[:, cols] = flipped[:64] + flipped[64:] + NUGGET * own_ref[:64, cols]


def final_kernel(own_ref, other_ref, far_ref, weights_ref, near_ref, basis_ref, transfer_ref, out_ref):
    first = jnp.full((32, LANES), lax.axis_index("gx") & 1, jnp.int32) == 0
    own = unfold(own_ref[...])
    other = unfold(other_ref[...])
    above = jnp.concatenate([jnp.where(first, own, other), jnp.where(first, other, own)], axis=0)
    down = far_ref[...] + multiply([(split_lanes(above), weights_ref[DOWN[0, 0]])])
    down = down[:, :HALF].astype(BF16)
    for block in range(4):
        cols = slice(block * 256, block * 256 + 256)
        leaf_down = jnp.dot(down, transfer_ref[:, cols], preferred_element_type=F32).astype(BF16)
        far = jnp.dot(leaf_down, block_diagonal(basis_ref[:, cols]), preferred_element_type=F32)
        out_ref[:, cols] = near_ref[:, cols] + far


def call(kernel, out_shape, in_specs, scratch_shapes, *operands, limit=40, cost=None, out=VMEM):
    shapes = tuple(jax.ShapeDtypeStruct(shape, dtype) for shape, dtype in out_shape)
    return pl.pallas_call(
        kernel,
        out_shape=shapes,
        in_specs=in_specs,
        out_specs=(out,) * len(shapes),
        scratch_shapes=scratch_shapes,
        cost_estimate=cost,
        compiler_params=pltpu.CompilerParams(vmem_limit_bytes=limit * 1024 * 1024),
    )(*operands)


def exchange(value, name, group):
    return lax.all_to_all(
        value, name, split_axis=0, concat_axis=0, axis_index_groups=[group], tiled=True
    )


def body(
    right_sides,
    points,
    leaf_basis,
    leaf_transfer,
    upper_transfer,
    coupling,
    near_leaves,
    admissible,
):
    width = right_sides.shape[1]
    lifted, send = call(
        up_kernel,
        [((2 ** len(SOURCE) * 2, 16, LANES), F32), ((72, width), F32)],
        [pl.BlockSpec(memory_space=pltpu.HBM)] * 5,
        [
            pltpu.VMEM((64, width), F32),
            pltpu.VMEM((8, width), F32),
            pltpu.VMEM((2 ** len(SOURCE) * 2, 16, LANES), F32),
            pltpu.VMEM((3, width), F32),
            pltpu.VMEM((64, width), BF16),
            pltpu.VMEM((64, width), BF16),
            pltpu.VMEM((64, 64), F32),
            pltpu.SemaphoreType.DMA((8,)),
        ],
        right_sides,
        points,
        leaf_basis,
        leaf_transfer,
        upper_transfer,
        limit=60,
        out=pl.BlockSpec(memory_space=pltpu.HBM),
    )
    swap = [(i, i ^ 1) for i in range(2**BITS_X)]
    from_x = lax.ppermute(send, "gx", swap)
    from_y = lax.ppermute(send, "gy", [(j, j ^ 1) for j in range(2**BITS_Y)])
    gathered = exchange(lifted, "gx", GROUP_X)
    (weights,) = call(
        weights_kernel,
        [((WEIGHTS, 128, LANES), BF16)],
        [VMEM] * 2 + [SMEM],
        [],
        upper_transfer,
        coupling,
        admissible.T,
    )
    partial, tie = call(
        tree_kernel,
        [((2 ** len(TARGET), 16, LANES), F32), ((8, LANES), F32)],
        [VMEM] * 2,
        [pltpu.VMEM((2 ** len(TARGET), 16, LANES), F32)],
        gathered,
        weights,
        cost=pl.CostEstimate(flops=4 * 10**9, bytes_accessed=12 * 10**6, transcendentals=0),
    )
    parts = exchange(partial, "gy", GROUP_Y)
    from_xy = lax.ppermute(from_y, "gx", swap)
    near, far = call(
        near_kernel,
        [((64, width), F32), ((64, LANES), F32)],
        [SMEM] + [VMEM] * 6,
        [
            pltpu.VMEM((4 * LEAVES, LEAF, LANES), BF16),
            pltpu.VMEM((4 * LEAVES, 8, LANES), F32),
            pltpu.VMEM((3, width, LANES), F32),
            pltpu.VMEM((width, LANES), F32),
        ],
        near_leaves,
        send,
        from_x,
        from_y,
        from_xy,
        weights,
        tie,
    )
    (own,) = call(sum_kernel, [((16, LANES), F32)], [VMEM, ANYWHERE], [], parts, far)
    other = lax.ppermute(own, "gx", swap)
    (product,) = call(
        final_kernel,
        [((64, width), F32)],
        [VMEM] * 7,
        [],
        own,
        other,
        far,
        weights,
        near,
        leaf_basis,
        leaf_transfer,
    )
    return product


def solution(mesh):
    split = P(None, ("gx", "gy"))
    in_specs = (split, split, split, split, P(), P(), P(("gx", "gy"), None), P())
    return jax.shard_map(body, mesh=mesh, in_specs=in_specs, out_specs=split, check_vma=False)
```

```python
import itertools

import jax
import jax.numpy as jnp
from jax import lax
from jax.experimental import pallas as pl
from jax.experimental.pallas import tpu as pltpu
from jax.sharding import PartitionSpec as P

ROOT_THREE = 1.7320508075688772
LENGTH_SCALE = 0.6
AMPLITUDE = 0.25
NUGGET = 0.5
LOG2_E = 1.4426950408889634
BITS_X = 4
BITS_Y = 5
DEVICES = 512
LEVELS = 9
LEAVES = 16
LEAF = 64
RANK = 64
HALF = 64
LANES = 128
F32 = jnp.float32
BF16 = jnp.bfloat16
NT = (((1,), (1,)), ((), ()))
VMEM = pl.BlockSpec(memory_space=pltpu.VMEM)
ANYWHERE = pl.BlockSpec(memory_space=pl.ANY)
SMEM = pl.BlockSpec(memory_space=pltpu.SMEM)


def places():
    listed = []
    for bit in range(max(BITS_X, BITS_Y)):
        if bit < BITS_X:
            listed.append(("x", bit))
        if bit < BITS_Y:
            listed.append(("y", bit))
    return listed


PLACES = places()
SOURCE = (2, 4, 6)
TARGET = (1, 3, 5, 7, 8)
GROUP_X = [z * 2 + core for z in (7, 3, 6, 2, 5, 1, 4, 0) for core in (1, 0)]
GROUP_Y = [x * 8 + y for y in (3, 7, 1, 5, 2, 6, 4, 0) for x in (1, 3, 2, 0)]

CLIMB, DOWN, CLIMB2, DOWN2, FAR = {}, {}, {}, {}, {}
ODD = (1, 3, 5)
_slots = itertools.count()
for _h in ODD:
    CLIMB[_h, 0] = next(_slots)
    for _side in range(2):
        DOWN[_h, _side] = next(_slots)
        CLIMB2[_h, _side] = next(_slots)
        DOWN2[_h, _side] = next(_slots)
DOWN[0, 0] = next(_slots)
for _h in range(LEVELS - 1):
    for _step in (1, 2, 3):
        FAR[_h, _step] = next(_slots)
WEIGHTS = next(_slots)


def above(chosen, h):
    return [place for place in chosen if place >= h]


def flipped(chosen, h, step):
    listed = above(chosen, h)
    return sum(1 << listed.index(h + p) for p in (0, 1) if step >> p & 1 and h + p in listed)


def low_lanes(rows):
    return lax.broadcasted_iota(jnp.int32, (rows, LANES), 1) < HALF


def split_lanes(value):
    high = value.astype(BF16).astype(F32)
    return jnp.where(low_lanes(value.shape[0]), high, value - high).astype(BF16)


def split_rows(wide):
    high = wide.astype(BF16)
    return jnp.concatenate([high, (wide - high.astype(F32)).astype(BF16)], axis=0)


def block_diagonal(basis):
    wide = basis.astype(F32)
    leaf = lax.broadcasted_iota(jnp.int32, wide.shape, 1) // LEAF
    return jnp.concatenate([jnp.where(leaf == l, wide, 0.0).astype(BF16) for l in range(4)], axis=0)


def up_kernel(
    right_ref,
    points_ref,
    basis_ref,
    transfer_ref,
    upper_ref,
    lifted_ref,
    send_ref,
    points_in,
    basis_in,
    transfer_in,
    upper_in,
    sems,
):
    copies = [
        pltpu.make_async_copy(right_ref, send_ref.at[pl.ds(0, 64)], sems.at[0]),
        pltpu.make_async_copy(basis_ref, basis_in, sems.at[1]),
        pltpu.make_async_copy(transfer_ref, transfer_in, sems.at[2]),
        pltpu.make_async_copy(points_ref, points_in, sems.at[3]),
        pltpu.make_async_copy(upper_ref.at[0, lax.axis_index("gx") & 1], upper_in, sems.at[4]),
    ]
    for copy in copies:
        copy.start()
    copies[1].wait()
    diagonals = [block_diagonal(basis_in[:, b * 256 : b * 256 + 256]) for b in range(4)]
    copies[0].wait()
    leaf_coeffs = [
        lax.dot_general(
            send_ref[:64, b * 256 : b * 256 + 256].astype(BF16),
            diagonals[b],
            NT,
            preferred_element_type=F32,
        ).astype(BF16)
        for b in range(4)
    ]
    for copy in copies[2:]:
        copy.wait()
    total = None
    for block in range(4):
        transfer = transfer_in[:, block * 256 : block * 256 + 256]
        part = lax.dot_general(
            leaf_coeffs[block],
            jnp.concatenate([transfer, transfer], axis=0),
            NT,
            preferred_element_type=F32,
        )
        total = part if total is None else total + part
    matrix = upper_in[...]
    wide = split_rows(jnp.concatenate([matrix, matrix], axis=1))
    lifted = multiply([(split_lanes(total), wide)])
    halves = [fold(lifted[:32]), fold(lifted[32:])]
    for target in range(lifted_ref.shape[0]):
        lifted_ref[target] = halves[GROUP_X[target] % 2]
    send_ref[64:67, :] = points_in[...]
    packed = fold(total)
    for tile in range(8):
        cols = slice(tile * LANES, tile * LANES + LANES)
        send_ref[67:71, cols] = packed[tile * 4 : tile * 4 + 4]
    send_ref[71:72, :] = jnp.zeros((1, LEAVES * LEAF), F32)


def as_nodes(value):
    return [value[row : row + 32] for row in range(0, value.shape[0], 32)]


def device_index():
    index_x = lax.axis_index("gx")
    return index_x, lax.axis_index("gy"), index_x & 1


def device_sides():
    index_x, index_y, _ = device_index()
    return [(index_x if axis == "x" else index_y) >> bit & 1 for axis, bit in PLACES]


def place_index(sides, listed):
    index = jnp.int32(0)
    for bit, place in enumerate(listed):
        index = index + sides[place] * 2**bit
    return index


def sent_coeff(ref):
    return jnp.concatenate(
        [ref[67:71, tile * LANES : tile * LANES + LANES] for tile in range(8)], axis=0
    )


def fold(value):
    rows = value.shape[0] // 2
    return jnp.where(low_lanes(rows), value[:rows], value[rows:])


def unfold(packed):
    low = low_lanes(packed.shape[0])
    rolled = pltpu.roll(packed, HALF, 1)
    return jnp.concatenate(
        [jnp.where(low, packed, rolled), jnp.where(low, rolled, packed)], axis=0
    )


def multiply(pairs):
    left = [piece for value, _ in pairs for piece in (value, value)]
    right = [piece for _, m in pairs for piece in (m[:64], m[:64], m[64:], m[64:])]
    return jnp.dot(
        jnp.concatenate(left, axis=1),
        jnp.concatenate(right, axis=0),
        preferred_element_type=F32,
    )


def weights_kernel(upper_ref, coupling_ref, admissible_ref, out_ref):
    sides = device_sides()
    code = place_index(sides, range(LEVELS))

    def plain(matrix):
        return jnp.concatenate([matrix, matrix], axis=1)

    def transposed(matrix):
        return jnp.concatenate([matrix, matrix], axis=0).T

    out_ref[DOWN[0, 0]] = split_rows(transposed(upper_ref[0, sides[0]]))
    for h in ODD:
        low = [upper_ref[h, sides[h] ^ side] for side in range(2)]
        high = [split_rows(plain(upper_ref[h + 1, sides[h + 1] ^ side])) for side in range(2)]
        own = split_lanes(plain(low[0]))
        both = [multiply([(own, matrix)]) for matrix in high]
        turned = multiply([(split_lanes(plain(low[1])), high[0])])
        out_ref[CLIMB[h, 0]] = split_rows(plain(low[0]))
        for side in range(2):
            out_ref[DOWN[h, side]] = split_rows(transposed(low[side]))
            out_ref[CLIMB2[h, side]] = split_rows(both[side])
        out_ref[DOWN2[h, 0]] = split_rows(transposed(both[0][:, :HALF]))
        out_ref[DOWN2[h, 1]] = split_rows(transposed(turned[:, :HALF]))
    for h in range(LEVELS - 1):
        first = 2 * DEVICES - 2 * DEVICES // 2**h
        for step in (1, 2, 3):
            turned = sum(1 << p for p in (0, 1) if step >> p & 1 and h + p in TARGET)
            target = (code >> h) ^ (turned if h else 0)
            here = target & 3
            there = here ^ step
            matrix = coupling_ref[h, jnp.abs(there - here) - 1]
            flag = admissible_ref[step - 1, first + target].astype(F32)
            upward = jnp.full((64, LANES), there - here, jnp.int32) > 0
            chosen = jnp.where(upward, transposed(matrix), plain(matrix))
            out_ref[FAR[h, step]] = split_rows(chosen * flag)


def tree_kernel(gathered_ref, weights_ref, out_ref, tie_ref, downs):
    sides = device_sides()
    own_source = place_index(sides, SOURCE)
    own_target = place_index(sides, TARGET)
    nodes = []
    for relative in range(2 ** len(SOURCE)):
        far_z = own_source ^ relative ^ 7
        first = (far_z & 3) * 4 + (far_z >> 2) * 2
        nodes.append(split_lanes(unfold(gathered_ref[first] + gathered_ref[first + 1])))
    levels = {1: nodes}
    for h in ODD:
        pairs = [
            (jnp.concatenate(nodes[bit::2], axis=0), weights_ref[CLIMB2[h, bit]])
            for bit in range(2)
        ]
        single = multiply([(jnp.concatenate(nodes, axis=0), weights_ref[CLIMB[h, 0]])])
        levels[h + 1] = as_nodes(split_lanes(single))
        nodes = as_nodes(split_lanes(multiply(pairs)))
        levels[h + 2] = nodes

    def coupled(h):
        terms = {}
        for step in (1, 2, 3):
            pair = levels[h][flipped(SOURCE, h, step)], weights_ref[FAR[h, step]]
            terms.setdefault(flipped(TARGET, h, step), []).append(pair)
        return {turned: multiply(pairs) for turned, pairs in terms.items()}

    far = coupled(LEVELS - 2)
    zero = jnp.zeros((32, LANES), F32)
    down = [far.get(n, zero) for n in range(2 ** len(above(TARGET, LEVELS - 2)))]
    for h in reversed(ODD):
        value = split_lanes(jnp.concatenate(down, axis=0))
        between = coupled(h + 1)
        extra = split_lanes(jnp.concatenate([between[0], between[1]], axis=0))
        parts = [as_nodes(multiply([(value, weights_ref[DOWN2[h, bit]])])) for bit in range(2)]
        down = [part for group in zip(*parts) for part in group]
        for bit in range(2):
            for parent, part in enumerate(as_nodes(multiply([(extra, weights_ref[DOWN[h, bit]])]))):
                down[2 * parent + bit] = down[2 * parent + bit] + part
        for turned, part in coupled(h).items():
            down[turned] = down[turned] + part
    for relative, part in enumerate(down):
        downs[relative] = fold(part)
    for member, node in enumerate(GROUP_Y):
        out_ref[member] = downs[own_target ^ node]
    tie_ref[...] = jnp.zeros_like(tie_ref)


def sum_kernel(parts_ref, tie_ref, out_ref):
    total = parts_ref[0]
    for source in range(1, parts_ref.shape[0]):
        total = total + parts_ref[source]
    out_ref[...] = total


def near_kernel(
    listed_ref,
    own_ref,
    x_ref,
    y_ref,
    xy_ref,
    weights_ref,
    tie_ref,
    out_ref,
    far_ref,
    values,
    rows,
    columns,
    sums,
):
    _, index_y, core = device_index()
    far_ref[...] = multiply(
        [
            (split_lanes(unfold(sent_coeff(ref))), weights_ref[FAR[0, step]])
            for step, ref in enumerate((x_ref, y_ref, xy_ref), 1)
        ]
    )
    low = low_lanes(8)
    for tile in range(LEAVES // 2):
        cols = slice(tile * LANES, tile * LANES + LANES)
        for axis in range(3):
            spread = jnp.broadcast_to(own_ref[64 + axis : 65 + axis, cols], (LANES, LANES))
            columns[axis, cols, :] = spread.T
    for block, ref in enumerate((own_ref, x_ref, y_ref, xy_ref)):
        for tile in range(LEAVES // 2):
            cols = slice(tile * LANES, tile * LANES + LANES)
            first = block * LEAVES + tile * 2
            values[first : first + 2] = split_rows(ref[:64, cols]).T.reshape(2, LEAF, LANES)
            point = ref[64:72, cols]
            rolled = pltpu.roll(point, HALF, 1)
            rows[first] = jnp.where(low, point, rolled)
            rows[first + 1] = jnp.where(low, rolled, point)

    def local(leaf, place):
        listed = listed_ref[leaf, place]
        owner = listed >> 4
        flip_x = (owner >> BITS_Y ^ core) & 1
        flip_y = (owner ^ index_y) & 1
        return (flip_x + 2 * flip_y) * LEAVES + (listed & LEAVES - 1)

    def one_leaf(leaf, carry):
        here = pl.ds(pl.multiple_of(leaf * LEAF, LEAF), LEAF)
        total = None
        for quad in range(3):
            ids = [local(leaf, quad * 4 + place) for place in range(4)]
            kernels = []
            for pair in range(2):
                source = jnp.where(low, rows[ids[pair * 2]], rows[ids[pair * 2 + 1]])
                square = None
                for axis in range(3):
                    delta = columns[axis, here, :] - source[axis : axis + 1]
                    square = delta * delta if square is None else square + delta * delta
                square = jnp.maximum(square, 1e-30)
                distance = square * lax.rsqrt(square)
                scale = ROOT_THREE / LENGTH_SCALE
                decay = jnp.exp2(distance * (-scale * LOG2_E))
                kernel = (distance * (AMPLITUDE * scale) + AMPLITUDE) * decay
                kernels.append(kernel.astype(BF16))
            weight = jnp.concatenate(kernels, axis=1)
            source_values = jnp.concatenate([values[n] for n in ids], axis=0)
            part = jnp.dot(weight, source_values, preferred_element_type=F32)
            total = part if total is None else total + part
        sums[here, :] = total
        return carry

    lax.fori_loop(0, LEAVES, one_leaf, 0, unroll=16)
    for tile in range(LEAVES // 2):
        cols = slice(tile * LANES, tile * LANES + LANES)
        flipped = sums[cols, :].T
        out_ref[:, cols] = flipped[:64] + flipped[64:] + NUGGET * own_ref[:64, cols]


def final_kernel(own_ref, other_ref, far_ref, weights_ref, near_ref, basis_ref, transfer_ref, out_ref):
    first = jnp.full((32, LANES), lax.axis_index("gx") & 1, jnp.int32) == 0
    own = unfold(own_ref[...])
    other = unfold(other_ref[...])
    above = jnp.concatenate([jnp.where(first, own, other), jnp.where(first, other, own)], axis=0)
    down = far_ref[...] + multiply([(split_lanes(above), weights_ref[DOWN[0, 0]])])
    down = down[:, :HALF].astype(BF16)
    for block in range(4):
        cols = slice(block * 256, block * 256 + 256)
        leaf_down = jnp.dot(down, transfer_ref[:, cols], preferred_element_type=F32).astype(BF16)
        far = jnp.dot(leaf_down, block_diagonal(basis_ref[:, cols]), preferred_element_type=F32)
        out_ref[:, cols] = near_ref[:, cols] + far


def call(kernel, out_shape, in_specs, scratch_shapes, *operands, limit=40, cost=None):
    shapes = tuple(jax.ShapeDtypeStruct(shape, dtype) for shape, dtype in out_shape)
    return pl.pallas_call(
        kernel,
        out_shape=shapes,
        in_specs=in_specs,
        out_specs=(VMEM,) * len(shapes),
        scratch_shapes=scratch_shapes,
        cost_estimate=cost,
        compiler_params=pltpu.CompilerParams(vmem_limit_bytes=limit * 1024 * 1024),
    )(*operands)


def exchange(value, name, group):
    return lax.all_to_all(
        value, name, split_axis=0, concat_axis=0, axis_index_groups=[group], tiled=True
    )


def body(
    right_sides,
    points,
    leaf_basis,
    leaf_transfer,
    upper_transfer,
    coupling,
    near_leaves,
    admissible,
):
    width = right_sides.shape[1]
    lifted, send = call(
        up_kernel,
        [((2 ** len(SOURCE) * 2, 16, LANES), F32), ((72, width), F32)],
        [pl.BlockSpec(memory_space=pltpu.HBM)] * 5,
        [
            pltpu.VMEM((3, width), F32),
            pltpu.VMEM((64, width), BF16),
            pltpu.VMEM((64, width), BF16),
            pltpu.VMEM((64, 64), F32),
            pltpu.SemaphoreType.DMA((5,)),
        ],
        right_sides,
        points,
        leaf_basis,
        leaf_transfer,
        upper_transfer,
        limit=60,
    )
    swap = [(i, i ^ 1) for i in range(2**BITS_X)]
    from_x = lax.ppermute(send, "gx", swap)
    from_y = lax.ppermute(send, "gy", [(j, j ^ 1) for j in range(2**BITS_Y)])
    gathered = exchange(lifted, "gx", GROUP_X)
    (weights,) = call(
        weights_kernel,
        [((WEIGHTS, 128, LANES), BF16)],
        [VMEM] * 2 + [SMEM],
        [],
        upper_transfer,
        coupling,
        admissible.T,
    )
    partial, tie = call(
        tree_kernel,
        [((2 ** len(TARGET), 16, LANES), F32), ((8, LANES), F32)],
        [VMEM] * 2,
        [pltpu.VMEM((2 ** len(TARGET), 16, LANES), F32)],
        gathered,
        weights,
        cost=pl.CostEstimate(flops=4 * 10**9, bytes_accessed=12 * 10**6, transcendentals=0),
    )
    parts = exchange(partial, "gy", GROUP_Y)
    from_xy = lax.ppermute(from_y, "gx", swap)
    near, far = call(
        near_kernel,
        [((64, width), F32), ((64, LANES), F32)],
        [SMEM] + [VMEM] * 6,
        [
            pltpu.VMEM((4 * LEAVES, LEAF, LANES), BF16),
            pltpu.VMEM((4 * LEAVES, 8, LANES), F32),
            pltpu.VMEM((3, width, LANES), F32),
            pltpu.VMEM((width, LANES), F32),
        ],
        near_leaves,
        send,
        from_x,
        from_y,
        from_xy,
        weights,
        tie,
    )
    (own,) = call(sum_kernel, [((16, LANES), F32)], [VMEM, ANYWHERE], [], parts, far)
    other = lax.ppermute(own, "gx", swap)
    (product,) = call(
        final_kernel,
        [((64, width), F32)],
        [VMEM] * 7,
        [],
        own,
        other,
        far,
        weights,
        near,
        leaf_basis,
        leaf_transfer,
    )
    return product


def solution(mesh):
    split = P(None, ("gx", "gy"))
    in_specs = (split, split, split, split, P(), P(), P(("gx", "gy"), None), P())
    return jax.shard_map(body, mesh=mesh, in_specs=in_specs, out_specs=split, check_vma=False)
```
